128 devices in a mesh: fsdp: 16 (over x, y), ctx: 4 (over z_lo, core), tp: 2 (over z_hi).
Axes of the slice: x: 4, y: 4, z: 4 (z_hi: 2, z_lo: 2; z = z_hi * 2 + z_lo), core: 2. Of those that a mesh axis runs over, the one named last changes fastest.
Arguments:
- tokens: bfloat16 [32, 512, 1536], P('fsdp', 'ctx'), may hold values from -6 to 6
- text: bfloat16 [32, 512, 1536], P('fsdp', 'ctx'), may hold values from -6 to 6
- time_embedding: float32 [32, 6, 1536], P('fsdp'), may hold values from -5 to 5
- positions: int32 [3, 32, 512], P(None, 'fsdp', 'ctx'), may hold values from 0 to 15, as said below
- cotangent: bfloat16 [32, 512, 1536], P('fsdp', 'ctx'), may hold values from -6 to 6
- attn_in: float32 [1536, 6, 1536], P(('fsdp', 'ctx'), None, 'tp'), may hold values from -0.15625 to 0.15625
- attn_out: float32 [1536, 2, 1536], P(('fsdp', 'ctx'), None, 'tp'), may hold values from -1.25 to 1.25
- mlp: float32 [1536, 2, 8960], P(('fsdp', 'ctx'), None, 'tp'), may hold values from -0.09375 to 0.09375
- head_vectors: float32 [10, 1536], P(None, 'tp'), may hold values from -1.2 to 1.2
- model_vectors: float32 [11, 1536], replicated, may hold values from -1.2 to 1.2
- up_bias: float32 [8960], P('tp'), may hold values from -0.6 to 0.6
- attn_in_moment: float32 [1536, 6, 1536], P(('fsdp', 'ctx'), None, 'tp'), may hold values from -80 to 80
- attn_out_moment: float32 [1536, 2, 1536], P(('fsdp', 'ctx'), None, 'tp'), may hold values from -80 to 80
- mlp_moment: float32 [1536, 2, 8960], P(('fsdp', 'ctx'), None, 'tp'), may hold values from -80 to 80
- head_moment: float32 [10, 1536], P(None, 'tp'), may hold values from -160 to 160
- model_moment: float32 [11, 1536], replicated, may hold values from -384 to 384
- up_moment: float32 [8960], P('tp'), may hold values from -80 to 80
Outputs:
- layer_out: bfloat16 [32, 512, 1536], P('fsdp', 'ctx')
- grad_tokens: float32 [32, 512, 1536], P('fsdp', 'ctx')
- grad_text: float32 [32, 512, 1536], P('fsdp', 'ctx')
- grad_time: float32 [32, 6, 1536], P('fsdp')
- new_attn_in: float32 [1536, 6, 1536], P(('fsdp', 'ctx'), None, 'tp')
- new_attn_out: float32 [1536, 2, 1536], P(('fsdp', 'ctx'), None, 'tp')
- new_mlp: float32 [1536, 2, 8960], P(('fsdp', 'ctx'), None, 'tp')
- new_attn_in_moment: float32 [1536, 6, 1536], P(('fsdp', 'ctx'), None, 'tp')
- new_attn_out_moment: float32 [1536, 2, 1536], P(('fsdp', 'ctx'), None, 'tp')
- new_mlp_moment: float32 [1536, 2, 8960], P(('fsdp', 'ctx'), None, 'tp')
- new_head_vectors: float32 [10, 1536], P(None, 'tp')
- new_model_vectors: float32 [11, 1536], replicated
- new_up_bias: float32 [8960], P('tp')
- new_head_moment: float32 [10, 1536], P(None, 'tp')
- new_model_moment: float32 [11, 1536], replicated
- new_up_moment: float32 [8960], P('tp')
The draws below stay inside these ranges and needn't reach their ends.
Inputs may be any that keep to these rules, and one draw needn't show every extreme that they name: `positions`: within each clip the 512 tokens take distinct places numbered 0 to 511 in a random order; a place n has frame n // 256, row (n // 16) % 16 and column n % 16.
All inputs are finite; a program needn't handle non-finite values.
Results may differ from the reference program's by a relative error of at most 0.015.
Values may be sent and summed in bfloat16 or wider, within the bound.
A program may use at most 704 MiB of HBM per device.

```python
import math
from functools import partial
import jax
import jax.numpy as jnp
from jax import lax

D = 1536
FF = 8960
HEAD = 128
TEXT = 512
MUON_ROWS = 24
NS_STEPS = 5
SEQ = 512
CLIPS = 32


def draw_positions(key, part):
    key = jax.random.fold_in(key, 3)
    clip_keys = jax.random.split(key, CLIPS)
    shuffled = jax.vmap(jax.random.permutation, in_axes=(0, None))(clip_keys, SEQ).astype(jnp.int32)
    return jnp.stack([shuffled // 256, shuffled // 16 % 16, shuffled % 16]).astype(jnp.int32)


def block_scale(rng, dims, pieces, least, largest):
    loudness, own = 1.0, jax.random.fold_in(rng, 6)
    for dim, blocks in pieces:
        draws = jnp.exp(jax.random.uniform(jax.random.fold_in(own, dim), (blocks,), jnp.float32, least / len(pieces), largest / len(pieces)))
        loudness = loudness * jnp.repeat(draws, dims[dim] // blocks).reshape([-1 if axis == dim else 1 for axis in range(len(dims))])
    return loudness


def scatter_about(stream_key, shape, width, most, cuts=(), held_as=jnp.bfloat16):
    array = jax.random.normal(stream_key, shape, jnp.float32) * width
    if len(cuts) > 0:
        array = block_scale(stream_key, shape, cuts, -0.22, 0.18) * array
    return jnp.clip(array, min=-most, max=most).astype(held_as)


def setup_inputs(seed: int = 0) -> dict:
    splits = jax.random.split(jax.random.key(seed), 18)
    return {
        "tokens": scatter_about(splits[0], (CLIPS, SEQ, D), 1.0, 6.0, ((0, 16), (1, 4))),
        "text": scatter_about(splits[1], (CLIPS, TEXT, D), 1.0, 6.0, ((0, 16), (1, 4))),
        "time_embedding": scatter_about(splits[2], (CLIPS, 6, D), 0.7, 5.0, ((0, 16),), jnp.float32),
        "positions": draw_positions(jax.random.fold_in(splits[17], 71), 0),
        "cotangent": scatter_about(splits[4], (CLIPS, SEQ, D), 1.0, 6.0, ((0, 16), (1, 4))),
        "attn_in": scatter_about(splits[5], (D, 6, D), D ** -0.5, 0.15625, ((0, 64), (2, 2)), jnp.float32),
        "attn_out": scatter_about(splits[6], (D, 2, D), (D // 64) ** -0.5, 1.25, ((0, 64), (2, 2)), jnp.float32),
        "mlp": scatter_about(splits[7], (D, 2, FF), (3 * D) ** -0.5, 0.09375, ((0, 64), (2, 2)), jnp.float32),
        "head_vectors": scatter_about(splits[8], (10, D), 0.2, 1.2, ((1, 2),), jnp.float32),
        "model_vectors": scatter_about(splits[9], (11, D), 0.2, 1.2, (), jnp.float32),
        "up_bias": scatter_about(splits[10], (FF,), 0.1, 0.6, ((0, 2),), jnp.float32),
        "attn_in_moment": scatter_about(splits[11], (D, 6, D), (0.1 * (CLIPS * SEQ) ** 0.5), 80.0, ((0, 64), (2, 2)), jnp.float32),
        "attn_out_moment": scatter_about(splits[12], (D, 2, D), (0.1 * (CLIPS * SEQ) ** 0.5), 80.0, ((0, 64), (2, 2)), jnp.float32),
        "mlp_moment": scatter_about(splits[13], (D, 2, FF), (0.1 * (CLIPS * SEQ) ** 0.5), 80.0, ((0, 64), (2, 2)), jnp.float32),
        "head_moment": scatter_about(splits[14], (10, D), (0.2 * (CLIPS * SEQ) ** 0.5), 160.0, ((1, 2),), jnp.float32),
        "model_moment": scatter_about(splits[15], (11, D), (0.5 * (CLIPS * SEQ) ** 0.5), 384.0, (), jnp.float32),
        "up_moment": scatter_about(splits[16], (FF,), (0.1 * (CLIPS * SEQ) ** 0.5), 80.0, ((0, 2),), jnp.float32),
    }


@jax.custom_vjp
def low(v):
    return lax.optimization_barrier(v.astype(jnp.bfloat16)).astype(jnp.float32)

@jax.custom_vjp
def low_back(v):
    return v

def low_keep(v):
    return (low(v), None)

def low_pass(kept, grad):
    return (grad,)

def back_keep(v):
    return (v, None)

def back_low(kept, grad):
    return (low(grad),)
low.defvjp(low_keep, low_pass)
low_back.defvjp(back_keep, back_low)
NORM_EPSILON = 1e-06
ORTHO_EPSILON = 1e-07
HIGHEST_PRECISION = lax.Precision.HIGHEST
NEWTON_FIRST = 3.4445
NEWTON_SECOND = -4.775
NEWTON_THIRD = 2.0315
MOMENTUM = 0.9
DECAY = 0.01
RATE_IN = 0.5
RATE_OUT = 4.0
RATE_MLP = 1.0
RATE_VECTOR = 0.005

def rope_tables(places):
    pair_index = jnp.arange(HEAD // 2, dtype=jnp.int32)
    side_pairs = HEAD // 6
    frame_pairs = (HEAD - 4 * side_pairs) // 2
    part_of = (pair_index >= frame_pairs).astype(jnp.int32) + (pair_index >= frame_pairs + side_pairs).astype(jnp.int32)
    offset = jnp.where(part_of == 0, 0, jnp.where(part_of == 1, frame_pairs, frame_pairs + side_pairs)).astype(jnp.int32)
    extent = jnp.where(part_of == 0, 2 * frame_pairs, 2 * side_pairs).astype(jnp.float32)
    frequency = jnp.exp((pair_index - offset).astype(jnp.float32) * (-2.0 * math.log(10000.0)) / extent)
    chosen = places[0][:, None] * (part_of == 0) + places[1][:, None] * (part_of == 1) + places[2][:, None] * (part_of == 2)
    angles = chosen.astype(jnp.float32) * frequency
    return (jnp.cos(angles), jnp.sin(angles))

def rotate(values, cosine, sine):
    half_head = HEAD // 2
    front_half = values[..., :half_head]
    back_half = values[..., half_head:]
    return jnp.concatenate([front_half * cosine - back_half * sine, back_half * cosine + front_half * sine], -1)

def plain_norm(values):
    centred = values - lax.optimization_barrier(jnp.mean(values, -1, keepdims=True))
    return centred * lax.rsqrt(lax.optimization_barrier(jnp.mean(centred * centred, -1, keepdims=True)) + NORM_EPSILON)

def root_norm(values, gain):
    return values * lax.rsqrt(lax.optimization_barrier(jnp.mean(values * values, -1, keepdims=True)) + NORM_EPSILON) * (1.0 + gain)

def split_heads(values):
    return values.reshape(values.shape[0], -1, HEAD)

def attention(query, keys, values):
    scores = low_back(jnp.einsum('qhe,khe->hqk', query, keys, precision=HIGHEST_PRECISION) * HEAD ** (-0.5))
    softmax_weights = low(jax.nn.softmax(scores, axis=-1))
    mixed = jnp.einsum('hqk,khe->qhe', softmax_weights, values, precision=HIGHEST_PRECISION)
    return mixed.reshape(mixed.shape[0], -1)

def matmul(left, right):
    return jnp.dot(left, right, precision=HIGHEST_PRECISION)

def clip_layer(weights, clip):
    attn_in, attn_out, mlp, head_vectors, model_vectors, up_bias = weights
    residual, words, modulation_row, places = clip
    modulation = model_vectors[5:] + modulation_row
    cosine, sine = rope_tables(places)
    cosine = cosine[:, None, :]
    sine = sine[:, None, :]
    input_one = low(plain_norm(residual) * (1.0 + modulation[1]) + modulation[0])
    query = low_back(matmul(input_one, attn_in[:, 0]) + head_vectors[0])
    key_lin = low_back(matmul(input_one, attn_in[:, 1]) + head_vectors[1])
    value_lin = low_back(matmul(input_one, attn_in[:, 2]) + head_vectors[2])
    query_rot = low(rotate(split_heads(root_norm(query, head_vectors[3])), cosine, sine))
    key_rot = low(rotate(split_heads(root_norm(key_lin, head_vectors[4])), cosine, sine))
    value_low = low(split_heads(value_lin))
    mixed = low(low_back(attention(query_rot, key_rot, value_low)))
    branch_one = low_back(matmul(mixed, attn_out[:, 0].T) + model_vectors[0])
    after_one = residual + modulation[2] * branch_one
    input_three = low(plain_norm(after_one) * (1.0 + model_vectors[3]) + model_vectors[4])
    query_two = low_back(matmul(input_three, attn_in[:, 3]) + head_vectors[5])
    key_two = low_back(matmul(words, attn_in[:, 4]) + head_vectors[6])
    value_two = low_back(matmul(words, attn_in[:, 5]) + head_vectors[7])
    query_two = low(split_heads(root_norm(query_two, head_vectors[8])))
    key_two = low(split_heads(root_norm(key_two, head_vectors[9])))
    value_two = low(split_heads(value_two))
    mixed_two = low(low_back(attention(query_two, key_two, value_two)))
    branch_two = low_back(matmul(mixed_two, attn_out[:, 1].T) + model_vectors[1])
    after_two = after_one + branch_two
    input_mlp = low(plain_norm(after_two) * (1.0 + modulation[4]) + modulation[3])
    hidden_lin = low_back(matmul(input_mlp, mlp[:, 0]) + up_bias)
    hidden_low = low(jax.nn.gelu(hidden_lin, approximate=True))
    branch_mlp = low_back(matmul(hidden_low, mlp[:, 1].T) + model_vectors[2])
    return after_two + modulation[5] * branch_mlp

def orthogonalize(moment):
    blocks = moment.reshape(moment.shape[0] // MUON_ROWS, MUON_ROWS, moment.shape[1], moment.shape[2])
    block_norms = jnp.sqrt(lax.optimization_barrier(jnp.sum(blocks * blocks, axis=(1, 3), keepdims=True)))
    current = blocks / (block_norms + ORTHO_EPSILON)
    for newton_turn in range(NS_STEPS):
        gram_matrix = jnp.einsum('bikc,bjkc->bkij', current, current, precision=HIGHEST_PRECISION)
        square = jnp.einsum('bkij,bkjl->bkil', gram_matrix, gram_matrix, precision=HIGHEST_PRECISION)
        polynomial = NEWTON_SECOND * gram_matrix + NEWTON_THIRD * square
        current = NEWTON_FIRST * current + jnp.einsum('bkij,bjkc->bikc', polynomial, current, precision=HIGHEST_PRECISION)
    return current.reshape(moment.shape)

def reference(tokens, text, time_embedding, positions, cotangent, attn_in, attn_out, mlp, head_vectors, model_vectors, up_bias, attn_in_moment, attn_out_moment, mlp_moment, head_moment, model_moment, up_moment):

    def forward(tokens_f, text_f, time_f, attn_in_f, attn_out_f, mlp_f, head_f, model_f, up_f):
        weights = (low(attn_in_f), low(attn_out_f), low(mlp_f), head_f, model_f, up_f)
        layer = jax.checkpoint(partial(clip_layer, weights))
        return lax.map(layer, (tokens_f, text_f, time_f, jnp.moveaxis(positions, 1, 0)))
    result, pullback = jax.vjp(forward, tokens.astype(jnp.float32), text.astype(jnp.float32), time_embedding, attn_in, attn_out, mlp, head_vectors, model_vectors, up_bias)
    grads = pullback(cotangent.astype(jnp.float32))
    grad_tokens, grad_text, grad_time, grad_in, grad_out, grad_mlp, grad_head, grad_model, grad_up = grads
    new_in_moment = MOMENTUM * attn_in_moment + grad_in
    new_out_moment = MOMENTUM * attn_out_moment + grad_out
    new_mlp_moment = MOMENTUM * mlp_moment + grad_mlp
    new_attn_in = attn_in * (1.0 - RATE_IN * DECAY) - RATE_IN * orthogonalize(new_in_moment)
    new_attn_out = attn_out * (1.0 - RATE_OUT * DECAY) - RATE_OUT * orthogonalize(new_out_moment)
    new_mlp = mlp * (1.0 - RATE_MLP * DECAY) - RATE_MLP * orthogonalize(new_mlp_moment)
    new_head_moment = MOMENTUM * head_moment + grad_head
    new_model_moment = MOMENTUM * model_moment + grad_model
    new_up_moment = MOMENTUM * up_moment + grad_up
    new_head = head_vectors - RATE_VECTOR * new_head_moment
    new_model = model_vectors - RATE_VECTOR * new_model_moment
    new_up = up_bias - RATE_VECTOR * new_up_moment
    return (result.astype(jnp.bfloat16), grad_tokens, grad_text, grad_time, new_attn_in, new_attn_out, new_mlp, new_in_moment, new_out_moment, new_mlp_moment, new_head, new_model, new_up, new_head_moment, new_model_moment, new_up_moment)
```

```python
from functools import partial
import math

import jax
import jax.numpy as jnp
from jax import lax
from jax.experimental import pallas as pl
from jax.experimental.pallas import tpu as pltpu
from jax.sharding import PartitionSpec as P

D = 1536
HEAD = 128
ROWS = 24
HEADS = 3
NORM_EPSILON = 1e-06
ORTHO_EPSILON = 1e-07
NEWTON_FIRST = 3.4445
NEWTON_SECOND = -4.775
NEWTON_THIRD = 2.0315
NS_STEPS = 5
MOMENTUM = 0.9
DECAY = 0.01
RATE_IN = 0.5
RATE_OUT = 4.0
RATE_MLP = 1.0
RATE_VECTOR = 0.005
HIGHEST = lax.Precision.HIGHEST

MESH = pl.DeviceIdType.MESH
BF = jnp.bfloat16
F32 = jnp.float32

SIDE = 4
TOK = 128
SEQ = SIDE * TOK
HW = HEADS * HEAD
FF_REAL = 2240
FF = 2304
C_IN, C_OUT, C_UP, C_DOWN = 0, 6 * HW, 8 * HW, 8 * HW + FF
COLS = 8 * HW + 2 * FF
HALF = COLS // 2
QUARTER = HALF // 2
PAIR = 2 * ROWS
VMEM_LIMIT = 60 * 1024 * 1024


def here():
    f = lax.axis_index("fsdp")
    c = lax.axis_index("ctx")
    t = lax.axis_index("tp")
    x, y = lax.div(f, SIDE), lax.rem(f, SIDE)
    zl, core = lax.div(c, 2), lax.rem(c, 2)
    return x, y, 2 * t + zl, core


def chip(x, y, z, core):
    x, y, z = lax.rem(x + SIDE, SIDE), lax.rem(y + SIDE, SIDE), lax.rem(z + SIDE, SIDE)
    return {"fsdp": x * SIDE + y, "ctx": lax.rem(z, 2) * 2 + core, "tp": lax.div(z, 2)}


def block_of(z):
    z = lax.rem(z + SIDE, SIDE)
    return 2 * lax.rem(z, 2) + lax.div(z, 2)


def greet(devices):
    barrier = pltpu.get_barrier_semaphore()
    for device in devices:
        pl.semaphore_signal(barrier, inc=1, device_id=device, device_id_type=MESH)
    pl.semaphore_wait(barrier, len(devices))


def column(x, y, z, core):
    return [chip(x, y, z + k, core) for k in (1, 2, 3)] + [
        chip(x, y, z + k, 1 - core) for k in range(4)
    ]


def remote(src, dst, send, recv, device):
    return pltpu.make_async_remote_copy(
        src_ref=src, dst_ref=dst, send_sem=send, recv_sem=recv, device_id=device, device_id_type=MESH
    )


def params(cid):
    return pltpu.CompilerParams(
        collective_id=cid, has_side_effects=True, vmem_limit_bytes=VMEM_LIMIT
    )


VM = pl.BlockSpec(memory_space=pltpu.VMEM)
HB = pl.BlockSpec(memory_space=pltpu.HBM)


def gather_kernel(
    wsend, tok, txt, cot, pos, wg, tok_all, txt_all, cot_all, pos_all,
    wrecv, own, wx_s, wx_r, ac_s, ac_r, loc, xs, xr, ks, kr,
):
    x, y, z, core = here()
    zl = lax.rem(z, 2)
    mine = x * SIDE + y
    greet(
        [chip(x + 1, y, z, core), chip(x - 1, y, z, core), chip(x, y + 1, z, core), chip(x, y - 1, z, core)]
        + column(x, y, z, core)
    )
    other = z + 1 - 2 * zl
    away = remote(
        wsend.at[1 - zl], wrecv.at[core], wx_s.at[0], wx_r.at[core], chip(x, y, other, zl)
    )
    away.start()
    near = remote(wsend.at[zl], wrecv.at[core], wx_s.at[1], wx_r.at[core], chip(x, y, z, zl))
    self_copy = pltpu.make_async_copy(wsend.at[zl], wrecv.at[core], loc.at[0])

    @pl.when(core == zl)
    def _():
        self_copy.start()

    @pl.when(core != zl)
    def _():
        near.start()

    block = 2 * zl + core
    acts, locals_ = [], []
    for i, (src, dst) in enumerate(
        ((tok, tok_all), (txt, txt_all), (cot, cot_all), (pos, pos_all))
    ):
        put = dst.at[block]
        acts.append(
            remote(src.at[1 - core], put, ac_s.at[i, 0], ac_r.at[i, 0], chip(x, y, z, 1 - core))
        )
        acts.append(
            remote(src.at[0], put, ac_s.at[i, 1], ac_r.at[i, 1 + core], chip(x, y, z + 1, 0))
        )
        acts.append(
            remote(src.at[1], put, ac_s.at[i, 2], ac_r.at[i, 1 + core], chip(x, y, z - 1, 1))
        )
        locals_.append(pltpu.make_async_copy(src.at[core], put, loc.at[1 + i]))
    for copy in acts + locals_:
        copy.start()

    def got(slot):
        remote(wsend.at[0], wrecv.at[slot], wx_s.at[0], wx_r.at[slot], chip(x, y, z, core)).wait_recv()

    @pl.when(core == zl)
    def _():
        self_copy.wait()
        got(1 - core)

    @pl.when(core != zl)
    def _():
        near.wait_send()
        got(0)
        got(1)

    first = wrecv[0].astype(F32)
    second = wrecv[1].astype(F32)
    own[0] = jnp.concatenate([first[:ROWS], second[:ROWS]], 0).astype(BF)
    own[1] = jnp.concatenate([first[ROWS:], second[ROWS:]], 0).astype(BF)

    flat = lambda a, b: lax.rem(a + SIDE, SIDE) * SIDE + lax.rem(b + SIDE, SIDE)

    def place(part, index, half=None):
        start, size = part * HALF, HALF
        if half is not None:
            start, size = start + half * QUARTER, QUARTER
        return wg.at[index, core, :, pl.ds(start, size)]

    sends, recvs, sibs = [], [], []

    def push(part, slot, src, index, device, half=None):
        copy = remote(src, place(part, index, half), xs.at[part, slot], xr.at[part, slot], device)
        copy.start()
        sends.append(copy)
        return copy

    def to_sibling(part, slot, src, index):
        copy = remote(
            src, place(part, index), ks.at[part, slot], kr.at[part, slot], chip(x, y, z, 1 - core)
        )
        copy.start()
        sibs.append(copy)

    steps = (
        (chip(x + 1, y, z, core), chip(x - 1, y, z, core)),
        (chip(x, y + 1, z, core), chip(x, y - 1, z, core)),
    )

    def index_of(part, first_off, second_off):
        if part == 0:
            return flat(x + first_off, y + second_off)
        return flat(x + second_off, y + first_off)

    one, two = {}, {}
    for part in (0, 1):
        a_next, a_prev = steps[part]
        one[part, "next"] = push(part, 0, own.at[part], mine, a_next)
        one[part, "prev"] = push(part, 1, own.at[part], mine, a_prev)
    for part in (0, 1):
        b_next, b_prev = steps[1 - part]
        two[part, 0, "next"] = push(part, 4, own.at[part], mine, b_next)
        two[part, 0, "prev"] = push(part, 5, own.at[part], mine, b_prev)
        to_sibling(part, 0, own.at[part], mine)
        local = pltpu.make_async_copy(own.at[part], place(part, mine), loc.at[5 + part])
        local.start()
        locals_.append(local)

    def second_start(part, k, offset):
        b_next, b_prev = steps[1 - part]
        index = index_of(part, offset, 0)
        src = place(part, index)
        two[part, k, "next"] = push(part, 4 + 4 * k, src, index, b_next)
        two[part, k, "prev"] = push(part, 5 + 4 * k, src, index, b_prev)
        to_sibling(part, 4 * k, src, index)

    offsets = (0, -1, 1, 2)
    for part in (0, 1):
        a_next, a_prev = steps[part]
        one[part, "next"].wait_recv()
        index = index_of(part, -1, 0)
        one[part, "far0"] = push(part, 2, place(part, index, 0), index, a_next, 0)
        second_start(part, 1, -1)
        one[part, "prev"].wait_recv()
        index = index_of(part, 1, 0)
        one[part, "far1"] = push(part, 3, place(part, index, 1), index, a_prev, 1)
        second_start(part, 2, 1)

    def second_forward(part, k):
        b_next, b_prev = steps[1 - part]
        two[part, k, "next"].wait_recv()
        index = index_of(part, offsets[k], -1)
        two[part, k, "far0"] = push(part, 6 + 4 * k, place(part, index, 0), index, b_next, 0)
        to_sibling(part, 4 * k + 1, place(part, index), index)
        two[part, k, "prev"].wait_recv()
        index = index_of(part, offsets[k], 1)
        two[part, k, "far1"] = push(part, 7 + 4 * k, place(part, index, 1), index, b_prev, 1)
        to_sibling(part, 4 * k + 2, place(part, index), index)

    def second_finish(part, k):
        two[part, k, "far0"].wait_recv()
        two[part, k, "far1"].wait_recv()
        index = index_of(part, offsets[k], 2)
        to_sibling(part, 4 * k + 3, place(part, index), index)

    for part in (0, 1):
        second_forward(part, 0)
    for part in (0, 1):
        one[part, "far0"].wait_recv()
        one[part, "far1"].wait_recv()
        second_start(part, 3, 2)
    for k in (1, 2, 3):
        for part in (0, 1):
            second_forward(part, k)
        for part in (0, 1):
            second_finish(part, k - 1)
    for part in (0, 1):
        second_finish(part, 3)

    away.wait_send()
    for copy in locals_:
        copy.wait()
    for copy in acts:
        copy.wait_send()
    for i in range(4):
        for slot in range(3):
            acts[3 * i].wait_recv() if slot == 0 else remote(
                (tok, txt, cot, pos)[i].at[0], (tok_all, txt_all, cot_all, pos_all)[i].at[0],
                ac_s.at[i, 0], ac_r.at[i, slot], chip(x, y, z, core),
            ).wait_recv()
    for copy in sends:
        copy.wait_send()
    for copy in sibs:
        copy.wait_send()
        copy.wait_recv()


def gather_all(wsend, tok, txt, cot, pos):
    acts = jax.ShapeDtypeStruct((SIDE, TOK, D), BF)
    dma = pltpu.SemaphoreType.DMA
    return pl.pallas_call(
        gather_kernel,
        out_shape=[
            jax.ShapeDtypeStruct((SIDE * SIDE, 2, PAIR, COLS), BF),
            acts,
            acts,
            acts,
            jax.ShapeDtypeStruct((SIDE, 8, TOK), F32),
        ],
        in_specs=[VM, HB, HB, HB, VM],
        out_specs=[HB, HB, HB, HB, VM],
        scratch_shapes=[
            pltpu.VMEM((2, PAIR, HALF), BF),
            pltpu.VMEM((2, PAIR, HALF), BF),
            dma((2,)), dma((2,)), dma((4, 3)), dma((4, 3)), dma((7,)),
            dma((2, 20)), dma((2, 20)), dma((2, 16)), dma((2, 16)),
        ],
        compiler_params=params(0),
        name="gather_weights",
    )(wsend, tok, txt, cot, pos)


def z_peers(x, y, z, core):
    return [chip(x, y, z + k, core) for k in (1, 2, 3)]


def total_kernel(part, out, got, send, recv):
    x, y, z, core = here()
    greet(z_peers(x, y, z, core))
    copies = []
    for k in (1, 2, 3):
        copies.append(
            remote(part, got.at[k - 1], send.at[k - 1], recv.at[k - 1], chip(x, y, z + k, core))
        )
        copies[-1].start()
    for copy in copies:
        copy.wait()
    out[...] = part[...] + got[0] + got[1] + got[2]


def z_total(values, cid):
    dma = pltpu.SemaphoreType.DMA
    return pl.pallas_call(
        total_kernel,
        out_shape=jax.ShapeDtypeStruct(values.shape, F32),
        in_specs=[VM],
        out_specs=VM,
        scratch_shapes=[pltpu.VMEM((3,) + values.shape, F32), dma((3,)), dma((3,))],
        compiler_params=params(cid),
        name=f"z_total_{cid}",
    )(values)


def scatter_start(parts, got, send, recv):
    x, y, z, core = here()
    copies = []
    for i, part in enumerate(parts):
        for k in (2, 1, 3):
            rows = pl.ds(pl.multiple_of(block_of(z + k) * TOK, TOK), TOK)
            copy = remote(
                part.at[rows], got.at[i, k - 1], send.at[i, k - 1], recv.at[i, k - 1],
                chip(x, y, z + k, core),
            )
            copy.start()
            copies.append(copy)
    return copies


def own_sum(part, got, i, z):
    rows = pl.ds(pl.multiple_of(block_of(z) * TOK, TOK), TOK)
    total = part[rows].astype(F32)
    for k in range(3):
        total = total + got[i, k].astype(F32)
    return total


def step_kernel(compute, extra_count, out_count, *refs):
    part = refs[0]
    extras = refs[1 : 1 + extra_count]
    gathered = refs[1 + extra_count]
    outs = refs[2 + extra_count : 2 + extra_count + out_count]
    got, send, recv, gsend, grecv = refs[2 + extra_count + out_count :]
    x, y, z, core = here()
    greet(z_peers(x, y, z, core))
    copies = scatter_start([part], got, send, recv)
    for copy in copies:
        copy.wait_recv()
    total = own_sum(part, got, 0, z)
    result = compute(total, extras, outs)
    rows = pl.ds(pl.multiple_of(block_of(z) * TOK, TOK), TOK)
    gathered[rows] = result
    gathers = []
    for k in (2, 1, 3):
        copy = remote(
            gathered.at[rows], gathered.at[rows], gsend.at[k - 1], grecv.at[k - 1],
            chip(x, y, z + k, core),
        )
        copy.start()
        gathers.append(copy)
    for copy in gathers:
        copy.wait()
    for copy in copies:
        copy.wait_send()


def z_step(part, extras, compute, out_shapes, cid):
    dma = pltpu.SemaphoreType.DMA
    return pl.pallas_call(
        partial(step_kernel, compute, len(extras), len(out_shapes)),
        out_shape=[jax.ShapeDtypeStruct((SEQ, D), BF)] + out_shapes,
        in_specs=[VM] * (1 + len(extras)),
        out_specs=[VM] * (1 + len(out_shapes)),
        scratch_shapes=[pltpu.VMEM((1, 3, TOK, D), BF), dma((1, 3)), dma((1, 3)), dma((3,)), dma((3,))],
        compiler_params=params(cid),
        name=f"z_step_{cid}",
    )(part, *extras)


def scatter_kernel(count, *refs):
    parts, outs = refs[:count], refs[count : 2 * count]
    got, send, recv = refs[2 * count :]
    x, y, z, core = here()
    greet(z_peers(x, y, z, core))
    copies = scatter_start(parts, got, send, recv)
    for i in range(count):
        for copy in copies[3 * i : 3 * i + 3]:
            copy.wait()
        outs[i][...] = own_sum(parts[i], got, i, z)


def z_scatter(parts, cid):
    count = len(parts)
    dma = pltpu.SemaphoreType.DMA
    return pl.pallas_call(
        partial(scatter_kernel, count),
        out_shape=[jax.ShapeDtypeStruct((TOK, D), F32)] * count,
        in_specs=[VM] * count,
        out_specs=[VM] * count,
        scratch_shapes=[pltpu.VMEM((count, 3, TOK, D), BF), dma((count, 3)), dma((count, 3))],
        compiler_params=params(cid),
        name=f"z_scatter_{cid}",
    )(*parts)


def deliver_kernel(count, *refs):
    srcs, dsts = refs[:count], refs[count : 2 * count]
    send, recv, loc = refs[2 * count :]
    x, y, z, core = here()
    zh = lax.div(z, 2)
    greet(column(x, y, z, core))
    far = [
        remote(s, d.at[core], send.at[i, 0], recv.at[i, core], chip(x, y, z + 2, zh))
        for i, (s, d) in enumerate(zip(srcs, dsts))
    ]
    near = [
        remote(s, d.at[core], send.at[i, 1], recv.at[i, core], chip(x, y, z, zh))
        for i, (s, d) in enumerate(zip(srcs, dsts))
    ]
    self_copies = [
        pltpu.make_async_copy(s, d.at[core], loc.at[i]) for i, (s, d) in enumerate(zip(srcs, dsts))
    ]
    for copy in far:
        copy.start()

    def got(i, slot):
        remote(
            srcs[i], dsts[i].at[slot], send.at[i, 0], recv.at[i, slot], chip(x, y, z, core)
        ).wait_recv()

    @pl.when(core == zh)
    def _():
        for copy in self_copies:
            copy.start()
        for i in range(count):
            self_copies[i].wait()
            got(i, 1 - core)

    @pl.when(core != zh)
    def _():
        for copy in near:
            copy.start()
        for i in range(count):
            near[i].wait_send()
            got(i, 0)
            got(i, 1)

    for copy in far:
        copy.wait_send()


def deliver(arrays, cid):
    count = len(arrays)
    dma = pltpu.SemaphoreType.DMA
    return pl.pallas_call(
        partial(deliver_kernel, count),
        out_shape=[jax.ShapeDtypeStruct((2,) + a.shape, a.dtype) for a in arrays],
        in_specs=[VM] * count,
        out_specs=[VM] * count,
        scratch_shapes=[dma((count, 2)), dma((count, 2)), dma((count,))],
        compiler_params=params(cid),
        name=f"deliver_{cid}",
    )(*arrays)


def vector_kernel(model, heads, time_out, model_out, head_out, col, hsib, mx, hx, sends, recvs):
    x, y, z, core = here()
    zl = lax.rem(z, 2)
    rows = [chip(x + k, y, z, core) for k in (1, 2, 3)]
    lines = [chip(x, y + k, z, core) for k in (1, 2, 3)]
    greet(column(x, y, z, core) + rows + lines)
    copies = []
    for k in (1, 2, 3):
        copies.append(
            remote(model, col.at[0, k - 1], sends.at[0, k], recvs.at[0, k], chip(x, y, z + k, core))
        )
    for k in range(4):
        copies.append(
            remote(model, col.at[1, k], sends.at[1, k], recvs.at[1, k], chip(x, y, z + k, 1 - core))
        )
    copies.append(remote(heads, hsib, sends.at[0, 0], recvs.at[0, 0], chip(x, y, z, 1 - core)))
    for copy in copies:
        copy.start()
    for copy in copies:
        copy.wait()
    same = model[...] + col[0, 0] + col[0, 1] + col[0, 2]
    sib = col[1, 0] + col[1, 1] + col[1, 2] + col[1, 3]
    time_out[core] = same
    time_out[1 - core] = sib
    mx[0] = same + sib
    hx[0] = heads[...] + hsib[...]
    for stage, peers in enumerate((rows, lines)):
        copies = []
        for k in (1, 2, 3):
            at = 1 + 3 * stage + k - 1
            copies.append(
                remote(mx.at[4 * stage], mx.at[4 * stage + k], sends.at[2 + 2 * stage, k],
                       recvs.at[2 + 2 * stage, k], peers[k - 1])
            )
            copies.append(
                remote(hx.at[4 * stage], hx.at[4 * stage + k], sends.at[3 + 2 * stage, k],
                       recvs.at[3 + 2 * stage, k], peers[k - 1])
            )
        for copy in copies:
            copy.start()
        for copy in copies:
            copy.wait()
        base = 4 * stage
        mx[base + 4] = mx[base] + mx[base + 1] + mx[base + 2] + mx[base + 3]
        hx[base + 4] = hx[base] + hx[base + 1] + hx[base + 2] + hx[base + 3]
    model_out[...] = mx[8]
    head_out[zl] = hx[8]
    last = remote(
        hx.at[8], head_out.at[zl], sends.at[6, 0], recvs.at[6, 0], chip(x, y, z + 1 - 2 * zl, core)
    )
    last.start()
    last.wait()


def vector_sums(model, heads, cid):
    dma = pltpu.SemaphoreType.DMA
    return pl.pallas_call(
        vector_kernel,
        out_shape=[
            jax.ShapeDtypeStruct((2, 16, D), F32),
            jax.ShapeDtypeStruct((16, D), F32),
            jax.ShapeDtypeStruct((2, 16, HW), F32),
        ],
        in_specs=[VM, VM],
        out_specs=[VM, VM, VM],
        scratch_shapes=[
            pltpu.VMEM((2, 4, 16, D), F32),
            pltpu.VMEM((16, HW), F32),
            pltpu.VMEM((9, 16, D), F32),
            pltpu.VMEM((9, 16, HW), F32),
            dma((7, 4)),
            dma((7, 4)),
        ],
        compiler_params=params(cid),
        name="vector_sums",
    )(model, heads)


GRAD_WIDTHS = (3 * HW, HW, 2 * HW, HW, HW, FF, FF)


def grad_kernel(*refs):
    grads = refs[: len(GRAD_WIDTHS)]
    out, own, sib, r1, r2, tosend, ls, ss, sr, s1, q1, s2, q2, s3, q3, l3 = refs[len(GRAD_WIDTHS) :]
    x, y, z, core = here()
    zl = lax.rem(z, 2)
    rows = [chip(x + k, y, z, core) for k in (1, 2, 3)]
    lines = [chip(x, y + k, z, core) for k in (1, 2, 3)]
    greet(column(x, y, z, core) + rows + lines)
    start, pairs = 0, []
    for i, width in enumerate(GRAD_WIDTHS):
        cols = pl.ds(start, width)
        mine = pltpu.make_async_copy(grads[i].at[:, :, core], own.at[:, :, :, cols], ls.at[i])
        theirs = remote(
            grads[i].at[:, :, 1 - core], sib.at[:, :, :, cols], ss.at[i], sr.at[i], chip(x, y, z, 1 - core)
        )
        mine.start()
        theirs.start()
        pairs.append((mine, theirs))
        start += width
    for mine, theirs in pairs:
        mine.wait()
        theirs.wait()

    def add_pair(k, carry):
        a, b = lax.div(k, SIDE), lax.rem(k, SIDE)
        own[a, b] = (own[a, b].astype(F32) + sib[a, b].astype(F32)).astype(BF)
        return carry

    lax.fori_loop(0, SIDE * SIDE, add_pair, 0)
    wrap = lambda v: lax.rem(v, SIDE)
    first, second = pl.ds(0, HALF), pl.ds(HALF, HALF)
    one = []
    for k in (2, 1, 3):
        one.append(
            remote(own.at[:, wrap(y + k), :, first], r1.at[0, k - 1], s1.at[0, k - 1], q1.at[0, k - 1], lines[k - 1])
        )
        one.append(
            remote(own.at[wrap(x + k), :, :, second], r1.at[1, k - 1], s1.at[1, k - 1], q1.at[1, k - 1], rows[k - 1])
        )
    for copy in one:
        copy.start()
    for copy in one:
        copy.wait()

    def add_line(k, carry):
        total = own[k, y, :, :HALF].astype(F32)
        for i in range(3):
            total = total + r1[0, i, k].astype(F32)
        own[k, y, :, :HALF] = total.astype(BF)
        total = own[x, k, :, HALF:].astype(F32)
        for i in range(3):
            total = total + r1[1, i, k].astype(F32)
        own[x, k, :, HALF:] = total.astype(BF)
        return carry

    lax.fori_loop(0, SIDE, add_line, 0)
    two = []
    for k in (2, 1, 3):
        two.append(
            remote(own.at[wrap(x + k), y, :, first], r2.at[0, k - 1], s2.at[0, k - 1], q2.at[0, k - 1], rows[k - 1])
        )
        two.append(
            remote(own.at[x, wrap(y + k), :, second], r2.at[1, k - 1], s2.at[1, k - 1], q2.at[1, k - 1], lines[k - 1])
        )
    for copy in two:
        copy.start()
    for copy in two:
        copy.wait()
    final = []
    for part in (0, 1):
        total = own[x, y, :, pl.ds(part * HALF, HALF)].astype(F32)
        for i in range(3):
            total = total + r2[part, i].astype(F32)
        final.append(total)
    for target in (0, 1):
        rows_of = slice(target * ROWS, target * ROWS + ROWS)
        tosend[target] = jnp.concatenate([final[0][rows_of], final[1][rows_of]], 0).astype(BF)
    other = z + 1 - 2 * zl
    far = [
        remote(tosend.at[t], out.at[zl], s3.at[t], q3.at[zl], chip(x, y, other, t)) for t in (0, 1)
    ]
    self_copy = pltpu.make_async_copy(tosend.at[core], out.at[zl], l3.at[0])
    near = remote(tosend.at[1 - core], out.at[zl], s3.at[0], q3.at[zl], chip(x, y, z, 1 - core))

    def got(slot):
        remote(tosend.at[0], out.at[slot], s3.at[0], q3.at[slot], chip(x, y, z, core)).wait_recv()

    @pl.when(core == zl)
    def _():
        self_copy.start()
        near.start()
        self_copy.wait()
        near.wait_send()
        got(1 - zl)

    @pl.when(core != zl)
    def _():
        for copy in far:
            copy.start()
        for copy in far:
            copy.wait_send()
        got(zl)
        got(1 - zl)


def grad_sums(grads, cid):
    dma = pltpu.SemaphoreType.DMA
    count = len(GRAD_WIDTHS)
    return pl.pallas_call(
        grad_kernel,
        out_shape=jax.ShapeDtypeStruct((2, PAIR, HALF), BF),
        in_specs=[HB] * count,
        out_specs=VM,
        scratch_shapes=[
            pltpu.VMEM((SIDE, SIDE, PAIR, COLS), BF),
            pltpu.VMEM((SIDE, SIDE, PAIR, COLS), BF),
            pltpu.VMEM((2, 3, SIDE, PAIR, HALF), BF),
            pltpu.VMEM((2, 3, PAIR, HALF), BF),
            pltpu.VMEM((2, PAIR, HALF), BF),
            dma((count,)), dma((count,)), dma((count,)),
            dma((2, 3)), dma((2, 3)), dma((2, 3)), dma((2, 3)),
            dma((2,)), dma((2,)), dma((1,)),
        ],
        compiler_params=params(cid),
        name="grad_sums",
    )(*grads)


def newton_kernel(narrow, wide, narrow_out, wide_out, mine, theirs, send, recv):
    x, y, z, core = here()
    partner = chip(x, y, z + 2, core)
    greet([partner])
    n, w = narrow.shape[0], wide.shape[0]
    size = n + w
    contract = (((1,), (1,)), ((), ()))
    mine[...] = jnp.zeros_like(mine)
    mine[:n, :n] = lax.dot_general(
        narrow[...], narrow[...], contract, precision=HIGHEST, preferred_element_type=F32
    )
    mine[n:, n:] = lax.dot_general(
        wide[...], wide[...], contract, precision=HIGHEST, preferred_element_type=F32
    )
    copy = remote(mine, theirs, send.at[0], recv.at[0], partner)
    copy.start()
    copy.wait()
    block_row = lax.div(lax.broadcasted_iota(jnp.int32, (size, size), 0), ROWS)
    block_col = lax.div(lax.broadcasted_iota(jnp.int32, (size, size), 1), ROWS)
    same = block_row == block_col
    eye = lax.broadcasted_iota(jnp.int32, (size, size), 0) == lax.broadcasted_iota(
        jnp.int32, (size, size), 1
    )
    gram = jnp.where(same, mine[...] + theirs[...], 0.0)
    diagonal = jnp.where(eye, gram, 0.0)
    by_row = jnp.sum(diagonal, 1, keepdims=True)
    by_col = jnp.sum(diagonal, 0, keepdims=True)
    total_row = jnp.sum(jnp.where(same, by_col, 0.0), 1, keepdims=True)
    total_col = jnp.sum(jnp.where(same, by_row, 0.0), 0, keepdims=True)
    scale_row = 1.0 / (jnp.sqrt(total_row) + ORTHO_EPSILON)
    scale_col = 1.0 / (jnp.sqrt(total_col) + ORTHO_EPSILON)
    current = gram * scale_row * scale_col

    def times(a, b):
        return jnp.dot(a, b, precision=HIGHEST, preferred_element_type=F32)

    whole = None
    for turn in range(NS_STEPS):
        square = times(current, current)
        step = NEWTON_SECOND * current + NEWTON_THIRD * square + jnp.where(eye, NEWTON_FIRST, 0.0)
        whole = step if whole is None else times(step, whole)
        if turn + 1 < NS_STEPS:
            current = times(times(step, current), step)
    whole = whole * scale_col
    narrow_out[...] = times(whole[:n, :n], narrow[...])
    wide_out[...] = times(whole[n:, n:], wide[...])


def newton(narrow, wide, cid):
    size = narrow.shape[0] + wide.shape[0]
    dma = pltpu.SemaphoreType.DMA
    return pl.pallas_call(
        newton_kernel,
        out_shape=[
            jax.ShapeDtypeStruct(narrow.shape, F32),
            jax.ShapeDtypeStruct(wide.shape, F32),
        ],
        in_specs=[VM, VM],
        out_specs=[VM, VM],
        scratch_shapes=[
            pltpu.VMEM((size, size), F32),
            pltpu.VMEM((size, size), F32),
            dma((1,)),
            dma((1,)),
        ],
        compiler_params=params(cid),
        name="newton",
    )(narrow, wide)


def rope_tables(places):
    pair_index = jnp.arange(HEAD // 2, dtype=jnp.int32)
    side_pairs = HEAD // 6
    frame_pairs = (HEAD - 4 * side_pairs) // 2
    part_of = (pair_index >= frame_pairs).astype(jnp.int32) + (
        pair_index >= frame_pairs + side_pairs
    ).astype(jnp.int32)
    offset = jnp.where(
        part_of == 0, 0, jnp.where(part_of == 1, frame_pairs, frame_pairs + side_pairs)
    ).astype(jnp.int32)
    extent = jnp.where(part_of == 0, 2 * frame_pairs, 2 * side_pairs).astype(jnp.float32)
    frequency = jnp.exp(
        (pair_index - offset).astype(jnp.float32) * (-2.0 * math.log(10000.0)) / extent
    )
    chosen = (
        places[0][:, None] * (part_of == 0)
        + places[1][:, None] * (part_of == 1)
        + places[2][:, None] * (part_of == 2)
    )
    angles = chosen.astype(jnp.float32) * frequency
    return (jnp.cos(angles), jnp.sin(angles))


def rotate(values, cosine, sine):
    half_head = HEAD // 2
    front_half = values[..., :half_head]
    back_half = values[..., half_head:]
    return jnp.concatenate(
        [front_half * cosine - back_half * sine, back_half * cosine + front_half * sine], -1
    )


def plain_norm(values):
    centred = values - jnp.mean(values, -1, keepdims=True)
    inverse = lax.rsqrt(jnp.mean(centred * centred, -1, keepdims=True) + NORM_EPSILON)
    return (centred * inverse, inverse)


def norm_back(grads, normed, inverse):
    return inverse * (
        grads
        - jnp.mean(grads, -1, keepdims=True)
        - normed * jnp.mean(grads * normed, -1, keepdims=True)
    )


def split_heads(values):
    return values.reshape(values.shape[0], -1, HEAD)


def merge_heads(values):
    return values.reshape(values.shape[0], -1)


def product(left, right):
    return jnp.dot(left, right, preferred_element_type=F32)


def contract_last(left, right):
    return lax.dot_general(left, right, (((1,), (1,)), ((), ())), preferred_element_type=F32)


def contract_rows(left, right):
    return lax.dot_general(left, right, (((0,), (0,)), ((), ())), preferred_element_type=F32)


def attend(query, keys, values):
    scores = jnp.einsum("qhe,khe->hqk", query, keys, preferred_element_type=F32) * HEAD ** (-0.5)
    row_peak = jnp.max(scores, -1, keepdims=True)
    log_total = row_peak + jnp.log(jnp.sum(jnp.exp(scores - row_peak), -1, keepdims=True))
    weights = jnp.exp(scores - log_total).astype(BF)
    mixed = jnp.einsum("hqk,khe->qhe", weights, values, preferred_element_type=F32)
    return (merge_heads(mixed), log_total)


def attend_back(query, keys, values, log_total, grad_mixed):
    scores = jnp.einsum("qhe,khe->hqk", query, keys, preferred_element_type=F32) * HEAD ** (-0.5)
    weights = jnp.exp(scores - log_total)
    grad_weights = jnp.einsum("qhe,khe->hqk", grad_mixed, values, preferred_element_type=F32)
    row_delta = jnp.sum(weights * grad_weights, -1, keepdims=True)
    grad_scores = (weights * (grad_weights - row_delta)).astype(BF)
    grad_query = jnp.einsum("hqk,khe->qhe", grad_scores, keys, preferred_element_type=F32) * HEAD ** (
        -0.5
    )
    grad_keys = jnp.einsum("hqk,qhe->khe", grad_scores, query, preferred_element_type=F32) * HEAD ** (
        -0.5
    )
    grad_values = jnp.einsum(
        "hqk,qhe->khe", weights.astype(BF), grad_mixed, preferred_element_type=F32
    )
    return grad_query, grad_keys, merge_heads(grad_values)


def block_struct():
    return jax.ShapeDtypeStruct((TOK, D), F32)


def after_self(total, extras, outs):
    residual, rows = extras
    branch = total + rows[0:1]
    after = residual[...].astype(F32) + rows[1:2] * branch
    normed, _ = plain_norm(after)
    outs[0][...] = branch
    outs[1][...] = after
    return (normed * (1.0 + rows[2:3]) + rows[3:4]).astype(BF)


def after_cross(total, extras, outs):
    residual, rows = extras
    after = residual[...] + total + rows[0:1]
    normed, _ = plain_norm(after)
    outs[0][...] = after
    return (normed * (1.0 + rows[1:2]) + rows[2:3]).astype(BF)


def back_mlp(total, extras, outs):
    after, grads, rows = extras
    normed, inverse = plain_norm(after[...])
    outs[1][0:1] = jnp.sum(total, 0, keepdims=True)
    outs[1][1:2] = jnp.sum(total * normed, 0, keepdims=True)
    result = grads[...].astype(F32) + norm_back(total * (1.0 + rows[0:1]), normed, inverse)
    outs[0][...] = result
    low = result.astype(BF)
    outs[1][2:3] = jnp.sum(low.astype(F32), 0, keepdims=True)
    return low


def back_cross(total, extras, outs):
    after, grads, branch, rows = extras
    normed, inverse = plain_norm(after[...])
    outs[1][0:1] = jnp.sum(total, 0, keepdims=True)
    outs[1][1:2] = jnp.sum(total * normed, 0, keepdims=True)
    result = grads[...] + norm_back(total * (1.0 + rows[0:1]), normed, inverse)
    outs[0][...] = result
    outs[1][2:3] = jnp.sum(result * branch[...], 0, keepdims=True)
    low = (result * rows[1:2]).astype(BF)
    outs[1][3:4] = jnp.sum(low.astype(F32), 0, keepdims=True)
    return low


def stack_rows(rows, count=8):
    out = jnp.stack(rows)
    return jnp.pad(out, ((0, count - len(rows)), (0, 0)))


def body(
    tokens, text, time_embedding, positions, cotangent, attn_in, attn_out, mlp, head_vectors,
    model_vectors, up_bias, attn_in_moment, attn_out_moment, mlp_moment, head_moment, model_moment,
    up_moment,
):
    x, y, z, core = here()
    zl = lax.rem(z, 2)
    block = block_of(z)

    low_in = attn_in.astype(BF).reshape(ROWS, 6, 2, HW).transpose(2, 0, 1, 3).reshape(2, ROWS, -1)
    low_out = attn_out.astype(BF).reshape(ROWS, 2, 2, HW).transpose(2, 0, 1, 3).reshape(2, ROWS, -1)
    low_mlp = jnp.pad(
        mlp.astype(BF).reshape(ROWS, 2, 2, FF_REAL).transpose(2, 0, 1, 3),
        ((0, 0), (0, 0), (0, 0), (0, FF - FF_REAL)),
    ).reshape(2, ROWS, -1)
    packed = jnp.concatenate([low_in, low_out, low_mlp], -1)
    packed = packed.reshape(2, ROWS, 2, HALF).transpose(0, 2, 1, 3).reshape(2, PAIR, HALF)
    places = jnp.pad(positions.transpose(1, 0, 2), ((0, 0), (0, 5), (0, 0))).astype(F32)
    gathered, tok_all, txt_all, cot_all, pos_all = gather_all(packed, tokens, text, cotangent, places)
    weights = gathered.reshape(D, COLS)

    def matrix(start, width):
        return lax.slice(weights, (0, start), (D, start + width))

    w_qkv = matrix(C_IN, 3 * HW)
    w_query = matrix(C_IN + 3 * HW, HW)
    w_text = matrix(C_IN + 4 * HW, 2 * HW)
    w_self = matrix(C_OUT, HW)
    w_cross = matrix(C_OUT + HW, HW)
    w_up = matrix(C_UP, FF)
    w_down = matrix(C_DOWN, FF)

    heads = lax.dynamic_slice(head_vectors, (0, zl * HW), (10, HW))
    bias_up = jnp.pad(lax.dynamic_slice(up_bias, (zl * FF_REAL,), (FF_REAL,)), (0, FF - FF_REAL))
    modulation = model_vectors[5:] + lax.dynamic_index_in_dim(time_embedding, core, 0, False)
    shift_one, scale_one, gate_one, shift_two, scale_two, gate_two = [modulation[i] for i in range(6)]
    cosine, sine = rope_tables(pos_all[:, :3].transpose(1, 0, 2).reshape(3, SEQ))
    cosine, sine = cosine[:, None, :], sine[:, None, :]

    def block_rows(values):
        return lax.dynamic_slice(values, (block * TOK, 0), (TOK, values.shape[1]))

    tok_all = tok_all.reshape(SEQ, D)
    words = txt_all.reshape(SEQ, D)
    cot_all = cot_all.reshape(SEQ, D)
    tok_own = block_rows(tok_all)
    cot_own = block_rows(cot_all)

    normed_one, _ = plain_norm(tok_all.astype(F32))
    input_one = (normed_one * (1.0 + scale_one) + shift_one).astype(BF)
    qkv = product(input_one, w_qkv) + heads[0:3].reshape(-1)
    query_lin, key_lin, value_lin = qkv[:, :HW], qkv[:, HW : 2 * HW], qkv[:, 2 * HW :]
    kv_two = product(words, w_text) + heads[6:8].reshape(-1)
    key_two_lin, value_two_lin = kv_two[:, :HW], kv_two[:, HW:]
    squares = z_total(
        stack_rows([jnp.sum(v * v, -1) for v in (query_lin, key_lin, key_two_lin)]), 1
    )
    inverses = lax.rsqrt(squares / D + NORM_EPSILON)
    inverse_query, inverse_key, inverse_key_two = [inverses[i][:, None] for i in range(3)]
    query_rot = rotate(
        split_heads(query_lin * inverse_query * (1.0 + heads[3])), cosine, sine
    ).astype(BF)
    key_rot = rotate(split_heads(key_lin * inverse_key * (1.0 + heads[4])), cosine, sine).astype(BF)
    value_low = split_heads(value_lin.astype(BF))
    mixed, log_one = attend(query_rot, key_rot, value_low)
    mixed_low = mixed.astype(BF)
    part = contract_last(mixed_low, w_self).astype(BF)
    input_three, branch_one, after_one = z_step(
        part,
        [tok_own, stack_rows([model_vectors[0], gate_one, model_vectors[3], model_vectors[4]])],
        after_self,
        [block_struct(), block_struct()],
        2,
    )
    query_two_lin = product(input_three, w_query) + heads[5]
    squares_two = z_total(stack_rows([jnp.sum(query_two_lin * query_two_lin, -1)]), 3)
    inverse_query_two = lax.rsqrt(squares_two[0] / D + NORM_EPSILON)[:, None]
    query_two = split_heads((query_two_lin * inverse_query_two * (1.0 + heads[8])).astype(BF))
    key_two = split_heads((key_two_lin * inverse_key_two * (1.0 + heads[9])).astype(BF))
    value_two = split_heads(value_two_lin.astype(BF))
    mixed_two, log_two = attend(query_two, key_two, value_two)
    mixed_two_low = mixed_two.astype(BF)
    part = contract_last(mixed_two_low, w_cross).astype(BF)
    input_mlp, after_two = z_step(
        part,
        [after_one, stack_rows([model_vectors[1], scale_two, shift_two])],
        after_cross,
        [block_struct()],
        4,
    )
    hidden_lin = product(input_mlp, w_up) + bias_up
    hidden_act, gelu_pullback = jax.vjp(partial(jax.nn.gelu, approximate=True), hidden_lin)
    hidden_low = hidden_act.astype(BF)
    part_mlp = contract_last(hidden_low, w_down).astype(BF)
    grad_branch_mlp = (cot_all.astype(F32) * gate_two).astype(BF)
    grad_hidden = gelu_pullback(product(grad_branch_mlp, w_down))[0].astype(BF)
    part = contract_last(grad_hidden, w_up).astype(BF)
    grad_branch_two, grad_after_two, sums_mlp = z_step(
        part,
        [after_two, cot_own, stack_rows([scale_two])],
        back_mlp,
        [block_struct(), jax.ShapeDtypeStruct((8, D), F32)],
        5,
    )
    grad_mixed_two = product(grad_branch_two, w_cross).astype(BF)
    grad_query_two, grad_key_two, grad_value_two = attend_back(
        query_two, key_two, value_two, log_two, split_heads(grad_mixed_two)
    )
    grad_query_two, grad_key_two = merge_heads(grad_query_two), merge_heads(grad_key_two)
    scaled_query_two = grad_query_two * (1.0 + heads[8])
    scaled_key_two = grad_key_two * (1.0 + heads[9])
    dots = z_total(
        stack_rows(
            [jnp.sum(query_two_lin * scaled_query_two, -1), jnp.sum(key_two_lin * scaled_key_two, -1)]
        ),
        6,
    )

    def root_back(linear, inverse, scaled, dot):
        return (inverse * scaled - linear * (inverse**3 * dot[:, None] / D)).astype(BF)

    grad_query_two_lin = root_back(query_two_lin, inverse_query_two, scaled_query_two, dots[0])
    grad_key_two_lin = root_back(key_two_lin, inverse_key_two, scaled_key_two, dots[1])
    grad_kv_two_lin = jnp.concatenate([grad_key_two_lin, grad_value_two.astype(BF)], 1)
    part = contract_last(grad_query_two_lin, w_query).astype(BF)
    part_words = contract_last(grad_kv_two_lin, w_text).astype(BF)
    grad_branch_one, grad_after_one, sums_cross = z_step(
        part,
        [after_one, grad_after_two, branch_one, stack_rows([model_vectors[3], gate_one])],
        back_cross,
        [block_struct(), jax.ShapeDtypeStruct((8, D), F32)],
        7,
    )
    grad_mixed = product(grad_branch_one, w_self).astype(BF)
    grad_query_rot, grad_key_rot, grad_value = attend_back(
        query_rot, key_rot, value_low, log_one, split_heads(grad_mixed)
    )
    grad_query_norm = merge_heads(rotate(grad_query_rot, cosine, -sine))
    grad_key_norm = merge_heads(rotate(grad_key_rot, cosine, -sine))
    scaled_query = grad_query_norm * (1.0 + heads[3])
    scaled_key = grad_key_norm * (1.0 + heads[4])
    dots_one = z_total(
        stack_rows([jnp.sum(query_lin * scaled_query, -1), jnp.sum(key_lin * scaled_key, -1)]), 8
    )
    grad_query_lin = root_back(query_lin, inverse_query, scaled_query, dots_one[0])
    grad_key_lin = root_back(key_lin, inverse_key, scaled_key, dots_one[1])
    grad_qkv = jnp.concatenate([grad_query_lin, grad_key_lin, grad_value.astype(BF)], 1)
    part_tokens = contract_last(grad_qkv, w_qkv).astype(BF)

    def rows_of(left, right):
        out = contract_rows(left, right).astype(BF)
        return out.reshape(SIDE, SIDE, 2, PAIR, out.shape[1])

    matrix_grads = [
        rows_of(input_one, grad_qkv),
        rows_of(input_three, grad_query_two_lin),
        rows_of(words, grad_kv_two_lin),
        rows_of(grad_branch_one, mixed_low),
        rows_of(grad_branch_two, mixed_two_low),
        rows_of(input_mlp, grad_hidden),
        rows_of(grad_branch_mlp, hidden_low),
    ]

    sum_mlp, sum_tokens, sum_words = z_scatter([part_mlp, part_tokens, part_words], 9)
    branch_mlp = sum_mlp + model_vectors[2]
    cot_f32 = cot_own.astype(F32)
    result = (after_two + gate_two * branch_mlp).astype(BF)
    normed_own, inverse_own = plain_norm(tok_own.astype(F32))
    grad_tokens = grad_after_one + norm_back(sum_tokens * (1.0 + scale_one), normed_own, inverse_own)
    column_sum = lambda v: jnp.sum(v.astype(F32), 0)
    model_part = stack_rows(
        [
            sums_cross[3],
            sums_mlp[2],
            column_sum(block_rows(grad_branch_mlp)),
            sums_cross[1],
            sums_cross[0],
            column_sum(sum_tokens),
            column_sum(sum_tokens * normed_own),
            sums_cross[2],
            sums_mlp[0],
            sums_mlp[1],
            column_sum(cot_f32 * branch_mlp),
        ],
        16,
    )
    grad_qkv_sum = column_sum(grad_qkv).reshape(3, HW)
    grad_kv_sum = column_sum(grad_kv_two_lin).reshape(2, HW)
    head_part = jnp.concatenate(
        [
            grad_qkv_sum,
            jnp.stack(
                [
                    column_sum(grad_query_norm * query_lin * inverse_query),
                    column_sum(grad_key_norm * key_lin * inverse_key),
                    column_sum(grad_query_two_lin),
                ]
            ),
            grad_kv_sum,
            jnp.stack(
                [
                    column_sum(grad_query_two * query_two_lin * inverse_query_two),
                    column_sum(grad_key_two * key_two_lin * inverse_key_two),
                ]
            ),
            column_sum(grad_hidden).reshape(6, HW),
        ],
        0,
    )
    out_result, out_tokens, out_words = deliver(
        [result, grad_tokens.astype(BF), sum_words.astype(BF)], 10
    )
    time_sums, model_sums, head_sums = vector_sums(model_part, head_part, 11)
    grad_time = time_sums[:, 5:11]
    model_total = model_sums[:11]
    head_total = head_sums[:, :10].transpose(1, 0, 2).reshape(10, 2 * HW)
    up_total = head_sums[:, 10:].reshape(2, FF)[:, :FF_REAL].reshape(-1)

    sums = grad_sums(matrix_grads, 12)
    sums = sums.reshape(2, 2, ROWS, HALF).transpose(0, 2, 1, 3).reshape(2, ROWS, COLS).astype(F32)
    def unpack(start, count, width, real):
        part = sums[:, :, start : start + count * width].reshape(2, ROWS, count, width)[..., :real]
        return part.transpose(2, 1, 0, 3).reshape(count, ROWS, 2 * real)

    swap = lambda v: v.transpose(1, 0, 2)
    new_in_moment = MOMENTUM * swap(attn_in_moment) + unpack(C_IN, 6, HW, HW)
    new_out_moment = MOMENTUM * swap(attn_out_moment) + unpack(C_OUT, 2, HW, HW)
    new_mlp_moment = MOMENTUM * swap(mlp_moment) + unpack(C_UP, 2, FF, FF_REAL)
    narrow = jnp.concatenate([new_in_moment, new_out_moment], 0).reshape(8 * ROWS, 2 * HW)
    wide = new_mlp_moment.reshape(2 * ROWS, 2 * FF_REAL)
    narrow_dir, wide_dir = newton(narrow, wide, 13)
    narrow_dir = narrow_dir.reshape(8, ROWS, 2 * HW)
    wide_dir = wide_dir.reshape(2, ROWS, 2 * FF_REAL)
    new_attn_in = attn_in * (1.0 - RATE_IN * DECAY) - RATE_IN * swap(narrow_dir[:6])
    new_attn_out = attn_out * (1.0 - RATE_OUT * DECAY) - RATE_OUT * swap(narrow_dir[6:])
    new_mlp = mlp * (1.0 - RATE_MLP * DECAY) - RATE_MLP * swap(wide_dir)
    new_head_moment = MOMENTUM * head_moment + head_total
    new_model_moment = MOMENTUM * model_moment + model_total
    new_up_moment = MOMENTUM * up_moment + up_total
    return (
        out_result,
        out_tokens.astype(F32),
        out_words.astype(F32),
        grad_time,
        new_attn_in,
        new_attn_out,
        new_mlp,
        swap(new_in_moment),
        swap(new_out_moment),
        swap(new_mlp_moment),
        head_vectors - RATE_VECTOR * new_head_moment,
        model_vectors - RATE_VECTOR * new_model_moment,
        up_bias - RATE_VECTOR * new_up_moment,
        new_head_moment,
        new_model_moment,
        new_up_moment,
    )


def solution(mesh):
    clip = P("fsdp", "ctx", None)
    whole = P("fsdp", None, None)
    matrix = P(("fsdp", "ctx"), None, "tp")
    in_specs = (
        clip, clip, whole, P(None, "fsdp", "ctx"), clip, matrix, matrix, matrix, P(None, "tp"), P(),
        P("tp"), matrix, matrix, matrix, P(None, "tp"), P(), P("tp"),
    )
    out_specs = (
        clip, clip, clip, whole, matrix, matrix, matrix, matrix, matrix, matrix, P(None, "tp"), P(),
        P("tp"), P(None, "tp"), P(), P("tp"),
    )
    return jax.shard_map(body, mesh=mesh, in_specs=in_specs, out_specs=out_specs, check_vma=False)
```

```python
from functools import partial
import math

import jax
import jax.numpy as jnp
from jax import lax
from jax.experimental import pallas as pl
from jax.experimental.pallas import tpu as pltpu
from jax.sharding import PartitionSpec as P

D = 1536
HEAD = 128
ROWS = 24
HEADS = 3
NORM_EPSILON = 1e-06
ORTHO_EPSILON = 1e-07
NEWTON_FIRST = 3.4445
NEWTON_SECOND = -4.775
NEWTON_THIRD = 2.0315
NS_STEPS = 5
MOMENTUM = 0.9
DECAY = 0.01
RATE_IN = 0.5
RATE_OUT = 4.0
RATE_MLP = 1.0
RATE_VECTOR = 0.005
HIGHEST = lax.Precision.HIGHEST

MESH = pl.DeviceIdType.MESH
BF = jnp.bfloat16
F32 = jnp.float32

SIDE = 4
TOK = 128
SEQ = SIDE * TOK
HW = HEADS * HEAD
FF_REAL = 2240
FF = 2304
C_IN, C_OUT, C_UP, C_DOWN = 0, 6 * HW, 8 * HW, 8 * HW + FF
COLS = 8 * HW + 2 * FF
HALF = COLS // 2
QUARTER = HALF // 2
PAIR = 2 * ROWS
VMEM_LIMIT = 60 * 1024 * 1024


def here():
    f = lax.axis_index("fsdp")
    c = lax.axis_index("ctx")
    t = lax.axis_index("tp")
    x, y = lax.div(f, SIDE), lax.rem(f, SIDE)
    zl, core = lax.div(c, 2), lax.rem(c, 2)
    return x, y, 2 * t + zl, core


def chip(x, y, z, core):
    x, y, z = lax.rem(x + SIDE, SIDE), lax.rem(y + SIDE, SIDE), lax.rem(z + SIDE, SIDE)
    return {"fsdp": x * SIDE + y, "ctx": lax.rem(z, 2) * 2 + core, "tp": lax.div(z, 2)}


def block_of(z):
    z = lax.rem(z + SIDE, SIDE)
    return 2 * lax.rem(z, 2) + lax.div(z, 2)


def greet(devices):
    barrier = pltpu.get_barrier_semaphore()
    for device in devices:
        pl.semaphore_signal(barrier, inc=1, device_id=device, device_id_type=MESH)
    pl.semaphore_wait(barrier, len(devices))


def column(x, y, z, core):
    return [chip(x, y, z + k, core) for k in (1, 2, 3)] + [
        chip(x, y, z + k, 1 - core) for k in range(4)
    ]


def remote(src, dst, send, recv, device):
    return pltpu.make_async_remote_copy(
        src_ref=src, dst_ref=dst, send_sem=send, recv_sem=recv, device_id=device, device_id_type=MESH
    )


def params(cid):
    return pltpu.CompilerParams(
        collective_id=cid, has_side_effects=True, vmem_limit_bytes=VMEM_LIMIT
    )


VM = pl.BlockSpec(memory_space=pltpu.VMEM)
HB = pl.BlockSpec(memory_space=pltpu.HBM)


def flat(a, b):
    return lax.rem(a + SIDE, SIDE) * SIDE + lax.rem(b + SIDE, SIDE)


def steps_of(x, y, z, core):
    return (
        (chip(x + 1, y, z, core), chip(x - 1, y, z, core)),
        (chip(x, y + 1, z, core), chip(x, y - 1, z, core)),
    )


def gather_xy(own, place, xs, xr, ks, kr):
    x, y, z, core = here()
    mine = x * SIDE + y
    steps = steps_of(x, y, z, core)
    sibling = chip(x, y, z, 1 - core)
    sends, sibs = [], []

    def push(part, slot, src, index, device, half=None):
        copy = remote(src, place(part, index, half), xs.at[part, slot], xr.at[part, slot], device)
        copy.start()
        sends.append(copy)
        return copy

    def to_sibling(part, slot, src, index):
        copy = remote(src, place(part, index), ks.at[part, slot], kr.at[part, slot], sibling)
        copy.start()
        sibs.append(copy)

    def index_of(part, first_off, second_off):
        if part == 0:
            return flat(x + first_off, y + second_off)
        return flat(x + second_off, y + first_off)

    one, two = {}, {}
    for part in (0, 1):
        a_next, a_prev = steps[part]
        one[part, "next"] = push(part, 0, own.at[part], mine, a_next)
        one[part, "prev"] = push(part, 1, own.at[part], mine, a_prev)
    for part in (0, 1):
        b_next, b_prev = steps[1 - part]
        two[part, 0, "next"] = push(part, 4, own.at[part], mine, b_next)
        two[part, 0, "prev"] = push(part, 5, own.at[part], mine, b_prev)
        to_sibling(part, 0, own.at[part], mine)

    def second_start(part, k, offset):
        b_next, b_prev = steps[1 - part]
        index = index_of(part, offset, 0)
        src = place(part, index)
        two[part, k, "next"] = push(part, 4 + 4 * k, src, index, b_next)
        two[part, k, "prev"] = push(part, 5 + 4 * k, src, index, b_prev)
        to_sibling(part, 4 * k, src, index)

    offsets = (0, -1, 1, 2)
    for part in (0, 1):
        a_next, a_prev = steps[part]
        yield
        one[part, "next"].wait_recv()
        index = index_of(part, -1, 0)
        one[part, "far0"] = push(part, 2, place(part, index, 0), index, a_next, 0)
        second_start(part, 1, -1)
        one[part, "prev"].wait_recv()
        index = index_of(part, 1, 0)
        one[part, "far1"] = push(part, 3, place(part, index, 1), index, a_prev, 1)
        second_start(part, 2, 1)

    def second_forward(part, k):
        b_next, b_prev = steps[1 - part]
        two[part, k, "next"].wait_recv()
        index = index_of(part, offsets[k], -1)
        two[part, k, "far0"] = push(part, 6 + 4 * k, place(part, index, 0), index, b_next, 0)
        to_sibling(part, 4 * k + 1, place(part, index), index)
        two[part, k, "prev"].wait_recv()
        index = index_of(part, offsets[k], 1)
        two[part, k, "far1"] = push(part, 7 + 4 * k, place(part, index, 1), index, b_prev, 1)
        to_sibling(part, 4 * k + 2, place(part, index), index)

    def second_finish(part, k):
        two[part, k, "far0"].wait_recv()
        two[part, k, "far1"].wait_recv()
        index = index_of(part, offsets[k], 2)
        to_sibling(part, 4 * k + 3, place(part, index), index)

    for part in (0, 1):
        yield
        second_forward(part, 0)
    for part in (0, 1):
        yield
        one[part, "far0"].wait_recv()
        one[part, "far1"].wait_recv()
        second_start(part, 3, 2)
    for k in (1, 2, 3):
        for part in (0, 1):
            yield
            second_forward(part, k)
        for part in (0, 1):
            second_finish(part, k - 1)
    for part in (0, 1):
        yield
        second_finish(part, 3)
    yield
    for copy in sends:
        copy.wait_send()
    for copy in sibs:
        copy.wait_send()
        copy.wait_recv()


GATHER_SEMS = ((2, 20), (2, 20), (2, 16), (2, 16))


def advance(job, count=1):
    for _ in range(count):
        next(job, None)


def finish(job):
    for _ in job:
        pass


def share_rows(send, recv, s, r, l):
    x, y, z, core = here()
    zl = lax.rem(z, 2)
    away = remote(send.at[1 - zl], recv.at[core], s.at[0], r.at[core], chip(x, y, z + 1 - 2 * zl, zl))
    near = remote(send.at[zl], recv.at[core], s.at[1], r.at[core], chip(x, y, z, zl))
    self_copy = pltpu.make_async_copy(send.at[zl], recv.at[core], l.at[0])

    def got(slot):
        remote(send.at[0], recv.at[slot], s.at[0], r.at[slot], chip(x, y, z, core)).wait_recv()

    def start():
        away.start()

        @pl.when(core == zl)
        def _():
            self_copy.start()

        @pl.when(core != zl)
        def _():
            near.start()

    def wait(own):
        @pl.when(core == zl)
        def _():
            self_copy.wait()
            got(1 - core)

        @pl.when(core != zl)
        def _():
            near.wait_send()
            got(0)
            got(1)

        first = recv[0].astype(F32)
        second = recv[1].astype(F32)
        own[0] = jnp.concatenate([first[:ROWS], second[:ROWS]], 0).astype(BF)
        own[1] = jnp.concatenate([first[ROWS:], second[ROWS:]], 0).astype(BF)

    return start, wait, away.wait_send


def share_clip(src, dst, s, r, l):
    x, y, z, core = here()
    put = dst.at[2 * lax.rem(z, 2) + core]
    copies = [
        remote(src.at[1 - core], put, s.at[0], r.at[0], chip(x, y, z, 1 - core)),
        remote(src.at[0], put, s.at[1], r.at[1 + core], chip(x, y, z + 1, 0)),
        remote(src.at[1], put, s.at[2], r.at[1 + core], chip(x, y, z - 1, 1)),
    ]
    local = pltpu.make_async_copy(src.at[core], put, l)

    def start():
        for copy in copies:
            copy.start()
        local.start()

    def wait():
        local.wait()
        for slot in range(3):
            remote(src.at[0], dst.at[0], s.at[0], r.at[slot], chip(x, y, z, core)).wait_recv()

    def drain():
        for copy in copies:
            copy.wait_send()

    return start, wait, drain


def split3(values):
    return [values[:, i * HW : (i + 1) * HW] for i in range(values.shape[1] // HW)]


def swap_halves(values):
    return pltpu.roll(values, HEAD // 2, 1)


def rope_pair(table):
    lane = lax.broadcasted_iota(jnp.int32, table.shape, 1)
    other = swap_halves(table)
    front = lane < HEAD // 2
    return jnp.where(front, table, other), jnp.where(front, -other, table)


def head_slice(h):
    return slice(h * HEAD, (h + 1) * HEAD)


SCALE = HEAD ** (-0.5)


def softmax_rows(query, keys):
    scores = contract_last(query, keys) * SCALE
    peak = jnp.max(scores, -1, keepdims=True)
    raised = jnp.exp(scores - peak)
    return raised * (1.0 / jnp.sum(raised, -1, keepdims=True))


def attend_clip(query, keys, values, out):
    for h in range(HEADS):
        cols = head_slice(h)
        for start in range(0, SEQ, 256):
            rows = slice(start, start + 256)
            weights = softmax_rows(query[rows, cols], keys[:, cols]).astype(BF)
            out[rows, cols] = product(weights, values[:, cols]).astype(BF)


class Stats:
    def __init__(self, buffer, send, recv):
        self.buffer, self.send, self.recv = buffer, send, recv

    def start(self, turn, columns):
        x, y, z, core = here()
        lane = lax.broadcasted_iota(jnp.int32, (SEQ, 128), 1)
        packed = jnp.zeros((SEQ, 128), F32)
        for i, column_values in enumerate(columns):
            packed = jnp.where(lane == i, column_values, packed)
        self.buffer[turn, 0] = packed.T[:8]
        copies = []
        for k in (2, 1, 3):
            copies.append(
                remote(self.buffer.at[turn, 0], self.buffer.at[turn, k], self.send.at[turn, k - 1],
                       self.recv.at[turn, k - 1], chip(x, y, z + k, core))
            )
            copies[-1].start()

        def wait():
            for copy in copies:
                copy.wait()
            total = (self.buffer[turn, 0] + self.buffer[turn, 1]) + (
                self.buffer[turn, 2] + self.buffer[turn, 3]
            )
            spread = jnp.concatenate([total, jnp.zeros((120, SEQ), F32)], 0).T
            return [spread[:, i : i + 1] for i in range(len(columns))]

        return wait


def block_slice(index):
    return pl.ds(pl.multiple_of(index * TOK, TOK), TOK)


def scatter_product(left, right, part, got, send, recv):
    x, y, z, core = here()
    copies = []
    for k in (2, 1, 3, 0):
        rows = block_slice(block_of(z + k))
        part[rows] = contract_last(left[rows], right).astype(BF)
        if k:
            copies.append(
                remote(part.at[rows], got.at[k - 1], send.at[k - 1], recv.at[k - 1], chip(x, y, z + k, core))
            )
            copies[-1].start()
    return copies


def collect(part, got, copies):
    z = here()[2]
    for copy in copies:
        copy.wait_recv()
    total = part[block_slice(block_of(z))].astype(F32)
    for k in range(3):
        total = total + got[k].astype(F32)
    return total


def spread_block(out, value, send, recv):
    x, y, z, core = here()
    rows = block_slice(block_of(z))
    out[rows] = value
    copies = []
    for k in (2, 1, 3):
        copies.append(
            remote(out.at[rows], out.at[rows], send.at[k - 1], recv.at[k - 1], chip(x, y, z + k, core))
        )
        copies[-1].start()
    return copies


def inverse_root(total):
    return lax.rsqrt(total * (1.0 / D) + NORM_EPSILON)


V_SELF, V_CROSS, V_DOWN, V_GAIN, V_BIAS = 6, 7, 8, 9, 10
W_QKV, W_QUERY, W_TEXT, W_SELF, W_CROSS = (
    slice(0, 3 * HW), slice(3 * HW, 4 * HW), slice(4 * HW, 6 * HW), slice(6 * HW, 7 * HW), slice(7 * HW, 8 * HW),
)
ATTN = 8 * HW


def forward_kernel(
    send_attn, send_mlp, tok, txt, cot, tab, heads, vec,
    w_attn, w_up, w_down, cot_all, tab_all, input_one, input_three, input_mlp, query_lin, key_lin,
    query_two_lin, key_two_lin, inv, query_rot, key_rot, value_low, query_two, key_two, value_two,
    mixed, mixed_two, branch_one, after_one, after_two, tok_all, txt_all,
    wa, got_attn, got_mlp, own_attn, own_mlp, part_one, part_two, blocks, stat,
    xs, xr, ks, kr, ms, mr, js, jr, rs, rr, cs, cr, loc, stat_s, stat_r, zs, zr, gs, gr,
):
    x, y, z, core = here()
    mine = x * SIDE + y
    greet(
        [device for pair in steps_of(x, y, z, core) for device in pair] + column(x, y, z, core)
    )
    attn_start, attn_wait, attn_drain = share_rows(send_attn, got_attn, rs.at[0], rr.at[0], loc.at[0])
    mlp_start, mlp_wait, mlp_drain = share_rows(send_mlp, got_mlp, rs.at[1], rr.at[1], loc.at[1])
    acts = [
        share_clip(src, dst, cs.at[i], cr.at[i], loc.at[2 + i, 0])
        for i, (src, dst) in enumerate(
            ((tok, tok_all), (tab, tab_all), (txt, txt_all), (cot, cot_all))
        )
    ]
    attn_start()
    acts[0][0]()
    acts[1][0]()
    attn_wait(own_attn)

    def attn_place(part, index, half=None):
        start, size = part * (ATTN // 2), ATTN // 2
        if half is not None:
            start, size = start + half * (ATTN // 4), ATTN // 4
        rows = pl.ds(pl.multiple_of(index * (2 * PAIR) + core * PAIR, PAIR), PAIR)
        return wa.at[rows, pl.ds(start, size)]

    def mlp_place(part, index, half=None):
        start, size = (0, FF) if half is None else (half * (FF // 2), FF // 2)
        rows = pl.ds(pl.multiple_of(index * (2 * PAIR) + core * PAIR, PAIR), PAIR)
        return (w_up, w_down)[part].at[rows, pl.ds(start, size)]

    gather_attn = gather_xy(own_attn, attn_place, xs, xr, ks, kr)
    advance(gather_attn)
    for part in (0, 1):
        attn_place(part, mine)[...] = own_attn[part]
    acts[2][0]()
    mlp_start()
    acts[3][0]()
    acts[0][1]()

    def norm_block(i, carry):
        normed, _ = plain_norm(tok_all[i].astype(F32))
        input_one[block_slice(i)] = (normed * (1.0 + vec[1:2]) + vec[0:1]).astype(BF)
        return carry

    advance(gather_attn, 2)
    lax.fori_loop(0, 2, norm_block, 0)
    advance(gather_attn, 2)
    lax.fori_loop(2, 4, norm_block, 0)
    advance(gather_attn, 2)
    mlp_wait(own_mlp)
    locals_ = []
    for part in (0, 1):
        locals_.append(pltpu.make_async_copy(own_mlp.at[part], mlp_place(part, mine), loc.at[6, part]))
        locals_[-1].start()
    finish(gather_attn)
    gather_mlp = gather_xy(own_mlp, mlp_place, ms, mr, js, jr)
    advance(gather_mlp)
    locals_.append(pltpu.make_async_copy(wa, w_attn, loc.at[7, 0]))
    locals_[-1].start()
    acts[1][1]()
    acts[2][1]()

    stats = Stats(stat, stat_s, stat_r)
    query_lin[...] = product(input_one[...], wa[:, 0:HW]) + heads[0:1]
    key_lin[...] = product(input_one[...], wa[:, HW : 2 * HW]) + heads[1:2]
    words = txt_all[...].reshape(SEQ, D)
    key_two_lin[...] = product(words, wa[:, 4 * HW : 5 * HW]) + heads[6:7]
    advance(gather_mlp)
    norm_wait = stats.start(
        0,
        [
            jnp.sum(ref[...] * ref[...], -1, keepdims=True)
            for ref in (query_lin, key_lin, key_two_lin)
        ],
    )
    value_low[...] = (product(input_one[...], wa[:, 2 * HW : 3 * HW]) + heads[2:3]).astype(BF)
    advance(gather_mlp)
    value_two[...] = (product(words, wa[:, 5 * HW : 6 * HW]) + heads[7:8]).astype(BF)
    advance(gather_mlp)
    lane = lax.broadcasted_iota(jnp.int32, (SEQ, 128), 1)
    inverse_query, inverse_key, inverse_key_two = [inverse_root(v) for v in norm_wait()]
    inv[...] = jnp.where(
        lane == 0, inverse_query, jnp.where(lane == 1, inverse_key, jnp.where(lane == 2, inverse_key_two, 0.0))
    )
    cosine, sine = rope_pair(tab_all[...].reshape(SEQ, HEAD))
    for h in range(HEADS):
        cols = head_slice(h)
        for lin, inverse, gain, out in (
            (query_lin, inverse_query, 3, query_rot),
            (key_lin, inverse_key, 4, key_rot),
        ):
            value = lin[:, cols] * inverse * (1.0 + heads[gain : gain + 1, cols])
            out[:, cols] = (value * cosine + swap_halves(value) * sine).astype(BF)
    key_two[...] = (key_two_lin[...] * inverse_key_two * (1.0 + heads[9:10])).astype(BF)
    attend_clip(query_rot, key_rot, value_low, mixed)
    advance(gather_mlp)
    copies = scatter_product(mixed, wa[:, W_SELF], part_one, blocks.at[0], zs.at[0], zr.at[0])
    drains = list(copies)
    advance(gather_mlp, 3)
    branch = collect(part_one, blocks.at[0], copies) + vec[V_SELF : V_SELF + 1]
    branch_one[...] = branch
    after = tok_all[block_of(z)].astype(F32) + vec[2:3] * branch
    after_one[...] = after
    normed, _ = plain_norm(after)
    copies = spread_block(
        input_three,
        (normed * (1.0 + vec[V_GAIN : V_GAIN + 1]) + vec[V_BIAS : V_BIAS + 1]).astype(BF),
        gs.at[0],
        gr.at[0],
    )
    drains += copies
    advance(gather_mlp, 3)
    for copy in copies:
        copy.wait_recv()
    query_two_lin[...] = product(input_three[...], wa[:, W_QUERY]) + heads[5:6]
    norm_wait = stats.start(1, [jnp.sum(query_two_lin[...] * query_two_lin[...], -1, keepdims=True)])
    advance(gather_mlp, 1)
    inverse_query_two = inverse_root(norm_wait()[0])
    inv[...] = jnp.where(lane == 3, inverse_query_two, inv[...])
    query_two[...] = (query_two_lin[...] * inverse_query_two * (1.0 + heads[8:9])).astype(BF)
    attend_clip(query_two, key_two, value_two, mixed_two)
    copies = scatter_product(mixed_two, wa[:, W_CROSS], part_two, blocks.at[1], zs.at[1], zr.at[1])
    drains += copies
    advance(gather_mlp, 2)
    after = after_one[...] + collect(part_two, blocks.at[1], copies) + vec[V_CROSS : V_CROSS + 1]
    after_two[...] = after
    normed, _ = plain_norm(after)
    copies = spread_block(
        input_mlp, (normed * (1.0 + vec[4:5]) + vec[3:4]).astype(BF), gs.at[1], gr.at[1]
    )
    drains += copies
    finish(gather_mlp)
    for copy in copies:
        copy.wait_recv()
    for copy in drains:
        copy.wait_send()
    for copy in locals_:
        copy.wait()
    acts[3][1]()
    for act in acts:
        act[2]()
    attn_drain()
    mlp_drain()


def forward(send_attn, send_mlp, tok, txt, cot, tab, heads, vec):
    dma = pltpu.SemaphoreType.DMA
    sds = jax.ShapeDtypeStruct
    wide, lin, low = sds((SEQ, D), BF), sds((SEQ, HW), F32), sds((SEQ, HW), BF)
    block = sds((TOK, D), F32)
    outs = [
        (sds((D, ATTN), BF), HB), (sds((D, FF), BF), HB), (sds((D, FF), BF), HB),
        (sds((SIDE, TOK, D), BF), HB), (sds((SIDE, TOK, HEAD), F32), VM),
        (wide, VM), (wide, VM), (wide, VM),
        (lin, VM), (lin, VM), (lin, VM), (lin, VM), (sds((SEQ, 128), F32), VM),
        (low, VM), (low, VM), (low, VM), (low, VM), (low, VM), (low, VM), (low, VM), (low, VM),
        (block, VM), (block, VM), (block, VM),
        (sds((SIDE, TOK, D), BF), VM), (sds((SIDE, TOK, D), BF), VM),
    ]
    return pl.pallas_call(
        forward_kernel,
        out_shape=[shape for shape, _ in outs],
        in_specs=[VM, VM, HB, HB, HB, VM, VM, VM],
        out_specs=[spec for _, spec in outs],
        scratch_shapes=[
            pltpu.VMEM((D, ATTN), BF),
            pltpu.VMEM((2, PAIR, ATTN // 2), BF),
            pltpu.VMEM((2, PAIR, FF), BF),
            pltpu.VMEM((2, PAIR, ATTN // 2), BF),
            pltpu.VMEM((2, PAIR, FF), BF),
            pltpu.VMEM((SEQ, D), BF),
            pltpu.VMEM((SEQ, D), BF),
            pltpu.VMEM((2, 3, TOK, D), BF),
            pltpu.VMEM((2, 4, 8, SEQ), F32),
            *[dma(s) for s in GATHER_SEMS],
            *[dma(s) for s in GATHER_SEMS],
            dma((2, 2)), dma((2, 2)), dma((4, 3)), dma((4, 3)), dma((8, 2)),
            dma((2, 3)), dma((2, 3)), dma((2, 3)), dma((2, 3)), dma((2, 3)), dma((2, 3)),
        ],
        compiler_params=params(0),
        name="forward",
    )(send_attn, send_mlp, tok, txt, cot, tab, heads, vec)


def z_peers(x, y, z, core):
    return [chip(x, y, z + k, core) for k in (1, 2, 3)]


def total_kernel(part, out, got, send, recv):
    x, y, z, core = here()
    greet(z_peers(x, y, z, core))
    copies = []
    for k in (1, 2, 3):
        copies.append(
            remote(part, got.at[k - 1], send.at[k - 1], recv.at[k - 1], chip(x, y, z + k, core))
        )
        copies[-1].start()
    for copy in copies:
        copy.wait()
    out[...] = part[...] + got[0] + got[1] + got[2]


def z_total(values, cid):
    dma = pltpu.SemaphoreType.DMA
    return pl.pallas_call(
        total_kernel,
        out_shape=jax.ShapeDtypeStruct(values.shape, F32),
        in_specs=[VM],
        out_specs=VM,
        scratch_shapes=[pltpu.VMEM((3,) + values.shape, F32), dma((3,)), dma((3,))],
        compiler_params=params(cid),
        name=f"z_total_{cid}",
    )(values)


def scatter_start(parts, got, send, recv):
    x, y, z, core = here()
    copies = []
    for i, part in enumerate(parts):
        for k in (2, 1, 3):
            rows = pl.ds(pl.multiple_of(block_of(z + k) * TOK, TOK), TOK)
            copy = remote(
                part.at[rows], got.at[i, k - 1], send.at[i, k - 1], recv.at[i, k - 1],
                chip(x, y, z + k, core),
            )
            copy.start()
            copies.append(copy)
    return copies


def own_sum(part, got, i, z):
    rows = pl.ds(pl.multiple_of(block_of(z) * TOK, TOK), TOK)
    total = part[rows].astype(F32)
    for k in range(3):
        total = total + got[i, k].astype(F32)
    return total


def step_kernel(compute, extra_count, out_count, *refs):
    part = refs[0]
    extras = refs[1 : 1 + extra_count]
    gathered = refs[1 + extra_count]
    outs = refs[2 + extra_count : 2 + extra_count + out_count]
    got, send, recv, gsend, grecv = refs[2 + extra_count + out_count :]
    x, y, z, core = here()
    greet(z_peers(x, y, z, core))
    copies = scatter_start([part], got, send, recv)
    for copy in copies:
        copy.wait_recv()
    total = own_sum(part, got, 0, z)
    result = compute(total, extras, outs)
    rows = pl.ds(pl.multiple_of(block_of(z) * TOK, TOK), TOK)
    gathered[rows] = result
    gathers = []
    for k in (2, 1, 3):
        copy = remote(
            gathered.at[rows], gathered.at[rows], gsend.at[k - 1], grecv.at[k - 1],
            chip(x, y, z + k, core),
        )
        copy.start()
        gathers.append(copy)
    for copy in gathers:
        copy.wait()
    for copy in copies:
        copy.wait_send()


def z_step(part, extras, compute, out_shapes, cid):
    dma = pltpu.SemaphoreType.DMA
    return pl.pallas_call(
        partial(step_kernel, compute, len(extras), len(out_shapes)),
        out_shape=[jax.ShapeDtypeStruct((SEQ, D), BF)] + out_shapes,
        in_specs=[VM] * (1 + len(extras)),
        out_specs=[VM] * (1 + len(out_shapes)),
        scratch_shapes=[pltpu.VMEM((1, 3, TOK, D), BF), dma((1, 3)), dma((1, 3)), dma((3,)), dma((3,))],
        compiler_params=params(cid),
        name=f"z_step_{cid}",
    )(part, *extras)


def scatter_kernel(count, *refs):
    parts, outs = refs[:count], refs[count : 2 * count]
    got, send, recv = refs[2 * count :]
    x, y, z, core = here()
    greet(z_peers(x, y, z, core))
    copies = scatter_start(parts, got, send, recv)
    for i in range(count):
        for copy in copies[3 * i : 3 * i + 3]:
            copy.wait()
        outs[i][...] = own_sum(parts[i], got, i, z)


def z_scatter(parts, cid):
    count = len(parts)
    dma = pltpu.SemaphoreType.DMA
    return pl.pallas_call(
        partial(scatter_kernel, count),
        out_shape=[jax.ShapeDtypeStruct((TOK, D), F32)] * count,
        in_specs=[VM] * count,
        out_specs=[VM] * count,
        scratch_shapes=[pltpu.VMEM((count, 3, TOK, D), BF), dma((count, 3)), dma((count, 3))],
        compiler_params=params(cid),
        name=f"z_scatter_{cid}",
    )(*parts)


def deliver_kernel(count, *refs):
    srcs, dsts = refs[:count], refs[count : 2 * count]
    send, recv, loc = refs[2 * count :]
    x, y, z, core = here()
    zh = lax.div(z, 2)
    greet(column(x, y, z, core))
    far = [
        remote(s, d.at[core], send.at[i, 0], recv.at[i, core], chip(x, y, z + 2, zh))
        for i, (s, d) in enumerate(zip(srcs, dsts))
    ]
    near = [
        remote(s, d.at[core], send.at[i, 1], recv.at[i, core], chip(x, y, z, zh))
        for i, (s, d) in enumerate(zip(srcs, dsts))
    ]
    self_copies = [
        pltpu.make_async_copy(s, d.at[core], loc.at[i]) for i, (s, d) in enumerate(zip(srcs, dsts))
    ]
    for copy in far:
        copy.start()

    def got(i, slot):
        remote(
            srcs[i], dsts[i].at[slot], send.at[i, 0], recv.at[i, slot], chip(x, y, z, core)
        ).wait_recv()

    @pl.when(core == zh)
    def _():
        for copy in self_copies:
            copy.start()
        for i in range(count):
            self_copies[i].wait()
            got(i, 1 - core)

    @pl.when(core != zh)
    def _():
        for copy in near:
            copy.start()
        for i in range(count):
            near[i].wait_send()
            got(i, 0)
            got(i, 1)

    for copy in far:
        copy.wait_send()


def deliver(arrays, cid):
    count = len(arrays)
    dma = pltpu.SemaphoreType.DMA
    return pl.pallas_call(
        partial(deliver_kernel, count),
        out_shape=[jax.ShapeDtypeStruct((2,) + a.shape, a.dtype) for a in arrays],
        in_specs=[VM] * count,
        out_specs=[VM] * count,
        scratch_shapes=[dma((count, 2)), dma((count, 2)), dma((count,))],
        compiler_params=params(cid),
        name=f"deliver_{cid}",
    )(*arrays)


def vector_kernel(model, heads, time_out, model_out, head_out, col, hsib, mx, hx, sends, recvs):
    x, y, z, core = here()
    zl = lax.rem(z, 2)
    rows = [chip(x + k, y, z, core) for k in (1, 2, 3)]
    lines = [chip(x, y + k, z, core) for k in (1, 2, 3)]
    greet(column(x, y, z, core) + rows + lines)
    copies = []
    for k in (1, 2, 3):
        copies.append(
            remote(model, col.at[0, k - 1], sends.at[0, k], recvs.at[0, k], chip(x, y, z + k, core))
        )
    for k in range(4):
        copies.append(
            remote(model, col.at[1, k], sends.at[1, k], recvs.at[1, k], chip(x, y, z + k, 1 - core))
        )
    copies.append(remote(heads, hsib, sends.at[0, 0], recvs.at[0, 0], chip(x, y, z, 1 - core)))
    for copy in copies:
        copy.start()
    for copy in copies:
        copy.wait()
    same = model[...] + col[0, 0] + col[0, 1] + col[0, 2]
    sib = col[1, 0] + col[1, 1] + col[1, 2] + col[1, 3]
    time_out[core] = same
    time_out[1 - core] = sib
    mx[0] = same + sib
    hx[0] = heads[...] + hsib[...]
    for stage, peers in enumerate((rows, lines)):
        copies = []
        for k in (1, 2, 3):
            at = 1 + 3 * stage + k - 1
            copies.append(
                remote(mx.at[4 * stage], mx.at[4 * stage + k], sends.at[2 + 2 * stage, k],
                       recvs.at[2 + 2 * stage, k], peers[k - 1])
            )
            copies.append(
                remote(hx.at[4 * stage], hx.at[4 * stage + k], sends.at[3 + 2 * stage, k],
                       recvs.at[3 + 2 * stage, k], peers[k - 1])
            )
        for copy in copies:
            copy.start()
        for copy in copies:
            copy.wait()
        base = 4 * stage
        mx[base + 4] = mx[base] + mx[base + 1] + mx[base + 2] + mx[base + 3]
        hx[base + 4] = hx[base] + hx[base + 1] + hx[base + 2] + hx[base + 3]
    model_out[...] = mx[8]
    head_out[zl] = hx[8]
    last = remote(
        hx.at[8], head_out.at[zl], sends.at[6, 0], recvs.at[6, 0], chip(x, y, z + 1 - 2 * zl, core)
    )
    last.start()
    last.wait()


def vector_sums(model, heads, cid):
    dma = pltpu.SemaphoreType.DMA
    return pl.pallas_call(
        vector_kernel,
        out_shape=[
            jax.ShapeDtypeStruct((2, 16, D), F32),
            jax.ShapeDtypeStruct((16, D), F32),
            jax.ShapeDtypeStruct((2, 16, HW), F32),
        ],
        in_specs=[VM, VM],
        out_specs=[VM, VM, VM],
        scratch_shapes=[
            pltpu.VMEM((2, 4, 16, D), F32),
            pltpu.VMEM((16, HW), F32),
            pltpu.VMEM((9, 16, D), F32),
            pltpu.VMEM((9, 16, HW), F32),
            dma((7, 4)),
            dma((7, 4)),
        ],
        compiler_params=params(cid),
        name="vector_sums",
    )(model, heads)


GRAD_WIDTHS = (3 * HW, HW, 2 * HW, HW, HW, FF, FF)


def grad_kernel(*refs):
    grads = refs[: len(GRAD_WIDTHS)]
    out, own, sib, r1, r2, tosend, ls, ss, sr, s1, q1, s2, q2, s3, q3, l3 = refs[len(GRAD_WIDTHS) :]
    x, y, z, core = here()
    zl = lax.rem(z, 2)
    rows = [chip(x + k, y, z, core) for k in (1, 2, 3)]
    lines = [chip(x, y + k, z, core) for k in (1, 2, 3)]
    greet(column(x, y, z, core) + rows + lines)
    start, pairs = 0, []
    for i, width in enumerate(GRAD_WIDTHS):
        cols = pl.ds(start, width)
        mine = pltpu.make_async_copy(grads[i].at[:, :, core], own.at[:, :, :, cols], ls.at[i])
        theirs = remote(
            grads[i].at[:, :, 1 - core], sib.at[:, :, :, cols], ss.at[i], sr.at[i], chip(x, y, z, 1 - core)
        )
        mine.start()
        theirs.start()
        pairs.append((mine, theirs))
        start += width
    for mine, theirs in pairs:
        mine.wait()
        theirs.wait()

    def add_pair(k, carry):
        a, b = lax.div(k, SIDE), lax.rem(k, SIDE)
        own[a, b] = (own[a, b].astype(F32) + sib[a, b].astype(F32)).astype(BF)
        return carry

    lax.fori_loop(0, SIDE * SIDE, add_pair, 0)
    wrap = lambda v: lax.rem(v, SIDE)
    first, second = pl.ds(0, HALF), pl.ds(HALF, HALF)
    one = []
    for k in (2, 1, 3):
        one.append(
            remote(own.at[:, wrap(y + k), :, first], r1.at[0, k - 1], s1.at[0, k - 1], q1.at[0, k - 1], lines[k - 1])
        )
        one.append(
            remote(own.at[wrap(x + k), :, :, second], r1.at[1, k - 1], s1.at[1, k - 1], q1.at[1, k - 1], rows[k - 1])
        )
    for copy in one:
        copy.start()
    for copy in one:
        copy.wait()

    def add_line(k, carry):
        total = own[k, y, :, :HALF].astype(F32)
        for i in range(3):
            total = total + r1[0, i, k].astype(F32)
        own[k, y, :, :HALF] = total.astype(BF)
        total = own[x, k, :, HALF:].astype(F32)
        for i in range(3):
            total = total + r1[1, i, k].astype(F32)
        own[x, k, :, HALF:] = total.astype(BF)
        return carry

    lax.fori_loop(0, SIDE, add_line, 0)
    two = []
    for k in (2, 1, 3):
        two.append(
            remote(own.at[wrap(x + k), y, :, first], r2.at[0, k - 1], s2.at[0, k - 1], q2.at[0, k - 1], rows[k - 1])
        )
        two.append(
            remote(own.at[x, wrap(y + k), :, second], r2.at[1, k - 1], s2.at[1, k - 1], q2.at[1, k - 1], lines[k - 1])
        )
    for copy in two:
        copy.start()
    for copy in two:
        copy.wait()
    final = []
    for part in (0, 1):
        total = own[x, y, :, pl.ds(part * HALF, HALF)].astype(F32)
        for i in range(3):
            total = total + r2[part, i].astype(F32)
        final.append(total)
    for target in (0, 1):
        rows_of = slice(target * ROWS, target * ROWS + ROWS)
        tosend[target] = jnp.concatenate([final[0][rows_of], final[1][rows_of]], 0).astype(BF)
    other = z + 1 - 2 * zl
    far = [
        remote(tosend.at[t], out.at[zl], s3.at[t], q3.at[zl], chip(x, y, other, t)) for t in (0, 1)
    ]
    self_copy = pltpu.make_async_copy(tosend.at[core], out.at[zl], l3.at[0])
    near = remote(tosend.at[1 - core], out.at[zl], s3.at[0], q3.at[zl], chip(x, y, z, 1 - core))

    def got(slot):
        remote(tosend.at[0], out.at[slot], s3.at[0], q3.at[slot], chip(x, y, z, core)).wait_recv()

    @pl.when(core == zl)
    def _():
        self_copy.start()
        near.start()
        self_copy.wait()
        near.wait_send()
        got(1 - zl)

    @pl.when(core != zl)
    def _():
        for copy in far:
            copy.start()
        for copy in far:
            copy.wait_send()
        got(zl)
        got(1 - zl)


def grad_sums(grads, cid):
    dma = pltpu.SemaphoreType.DMA
    count = len(GRAD_WIDTHS)
    return pl.pallas_call(
        grad_kernel,
        out_shape=jax.ShapeDtypeStruct((2, PAIR, HALF), BF),
        in_specs=[HB] * count,
        out_specs=VM,
        scratch_shapes=[
            pltpu.VMEM((SIDE, SIDE, PAIR, COLS), BF),
            pltpu.VMEM((SIDE, SIDE, PAIR, COLS), BF),
            pltpu.VMEM((2, 3, SIDE, PAIR, HALF), BF),
            pltpu.VMEM((2, 3, PAIR, HALF), BF),
            pltpu.VMEM((2, PAIR, HALF), BF),
            dma((count,)), dma((count,)), dma((count,)),
            dma((2, 3)), dma((2, 3)), dma((2, 3)), dma((2, 3)),
            dma((2,)), dma((2,)), dma((1,)),
        ],
        compiler_params=params(cid),
        name="grad_sums",
    )(*grads)


def newton_kernel(narrow, wide, narrow_out, wide_out, mine, theirs, send, recv):
    x, y, z, core = here()
    partner = chip(x, y, z + 2, core)
    greet([partner])
    n, w = narrow.shape[0], wide.shape[0]
    size = n + w
    contract = (((1,), (1,)), ((), ()))
    mine[...] = jnp.zeros_like(mine)
    mine[:n, :n] = lax.dot_general(
        narrow[...], narrow[...], contract, precision=HIGHEST, preferred_element_type=F32
    )
    mine[n:, n:] = lax.dot_general(
        wide[...], wide[...], contract, precision=HIGHEST, preferred_element_type=F32
    )
    copy = remote(mine, theirs, send.at[0], recv.at[0], partner)
    copy.start()
    copy.wait()
    block_row = lax.div(lax.broadcasted_iota(jnp.int32, (size, size), 0), ROWS)
    block_col = lax.div(lax.broadcasted_iota(jnp.int32, (size, size), 1), ROWS)
    same = block_row == block_col
    eye = lax.broadcasted_iota(jnp.int32, (size, size), 0) == lax.broadcasted_iota(
        jnp.int32, (size, size), 1
    )
    gram = jnp.where(same, mine[...] + theirs[...], 0.0)
    diagonal = jnp.where(eye, gram, 0.0)
    by_row = jnp.sum(diagonal, 1, keepdims=True)
    by_col = jnp.sum(diagonal, 0, keepdims=True)
    total_row = jnp.sum(jnp.where(same, by_col, 0.0), 1, keepdims=True)
    total_col = jnp.sum(jnp.where(same, by_row, 0.0), 0, keepdims=True)
    scale_row = 1.0 / (jnp.sqrt(total_row) + ORTHO_EPSILON)
    scale_col = 1.0 / (jnp.sqrt(total_col) + ORTHO_EPSILON)
    current = gram * scale_row * scale_col

    def times(a, b):
        return jnp.dot(a, b, precision=HIGHEST, preferred_element_type=F32)

    whole = None
    for turn in range(NS_STEPS):
        square = times(current, current)
        step = NEWTON_SECOND * current + NEWTON_THIRD * square + jnp.where(eye, NEWTON_FIRST, 0.0)
        whole = step if whole is None else times(step, whole)
        if turn + 1 < NS_STEPS:
            current = times(times(step, current), step)
    whole = whole * scale_col
    narrow_out[...] = times(whole[:n, :n], narrow[...])
    wide_out[...] = times(whole[n:, n:], wide[...])


def newton(narrow, wide, cid):
    size = narrow.shape[0] + wide.shape[0]
    dma = pltpu.SemaphoreType.DMA
    return pl.pallas_call(
        newton_kernel,
        out_shape=[
            jax.ShapeDtypeStruct(narrow.shape, F32),
            jax.ShapeDtypeStruct(wide.shape, F32),
        ],
        in_specs=[VM, VM],
        out_specs=[VM, VM],
        scratch_shapes=[
            pltpu.VMEM((size, size), F32),
            pltpu.VMEM((size, size), F32),
            dma((1,)),
            dma((1,)),
        ],
        compiler_params=params(cid),
        name="newton",
    )(narrow, wide)


def rope_tables(places):
    pair_index = jnp.arange(HEAD // 2, dtype=jnp.int32)
    side_pairs = HEAD // 6
    frame_pairs = (HEAD - 4 * side_pairs) // 2
    part_of = (pair_index >= frame_pairs).astype(jnp.int32) + (
        pair_index >= frame_pairs + side_pairs
    ).astype(jnp.int32)
    offset = jnp.where(
        part_of == 0, 0, jnp.where(part_of == 1, frame_pairs, frame_pairs + side_pairs)
    ).astype(jnp.int32)
    extent = jnp.where(part_of == 0, 2 * frame_pairs, 2 * side_pairs).astype(jnp.float32)
    frequency = jnp.exp(
        (pair_index - offset).astype(jnp.float32) * (-2.0 * math.log(10000.0)) / extent
    )
    chosen = (
        places[0][:, None] * (part_of == 0)
        + places[1][:, None] * (part_of == 1)
        + places[2][:, None] * (part_of == 2)
    )
    angles = chosen.astype(jnp.float32) * frequency
    return (jnp.cos(angles), jnp.sin(angles))


def rotate(values, cosine, sine):
    half_head = HEAD // 2
    front_half = values[..., :half_head]
    back_half = values[..., half_head:]
    return jnp.concatenate(
        [front_half * cosine - back_half * sine, back_half * cosine + front_half * sine], -1
    )


def plain_norm(values):
    centred = values - jnp.mean(values, -1, keepdims=True)
    inverse = lax.rsqrt(jnp.mean(centred * centred, -1, keepdims=True) + NORM_EPSILON)
    return (centred * inverse, inverse)


def norm_back(grads, normed, inverse):
    return inverse * (
        grads
        - jnp.mean(grads, -1, keepdims=True)
        - normed * jnp.mean(grads * normed, -1, keepdims=True)
    )


def split_heads(values):
    return values.reshape(values.shape[0], -1, HEAD)


def merge_heads(values):
    return values.reshape(values.shape[0], -1)


def product(left, right):
    return jnp.dot(left, right, preferred_element_type=F32)


def contract_last(left, right):
    return lax.dot_general(left, right, (((1,), (1,)), ((), ())), preferred_element_type=F32)


def contract_rows(left, right):
    return lax.dot_general(left, right, (((0,), (0,)), ((), ())), preferred_element_type=F32)


def attend_back(query, keys, values, grad_mixed):
    scores = jnp.einsum("qhe,khe->hqk", query, keys, preferred_element_type=F32) * HEAD ** (-0.5)
    weights = jax.nn.softmax(scores, -1)
    grad_weights = jnp.einsum("qhe,khe->hqk", grad_mixed, values, preferred_element_type=F32)
    row_delta = jnp.sum(weights * grad_weights, -1, keepdims=True)
    grad_scores = (weights * (grad_weights - row_delta)).astype(BF)
    grad_query = jnp.einsum("hqk,khe->qhe", grad_scores, keys, preferred_element_type=F32) * HEAD ** (
        -0.5
    )
    grad_keys = jnp.einsum("hqk,qhe->khe", grad_scores, query, preferred_element_type=F32) * HEAD ** (
        -0.5
    )
    grad_values = jnp.einsum(
        "hqk,qhe->khe", weights.astype(BF), grad_mixed, preferred_element_type=F32
    )
    return grad_query, grad_keys, merge_heads(grad_values)


def block_struct():
    return jax.ShapeDtypeStruct((TOK, D), F32)


def back_mlp(total, extras, outs):
    after, grads, rows = extras
    normed, inverse = plain_norm(after[...])
    outs[1][0:1] = jnp.sum(total, 0, keepdims=True)
    outs[1][1:2] = jnp.sum(total * normed, 0, keepdims=True)
    result = grads[...].astype(F32) + norm_back(total * (1.0 + rows[0:1]), normed, inverse)
    outs[0][...] = result
    low = result.astype(BF)
    outs[1][2:3] = jnp.sum(low.astype(F32), 0, keepdims=True)
    return low


def back_cross(total, extras, outs):
    after, grads, branch, rows = extras
    normed, inverse = plain_norm(after[...])
    outs[1][0:1] = jnp.sum(total, 0, keepdims=True)
    outs[1][1:2] = jnp.sum(total * normed, 0, keepdims=True)
    result = grads[...] + norm_back(total * (1.0 + rows[0:1]), normed, inverse)
    outs[0][...] = result
    outs[1][2:3] = jnp.sum(result * branch[...], 0, keepdims=True)
    low = (result * rows[1:2]).astype(BF)
    outs[1][3:4] = jnp.sum(low.astype(F32), 0, keepdims=True)
    return low


def stack_rows(rows, count=8):
    out = jnp.stack(rows)
    return jnp.pad(out, ((0, count - len(rows)), (0, 0)))


def body(
    tokens, text, time_embedding, positions, cotangent, attn_in, attn_out, mlp, head_vectors,
    model_vectors, up_bias, attn_in_moment, attn_out_moment, mlp_moment, head_moment, model_moment,
    up_moment,
):
    x, y, z, core = here()
    zl = lax.rem(z, 2)
    block = block_of(z)

    low_in = attn_in.astype(BF).reshape(ROWS, 6, 2, HW).transpose(2, 0, 1, 3).reshape(2, ROWS, -1)
    low_out = attn_out.astype(BF).reshape(ROWS, 2, 2, HW).transpose(2, 0, 1, 3).reshape(2, ROWS, -1)
    send_attn = jnp.concatenate([low_in, low_out], -1).reshape(2, ROWS, 2, ATTN // 2)
    send_attn = send_attn.transpose(0, 2, 1, 3).reshape(2, PAIR, ATTN // 2)
    send_mlp = jnp.pad(
        mlp.astype(BF).reshape(ROWS, 2, 2, FF_REAL).transpose(2, 1, 0, 3),
        ((0, 0), (0, 0), (0, 0), (0, FF - FF_REAL)),
    ).reshape(2, PAIR, FF)
    cosine, sine = rope_tables(positions.reshape(3, 2 * TOK))
    table = jnp.concatenate([cosine, sine], -1).reshape(2, TOK, HEAD)

    heads = lax.dynamic_slice(head_vectors, (0, zl * HW), (10, HW))
    bias_up = jnp.pad(lax.dynamic_slice(up_bias, (zl * FF_REAL,), (FF_REAL,)), (0, FF - FF_REAL))
    modulation = model_vectors[5:] + lax.dynamic_index_in_dim(time_embedding, core, 0, False)
    shift_one, scale_one, gate_one, shift_two, scale_two, gate_two = [modulation[i] for i in range(6)]
    vectors = jnp.pad(jnp.concatenate([modulation, model_vectors[:5]], 0), ((0, 5), (0, 0)))

    (
        w_attn, w_up, w_down, cot_all, tab_all, input_one, input_three, input_mlp, query_lin, key_lin,
        query_two_lin, key_two_lin, inv, query_rot, key_rot, value_low, query_two, key_two, value_two,
        mixed_low, mixed_two_low, branch_one, after_one, after_two, tok_all, txt_all,
    ) = forward(
        send_attn, send_mlp, tokens, text, cotangent, table,
        jnp.pad(heads, ((0, 6), (0, 0))), vectors,
    )
    w_qkv, w_query, w_text, w_self, w_cross = [
        w_attn[:, s] for s in (W_QKV, W_QUERY, W_TEXT, W_SELF, W_CROSS)
    ]
    inverse_query, inverse_key, inverse_key_two, inverse_query_two = [
        inv[:, i : i + 1] for i in range(4)
    ]
    query_rot, key_rot, value_low, query_two, key_two, value_two = [
        split_heads(v) for v in (query_rot, key_rot, value_low, query_two, key_two, value_two)
    ]
    tab_all = tab_all.reshape(SEQ, 1, HEAD)
    cosine, sine = tab_all[..., : HEAD // 2], tab_all[..., HEAD // 2 :]

    def block_rows(values):
        return lax.dynamic_slice(values, (block * TOK, 0), (TOK, values.shape[1]))

    cot_all = cot_all.reshape(SEQ, D)
    words = txt_all.reshape(SEQ, D)
    tok_own = lax.dynamic_index_in_dim(tok_all, block, 0, False)
    cot_own = block_rows(cot_all)

    hidden_lin = product(input_mlp, w_up) + bias_up
    hidden_act, gelu_pullback = jax.vjp(partial(jax.nn.gelu, approximate=True), hidden_lin)
    hidden_low = hidden_act.astype(BF)
    part_mlp = contract_last(hidden_low, w_down).astype(BF)
    grad_branch_mlp = (cot_all.astype(F32) * gate_two).astype(BF)
    grad_hidden = gelu_pullback(product(grad_branch_mlp, w_down))[0].astype(BF)
    part = contract_last(grad_hidden, w_up).astype(BF)
    grad_branch_two, grad_after_two, sums_mlp = z_step(
        part,
        [after_two, cot_own, stack_rows([scale_two])],
        back_mlp,
        [block_struct(), jax.ShapeDtypeStruct((8, D), F32)],
        5,
    )
    grad_mixed_two = product(grad_branch_two, w_cross).astype(BF)
    grad_query_two, grad_key_two, grad_value_two = attend_back(
        query_two, key_two, value_two, split_heads(grad_mixed_two)
    )
    grad_query_two, grad_key_two = merge_heads(grad_query_two), merge_heads(grad_key_two)
    scaled_query_two = grad_query_two * (1.0 + heads[8])
    scaled_key_two = grad_key_two * (1.0 + heads[9])
    dots = z_total(
        stack_rows(
            [jnp.sum(query_two_lin * scaled_query_two, -1), jnp.sum(key_two_lin * scaled_key_two, -1)]
        ),
        6,
    )

    def root_back(linear, inverse, scaled, dot):
        return (inverse * scaled - linear * (inverse**3 * dot[:, None] / D)).astype(BF)

    grad_query_two_lin = root_back(query_two_lin, inverse_query_two, scaled_query_two, dots[0])
    grad_key_two_lin = root_back(key_two_lin, inverse_key_two, scaled_key_two, dots[1])
    grad_kv_two_lin = jnp.concatenate([grad_key_two_lin, grad_value_two.astype(BF)], 1)
    part = contract_last(grad_query_two_lin, w_query).astype(BF)
    part_words = contract_last(grad_kv_two_lin, w_text).astype(BF)
    grad_branch_one, grad_after_one, sums_cross = z_step(
        part,
        [after_one, grad_after_two, branch_one, stack_rows([model_vectors[3], gate_one])],
        back_cross,
        [block_struct(), jax.ShapeDtypeStruct((8, D), F32)],
        7,
    )
    grad_mixed = product(grad_branch_one, w_self).astype(BF)
    grad_query_rot, grad_key_rot, grad_value = attend_back(
        query_rot, key_rot, value_low, split_heads(grad_mixed)
    )
    grad_query_norm = merge_heads(rotate(grad_query_rot, cosine, -sine))
    grad_key_norm = merge_heads(rotate(grad_key_rot, cosine, -sine))
    scaled_query = grad_query_norm * (1.0 + heads[3])
    scaled_key = grad_key_norm * (1.0 + heads[4])
    dots_one = z_total(
        stack_rows([jnp.sum(query_lin * scaled_query, -1), jnp.sum(key_lin * scaled_key, -1)]), 8
    )
    grad_query_lin = root_back(query_lin, inverse_query, scaled_query, dots_one[0])
    grad_key_lin = root_back(key_lin, inverse_key, scaled_key, dots_one[1])
    grad_qkv = jnp.concatenate([grad_query_lin, grad_key_lin, grad_value.astype(BF)], 1)
    part_tokens = contract_last(grad_qkv, w_qkv).astype(BF)

    def rows_of(left, right):
        out = contract_rows(left, right).astype(BF)
        return out.reshape(SIDE, SIDE, 2, PAIR, out.shape[1])

    matrix_grads = [
        rows_of(input_one, grad_qkv),
        rows_of(input_three, grad_query_two_lin),
        rows_of(words, grad_kv_two_lin),
        rows_of(grad_branch_one, mixed_low),
        rows_of(grad_branch_two, mixed_two_low),
        rows_of(input_mlp, grad_hidden),
        rows_of(grad_branch_mlp, hidden_low),
    ]

    sum_mlp, sum_tokens, sum_words = z_scatter([part_mlp, part_tokens, part_words], 9)
    branch_mlp = sum_mlp + model_vectors[2]
    cot_f32 = cot_own.astype(F32)
    result = (after_two + gate_two * branch_mlp).astype(BF)
    normed_own, inverse_own = plain_norm(tok_own.astype(F32))
    grad_tokens = grad_after_one + norm_back(sum_tokens * (1.0 + scale_one), normed_own, inverse_own)
    column_sum = lambda v: jnp.sum(v.astype(F32), 0)
    model_part = stack_rows(
        [
            sums_cross[3],
            sums_mlp[2],
            column_sum(block_rows(grad_branch_mlp)),
            sums_cross[1],
            sums_cross[0],
            column_sum(sum_tokens),
            column_sum(sum_tokens * normed_own),
            sums_cross[2],
            sums_mlp[0],
            sums_mlp[1],
            column_sum(cot_f32 * branch_mlp),
        ],
        16,
    )
    grad_qkv_sum = column_sum(grad_qkv).reshape(3, HW)
    grad_kv_sum = column_sum(grad_kv_two_lin).reshape(2, HW)
    head_part = jnp.concatenate(
        [
            grad_qkv_sum,
            jnp.stack(
                [
                    column_sum(grad_query_norm * query_lin * inverse_query),
                    column_sum(grad_key_norm * key_lin * inverse_key),
                    column_sum(grad_query_two_lin),
                ]
            ),
            grad_kv_sum,
            jnp.stack(
                [
                    column_sum(grad_query_two * query_two_lin * inverse_query_two),
                    column_sum(grad_key_two * key_two_lin * inverse_key_two),
                ]
            ),
            column_sum(grad_hidden).reshape(6, HW),
        ],
        0,
    )
    out_result, out_tokens, out_words = deliver(
        [result, grad_tokens.astype(BF), sum_words.astype(BF)], 10
    )
    time_sums, model_sums, head_sums = vector_sums(model_part, head_part, 11)
    grad_time = time_sums[:, 5:11]
    model_total = model_sums[:11]
    head_total = head_sums[:, :10].transpose(1, 0, 2).reshape(10, 2 * HW)
    up_total = head_sums[:, 10:].reshape(2, FF)[:, :FF_REAL].reshape(-1)

    sums = grad_sums(matrix_grads, 12)
    sums = sums.reshape(2, 2, ROWS, HALF).transpose(0, 2, 1, 3).reshape(2, ROWS, COLS).astype(F32)
    def unpack(start, count, width, real):
        part = sums[:, :, start : start + count * width].reshape(2, ROWS, count, width)[..., :real]
        return part.transpose(2, 1, 0, 3).reshape(count, ROWS, 2 * real)

    swap = lambda v: v.transpose(1, 0, 2)
    new_in_moment = MOMENTUM * swap(attn_in_moment) + unpack(C_IN, 6, HW, HW)
    new_out_moment = MOMENTUM * swap(attn_out_moment) + unpack(C_OUT, 2, HW, HW)
    new_mlp_moment = MOMENTUM * swap(mlp_moment) + unpack(C_UP, 2, FF, FF_REAL)
    narrow = jnp.concatenate([new_in_moment, new_out_moment], 0).reshape(8 * ROWS, 2 * HW)
    wide = new_mlp_moment.reshape(2 * ROWS, 2 * FF_REAL)
    narrow_dir, wide_dir = newton(narrow, wide, 13)
    narrow_dir = narrow_dir.reshape(8, ROWS, 2 * HW)
    wide_dir = wide_dir.reshape(2, ROWS, 2 * FF_REAL)
    new_attn_in = attn_in * (1.0 - RATE_IN * DECAY) - RATE_IN * swap(narrow_dir[:6])
    new_attn_out = attn_out * (1.0 - RATE_OUT * DECAY) - RATE_OUT * swap(narrow_dir[6:])
    new_mlp = mlp * (1.0 - RATE_MLP * DECAY) - RATE_MLP * swap(wide_dir)
    new_head_moment = MOMENTUM * head_moment + head_total
    new_model_moment = MOMENTUM * model_moment + model_total
    new_up_moment = MOMENTUM * up_moment + up_total
    return (
        out_result,
        out_tokens.astype(F32),
        out_words.astype(F32),
        grad_time,
        new_attn_in,
        new_attn_out,
        new_mlp,
        swap(new_in_moment),
        swap(new_out_moment),
        swap(new_mlp_moment),
        head_vectors - RATE_VECTOR * new_head_moment,
        model_vectors - RATE_VECTOR * new_model_moment,
        up_bias - RATE_VECTOR * new_up_moment,
        new_head_moment,
        new_model_moment,
        new_up_moment,
    )


def solution(mesh):
    clip = P("fsdp", "ctx", None)
    whole = P("fsdp", None, None)
    matrix = P(("fsdp", "ctx"), None, "tp")
    in_specs = (
        clip, clip, whole, P(None, "fsdp", "ctx"), clip, matrix, matrix, matrix, P(None, "tp"), P(),
        P("tp"), matrix, matrix, matrix, P(None, "tp"), P(), P("tp"),
    )
    out_specs = (
        clip, clip, clip, whole, matrix, matrix, matrix, matrix, matrix, matrix, P(None, "tp"), P(),
        P("tp"), P(None, "tp"), P(), P("tp"),
    )
    return jax.shard_map(body, mesh=mesh, in_specs=in_specs, out_specs=out_specs, check_vma=False)
```

```python
from functools import partial
import math

import jax
import jax.numpy as jnp
from jax import lax
from jax.experimental import pallas as pl
from jax.experimental.pallas import tpu as pltpu
from jax.sharding import PartitionSpec as P

D = 1536
HEAD = 128
ROWS = 24
HEADS = 3
NORM_EPSILON = 1e-06
ORTHO_EPSILON = 1e-07
NEWTON_FIRST = 3.4445
NEWTON_SECOND = -4.775
NEWTON_THIRD = 2.0315
NS_STEPS = 5
MOMENTUM = 0.9
DECAY = 0.01
RATE_IN = 0.5
RATE_OUT = 4.0
RATE_MLP = 1.0
RATE_VECTOR = 0.005
HIGHEST = lax.Precision.HIGHEST

MESH = pl.DeviceIdType.MESH
BF = jnp.bfloat16
F32 = jnp.float32

SIDE = 4
TOK = 128
SEQ = SIDE * TOK
HW = HEADS * HEAD
FF_REAL = 2240
FF = 2304
PAIR = 2 * ROWS
VMEM_LIMIT = 60 * 1024 * 1024


def here():
    f = lax.axis_index("fsdp")
    c = lax.axis_index("ctx")
    t = lax.axis_index("tp")
    x, y = lax.div(f, SIDE), lax.rem(f, SIDE)
    zl, core = lax.div(c, 2), lax.rem(c, 2)
    return x, y, 2 * t + zl, core


def chip(x, y, z, core):
    x, y, z = lax.rem(x + SIDE, SIDE), lax.rem(y + SIDE, SIDE), lax.rem(z + SIDE, SIDE)
    return {"fsdp": x * SIDE + y, "ctx": lax.rem(z, 2) * 2 + core, "tp": lax.div(z, 2)}


def block_of(z):
    z = lax.rem(z + SIDE, SIDE)
    return 2 * lax.rem(z, 2) + lax.div(z, 2)


def greet(devices):
    barrier = pltpu.get_barrier_semaphore()
    for device in devices:
        pl.semaphore_signal(barrier, inc=1, device_id=device, device_id_type=MESH)
    pl.semaphore_wait(barrier, len(devices))


def column(x, y, z, core):
    return [chip(x, y, z + k, core) for k in (1, 2, 3)] + [
        chip(x, y, z + k, 1 - core) for k in range(4)
    ]


def remote(src, dst, send, recv, device):
    return pltpu.make_async_remote_copy(
        src_ref=src, dst_ref=dst, send_sem=send, recv_sem=recv, device_id=device, device_id_type=MESH
    )


def params(cid):
    return pltpu.CompilerParams(
        collective_id=cid, has_side_effects=True, vmem_limit_bytes=VMEM_LIMIT
    )


VM = pl.BlockSpec(memory_space=pltpu.VMEM)
HB = pl.BlockSpec(memory_space=pltpu.HBM)


def flat(a, b):
    return lax.rem(a + SIDE, SIDE) * SIDE + lax.rem(b + SIDE, SIDE)


def steps_of(x, y, z, core):
    return (
        (chip(x + 1, y, z, core), chip(x - 1, y, z, core)),
        (chip(x, y + 1, z, core), chip(x, y - 1, z, core)),
    )


def gather_xy(own, place, xs, xr, ks, kr):
    x, y, z, core = here()
    mine = x * SIDE + y
    steps = steps_of(x, y, z, core)
    sibling = chip(x, y, z, 1 - core)
    sends, sibs = [], []

    def push(part, slot, src, index, device, half=None):
        copy = remote(src, place(part, index, half), xs.at[part, slot], xr.at[part, slot], device)
        copy.start()
        sends.append(copy)
        return copy

    def to_sibling(part, slot, src, index):
        copy = remote(src, place(part, index), ks.at[part, slot], kr.at[part, slot], sibling)
        copy.start()
        sibs.append(copy)

    def index_of(part, first_off, second_off):
        if part == 0:
            return flat(x + first_off, y + second_off)
        return flat(x + second_off, y + first_off)

    one, two = {}, {}
    for part in (0, 1):
        a_next, a_prev = steps[part]
        one[part, "next"] = push(part, 0, own.at[part], mine, a_next)
        one[part, "prev"] = push(part, 1, own.at[part], mine, a_prev)
    for part in (0, 1):
        b_next, b_prev = steps[1 - part]
        two[part, 0, "next"] = push(part, 4, own.at[part], mine, b_next)
        two[part, 0, "prev"] = push(part, 5, own.at[part], mine, b_prev)
        to_sibling(part, 0, own.at[part], mine)

    def second_start(part, k, offset):
        b_next, b_prev = steps[1 - part]
        index = index_of(part, offset, 0)
        src = place(part, index)
        two[part, k, "next"] = push(part, 4 + 4 * k, src, index, b_next)
        two[part, k, "prev"] = push(part, 5 + 4 * k, src, index, b_prev)
        to_sibling(part, 4 * k, src, index)

    offsets = (0, -1, 1, 2)
    for part in (0, 1):
        a_next, a_prev = steps[part]
        yield
        one[part, "next"].wait_recv()
        index = index_of(part, -1, 0)
        one[part, "far0"] = push(part, 2, place(part, index, 0), index, a_next, 0)
        second_start(part, 1, -1)
        one[part, "prev"].wait_recv()
        index = index_of(part, 1, 0)
        one[part, "far1"] = push(part, 3, place(part, index, 1), index, a_prev, 1)
        second_start(part, 2, 1)

    def second_forward(part, k):
        b_next, b_prev = steps[1 - part]
        two[part, k, "next"].wait_recv()
        index = index_of(part, offsets[k], -1)
        two[part, k, "far0"] = push(part, 6 + 4 * k, place(part, index, 0), index, b_next, 0)
        to_sibling(part, 4 * k + 1, place(part, index), index)
        two[part, k, "prev"].wait_recv()
        index = index_of(part, offsets[k], 1)
        two[part, k, "far1"] = push(part, 7 + 4 * k, place(part, index, 1), index, b_prev, 1)
        to_sibling(part, 4 * k + 2, place(part, index), index)

    def second_finish(part, k):
        two[part, k, "far0"].wait_recv()
        two[part, k, "far1"].wait_recv()
        index = index_of(part, offsets[k], 2)
        to_sibling(part, 4 * k + 3, place(part, index), index)

    for part in (0, 1):
        yield
        second_forward(part, 0)
    for part in (0, 1):
        yield
        one[part, "far0"].wait_recv()
        one[part, "far1"].wait_recv()
        second_start(part, 3, 2)
    for k in (1, 2, 3):
        for part in (0, 1):
            yield
            second_forward(part, k)
        for part in (0, 1):
            second_finish(part, k - 1)
    for part in (0, 1):
        yield
        second_finish(part, 3)
    yield
    for copy in sends:
        copy.wait_send()
    for copy in sibs:
        copy.wait_send()
        copy.wait_recv()


GATHER_SEMS = ((2, 20), (2, 20), (2, 16), (2, 16))


def advance(job, count=1):
    for _ in range(count):
        next(job, None)


def finish(job):
    for _ in job:
        pass


def share_rows(send, recv, s, r, l):
    x, y, z, core = here()
    zl = lax.rem(z, 2)
    away = remote(send.at[1 - zl], recv.at[core], s.at[0], r.at[core], chip(x, y, z + 1 - 2 * zl, zl))
    near = remote(send.at[zl], recv.at[core], s.at[1], r.at[core], chip(x, y, z, zl))
    self_copy = pltpu.make_async_copy(send.at[zl], recv.at[core], l.at[0])

    def got(slot):
        remote(send.at[0], recv.at[slot], s.at[0], r.at[slot], chip(x, y, z, core)).wait_recv()

    def start():
        away.start()

        @pl.when(core == zl)
        def _():
            self_copy.start()

        @pl.when(core != zl)
        def _():
            near.start()

    def wait(own):
        @pl.when(core == zl)
        def _():
            self_copy.wait()
            got(1 - core)

        @pl.when(core != zl)
        def _():
            near.wait_send()
            got(0)
            got(1)

        first = recv[0].astype(F32)
        second = recv[1].astype(F32)
        own[0] = jnp.concatenate([first[:ROWS], second[:ROWS]], 0).astype(BF)
        own[1] = jnp.concatenate([first[ROWS:], second[ROWS:]], 0).astype(BF)

    return start, wait, away.wait_send


def share_clip(src, dst, s, r, l):
    x, y, z, core = here()
    put = dst.at[2 * lax.rem(z, 2) + core]
    copies = [
        remote(src.at[1 - core], put, s.at[0], r.at[0], chip(x, y, z, 1 - core)),
        remote(src.at[0], put, s.at[1], r.at[1 + core], chip(x, y, z + 1, 0)),
        remote(src.at[1], put, s.at[2], r.at[1 + core], chip(x, y, z - 1, 1)),
    ]
    local = pltpu.make_async_copy(src.at[core], put, l)

    def start():
        for copy in copies:
            copy.start()
        local.start()

    def wait():
        local.wait()
        for slot in range(3):
            remote(src.at[0], dst.at[0], s.at[0], r.at[slot], chip(x, y, z, core)).wait_recv()

    def drain():
        for copy in copies:
            copy.wait_send()

    return start, wait, drain


def split3(values):
    return [values[:, i * HW : (i + 1) * HW] for i in range(values.shape[1] // HW)]


def swap_halves(values):
    return pltpu.roll(values, HEAD // 2, 1)


def rope_pair(table):
    lane = lax.broadcasted_iota(jnp.int32, table.shape, 1)
    other = swap_halves(table)
    front = lane < HEAD // 2
    return jnp.where(front, table, other), jnp.where(front, -other, table)


def head_slice(h):
    return slice(h * HEAD, (h + 1) * HEAD)


SCALE = HEAD ** (-0.5)


def softmax_rows(query, keys):
    scores = contract_last(query, keys) * SCALE
    peak = jnp.max(scores, -1, keepdims=True)
    raised = jnp.exp(scores - peak)
    return raised * (1.0 / jnp.sum(raised, -1, keepdims=True))


def attend_clip(query, keys, values, out):
    for h in range(HEADS):
        cols = head_slice(h)
        for start in range(0, SEQ, 256):
            rows = slice(start, start + 256)
            weights = softmax_rows(query[rows, cols], keys[:, cols]).astype(BF)
            out[rows, cols] = product(weights, values[:, cols]).astype(BF)


class Stats:
    def __init__(self, buffer, send, recv):
        self.buffer, self.send, self.recv = buffer, send, recv

    def start(self, turn, columns):
        x, y, z, core = here()
        lane = lax.broadcasted_iota(jnp.int32, (SEQ, 128), 1)
        packed = jnp.zeros((SEQ, 128), F32)
        for i, column_values in enumerate(columns):
            packed = jnp.where(lane == i, column_values, packed)
        self.buffer[turn, 0] = packed.T[:8]
        copies = []
        for k in (2, 1, 3):
            copies.append(
                remote(self.buffer.at[turn, 0], self.buffer.at[turn, k], self.send.at[turn, k - 1],
                       self.recv.at[turn, k - 1], chip(x, y, z + k, core))
            )
            copies[-1].start()

        def wait():
            for copy in copies:
                copy.wait()
            total = (self.buffer[turn, 0] + self.buffer[turn, 1]) + (
                self.buffer[turn, 2] + self.buffer[turn, 3]
            )
            spread = jnp.concatenate([total, jnp.zeros((120, SEQ), F32)], 0).T
            return [spread[:, i : i + 1] for i in range(len(columns))]

        return wait


def block_slice(index):
    return pl.ds(pl.multiple_of(index * TOK, TOK), TOK)


def scatter_product(left, right, part, got, send, recv):
    x, y, z, core = here()
    copies = []
    for k in (2, 1, 3, 0):
        rows = block_slice(block_of(z + k))
        part[rows] = contract_last(left[rows], right).astype(BF)
        if k:
            copies.append(
                remote(part.at[rows], got.at[k - 1], send.at[k - 1], recv.at[k - 1], chip(x, y, z + k, core))
            )
            copies[-1].start()
    return copies


def collect(part, got, copies):
    z = here()[2]
    for copy in copies:
        copy.wait_recv()
    total = part[block_slice(block_of(z))].astype(F32)
    for k in range(3):
        total = total + got[k].astype(F32)
    return total


def spread_block(out, value, send, recv):
    x, y, z, core = here()
    rows = block_slice(block_of(z))
    out[rows] = value
    copies = []
    for k in (2, 1, 3):
        copies.append(
            remote(out.at[rows], out.at[rows], send.at[k - 1], recv.at[k - 1], chip(x, y, z + k, core))
        )
        copies[-1].start()
    return copies


def inverse_root(total):
    return lax.rsqrt(total * (1.0 / D) + NORM_EPSILON)


V_SELF, V_CROSS, V_DOWN, V_GAIN, V_BIAS = 6, 7, 8, 9, 10
W_QKV, W_QUERY, W_TEXT, W_SELF, W_CROSS = (
    slice(0, 3 * HW), slice(3 * HW, 4 * HW), slice(4 * HW, 6 * HW), slice(6 * HW, 7 * HW), slice(7 * HW, 8 * HW),
)
ATTN = 8 * HW


def forward_kernel(
    send_attn, send_mlp, tok, txt, cot, tab, heads, vec,
    w_attn, w_up, w_down, cot_all, tab_all, input_one, input_three, input_mlp, query_lin, key_lin,
    query_two_lin, key_two_lin, inv, query_rot, key_rot, value_low, query_two, key_two, value_two,
    mixed, mixed_two, branch_one, after_one, after_two, tok_all, txt_all,
    wa, got_attn, got_mlp, own_attn, own_mlp, part_one, part_two, blocks, stat,
    xs, xr, ks, kr, ms, mr, js, jr, rs, rr, cs, cr, loc, stat_s, stat_r, zs, zr, gs, gr,
):
    x, y, z, core = here()
    mine = x * SIDE + y
    greet(
        [device for pair in steps_of(x, y, z, core) for device in pair] + column(x, y, z, core)
    )
    attn_start, attn_wait, attn_drain = share_rows(send_attn, got_attn, rs.at[0], rr.at[0], loc.at[0])
    mlp_start, mlp_wait, mlp_drain = share_rows(send_mlp, got_mlp, rs.at[1], rr.at[1], loc.at[1])
    acts = [
        share_clip(src, dst, cs.at[i], cr.at[i], loc.at[2 + i, 0])
        for i, (src, dst) in enumerate(
            ((tok, tok_all), (tab, tab_all), (txt, txt_all), (cot, cot_all))
        )
    ]
    attn_start()
    acts[0][0]()
    acts[1][0]()
    attn_wait(own_attn)

    def attn_place(part, index, half=None):
        start, size = part * (ATTN // 2), ATTN // 2
        if half is not None:
            start, size = start + half * (ATTN // 4), ATTN // 4
        rows = pl.ds(pl.multiple_of(index * (2 * PAIR) + core * PAIR, PAIR), PAIR)
        return wa.at[rows, pl.ds(start, size)]

    def mlp_place(part, index, half=None):
        start, size = (0, FF) if half is None else (half * (FF // 2), FF // 2)
        rows = pl.ds(pl.multiple_of(index * (2 * PAIR) + core * PAIR, PAIR), PAIR)
        return (w_up, w_down)[part].at[rows, pl.ds(start, size)]

    gather_attn = gather_xy(own_attn, attn_place, xs, xr, ks, kr)
    advance(gather_attn)
    for part in (0, 1):
        attn_place(part, mine)[...] = own_attn[part]
    acts[2][0]()
    mlp_start()
    acts[3][0]()
    acts[0][1]()

    def norm_block(i, carry):
        normed, _ = plain_norm(tok_all[i].astype(F32))
        input_one[block_slice(i)] = (normed * (1.0 + vec[1:2]) + vec[0:1]).astype(BF)
        return carry

    advance(gather_attn, 2)
    lax.fori_loop(0, 2, norm_block, 0)
    advance(gather_attn, 2)
    lax.fori_loop(2, 4, norm_block, 0)
    advance(gather_attn, 2)
    mlp_wait(own_mlp)
    locals_ = []
    for part in (0, 1):
        locals_.append(pltpu.make_async_copy(own_mlp.at[part], mlp_place(part, mine), loc.at[6, part]))
        locals_[-1].start()
    finish(gather_attn)
    gather_mlp = gather_xy(own_mlp, mlp_place, ms, mr, js, jr)
    advance(gather_mlp)
    locals_.append(pltpu.make_async_copy(wa, w_attn, loc.at[7, 0]))
    locals_[-1].start()
    acts[1][1]()
    acts[2][1]()

    stats = Stats(stat, stat_s, stat_r)
    query_lin[...] = product(input_one[...], wa[:, 0:HW]) + heads[0:1]
    key_lin[...] = product(input_one[...], wa[:, HW : 2 * HW]) + heads[1:2]
    words = txt_all[...].reshape(SEQ, D)
    key_two_lin[...] = product(words, wa[:, 4 * HW : 5 * HW]) + heads[6:7]
    advance(gather_mlp)
    norm_wait = stats.start(
        0,
        [
            jnp.sum(ref[...] * ref[...], -1, keepdims=True)
            for ref in (query_lin, key_lin, key_two_lin)
        ],
    )
    value_low[...] = (product(input_one[...], wa[:, 2 * HW : 3 * HW]) + heads[2:3]).astype(BF)
    advance(gather_mlp)
    value_two[...] = (product(words, wa[:, 5 * HW : 6 * HW]) + heads[7:8]).astype(BF)
    advance(gather_mlp)
    lane = lax.broadcasted_iota(jnp.int32, (SEQ, 128), 1)
    inverse_query, inverse_key, inverse_key_two = [inverse_root(v) for v in norm_wait()]
    inv[...] = jnp.where(
        lane == 0, inverse_query, jnp.where(lane == 1, inverse_key, jnp.where(lane == 2, inverse_key_two, 0.0))
    )
    cosine, sine = rope_pair(tab_all[...].reshape(SEQ, HEAD))
    for h in range(HEADS):
        cols = head_slice(h)
        for lin, inverse, gain, out in (
            (query_lin, inverse_query, 3, query_rot),
            (key_lin, inverse_key, 4, key_rot),
        ):
            value = lin[:, cols] * inverse * (1.0 + heads[gain : gain + 1, cols])
            out[:, cols] = (value * cosine + swap_halves(value) * sine).astype(BF)
    key_two[...] = (key_two_lin[...] * inverse_key_two * (1.0 + heads[9:10])).astype(BF)
    attend_clip(query_rot, key_rot, value_low, mixed)
    advance(gather_mlp)
    copies = scatter_product(mixed, wa[:, W_SELF], part_one, blocks.at[0], zs.at[0], zr.at[0])
    drains = list(copies)
    advance(gather_mlp, 3)
    branch = collect(part_one, blocks.at[0], copies) + vec[V_SELF : V_SELF + 1]
    branch_one[...] = branch
    after = tok_all[block_of(z)].astype(F32) + vec[2:3] * branch
    after_one[...] = after
    normed, _ = plain_norm(after)
    copies = spread_block(
        input_three,
        (normed * (1.0 + vec[V_GAIN : V_GAIN + 1]) + vec[V_BIAS : V_BIAS + 1]).astype(BF),
        gs.at[0],
        gr.at[0],
    )
    drains += copies
    advance(gather_mlp, 3)
    for copy in copies:
        copy.wait_recv()
    query_two_lin[...] = product(input_three[...], wa[:, W_QUERY]) + heads[5:6]
    norm_wait = stats.start(1, [jnp.sum(query_two_lin[...] * query_two_lin[...], -1, keepdims=True)])
    advance(gather_mlp, 1)
    inverse_query_two = inverse_root(norm_wait()[0])
    inv[...] = jnp.where(lane == 3, inverse_query_two, inv[...])
    query_two[...] = (query_two_lin[...] * inverse_query_two * (1.0 + heads[8:9])).astype(BF)
    attend_clip(query_two, key_two, value_two, mixed_two)
    copies = scatter_product(mixed_two, wa[:, W_CROSS], part_two, blocks.at[1], zs.at[1], zr.at[1])
    drains += copies
    advance(gather_mlp, 2)
    after = after_one[...] + collect(part_two, blocks.at[1], copies) + vec[V_CROSS : V_CROSS + 1]
    after_two[...] = after
    normed, _ = plain_norm(after)
    copies = spread_block(
        input_mlp, (normed * (1.0 + vec[4:5]) + vec[3:4]).astype(BF), gs.at[1], gr.at[1]
    )
    drains += copies
    finish(gather_mlp)
    for copy in copies:
        copy.wait_recv()
    for copy in drains:
        copy.wait_send()
    for copy in locals_:
        copy.wait()
    acts[3][1]()
    for act in acts:
        act[2]()
    attn_drain()
    mlp_drain()


def forward(send_attn, send_mlp, tok, txt, cot, tab, heads, vec):
    dma = pltpu.SemaphoreType.DMA
    sds = jax.ShapeDtypeStruct
    wide, lin, low = sds((SEQ, D), BF), sds((SEQ, HW), F32), sds((SEQ, HW), BF)
    block = sds((TOK, D), F32)
    outs = [
        (sds((D, ATTN), BF), HB), (sds((D, FF), BF), HB), (sds((D, FF), BF), HB),
        (sds((SIDE, TOK, D), BF), HB), (sds((SIDE, TOK, HEAD), F32), VM),
        (wide, VM), (wide, VM), (wide, VM),
        (lin, VM), (lin, VM), (lin, VM), (lin, VM), (sds((SEQ, 128), F32), VM),
        (low, VM), (low, VM), (low, VM), (low, VM), (low, VM), (low, VM), (low, VM), (low, VM),
        (block, VM), (block, VM), (block, VM),
        (sds((SIDE, TOK, D), BF), VM), (sds((SIDE, TOK, D), BF), VM),
    ]
    return pl.pallas_call(
        forward_kernel,
        out_shape=[shape for shape, _ in outs],
        in_specs=[VM, VM, HB, HB, HB, VM, VM, VM],
        out_specs=[spec for _, spec in outs],
        scratch_shapes=[
            pltpu.VMEM((D, ATTN), BF),
            pltpu.VMEM((2, PAIR, ATTN // 2), BF),
            pltpu.VMEM((2, PAIR, FF), BF),
            pltpu.VMEM((2, PAIR, ATTN // 2), BF),
            pltpu.VMEM((2, PAIR, FF), BF),
            pltpu.VMEM((SEQ, D), BF),
            pltpu.VMEM((SEQ, D), BF),
            pltpu.VMEM((2, 3, TOK, D), BF),
            pltpu.VMEM((2, 4, 8, SEQ), F32),
            *[dma(s) for s in GATHER_SEMS],
            *[dma(s) for s in GATHER_SEMS],
            dma((2, 2)), dma((2, 2)), dma((4, 3)), dma((4, 3)), dma((8, 2)),
            dma((2, 3)), dma((2, 3)), dma((2, 3)), dma((2, 3)), dma((2, 3)), dma((2, 3)),
        ],
        compiler_params=params(0),
        name="forward",
    )(send_attn, send_mlp, tok, txt, cot, tab, heads, vec)


TILE = 256
CUBE = 0.044715
ROOT = math.sqrt(2.0 / math.pi)


def gelu_pair(u):
    square = u * u
    t = jnp.tanh(ROOT * u * (1.0 + CUBE * square))
    half = 0.5 * (1.0 + t)
    return u * half, half + 0.5 * u * (1.0 - t * t) * (ROOT * (1.0 + 3.0 * CUBE * square))


def mlp_kernel(
    a_ref, cot_ref, gate, bias, up, down, part_out, part_back, grad_up, grad_down, bias_sum,
    acc_out, acc_back, low, a_turned, low_turned,
):
    step = pl.program_id(0)

    @pl.when(step == 0)
    def _():
        acc_out[...] = jnp.zeros_like(acc_out)
        acc_back[...] = jnp.zeros_like(acc_back)
        for start in range(0, SEQ, TOK):
            rows = slice(start, start + TOK)
            value = (cot_ref[rows].astype(F32) * gate[0:1]).astype(BF)
            low[rows] = value
            low_turned[:, rows] = value.T
            a_turned[:, rows] = a_ref[rows].T

    u = product(a_ref[...], up[...]) + bias[0:1]
    act, slope = gelu_pair(u)
    act = act.astype(BF)
    acc_out[...] += contract_last(act, down[...])
    grad_down[...] = product(low_turned[...], act).astype(BF)
    back = (product(low[...], down[...]) * slope).astype(BF)
    acc_back[...] += contract_last(back, up[...])
    grad_up[...] = product(a_turned[...], back).astype(BF)
    bias_sum[...] = jnp.broadcast_to(jnp.sum(back.astype(F32), 0, keepdims=True), bias_sum.shape)

    @pl.when(step == FF // TILE - 1)
    def _():
        part_out[...] = acc_out[...].astype(BF)
        part_back[...] = acc_back[...].astype(BF)


def mlp_pass(a, cot, gate, bias, up, down):
    sds = jax.ShapeDtypeStruct
    fixed = pl.BlockSpec((SEQ, D), lambda i: (0, 0))
    tile = pl.BlockSpec((D, TILE), lambda i: (0, i))
    line = pl.BlockSpec((8, TILE), lambda i: (0, i))
    return pl.pallas_call(
        mlp_kernel,
        grid=(FF // TILE,),
        in_specs=[fixed, fixed, pl.BlockSpec((8, D), lambda i: (0, 0)), line, tile, tile],
        out_specs=[fixed, fixed, tile, tile, line],
        out_shape=[sds((SEQ, D), BF), sds((SEQ, D), BF), sds((D, FF), BF), sds((D, FF), BF), sds((8, FF), F32)],
        scratch_shapes=[
            pltpu.VMEM((SEQ, D), F32), pltpu.VMEM((SEQ, D), F32), pltpu.VMEM((SEQ, D), BF),
            pltpu.VMEM((D, SEQ), BF), pltpu.VMEM((D, SEQ), BF),
        ],
        compiler_params=pltpu.CompilerParams(vmem_limit_bytes=VMEM_LIMIT, dimension_semantics=("arbitrary",)),
        name="mlp",
    )(a, cot, gate, bias, up, down)


def peers_xy(x, y, z, core):
    rows = [chip(x + k, y, z, core) for k in (1, 2, 3)]
    lines = [chip(x, y + k, z, core) for k in (1, 2, 3)]
    return rows, lines


def reduce_xy(sources, out, own, sib, r1, r2, tosend, ls, ss, sr, s1, q1, s2, q2, s3, q3, l3, credit):
    x, y, z, core = here()
    zl = lax.rem(z, 2)
    rows, lines = peers_xy(x, y, z, core)
    sibling = chip(x, y, z, 1 - core)
    pairs = {0: [], 1: []}
    for i, (ref, part, start) in enumerate(sources):
        cols = pl.ds(start, ref.shape[-1])
        mine = pltpu.make_async_copy(ref.at[:, :, core], own.at[part, :, :, :, cols], ls.at[i])
        theirs = remote(
            ref.at[:, :, 1 - core], sib.at[:, :, :, cols], ss.at[i], sr.at[i], sibling
        )
        mine.start()
        if part == 0:
            theirs.start()
        pairs[part].append((mine, theirs))
    wrap = lambda v: lax.rem(v, SIDE)
    one = {0: [], 1: []}
    for part in (0, 1):
        yield
        for mine, theirs in pairs[part]:
            mine.wait()
            theirs.wait_recv()

        def add_pair(k, carry):
            a, b = lax.div(k, SIDE), lax.rem(k, SIDE)
            own[part, a, b] = own[part, a, b] + sib[a, b]
            return carry

        lax.fori_loop(0, SIDE * SIDE, add_pair, 0)
        if part == 0:
            pl.semaphore_signal(credit, inc=1, device_id=sibling, device_id_type=MESH)
            pl.semaphore_wait(credit, 1)
            for _, theirs in pairs[1]:
                theirs.start()
        for k in (2, 1, 3):
            src = own.at[0, :, wrap(y + k)] if part == 0 else own.at[1, wrap(x + k)]
            device = (lines, rows)[part][k - 1]
            copy = remote(src, r1.at[part, k - 1], s1.at[part, k - 1], q1.at[part, k - 1], device)
            copy.start()
            one[part].append(copy)
    two = {0: [], 1: []}
    for part in (0, 1):
        yield
        for copy in one[part]:
            copy.wait_recv()

        def add_line(k, carry):
            a, b = (k, y) if part == 0 else (x, k)
            total = own[part, a, b].astype(F32)
            for i in range(3):
                total = total + r1[part, i, k].astype(F32)
            own[part, a, b] = total.astype(BF)
            return carry

        lax.fori_loop(0, SIDE, add_line, 0)
        for k in (2, 1, 3):
            src = own.at[0, wrap(x + k), y] if part == 0 else own.at[1, x, wrap(y + k)]
            device = (rows, lines)[part][k - 1]
            copy = remote(src, r2.at[part, k - 1], s2.at[part, k - 1], q2.at[part, k - 1], device)
            copy.start()
            two[part].append(copy)
    final = []
    for part in (0, 1):
        yield
        for copy in two[part]:
            copy.wait_recv()
        total = own[part, x, y].astype(F32)
        for i in range(3):
            total = total + r2[part, i].astype(F32)
        for target in (0, 1):
            tosend[target, part * ROWS : part * ROWS + ROWS] = total[target * ROWS : target * ROWS + ROWS]
    other = z + 1 - 2 * zl
    far = [
        remote(tosend.at[t], out.at[zl], s3.at[t], q3.at[zl], chip(x, y, other, t)) for t in (0, 1)
    ]
    self_copy = pltpu.make_async_copy(tosend.at[core], out.at[zl], l3.at[0])
    near = remote(tosend.at[1 - core], out.at[zl], s3.at[0], q3.at[zl], sibling)

    def got(slot):
        remote(tosend.at[0], out.at[slot], s3.at[0], q3.at[slot], chip(x, y, z, core)).wait_recv()

    @pl.when(core == zl)
    def _():
        self_copy.start()
        near.start()

    @pl.when(core != zl)
    def _():
        for copy in far:
            copy.start()

    yield

    @pl.when(core == zl)
    def _():
        self_copy.wait()
        near.wait_send()
        got(1 - zl)

    @pl.when(core != zl)
    def _():
        for copy in far:
            copy.wait_send()
        got(zl)
        got(1 - zl)

    for part in (0, 1):
        for mine, theirs in pairs[part]:
            theirs.wait_send()
        for copy in one[part] + two[part]:
            copy.wait_send()


def reduce_scratch(width, count):
    dma = pltpu.SemaphoreType.DMA
    return [
        pltpu.VMEM((2, SIDE, SIDE, PAIR, width), BF),
        pltpu.VMEM((SIDE, SIDE, PAIR, width), BF),
        pltpu.VMEM((2, 3, SIDE, PAIR, width), BF),
        pltpu.VMEM((2, 3, PAIR, width), BF),
        pltpu.VMEM((2, PAIR, width), F32),
        dma((count,)), dma((count,)), dma((count,)),
        dma((2, 3)), dma((2, 3)), dma((2, 3)), dma((2, 3)),
        dma((2,)), dma((2,)), dma((1,)), pltpu.SemaphoreType.REGULAR,
    ]


def attend_clip_back(query, keys, values, grad, grad_query, grad_keys, grad_values):
    for h in range(HEADS):
        cols = head_slice(h)
        k, v = keys[:, cols], values[:, cols]
        for start in range(0, SEQ, 256):
            rows = slice(start, start + 256)
            q, do = query[rows, cols], grad[rows, cols]
            weights = softmax_rows(q, k)
            grad_weights = contract_last(do, v)
            delta = jnp.sum(weights * grad_weights, -1, keepdims=True)
            grad_scores = (weights * (grad_weights - delta)).astype(BF)
            grad_query[rows, cols] = product(grad_scores, k) * SCALE
            to_keys = contract_rows(grad_scores, q) * SCALE
            to_values = contract_rows(weights.astype(BF), do)
            if start:
                grad_keys[:, cols] += to_keys
                grad_values[:, cols] += to_values
            else:
                grad_keys[:, cols] = to_keys
                grad_values[:, cols] = to_values


def column_sum(values):
    return jnp.sum(values.astype(F32), 0, keepdims=True)


def scatter_held(part, got, send, recv):
    x, y, z, core = here()
    copies = []
    for k in (2, 1, 3):
        rows = block_slice(block_of(z + k))
        copies.append(
            remote(part.at[rows], got.at[k - 1], send.at[k - 1], recv.at[k - 1], chip(x, y, z + k, core))
        )
        copies[-1].start()
    return copies


def root_back(linear, inverse, scaled, dot):
    return (inverse * scaled - linear * (inverse * inverse * inverse * dot * (1.0 / D))).astype(BF)


def backward_kernel(
    part_back, part_down, grad_up, grad_down, wa, after_two, cot_own, vec, heads, query_lin, key_lin,
    query_two_lin, key_two_lin, inv, query_rot, key_rot, value_low, query_two, key_two, value_two,
    tab, branch_one, after_one,
    low_two, low_one, grad_query_two, grad_kv_two, grad_qkv, part_tokens, grad_after_one, sums,
    head_sums, result, grad_words, mlp_sums,
    mine_back, mine_down, part_cross, part_words, blocks, held, gq, gk, gv, stat,
    stat_s, stat_r, zs, zr, gs, gr, loc, *reduce_refs,
):
    x, y, z, core = here()
    rows, lines = peers_xy(x, y, z, core)
    greet(column(x, y, z, core) + rows + lines)
    own_rows = block_slice(block_of(z))
    copies = scatter_held(part_back, blocks.at[0], zs.at[0], zr.at[0])
    drains = list(copies)
    fetch_back = pltpu.make_async_copy(part_back.at[own_rows], mine_back, loc.at[0])
    fetch_down = pltpu.make_async_copy(part_down.at[own_rows], mine_down, loc.at[1])
    fetch_back.start()
    fetch_down.start()
    job = reduce_xy([(grad_up, 0, 0), (grad_down, 1, 0)], mlp_sums, *reduce_refs)
    advance(job)
    sums[...] = jnp.zeros_like(sums)
    head_sums[...] = jnp.zeros_like(head_sums)
    dy = cot_own[...].astype(F32)
    sums[2:3] = column_sum((dy * vec[5:6]).astype(BF))
    advance(job)

    def total_of(mine, i):
        total = mine[...].astype(F32)
        for k in range(3):
            total = total + blocks[i, k].astype(F32)
        return total

    fetch_back.wait()
    for copy in copies:
        copy.wait_recv()
    total = total_of(mine_back, 0)
    normed, inverse = plain_norm(after_two[...])
    sums[8:9] = column_sum(total)
    sums[9:10] = column_sum(total * normed)
    value = dy + norm_back(total * (1.0 + vec[4:5]), normed, inverse)
    grad_after_one[...] = value
    low = value.astype(BF)
    sums[1:2] = column_sum(low)
    copies = spread_block(low_two, low, gs.at[0], gr.at[0])
    drains += copies
    down_copies = scatter_held(part_down, blocks.at[1], zs.at[1], zr.at[1])
    drains += down_copies
    advance(job)
    for copy in copies:
        copy.wait_recv()

    stats = Stats(stat, stat_s, stat_r)
    inverse_query, inverse_key, inverse_key_two, inverse_query_two = [inv[:, i : i + 1] for i in range(4)]
    held[...] = product(low_two[...], wa[:, W_CROSS]).astype(BF)
    attend_clip_back(query_two, key_two, value_two, held, gq, gk, gv)
    scaled_query = gq[...] * (1.0 + heads[8:9])
    scaled_key = gk[...] * (1.0 + heads[9:10])
    dots = stats.start(
        0,
        [
            jnp.sum(query_two_lin[...] * scaled_query, -1, keepdims=True),
            jnp.sum(key_two_lin[...] * scaled_key, -1, keepdims=True),
        ],
    )
    head_sums[8:9] = column_sum(gq[...] * query_two_lin[...] * inverse_query_two)
    head_sums[9:10] = column_sum(gk[...] * key_two_lin[...] * inverse_key_two)
    low = gv[...].astype(BF)
    grad_kv_two[:, HW:] = low
    head_sums[7:8] = column_sum(low)
    advance(job)
    dot_query, dot_key = dots()
    low = root_back(query_two_lin[...], inverse_query_two, gq[...] * (1.0 + heads[8:9]), dot_query)
    grad_query_two[...] = low
    head_sums[5:6] = column_sum(low)
    cross_copies = scatter_product(
        grad_query_two, wa[:, W_QUERY], part_cross, blocks.at[2], zs.at[2], zr.at[2]
    )
    low = root_back(key_two_lin[...], inverse_key_two, gk[...] * (1.0 + heads[9:10]), dot_key)
    grad_kv_two[:, :HW] = low
    head_sums[6:7] = column_sum(low)
    word_copies = scatter_product(grad_kv_two, wa[:, W_TEXT], part_words, blocks.at[3], zs.at[3], zr.at[3])
    drains += word_copies
    for copy in down_copies:
        copy.wait_recv()
    fetch_down.wait()
    branch = total_of(mine_down, 1) + vec[V_DOWN : V_DOWN + 1]
    result[...] = (after_two[...] + vec[5:6] * branch).astype(BF)
    sums[10:11] = column_sum(cot_own[...].astype(F32) * branch)
    advance(job)

    total = collect(part_cross, blocks.at[2], cross_copies)
    normed, inverse = plain_norm(after_one[...])
    sums[4:5] = column_sum(total)
    sums[3:4] = column_sum(total * normed)
    value = grad_after_one[...] + norm_back(total * (1.0 + vec[V_GAIN : V_GAIN + 1]), normed, inverse)
    grad_after_one[...] = value
    sums[7:8] = column_sum(value * branch_one[...])
    low = (value * vec[2:3]).astype(BF)
    sums[0:1] = column_sum(low)
    copies = spread_block(low_one, low, gs.at[1], gr.at[1])
    drains += copies
    advance(job)
    for copy in copies:
        copy.wait_recv()

    held[...] = product(low_one[...], wa[:, W_SELF]).astype(BF)
    attend_clip_back(query_rot, key_rot, value_low, held, gq, gk, gv)
    cosine, sine = rope_pair(tab[...].reshape(SEQ, HEAD))
    for ref in (gq, gk):
        for h in range(HEADS):
            cols = head_slice(h)
            value = ref[:, cols]
            ref[:, cols] = value * cosine - swap_halves(value) * sine
    dots = stats.start(
        1,
        [
            jnp.sum(query_lin[...] * (gq[...] * (1.0 + heads[3:4])), -1, keepdims=True),
            jnp.sum(key_lin[...] * (gk[...] * (1.0 + heads[4:5])), -1, keepdims=True),
        ],
    )
    head_sums[3:4] = column_sum(gq[...] * query_lin[...] * inverse_query)
    head_sums[4:5] = column_sum(gk[...] * key_lin[...] * inverse_key)
    low = gv[...].astype(BF)
    grad_qkv[:, 2 * HW :] = low
    head_sums[2:3] = column_sum(low)
    advance(job)
    dot_query, dot_key = dots()
    for i, (lin, inverse, ref, dot) in enumerate(
        ((query_lin, inverse_query, gq, dot_query), (key_lin, inverse_key, gk, dot_key))
    ):
        low = root_back(lin[...], inverse, ref[...] * (1.0 + heads[3 + i : 4 + i]), dot)
        grad_qkv[:, i * HW : (i + 1) * HW] = low
        head_sums[i : i + 1] = column_sum(low)
    for copy in cross_copies:
        copy.wait_send()
    part_cross[...] = contract_last(grad_qkv[...], wa[:, W_QKV]).astype(BF)
    store = pltpu.make_async_copy(part_cross, part_tokens, loc.at[2])
    store.start()
    grad_words[...] = collect(part_words, blocks.at[3], word_copies).astype(BF)
    finish(job)
    store.wait()
    for copy in drains:
        copy.wait_send()


def backward(hbm, vmem):
    dma = pltpu.SemaphoreType.DMA
    sds = jax.ShapeDtypeStruct
    wide, low = sds((SEQ, D), BF), sds((SEQ, HW), BF)
    block, low_block = sds((TOK, D), F32), sds((TOK, D), BF)
    lin = pltpu.VMEM((SEQ, HW), F32)
    outs = [
        wide, wide, low, sds((SEQ, 2 * HW), BF), sds((SEQ, 3 * HW), BF), wide, block,
        sds((16, D), F32), sds((16, HW), F32), low_block, low_block, sds((2, PAIR, FF), F32),
    ]
    return pl.pallas_call(
        backward_kernel,
        out_shape=outs,
        in_specs=[HB] * len(hbm) + [VM] * len(vmem),
        out_specs=[HB if i == 5 else VM for i in range(len(outs))],
        scratch_shapes=[
            pltpu.VMEM((TOK, D), BF), pltpu.VMEM((TOK, D), BF),
            pltpu.VMEM((SEQ, D), BF), pltpu.VMEM((SEQ, D), BF),
            pltpu.VMEM((4, 3, TOK, D), BF), pltpu.VMEM((SEQ, HW), BF),
            lin, lin, lin, pltpu.VMEM((2, 4, 8, SEQ), F32),
            dma((2, 3)), dma((2, 3)), dma((4, 3)), dma((4, 3)), dma((2, 3)), dma((2, 3)), dma((3,)),
            *reduce_scratch(FF, 2),
        ],
        compiler_params=params(1),
        name="backward",
    )(*hbm, *vmem)


def deliver(src, dst, s, r, l):
    x, y, z, core = here()
    zh = lax.div(z, 2)
    far = remote(src, dst.at[core], s.at[0], r.at[core], chip(x, y, z + 2, zh))
    near = remote(src, dst.at[core], s.at[1], r.at[core], chip(x, y, z, zh))
    self_copy = pltpu.make_async_copy(src, dst.at[core], l)

    def got(slot):
        remote(src, dst.at[slot], s.at[0], r.at[slot], chip(x, y, z, core)).wait_recv()

    def start():
        far.start()

        @pl.when(core == zh)
        def _():
            self_copy.start()

        @pl.when(core != zh)
        def _():
            near.start()

    def wait():
        @pl.when(core == zh)
        def _():
            self_copy.wait()
            got(1 - core)

        @pl.when(core != zh)
        def _():
            near.wait_send()
            got(0)
            got(1)

        far.wait_send()

    return start, wait


def vector_job(model, heads, time_out, model_out, head_out, col, hsib, mx, hx, sends, recvs):
    x, y, z, core = here()
    zl = lax.rem(z, 2)
    rows, lines = peers_xy(x, y, z, core)
    copies = []
    for k in (1, 2, 3):
        copies.append(
            remote(model, col.at[0, k - 1], sends.at[0, k], recvs.at[0, k], chip(x, y, z + k, core))
        )
    for k in range(4):
        copies.append(
            remote(model, col.at[1, k], sends.at[1, k], recvs.at[1, k], chip(x, y, z + k, 1 - core))
        )
    copies.append(remote(heads, hsib, sends.at[0, 0], recvs.at[0, 0], chip(x, y, z, 1 - core)))
    for copy in copies:
        copy.start()
    yield
    for copy in copies:
        copy.wait()
    same = model[...] + col[0, 0] + col[0, 1] + col[0, 2]
    sib = col[1, 0] + col[1, 1] + col[1, 2] + col[1, 3]
    time_out[core] = same
    time_out[1 - core] = sib
    mx[0] = same + sib
    hx[0] = heads[...] + hsib[...]
    for stage, peers in enumerate((rows, lines)):
        copies = []
        for k in (1, 2, 3):
            copies.append(
                remote(mx.at[4 * stage], mx.at[4 * stage + k], sends.at[2 + 2 * stage, k],
                       recvs.at[2 + 2 * stage, k], peers[k - 1])
            )
            copies.append(
                remote(hx.at[4 * stage], hx.at[4 * stage + k], sends.at[3 + 2 * stage, k],
                       recvs.at[3 + 2 * stage, k], peers[k - 1])
            )
        for copy in copies:
            copy.start()
        yield
        for copy in copies:
            copy.wait()
        base = 4 * stage
        mx[base + 4] = mx[base] + mx[base + 1] + mx[base + 2] + mx[base + 3]
        hx[base + 4] = hx[base] + hx[base + 1] + hx[base + 2] + hx[base + 3]
    model_out[...] = mx[8]
    head_out[zl] = hx[8]
    last = remote(
        hx.at[8], head_out.at[zl], sends.at[6, 0], recvs.at[6, 0], chip(x, y, z + 1 - 2 * zl, core)
    )
    last.start()
    yield
    last.wait()


def vector_scratch():
    dma = pltpu.SemaphoreType.DMA
    return [
        pltpu.VMEM((2, 4, 16, D), F32),
        pltpu.VMEM((16, HW), F32),
        pltpu.VMEM((9, 16, D), F32),
        pltpu.VMEM((9, 16, HW), F32),
        dma((7, 4)),
        dma((7, 4)),
    ]


GRAD_PLACES = ((0, 0, 3 * HW), (0, 3 * HW, HW), (1, 0, 2 * HW), (1, 2 * HW, HW), (1, 3 * HW, HW))


def tail_kernel(*refs):
    count = len(GRAD_PLACES)
    grads, refs = refs[:count], refs[count:]
    (
        part_tokens, tok_own, grad_after_one, vec, sums, head_sums, result, words,
        out_result, out_tokens, out_words, time_out, model_out, head_out, attn_sums,
        mine, blocks, model, low_tokens, got_tokens, got_words, zs, zr, ds, dr, loc,
    ), refs = refs[:26], refs[26:]
    vector_refs, reduce_refs = refs[:6], refs[6:]
    x, y, z, core = here()
    rows, lines = peers_xy(x, y, z, core)
    greet(column(x, y, z, core) + rows + lines)
    copies = scatter_held(part_tokens, blocks, zs, zr)
    fetch = pltpu.make_async_copy(part_tokens.at[block_slice(block_of(z))], mine, loc.at[0])
    fetch.start()
    job = reduce_xy(
        [(ref, part, start) for ref, (part, start, _) in zip(grads, GRAD_PLACES)], attn_sums, *reduce_refs
    )
    advance(job)
    sends = [
        deliver(src, dst, ds.at[i], dr.at[i], loc.at[1 + i])
        for i, (src, dst) in enumerate(
            ((result, out_result), (words, got_words), (low_tokens, got_tokens))
        )
    ]
    sends[0][0]()
    sends[1][0]()
    advance(job, 2)
    fetch.wait()
    for copy in copies:
        copy.wait_recv()
    total = mine[...].astype(F32)
    for k in range(3):
        total = total + blocks[k].astype(F32)
    normed, inverse = plain_norm(tok_own[...].astype(F32))
    model[...] = sums[...]
    model[5:6] = column_sum(total)
    model[6:7] = column_sum(total * normed)
    vectors = vector_job(model, head_sums, time_out, model_out, head_out, *vector_refs)
    advance(vectors)
    value = grad_after_one[...] + norm_back(total * (1.0 + vec[1:2]), normed, inverse)
    low_tokens[...] = value.astype(BF)
    sends[2][0]()
    advance(job)
    advance(vectors)
    advance(job)
    advance(vectors)
    advance(job)
    advance(vectors)
    advance(job)
    finish(vectors)
    for send in sends:
        send[1]()
    out_tokens[...] = got_tokens[...].astype(F32)
    out_words[...] = got_words[...].astype(F32)
    finish(job)
    for copy in copies:
        copy.wait_send()


def tail(grads, part_tokens, vmem):
    dma = pltpu.SemaphoreType.DMA
    sds = jax.ShapeDtypeStruct
    outs = [
        sds((2, TOK, D), BF), sds((2, TOK, D), F32), sds((2, TOK, D), F32), sds((2, 16, D), F32),
        sds((16, D), F32), sds((2, 16, HW), F32), sds((2, PAIR, ATTN // 2), F32),
    ]
    return pl.pallas_call(
        tail_kernel,
        out_shape=outs,
        in_specs=[HB] * (len(grads) + 1) + [VM] * len(vmem),
        out_specs=[VM] * len(outs),
        scratch_shapes=[
            pltpu.VMEM((TOK, D), BF), pltpu.VMEM((3, TOK, D), BF), pltpu.VMEM((16, D), F32),
            pltpu.VMEM((TOK, D), BF), pltpu.VMEM((2, TOK, D), BF), pltpu.VMEM((2, TOK, D), BF),
            dma((3,)), dma((3,)), dma((3, 2)), dma((3, 2)), dma((4,)),
            *vector_scratch(),
            *reduce_scratch(ATTN // 2, len(grads)),
        ],
        compiler_params=params(2),
        name="tail",
    )(*grads, part_tokens, *vmem)


def newton_kernel(narrow, wide, narrow_out, wide_out, mine, theirs, send, recv):
    x, y, z, core = here()
    partner = chip(x, y, z + 2, core)
    greet([partner])
    n, w = narrow.shape[0], wide.shape[0]
    size = n + w
    contract = (((1,), (1,)), ((), ()))
    mine[...] = jnp.zeros_like(mine)
    mine[:n, :n] = lax.dot_general(
        narrow[...], narrow[...], contract, precision=HIGHEST, preferred_element_type=F32
    )
    mine[n:, n:] = lax.dot_general(
        wide[...], wide[...], contract, precision=HIGHEST, preferred_element_type=F32
    )
    copy = remote(mine, theirs, send.at[0], recv.at[0], partner)
    copy.start()
    copy.wait()
    block_row = lax.div(lax.broadcasted_iota(jnp.int32, (size, size), 0), ROWS)
    block_col = lax.div(lax.broadcasted_iota(jnp.int32, (size, size), 1), ROWS)
    same = block_row == block_col
    eye = lax.broadcasted_iota(jnp.int32, (size, size), 0) == lax.broadcasted_iota(
        jnp.int32, (size, size), 1
    )
    gram = jnp.where(same, mine[...] + theirs[...], 0.0)
    diagonal = jnp.where(eye, gram, 0.0)
    by_row = jnp.sum(diagonal, 1, keepdims=True)
    by_col = jnp.sum(diagonal, 0, keepdims=True)
    total_row = jnp.sum(jnp.where(same, by_col, 0.0), 1, keepdims=True)
    total_col = jnp.sum(jnp.where(same, by_row, 0.0), 0, keepdims=True)
    scale_row = 1.0 / (jnp.sqrt(total_row) + ORTHO_EPSILON)
    scale_col = 1.0 / (jnp.sqrt(total_col) + ORTHO_EPSILON)
    current = gram * scale_row * scale_col

    def times(a, b):
        return jnp.dot(a, b, precision=HIGHEST, preferred_element_type=F32)

    whole = None
    for turn in range(NS_STEPS):
        square = times(current, current)
        step = NEWTON_SECOND * current + NEWTON_THIRD * square + jnp.where(eye, NEWTON_FIRST, 0.0)
        whole = step if whole is None else times(step, whole)
        if turn + 1 < NS_STEPS:
            current = times(times(step, current), step)
    whole = whole * scale_col
    narrow_out[...] = times(whole[:n, :n], narrow[...])
    wide_out[...] = times(whole[n:, n:], wide[...])


def newton(narrow, wide, cid):
    size = narrow.shape[0] + wide.shape[0]
    dma = pltpu.SemaphoreType.DMA
    return pl.pallas_call(
        newton_kernel,
        out_shape=[
            jax.ShapeDtypeStruct(narrow.shape, F32),
            jax.ShapeDtypeStruct(wide.shape, F32),
        ],
        in_specs=[VM, VM],
        out_specs=[VM, VM],
        scratch_shapes=[
            pltpu.VMEM((size, size), F32),
            pltpu.VMEM((size, size), F32),
            dma((1,)),
            dma((1,)),
        ],
        compiler_params=params(cid),
        name="newton",
    )(narrow, wide)


def rope_tables(places):
    pair_index = jnp.arange(HEAD // 2, dtype=jnp.int32)
    side_pairs = HEAD // 6
    frame_pairs = (HEAD - 4 * side_pairs) // 2
    part_of = (pair_index >= frame_pairs).astype(jnp.int32) + (
        pair_index >= frame_pairs + side_pairs
    ).astype(jnp.int32)
    offset = jnp.where(
        part_of == 0, 0, jnp.where(part_of == 1, frame_pairs, frame_pairs + side_pairs)
    ).astype(jnp.int32)
    extent = jnp.where(part_of == 0, 2 * frame_pairs, 2 * side_pairs).astype(jnp.float32)
    frequency = jnp.exp(
        (pair_index - offset).astype(jnp.float32) * (-2.0 * math.log(10000.0)) / extent
    )
    chosen = (
        places[0][:, None] * (part_of == 0)
        + places[1][:, None] * (part_of == 1)
        + places[2][:, None] * (part_of == 2)
    )
    angles = chosen.astype(jnp.float32) * frequency
    return (jnp.cos(angles), jnp.sin(angles))


def plain_norm(values):
    centred = values - jnp.mean(values, -1, keepdims=True)
    inverse = lax.rsqrt(jnp.mean(centred * centred, -1, keepdims=True) + NORM_EPSILON)
    return (centred * inverse, inverse)


def norm_back(grads, normed, inverse):
    return inverse * (
        grads
        - jnp.mean(grads, -1, keepdims=True)
        - normed * jnp.mean(grads * normed, -1, keepdims=True)
    )


def product(left, right):
    return jnp.dot(left, right, preferred_element_type=F32)


def contract_last(left, right):
    return lax.dot_general(left, right, (((1,), (1,)), ((), ())), preferred_element_type=F32)


def contract_rows(left, right):
    return lax.dot_general(left, right, (((0,), (0,)), ((), ())), preferred_element_type=F32)


def body(
    tokens, text, time_embedding, positions, cotangent, attn_in, attn_out, mlp, head_vectors,
    model_vectors, up_bias, attn_in_moment, attn_out_moment, mlp_moment, head_moment, model_moment,
    up_moment,
):
    x, y, z, core = here()
    zl = lax.rem(z, 2)
    block = block_of(z)

    low_in = attn_in.astype(BF).reshape(ROWS, 6, 2, HW).transpose(2, 0, 1, 3).reshape(2, ROWS, -1)
    low_out = attn_out.astype(BF).reshape(ROWS, 2, 2, HW).transpose(2, 0, 1, 3).reshape(2, ROWS, -1)
    send_attn = jnp.concatenate([low_in, low_out], -1).reshape(2, ROWS, 2, ATTN // 2)
    send_attn = send_attn.transpose(0, 2, 1, 3).reshape(2, PAIR, ATTN // 2)
    send_mlp = jnp.pad(
        mlp.astype(BF).reshape(ROWS, 2, 2, FF_REAL).transpose(2, 1, 0, 3),
        ((0, 0), (0, 0), (0, 0), (0, FF - FF_REAL)),
    ).reshape(2, PAIR, FF)
    cosine, sine = rope_tables(positions.reshape(3, 2 * TOK))
    table = jnp.concatenate([cosine, sine], -1).reshape(2, TOK, HEAD)

    heads = jnp.pad(lax.dynamic_slice(head_vectors, (0, zl * HW), (10, HW)), ((0, 6), (0, 0)))
    bias_up = jnp.pad(lax.dynamic_slice(up_bias, (zl * FF_REAL,), (FF_REAL,)), (0, FF - FF_REAL))
    modulation = model_vectors[5:] + lax.dynamic_index_in_dim(time_embedding, core, 0, False)
    shift_one, scale_one, gate_one, shift_two, scale_two, gate_two = [modulation[i] for i in range(6)]
    vectors = jnp.pad(jnp.concatenate([modulation, model_vectors[:5]], 0), ((0, 5), (0, 0)))

    (
        w_attn, w_up, w_down, cot_all, tab_all, input_one, input_three, input_mlp, query_lin, key_lin,
        query_two_lin, key_two_lin, inv, query_rot, key_rot, value_low, query_two, key_two, value_two,
        mixed_low, mixed_two_low, branch_one, after_one, after_two, tok_all, txt_all,
    ) = forward(
        send_attn, send_mlp, tokens, text, cotangent, table, heads, vectors,
    )
    tok_own = lax.dynamic_index_in_dim(tok_all, block, 0, False)
    cot_own = lax.dynamic_index_in_dim(cot_all, block, 0, False)
    words = txt_all.reshape(SEQ, D)
    part_down, part_back, grad_up, grad_down, up_sum = mlp_pass(
        input_mlp, cot_all.reshape(SEQ, D), jnp.broadcast_to(gate_two[None], (8, D)),
        jnp.broadcast_to(bias_up[None], (8, FF)), w_up, w_down,
    )

    def by_chip(grads):
        return grads.reshape(SIDE, SIDE, 2, PAIR, grads.shape[1])

    (
        low_two, low_one, grad_query_two, grad_kv_two, grad_qkv, part_tokens, grad_after_one, sums,
        head_sums, result, grad_words, mlp_sums,
    ) = backward(
        [part_back, part_down, by_chip(grad_up), by_chip(grad_down)],
        [
            w_attn, after_two, cot_own, vectors, heads, query_lin, key_lin, query_two_lin, key_two_lin,
            inv, query_rot, key_rot, value_low, query_two, key_two, value_two, tab_all, branch_one, after_one,
        ],
    )

    def rows_of(left, right):
        return by_chip(contract_rows(left, right).astype(BF))

    matrix_grads = [
        rows_of(input_one, grad_qkv),
        rows_of(input_three, grad_query_two),
        rows_of(words, grad_kv_two),
        rows_of(low_one, mixed_low),
        rows_of(low_two, mixed_two_low),
    ]
    head_part = jnp.concatenate([head_sums[:10], up_sum[0].reshape(6, HW)], 0)
    out_result, out_tokens, out_words, time_sums, model_sums, head_totals, attn_sums = tail(
        matrix_grads, part_tokens,
        [tok_own, grad_after_one, vectors, sums, head_part, result, grad_words],
    )
    grad_time = time_sums[:, 5:11]
    model_total = model_sums[:11]
    head_total = head_totals[:, :10].transpose(1, 0, 2).reshape(10, 2 * HW)
    up_total = head_totals[:, 10:].reshape(2, FF)[:, :FF_REAL].reshape(-1)

    attn_sums = attn_sums.reshape(2, 2, ROWS, ATTN // 2).transpose(0, 2, 1, 3).reshape(2, ROWS, ATTN)
    mlp_sums = mlp_sums.reshape(2, 2, ROWS, FF)[..., :FF_REAL]

    def unpack(first, count):
        part = attn_sums[:, :, first * HW : (first + count) * HW].reshape(2, ROWS, count, HW)
        return part.transpose(2, 1, 0, 3).reshape(count, ROWS, 2 * HW)

    mlp_grad = mlp_sums.transpose(1, 2, 0, 3).reshape(2, ROWS, 2 * FF_REAL)
    swap = lambda v: v.transpose(1, 0, 2)
    new_in_moment = MOMENTUM * swap(attn_in_moment) + unpack(0, 6)
    new_out_moment = MOMENTUM * swap(attn_out_moment) + unpack(6, 2)
    new_mlp_moment = MOMENTUM * swap(mlp_moment) + mlp_grad
    narrow = jnp.concatenate([new_in_moment, new_out_moment], 0).reshape(8 * ROWS, 2 * HW)
    wide = new_mlp_moment.reshape(2 * ROWS, 2 * FF_REAL)
    narrow_dir, wide_dir = newton(narrow, wide, 3)
    narrow_dir = narrow_dir.reshape(8, ROWS, 2 * HW)
    wide_dir = wide_dir.reshape(2, ROWS, 2 * FF_REAL)
    new_attn_in = attn_in * (1.0 - RATE_IN * DECAY) - RATE_IN * swap(narrow_dir[:6])
    new_attn_out = attn_out * (1.0 - RATE_OUT * DECAY) - RATE_OUT * swap(narrow_dir[6:])
    new_mlp = mlp * (1.0 - RATE_MLP * DECAY) - RATE_MLP * swap(wide_dir)
    new_head_moment = MOMENTUM * head_moment + head_total
    new_model_moment = MOMENTUM * model_moment + model_total
    new_up_moment = MOMENTUM * up_moment + up_total
    return (
        out_result,
        out_tokens,
        out_words,
        grad_time,
        new_attn_in,
        new_attn_out,
        new_mlp,
        swap(new_in_moment),
        swap(new_out_moment),
        swap(new_mlp_moment),
        head_vectors - RATE_VECTOR * new_head_moment,
        model_vectors - RATE_VECTOR * new_model_moment,
        up_bias - RATE_VECTOR * new_up_moment,
        new_head_moment,
        new_model_moment,
        new_up_moment,
    )


def solution(mesh):
    clip = P("fsdp", "ctx", None)
    whole = P("fsdp", None, None)
    matrix = P(("fsdp", "ctx"), None, "tp")
    in_specs = (
        clip, clip, whole, P(None, "fsdp", "ctx"), clip, matrix, matrix, matrix, P(None, "tp"), P(),
        P("tp"), matrix, matrix, matrix, P(None, "tp"), P(), P("tp"),
    )
    out_specs = (
        clip, clip, clip, whole, matrix, matrix, matrix, matrix, matrix, matrix, P(None, "tp"), P(),
        P("tp"), P(None, "tp"), P(), P("tp"),
    )
    return jax.shard_map(body, mesh=mesh, in_specs=in_specs, out_specs=out_specs, check_vma=False)
```

```python
from functools import partial
import math

import jax
import jax.numpy as jnp
from jax import lax
from jax.experimental import pallas as pl
from jax.experimental.pallas import tpu as pltpu
from jax.sharding import PartitionSpec as P

D = 1536
HEAD = 128
ROWS = 24
HEADS = 3
NORM_EPSILON = 1e-06
ORTHO_EPSILON = 1e-07
NEWTON_FIRST = 3.4445
NEWTON_SECOND = -4.775
NEWTON_THIRD = 2.0315
NS_STEPS = 5
MOMENTUM = 0.9
DECAY = 0.01
RATE_IN = 0.5
RATE_OUT = 4.0
RATE_MLP = 1.0
RATE_VECTOR = 0.005
HIGHEST = lax.Precision.HIGHEST

MESH = pl.DeviceIdType.MESH
BF = jnp.bfloat16
F32 = jnp.float32

SIDE = 4
TOK = 128
SEQ = SIDE * TOK
HW = HEADS * HEAD
FF_REAL = 2240
FF = 2304
PAIR = 2 * ROWS
VMEM_LIMIT = 57 * 1024 * 1024


def here():
    f = lax.axis_index("fsdp")
    c = lax.axis_index("ctx")
    t = lax.axis_index("tp")
    x, y = lax.div(f, SIDE), lax.rem(f, SIDE)
    zl, core = lax.div(c, 2), lax.rem(c, 2)
    return x, y, 2 * t + zl, core


def chip(x, y, z, core):
    x, y, z = lax.rem(x + SIDE, SIDE), lax.rem(y + SIDE, SIDE), lax.rem(z + SIDE, SIDE)
    return {"fsdp": x * SIDE + y, "ctx": lax.rem(z, 2) * 2 + core, "tp": lax.div(z, 2)}


def block_of(z):
    z = lax.rem(z + SIDE, SIDE)
    return 2 * lax.rem(z, 2) + lax.div(z, 2)


def greet(devices):
    barrier = pltpu.get_barrier_semaphore()
    for device in devices:
        pl.semaphore_signal(barrier, inc=1, device_id=device, device_id_type=MESH)
    pl.semaphore_wait(barrier, len(devices))


def column(x, y, z, core):
    return [chip(x, y, z + k, core) for k in (1, 2, 3)] + [
        chip(x, y, z + k, 1 - core) for k in range(4)
    ]


def remote(src, dst, send, recv, device):
    return pltpu.make_async_remote_copy(
        src_ref=src, dst_ref=dst, send_sem=send, recv_sem=recv, device_id=device, device_id_type=MESH
    )


def params(cid):
    return pltpu.CompilerParams(
        collective_id=cid, has_side_effects=True, vmem_limit_bytes=VMEM_LIMIT
    )


VM = pl.BlockSpec(memory_space=pltpu.VMEM)
HB = pl.BlockSpec(memory_space=pltpu.HBM)


def flat(a, b):
    return lax.rem(a + SIDE, SIDE) * SIDE + lax.rem(b + SIDE, SIDE)


def steps_of(x, y, z, core):
    return (
        (chip(x + 1, y, z, core), chip(x - 1, y, z, core)),
        (chip(x, y + 1, z, core), chip(x, y - 1, z, core)),
    )


def gather_xy(own, place, xs, xr, ks, kr):
    x, y, z, core = here()
    mine = x * SIDE + y
    steps = steps_of(x, y, z, core)
    sibling = chip(x, y, z, 1 - core)
    sends, sibs = [], []

    def push(part, slot, src, index, device, half=None):
        copy = remote(src, place(part, index, half), xs.at[part, slot], xr.at[part, slot], device)
        copy.start()
        sends.append(copy)
        return copy

    def to_sibling(part, slot, src, index):
        copy = remote(src, place(part, index), ks.at[part, slot], kr.at[part, slot], sibling)
        copy.start()
        sibs.append(copy)

    def index_of(part, first_off, second_off):
        if part == 0:
            return flat(x + first_off, y + second_off)
        return flat(x + second_off, y + first_off)

    one, two = {}, {}
    for part in (0, 1):
        a_next, a_prev = steps[part]
        one[part, "next"] = push(part, 0, own.at[part], mine, a_next)
        one[part, "prev"] = push(part, 1, own.at[part], mine, a_prev)
    for part in (0, 1):
        b_next, b_prev = steps[1 - part]
        two[part, 0, "next"] = push(part, 4, own.at[part], mine, b_next)
        two[part, 0, "prev"] = push(part, 5, own.at[part], mine, b_prev)
        to_sibling(part, 0, own.at[part], mine)

    def second_start(part, k, offset):
        b_next, b_prev = steps[1 - part]
        index = index_of(part, offset, 0)
        src = place(part, index)
        two[part, k, "next"] = push(part, 4 + 4 * k, src, index, b_next)
        two[part, k, "prev"] = push(part, 5 + 4 * k, src, index, b_prev)
        to_sibling(part, 4 * k, src, index)

    offsets = (0, -1, 1, 2)
    for part in (0, 1):
        a_next, a_prev = steps[part]
        yield
        one[part, "next"].wait_recv()
        index = index_of(part, -1, 0)
        one[part, "far0"] = push(part, 2, place(part, index, 0), index, a_next, 0)
        second_start(part, 1, -1)
        one[part, "prev"].wait_recv()
        index = index_of(part, 1, 0)
        one[part, "far1"] = push(part, 3, place(part, index, 1), index, a_prev, 1)
        second_start(part, 2, 1)

    def second_forward(part, k):
        b_next, b_prev = steps[1 - part]
        two[part, k, "next"].wait_recv()
        index = index_of(part, offsets[k], -1)
        two[part, k, "far0"] = push(part, 6 + 4 * k, place(part, index, 0), index, b_next, 0)
        to_sibling(part, 4 * k + 1, place(part, index), index)
        two[part, k, "prev"].wait_recv()
        index = index_of(part, offsets[k], 1)
        two[part, k, "far1"] = push(part, 7 + 4 * k, place(part, index, 1), index, b_prev, 1)
        to_sibling(part, 4 * k + 2, place(part, index), index)

    def second_finish(part, k):
        two[part, k, "far0"].wait_recv()
        two[part, k, "far1"].wait_recv()
        index = index_of(part, offsets[k], 2)
        to_sibling(part, 4 * k + 3, place(part, index), index)

    for part in (0, 1):
        yield
        second_forward(part, 0)
    for part in (0, 1):
        yield
        one[part, "far0"].wait_recv()
        one[part, "far1"].wait_recv()
        second_start(part, 3, 2)
    for k in (1, 2, 3):
        for part in (0, 1):
            yield
            second_forward(part, k)
        for part in (0, 1):
            second_finish(part, k - 1)
    for part in (0, 1):
        yield
        second_finish(part, 3)
    yield
    for copy in sends:
        copy.wait_send()
    for copy in sibs:
        copy.wait_send()
        copy.wait_recv()


GATHER_SEMS = ((2, 20), (2, 20), (2, 16), (2, 16))


def advance(job, count=1):
    for _ in range(count):
        next(job, None)


def finish(job):
    for _ in job:
        pass


def share_rows(send, recv, s, r, l):
    x, y, z, core = here()
    zl = lax.rem(z, 2)
    away = remote(send.at[1 - zl], recv.at[core], s.at[0], r.at[core], chip(x, y, z + 1 - 2 * zl, zl))
    near = remote(send.at[zl], recv.at[core], s.at[1], r.at[core], chip(x, y, z, zl))
    self_copy = pltpu.make_async_copy(send.at[zl], recv.at[core], l.at[0])

    def got(slot):
        remote(send.at[0], recv.at[slot], s.at[0], r.at[slot], chip(x, y, z, core)).wait_recv()

    def start():
        away.start()

        @pl.when(core == zl)
        def _():
            self_copy.start()

        @pl.when(core != zl)
        def _():
            near.start()

    def wait(own):
        @pl.when(core == zl)
        def _():
            self_copy.wait()
            got(1 - core)

        @pl.when(core != zl)
        def _():
            near.wait_send()
            got(0)
            got(1)

        first = recv[0].astype(F32)
        second = recv[1].astype(F32)
        own[0] = jnp.concatenate([first[:ROWS], second[:ROWS]], 0).astype(BF)
        own[1] = jnp.concatenate([first[ROWS:], second[ROWS:]], 0).astype(BF)

    return start, wait, away.wait_send


def share_clip(src, dst, s, r, l):
    x, y, z, core = here()
    put = dst.at[2 * lax.rem(z, 2) + core]
    copies = [
        remote(src.at[1 - core], put, s.at[0], r.at[0], chip(x, y, z, 1 - core)),
        remote(src.at[0], put, s.at[1], r.at[1 + core], chip(x, y, z + 1, 0)),
        remote(src.at[1], put, s.at[2], r.at[1 + core], chip(x, y, z - 1, 1)),
    ]
    local = pltpu.make_async_copy(src.at[core], put, l)

    def start():
        for copy in copies:
            copy.start()
        local.start()

    def wait():
        local.wait()
        for slot in range(3):
            remote(src.at[0], dst.at[0], s.at[0], r.at[slot], chip(x, y, z, core)).wait_recv()

    def drain():
        for copy in copies:
            copy.wait_send()

    return start, wait, drain


def split3(values):
    return [values[:, i * HW : (i + 1) * HW] for i in range(values.shape[1] // HW)]


def swap_halves(values):
    return pltpu.roll(values, HEAD // 2, 1)


def rope_pair(table):
    lane = lax.broadcasted_iota(jnp.int32, table.shape, 1)
    other = swap_halves(table)
    front = lane < HEAD // 2
    return jnp.where(front, table, other), jnp.where(front, -other, table)


def head_slice(h):
    return slice(h * HEAD, (h + 1) * HEAD)


SCALE = HEAD ** (-0.5)


def softmax_rows(query, keys):
    scores = contract_last(query, keys) * SCALE
    peak = jnp.max(scores, -1, keepdims=True)
    raised = jnp.exp(scores - peak)
    return raised * (1.0 / jnp.sum(raised, -1, keepdims=True))


def attend_clip(query, keys, values, out):
    for h in range(HEADS):
        cols = head_slice(h)
        for start in range(0, SEQ, 256):
            rows = slice(start, start + 256)
            weights = softmax_rows(query[rows, cols], keys[:, cols]).astype(BF)
            out[rows, cols] = product(weights, values[:, cols]).astype(BF)


class Stats:
    def __init__(self, buffer, send, recv):
        self.buffer, self.send, self.recv = buffer, send, recv

    def start(self, turn, columns):
        x, y, z, core = here()
        lane = lax.broadcasted_iota(jnp.int32, (SEQ, 128), 1)
        packed = jnp.zeros((SEQ, 128), F32)
        for i, column_values in enumerate(columns):
            packed = jnp.where(lane == i, column_values, packed)
        self.buffer[turn, 0] = packed.T[:8]
        copies = []
        for k in (2, 1, 3):
            copies.append(
                remote(self.buffer.at[turn, 0], self.buffer.at[turn, k], self.send.at[turn, k - 1],
                       self.recv.at[turn, k - 1], chip(x, y, z + k, core))
            )
            copies[-1].start()

        def wait():
            for copy in copies:
                copy.wait()
            total = (self.buffer[turn, 0] + self.buffer[turn, 1]) + (
                self.buffer[turn, 2] + self.buffer[turn, 3]
            )
            spread = jnp.concatenate([total, jnp.zeros((120, SEQ), F32)], 0).T
            return [spread[:, i : i + 1] for i in range(len(columns))]

        return wait


def block_slice(index):
    return pl.ds(pl.multiple_of(index * TOK, TOK), TOK)


def scatter_product(left, right, part, got, send, recv):
    x, y, z, core = here()
    copies = []
    for k in (2, 1, 3, 0):
        rows = block_slice(block_of(z + k))
        part[rows] = contract_last(left[rows], right).astype(BF)
        if k:
            copies.append(
                remote(part.at[rows], got.at[k - 1], send.at[k - 1], recv.at[k - 1], chip(x, y, z + k, core))
            )
            copies[-1].start()
    return copies


def collect(part, got, copies):
    z = here()[2]
    for copy in copies:
        copy.wait_recv()
    total = part[block_slice(block_of(z))].astype(F32)
    for k in range(3):
        total = total + got[k].astype(F32)
    return total


def spread_block(out, value, send, recv):
    x, y, z, core = here()
    rows = block_slice(block_of(z))
    out[rows] = value
    copies = []
    for k in (2, 1, 3):
        copies.append(
            remote(out.at[rows], out.at[rows], send.at[k - 1], recv.at[k - 1], chip(x, y, z + k, core))
        )
        copies[-1].start()
    return copies


def inverse_root(total):
    return lax.rsqrt(total * (1.0 / D) + NORM_EPSILON)


V_SELF, V_CROSS, V_DOWN, V_GAIN, V_BIAS = 6, 7, 8, 9, 10
W_QKV, W_QUERY, W_TEXT, W_SELF, W_CROSS = (
    slice(0, 3 * HW), slice(3 * HW, 4 * HW), slice(4 * HW, 6 * HW), slice(6 * HW, 7 * HW), slice(7 * HW, 8 * HW),
)
ATTN = 8 * HW


SAVED = 22


def forward_kernel(
    send_attn, send_mlp, tok, txt, cot, tab, heads, vec,
    w_attn, w_up, w_down, cot_all, *rest,
):
    saved, held, rest = rest[:SAVED], rest[SAVED : 2 * SAVED], rest[2 * SAVED :]
    (
        tab_all, input_one, input_three, input_mlp, query_lin, key_lin, query_two_lin, key_two_lin, inv,
        query_rot, key_rot, value_low, query_two, key_two, value_two, mixed, mixed_two, branch_one,
        after_one, after_two, tok_all, txt_all,
    ) = held
    (
        wa, got_attn, got_mlp, own_attn, own_mlp, part_one, part_two, blocks, stat,
        xs, xr, ks, kr, ms, mr, js, jr, rs, rr, cs, cr, loc, stat_s, stat_r, zs, zr, gs, gr, keep,
    ) = rest
    x, y, z, core = here()
    mine = x * SIDE + y
    stores = []

    def save(*refs):
        for ref in refs:
            i = [ref is other for other in held].index(True)
            stores.append(pltpu.make_async_copy(ref, saved[i], keep.at[i]))
            stores[-1].start()

    greet(
        [device for pair in steps_of(x, y, z, core) for device in pair] + column(x, y, z, core)
    )
    attn_start, attn_wait, attn_drain = share_rows(send_attn, got_attn, rs.at[0], rr.at[0], loc.at[0])
    mlp_start, mlp_wait, mlp_drain = share_rows(send_mlp, got_mlp, rs.at[1], rr.at[1], loc.at[1])
    acts = [
        share_clip(src, dst, cs.at[i], cr.at[i], loc.at[2 + i, 0])
        for i, (src, dst) in enumerate(
            ((tok, tok_all), (tab, tab_all), (txt, txt_all), (cot, cot_all))
        )
    ]
    attn_start()
    acts[0][0]()
    acts[1][0]()
    attn_wait(own_attn)

    def attn_place(part, index, half=None):
        start, size = part * (ATTN // 2), ATTN // 2
        if half is not None:
            start, size = start + half * (ATTN // 4), ATTN // 4
        rows = pl.ds(pl.multiple_of(index * (2 * PAIR) + core * PAIR, PAIR), PAIR)
        return wa.at[rows, pl.ds(start, size)]

    def mlp_place(part, index, half=None):
        start, size = (0, FF) if half is None else (half * (FF // 2), FF // 2)
        rows = pl.ds(pl.multiple_of(index * (2 * PAIR) + core * PAIR, PAIR), PAIR)
        return (w_up, w_down)[part].at[rows, pl.ds(start, size)]

    gather_attn = gather_xy(own_attn, attn_place, xs, xr, ks, kr)
    advance(gather_attn)
    for part in (0, 1):
        attn_place(part, mine)[...] = own_attn[part]
    acts[2][0]()
    mlp_start()

    def norm_block(i, carry):
        normed, _ = plain_norm(tok_all[i].astype(F32))
        input_one[block_slice(i)] = (normed * (1.0 + vec[1:2]) + vec[0:1]).astype(BF)
        return carry

    advance(gather_attn, 4)
    acts[3][0]()
    advance(gather_attn, 2)
    acts[0][1]()
    lax.fori_loop(0, 2, norm_block, 0)
    advance(gather_attn, 2)
    lax.fori_loop(2, 4, norm_block, 0)
    save(input_one, tok_all)
    advance(gather_attn, 2)
    mlp_wait(own_mlp)
    locals_ = []
    for part in (0, 1):
        locals_.append(pltpu.make_async_copy(own_mlp.at[part], mlp_place(part, mine), loc.at[6, part]))
        locals_[-1].start()
    advance(gather_attn, 2)
    gather_mlp = gather_xy(own_mlp, mlp_place, ms, mr, js, jr)
    advance(gather_mlp)
    finish(gather_attn)
    locals_.append(pltpu.make_async_copy(wa, w_attn, loc.at[7, 0]))
    locals_[-1].start()
    acts[1][1]()
    acts[2][1]()
    save(tab_all, txt_all)

    stats = Stats(stat, stat_s, stat_r)
    query_lin[...] = product(input_one[...], wa[:, 0:HW]) + heads[0:1]
    key_lin[...] = product(input_one[...], wa[:, HW : 2 * HW]) + heads[1:2]
    words = txt_all[...].reshape(SEQ, D)
    key_two_lin[...] = product(words, wa[:, 4 * HW : 5 * HW]) + heads[6:7]
    norm_wait = stats.start(
        0,
        [
            jnp.sum(ref[...] * ref[...], -1, keepdims=True)
            for ref in (query_lin, key_lin, key_two_lin)
        ],
    )
    value_low[...] = (product(input_one[...], wa[:, 2 * HW : 3 * HW]) + heads[2:3]).astype(BF)
    value_two[...] = (product(words, wa[:, 5 * HW : 6 * HW]) + heads[7:8]).astype(BF)
    save(query_lin, key_lin, key_two_lin, value_low, value_two)
    lane = lax.broadcasted_iota(jnp.int32, (SEQ, 128), 1)
    inverse_query, inverse_key, inverse_key_two = [inverse_root(v) for v in norm_wait()]
    inv[...] = jnp.where(
        lane == 0, inverse_query, jnp.where(lane == 1, inverse_key, jnp.where(lane == 2, inverse_key_two, 0.0))
    )
    cosine, sine = rope_pair(tab_all[...].reshape(SEQ, HEAD))
    for h in range(HEADS):
        cols = head_slice(h)
        for lin, inverse, gain, out in (
            (query_lin, inverse_query, 3, query_rot),
            (key_lin, inverse_key, 4, key_rot),
        ):
            value = lin[:, cols] * inverse * (1.0 + heads[gain : gain + 1, cols])
            out[:, cols] = (value * cosine + swap_halves(value) * sine).astype(BF)
    advance(gather_mlp, 2)
    attend_clip(query_rot, key_rot, value_low, mixed)
    copies = scatter_product(mixed, wa[:, W_SELF], part_one, blocks.at[0], zs.at[0], zr.at[0])
    drains = list(copies)
    key_two[...] = (key_two_lin[...] * inverse_key_two * (1.0 + heads[9:10])).astype(BF)
    save(query_rot, key_rot, key_two, mixed)
    advance(gather_mlp, 8)
    branch = collect(part_one, blocks.at[0], copies) + vec[V_SELF : V_SELF + 1]
    branch_one[...] = branch
    after = tok_all[block_of(z)].astype(F32) + vec[2:3] * branch
    after_one[...] = after
    normed, _ = plain_norm(after)
    copies = spread_block(
        input_three,
        (normed * (1.0 + vec[V_GAIN : V_GAIN + 1]) + vec[V_BIAS : V_BIAS + 1]).astype(BF),
        gs.at[0],
        gr.at[0],
    )
    drains += copies
    save(branch_one, after_one)
    finish(gather_mlp)
    for copy in copies:
        copy.wait_recv()
    query_two_lin[...] = product(input_three[...], wa[:, W_QUERY]) + heads[5:6]
    norm_wait = stats.start(1, [jnp.sum(query_two_lin[...] * query_two_lin[...], -1, keepdims=True)])
    save(input_three, query_two_lin)
    inverse_query_two = inverse_root(norm_wait()[0])
    inv[...] = jnp.where(lane == 3, inverse_query_two, inv[...])
    query_two[...] = (query_two_lin[...] * inverse_query_two * (1.0 + heads[8:9])).astype(BF)
    attend_clip(query_two, key_two, value_two, mixed_two)
    copies = scatter_product(mixed_two, wa[:, W_CROSS], part_two, blocks.at[1], zs.at[1], zr.at[1])
    drains += copies
    save(inv, query_two, mixed_two)
    after = after_one[...] + collect(part_two, blocks.at[1], copies) + vec[V_CROSS : V_CROSS + 1]
    after_two[...] = after
    normed, _ = plain_norm(after)
    copies = spread_block(
        input_mlp, (normed * (1.0 + vec[4:5]) + vec[3:4]).astype(BF), gs.at[1], gr.at[1]
    )
    drains += copies
    save(after_two)
    for copy in locals_:
        copy.wait()
    acts[3][1]()
    for act in acts:
        act[2]()
    attn_drain()
    mlp_drain()
    for copy in copies:
        copy.wait_recv()
    save(input_mlp)
    for copy in drains:
        copy.wait_send()
    for copy in stores:
        copy.wait()


def forward(send_attn, send_mlp, tok, txt, cot, tab, heads, vec):
    dma = pltpu.SemaphoreType.DMA
    sds = jax.ShapeDtypeStruct
    wide, lin, low = sds((SEQ, D), BF), sds((SEQ, HW), F32), sds((SEQ, HW), BF)
    block = sds((TOK, D), F32)
    outs = [
        sds((SIDE, TOK, HEAD), F32), wide, wide, wide, lin, lin, lin, lin, sds((SEQ, 128), F32),
        low, low, low, low, low, low, low, low, block, block, block,
        sds((SIDE, TOK, D), BF), sds((SIDE, TOK, D), BF),
    ]
    weights = [sds((D, ATTN), BF), sds((D, FF), BF), sds((D, FF), BF), sds((SIDE, TOK, D), BF)]
    return pl.pallas_call(
        forward_kernel,
        out_shape=weights + outs,
        in_specs=[VM, VM, HB, HB, HB, VM, VM, VM],
        out_specs=[HB] * (len(weights) + len(outs)),
        scratch_shapes=[
            *[pltpu.VMEM(shape.shape, shape.dtype) for shape in outs],
            pltpu.VMEM((D, ATTN), BF),
            pltpu.VMEM((2, PAIR, ATTN // 2), BF),
            pltpu.VMEM((2, PAIR, FF), BF),
            pltpu.VMEM((2, PAIR, ATTN // 2), BF),
            pltpu.VMEM((2, PAIR, FF), BF),
            pltpu.VMEM((SEQ, D), BF),
            pltpu.VMEM((SEQ, D), BF),
            pltpu.VMEM((2, 3, TOK, D), BF),
            pltpu.VMEM((2, 4, 8, SEQ), F32),
            *[dma(s) for s in GATHER_SEMS],
            *[dma(s) for s in GATHER_SEMS],
            dma((2, 2)), dma((2, 2)), dma((4, 3)), dma((4, 3)), dma((8, 2)),
            dma((2, 3)), dma((2, 3)), dma((2, 3)), dma((2, 3)), dma((2, 3)), dma((2, 3)),
            dma((SAVED,)),
        ],
        compiler_params=params(0),
        name="forward",
    )(send_attn, send_mlp, tok, txt, cot, tab, heads, vec)


BATCH = 768


def peers_xy(x, y, z, core):
    rows = [chip(x + k, y, z, core) for k in (1, 2, 3)]
    lines = [chip(x, y + k, z, core) for k in (1, 2, 3)]
    return rows, lines


def reduce_batch(grads, out, sib, r1, r2, tosend, ss, sr, s1, q1, s2, q2, *swap_sems, gates=None):
    x, y, z, core = here()
    zl = lax.rem(z, 2)
    rows, lines = peers_xy(x, y, z, core)
    sibling = chip(x, y, z, 1 - core)
    wrap = lambda v: lax.rem(v, SIDE)
    swaps, one, two = [], {0: [], 1: []}, {0: [], 1: []}
    free = gates if gates is not None else (None, None)
    if free[1] is not None:
        pl.semaphore_wait(free[1], 7)
    for part in (0, 1):
        swaps.append(
            remote(grads.at[part, :, :, 1 - core], sib.at[part], ss.at[part], sr.at[part], sibling)
        )
        swaps[part].start()
    yield
    for part in (0, 1):
        swaps[part].wait_recv()

        def add_pair(k, carry):
            a, b = lax.div(k, SIDE), lax.rem(k, SIDE)
            grads[part, a, b, core] = grads[part, a, b, core] + sib[part, a, b]
            return carry

        lax.fori_loop(0, SIDE * SIDE, add_pair, 0)
        for k in (2, 1, 3):
            src = grads.at[0, :, wrap(y + k), core] if part == 0 else grads.at[1, wrap(x + k), :, core]
            device = (lines, rows)[part][k - 1]
            copy = remote(src, r1.at[part, k - 1], s1.at[part, k - 1], q1.at[part, k - 1], device)
            copy.start()
            one[part].append(copy)
    yield
    for part in (0, 1):
        for copy in one[part]:
            copy.wait_recv()

        def add_line(k, carry):
            a, b = (k, y) if part == 0 else (x, k)
            total = grads[part, a, b, core].astype(F32)
            for i in range(3):
                total = total + r1[part, i, k].astype(F32)
            grads[part, a, b, core] = total.astype(BF)
            return carry

        lax.fori_loop(0, SIDE, add_line, 0)
        for k in (2, 1, 3):
            src = grads.at[0, wrap(x + k), y, core] if part == 0 else grads.at[1, x, wrap(y + k), core]
            device = (rows, lines)[part][k - 1]
            copy = remote(src, r2.at[part, k - 1], s2.at[part, k - 1], q2.at[part, k - 1], device)
            copy.start()
            two[part].append(copy)
    yield
    final = []
    for part in (0, 1):
        for copy in two[part]:
            copy.wait_recv()
        total = grads[part, x, y, core].astype(F32)
        for i in range(3):
            total = total + r2[part, i].astype(F32)
        final.append(total)
    if free[0] is not None:
        for device in [*rows, *lines, sibling]:
            pl.semaphore_signal(free[0], inc=1, device_id=device, device_id_type=MESH)
    for target in (0, 1):
        span = slice(target * ROWS, target * ROWS + ROWS)
        tosend[target] = jnp.concatenate([final[0][span], final[1][span]], 0).astype(tosend.dtype)
    if out is not None:
        exchange = swap_rows(tosend, out, *swap_sems)
        next(exchange)
        yield
        finish(exchange)
    for copy in swaps + one[0] + one[1] + two[0] + two[1]:
        copy.wait_send()


def swap_rows(owned, out, s3, q3, l3):
    x, y, z, core = here()
    zl = lax.rem(z, 2)
    other = z + 1 - 2 * zl
    far = [
        remote(owned.at[t], out.at[zl], s3.at[t], q3.at[zl], chip(x, y, other, t)) for t in (0, 1)
    ]
    self_copy = pltpu.make_async_copy(owned.at[core], out.at[zl], l3.at[0])
    near = remote(owned.at[1 - core], out.at[zl], s3.at[0], q3.at[zl], chip(x, y, z, 1 - core))

    def got(slot):
        remote(owned.at[0], out.at[slot], s3.at[0], q3.at[slot], chip(x, y, z, core)).wait_recv()

    @pl.when(core == zl)
    def _():
        self_copy.start()
        near.start()

    @pl.when(core != zl)
    def _():
        for copy in far:
            copy.start()

    yield

    @pl.when(core == zl)
    def _():
        self_copy.wait()
        near.wait_send()
        got(1 - zl)

    @pl.when(core != zl)
    def _():
        for copy in far:
            copy.wait_send()
        got(zl)
        got(1 - zl)


def reduce_buffers():
    return [
        pltpu.VMEM((2, SIDE, SIDE, PAIR, BATCH), BF),
        pltpu.VMEM((2, 3, SIDE, PAIR, BATCH), BF),
        pltpu.VMEM((2, 3, PAIR, BATCH), BF),
    ]


def reduce_sems():
    dma = pltpu.SemaphoreType.DMA
    return [dma((2,)), dma((2,)), dma((2, 3)), dma((2, 3)), dma((2, 3)), dma((2, 3))]


def swap_sems():
    dma = pltpu.SemaphoreType.DMA
    return [dma((2,)), dma((2,)), dma((1,))]


def reduce_scratch():
    return [*reduce_buffers(), pltpu.VMEM((2, PAIR, BATCH), F32), *reduce_sems(), *swap_sems()]


GRADS = (2, SIDE, SIDE, 2, PAIR, BATCH)
SLAB = D // SIDE


def weight_grad(left, right, grads, part, start):
    width = right.shape[1]

    def slab(i, carry):
        turned = left[:, pl.ds(pl.multiple_of(i * SLAB, SLAB), SLAB)].T
        value = product(turned, right).astype(BF).reshape(SIDE, 2, PAIR, width)
        grads[part, i, :, :, :, start : start + width] = value
        return carry

    lax.fori_loop(0, SIDE, slab, 0)


def column_sum(values):
    return jnp.sum(values.astype(F32), 0, keepdims=True)


def scatter_held(part, got, send, recv, first=0, count=TOK):
    x, y, z, core = here()
    copies = []
    for k in (2, 1, 3):
        rows = pl.ds(pl.multiple_of(block_of(z + k) * TOK + first, count), count)
        copies.append(
            remote(part.at[rows], got.at[k - 1, pl.ds(first, count)], send.at[k - 1], recv.at[k - 1],
                   chip(x, y, z + k, core))
        )
        copies[-1].start()
    return copies


def deliver(src, dst, s, r, l):
    x, y, z, core = here()
    zh = lax.div(z, 2)
    far = remote(src, dst.at[core], s.at[0], r.at[core], chip(x, y, z + 2, zh))
    near = remote(src, dst.at[core], s.at[1], r.at[core], chip(x, y, z, zh))
    self_copy = pltpu.make_async_copy(src, dst.at[core], l)

    def got(slot):
        remote(src, dst.at[slot], s.at[0], r.at[slot], chip(x, y, z, core)).wait_recv()

    def start():
        far.start()

        @pl.when(core == zh)
        def _():
            self_copy.start()

        @pl.when(core != zh)
        def _():
            near.start()

    def wait():
        @pl.when(core == zh)
        def _():
            self_copy.wait()
            got(1 - core)

        @pl.when(core != zh)
        def _():
            near.wait_send()
            got(0)
            got(1)

        far.wait_send()

    return start, wait


CUBE = 0.044715
ROOT = math.sqrt(2.0 / math.pi)


def gelu_pair(u):
    square = u * u
    t = jnp.tanh(ROOT * u * (1.0 + CUBE * square))
    half = 0.5 * (1.0 + t)
    return u * half, half + 0.5 * u * (1.0 - t * t) * (ROOT * (1.0 + 3.0 * CUBE * square))


def total_of(mine, blocks):
    total = mine.astype(F32)
    for k in range(3):
        total = total + blocks[k].astype(F32)
    return total


def mlp_kernel(
    a_in, cot_all, w_up, w_down, after_in, vec, bias,
    low_out, grad_after, sums, bias_sum, out_result, owned_a, owned_b, owned_c,
    a, low, ahead, behind, hidden, act, back, acc, part, after_two, low_two,
    blocks, result, zs, zr, gs, gr, ds, dr, loc, ring, gate, *rest,
):
    x, y, z, core = here()
    rows, lines = peers_xy(x, y, z, core)
    own_rows = block_slice(block_of(z))

    def load(src, dst, sem):
        copy = pltpu.make_async_copy(src, dst, sem)
        copy.start()
        return copy

    def third(n):
        return pl.ds(n % 3 * BATCH, BATCH)

    def load_ahead(n):
        return load((w_up, w_down)[n // 3].at[:, third(n)], ahead.at[n % 2], ring.at[0, n % 2])

    def load_behind(n):
        return load((w_down, w_up)[n // 3].at[:, third(n)], behind.at[n % 2], ring.at[1, n % 2])

    aheads, behinds = {0: load_ahead(0)}, {}
    fetch_a = load(a_in, a, loc.at[0])
    behinds[0] = load_behind(0)
    fetch_low = load(cot_all.reshape(SEQ, D), low, loc.at[1])
    aheads[1], behinds[1] = load_ahead(1), load_behind(1)
    fetch_after = load(after_in, after_two, loc.at[2])
    greet(column(x, y, z, core) + rows + lines)
    sums[...] = jnp.zeros_like(sums)
    fetch_a.wait()
    aheads[0].wait()
    hidden[0] = product(a[...], ahead[0])
    aheads[2] = load_ahead(2)
    fetch_low.wait()
    dy = low[own_rows].astype(F32)
    for start in range(0, SEQ, TOK):
        block = slice(start, start + TOK)
        low[block] = (low[block].astype(F32) * vec[5:6]).astype(BF)
    sums[2:3] = column_sum(low[own_rows])
    fetch_after.wait()

    grads = [rest[0], rest[1], rest[0]]
    first, second, sems = rest[2:5], rest[5:8], rest[8:]
    owned = (owned_a, owned_b, owned_c)
    jobs = [
        reduce_batch(
            grads[b], None, *(first, second, first)[b], owned[b], *sems[6 * b : 6 * b + 6],
            gates=((gate, None), None, (None, gate))[b],
        )
        for b in range(3)
    ]

    def step(n):
        if n < 5:
            aheads[n + 1].wait()
            left = a if n < 2 else low
            hidden[(n + 1) % 2] = product(left[...], ahead[(n + 1) % 2])
        cols = slice(n % 3 * BATCH, (n % 3 + 1) * BATCH)
        if n < 3:
            value, slope = gelu_pair(hidden[n % 2] + bias[0:1, cols])
            value = value.astype(BF)
            act[:, cols] = value
            back[:, cols] = slope.astype(BF)
        else:
            value = (hidden[n % 2] * back[:, cols].astype(F32)).astype(BF)
            back[:, cols] = value
            bias_sum[0:1, cols] = column_sum(value)
        behinds[n].wait()
        moved = contract_last(value, behind[n % 2])
        if n % 3 == 0:
            acc[...] = moved
        elif n % 3 == 1:
            acc[...] += moved
        else:
            part[...] = (acc[...] + moved).astype(BF)
        if n < 3:
            aheads[n + 3] = load_ahead(n + 3)
        if n < 4:
            behinds[n + 2] = load_behind(n + 2)

    def third_grads(n, b, half):
        cols = slice(n % 3 * BATCH, (n % 3 + 1) * BATCH)
        left, right = ((low, act), (a, back))[n // 3]
        weight_grad(left, right[:, cols], grads[b], half, 0)

    step(0)
    third_grads(0, 0, 0)
    step(1)
    third_grads(1, 0, 1)
    advance(jobs[0])
    step(2)
    down_copies = scatter_held(part, blocks.at[0], zs.at[0], zr.at[0])
    advance(jobs[0])
    third_grads(2, 1, 0)
    step(3)
    third_grads(3, 1, 1)
    advance(jobs[1])
    step(4)
    advance(jobs[1])
    advance(jobs[0])
    for copy in down_copies:
        copy.wait()
    branch = total_of(part[own_rows], blocks.at[0]) + vec[V_DOWN : V_DOWN + 1]
    result[...] = (after_two[...] + vec[5:6] * branch).astype(BF)
    sums[10:11] = column_sum(dy * branch)
    step(5)
    copies = scatter_held(part, blocks.at[1], zs.at[1], zr.at[1])
    drains = list(copies)
    send_result, wait_result = deliver(result, out_result, ds, dr, loc.at[3])
    finish(jobs[0])
    third_grads(4, 2, 0)
    third_grads(5, 2, 1)
    advance(jobs[2])
    advance(jobs[1])
    advance(jobs[2])
    for copy in copies:
        copy.wait_recv()
    total = total_of(part[own_rows], blocks.at[1])
    normed, inverse = plain_norm(after_two[...])
    sums[8:9] = column_sum(total)
    sums[9:10] = column_sum(total * normed)
    value = dy + norm_back(total * (1.0 + vec[4:5]), normed, inverse)
    grad_after[...] = value
    value = value.astype(BF)
    sums[1:2] = column_sum(value)
    copies = spread_block(low_two, value, gs, gr)
    drains += copies
    send_result()
    finish(jobs[1])
    advance(jobs[2])
    finish(jobs[2])
    for copy in copies:
        copy.wait_recv()
    store = pltpu.make_async_copy(low_two, low_out, loc.at[4])
    store.start()
    wait_result()
    store.wait()
    for copy in drains:
        copy.wait_send()


def mlp_pass(a, cot, up, down, after, vec, bias):
    dma = pltpu.SemaphoreType.DMA
    sds = jax.ShapeDtypeStruct
    wide = pltpu.VMEM((SEQ, D), BF)
    tiles = pltpu.VMEM((2, D, BATCH), BF)
    units = pltpu.VMEM((SEQ, FF), BF)
    owned = sds((2, PAIR, BATCH), BF)
    outs = [
        (sds((SEQ, D), BF), HB), (sds((TOK, D), F32), VM), (sds((16, D), F32), VM),
        (sds((8, FF), F32), VM), (sds((2, TOK, D), BF), HB), (owned, VM), (owned, VM), (owned, VM),
    ]
    return pl.pallas_call(
        mlp_kernel,
        out_shape=[shape for shape, _ in outs],
        in_specs=[HB] * 5 + [VM] * 2,
        out_specs=[spec for _, spec in outs],
        scratch_shapes=[
            wide, wide, tiles, tiles, pltpu.VMEM((2, SEQ, BATCH), F32), units, units,
            pltpu.VMEM((SEQ, D), F32), wide, pltpu.VMEM((TOK, D), F32), wide,
            pltpu.VMEM((2, 3, TOK, D), BF), pltpu.VMEM((TOK, D), BF), dma((2, 3)), dma((2, 3)),
            dma((3,)), dma((3,)), dma((2,)), dma((2,)), dma((5,)), dma((2, 2)),
            pltpu.SemaphoreType.REGULAR, pltpu.VMEM(GRADS, BF), pltpu.VMEM(GRADS, BF),
            *reduce_buffers(), *reduce_buffers(), *reduce_sems(), *reduce_sems(), *reduce_sems(),
        ],
        compiler_params=params(1),
        name="mlp",
    )(a, cot, up, down, after, vec, bias)


def vector_job(model, heads, time_out, model_out, head_out, *refs):
    col, mx, sends, recvs, *head_refs = refs
    x, y, z, core = here()
    zl = lax.rem(z, 2)
    rows, lines = peers_xy(x, y, z, core)
    sibling = chip(x, y, z, 1 - core)
    copies = []
    for k in (2, 1, 3):
        copies.append(remote(model, col.at[k], sends.at[0, k], recvs.at[0, k], chip(x, y, z + k, core)))
    if heads is not None:
        hsib, hx = head_refs
        copies.append(remote(heads, hsib, sends.at[0, 0], recvs.at[0, 0], sibling))
    for copy in copies:
        copy.start()
    yield
    for copy in copies:
        copy.wait()
    time_out[core] = model[...] + col[1] + col[2] + col[3]
    swap = remote(time_out.at[core], time_out.at[core], sends.at[1, 0], recvs.at[1, 0], sibling)
    swap.start()
    if heads is not None:
        hx[0] = heads[...] + hsib[...]
    yield
    swap.wait()
    mx[0] = time_out[0] + time_out[1]
    for stage, peers in enumerate((rows, lines)):
        copies = []
        for k in (1, 2, 3):
            copies.append(
                remote(mx.at[4 * stage], mx.at[4 * stage + k], sends.at[2 + 2 * stage, k],
                       recvs.at[2 + 2 * stage, k], peers[k - 1])
            )
            if heads is not None:
                copies.append(
                    remote(hx.at[4 * stage], hx.at[4 * stage + k], sends.at[3 + 2 * stage, k],
                           recvs.at[3 + 2 * stage, k], peers[k - 1])
                )
        for copy in copies:
            copy.start()
        yield
        for copy in copies:
            copy.wait()
        base = 4 * stage
        mx[base + 4] = mx[base] + mx[base + 1] + mx[base + 2] + mx[base + 3]
        if heads is not None:
            hx[base + 4] = hx[base] + hx[base + 1] + hx[base + 2] + hx[base + 3]
    model_out[...] = mx[8]
    if heads is not None:
        head_out[zl] = hx[8]
        last = remote(
            hx.at[8], head_out.at[zl], sends.at[6, 0], recvs.at[6, 0], chip(x, y, z + 1 - 2 * zl, core)
        )
        last.start()
        yield
        last.wait()


def vector_scratch(rows, heads):
    dma = pltpu.SemaphoreType.DMA
    refs = [pltpu.VMEM((4, rows, D), F32), pltpu.VMEM((9, rows, D), F32), dma((7, 4)), dma((7, 4))]
    if heads:
        refs += [pltpu.VMEM((16, HW), F32), pltpu.VMEM((9, 16, HW), F32)]
    return refs


def attend_clip_back(query, keys, values, grad, grad_query, grad_keys, grad_values):
    for h in range(HEADS):
        cols = head_slice(h)
        k, v = keys[:, cols], values[:, cols]
        for start in range(0, SEQ, 256):
            rows = slice(start, start + 256)
            q, do = query[rows, cols], grad[rows, cols]
            weights = softmax_rows(q, k)
            grad_weights = contract_last(do, v)
            delta = jnp.sum(weights * grad_weights, -1, keepdims=True)
            grad_scores = (weights * (grad_weights - delta)).astype(BF)
            grad_query[rows, cols] = product(grad_scores, k) * SCALE
            to_keys = contract_rows(grad_scores, q) * SCALE
            to_values = contract_rows(weights.astype(BF), do)
            if start:
                grad_keys[:, cols] += to_keys
                grad_values[:, cols] += to_values
            else:
                grad_keys[:, cols] = to_keys
                grad_values[:, cols] = to_values


def root_back(linear, inverse, scaled, dot):
    return (inverse * scaled - linear * (inverse * inverse * inverse * dot * (1.0 / D))).astype(BF)


def backward_kernel(
    wa_in, low_in, after_in, branch_in, query_lin_in, key_lin_in, query_two_lin_in, key_two_lin_in,
    query_rot_in, key_rot_in, value_low_in, query_two_in, key_two_in, value_two_in, mixed_in,
    mixed_two_in, words_in, three_in, one_in, tok_in, grad_in, tab_in, inv_in,
    vec, heads, sums, bias_sum, owned_a, owned_b, owned_c,
    out_tokens, out_words, time_out, model_out, head_out, sums_a, sums_b, mlp_a, mlp_b, mlp_c,
    wa, low_wide, after_one, branch_one, lin_a, lin_b, qa, ka, va, mixed, mixed_two, operand, tok_own,
    grad_after, tab, inv, grad_query, grad_kv, grad_qkv, part_cross, part_words, blocks,
    held, gq, gk, gv, model, head_sums, low_words, low_tokens,
    stat, stat_s, stat_r, zs, zr, gs, gr, ds, dr, loc, *rest,
):
    x, y, z, core = here()
    rows, lines = peers_xy(x, y, z, core)
    slots = iter(range(32))
    own_block = block_of(z)

    def fetch(src, dst):
        copy = pltpu.make_async_copy(src, dst, loc.at[next(slots)])
        copy.start()
        return copy

    out_cols, in_cols = pl.ds(6 * HW, 2 * HW), pl.ds(0, 6 * HW)
    first = [fetch(low_in, low_wide), fetch(wa_in.at[:, out_cols], wa.at[:, out_cols])]
    cross = [
        fetch(query_two_in, qa), fetch(key_two_in, ka), fetch(value_two_in, va),
        fetch(query_two_lin_in, lin_a), fetch(key_two_lin_in, lin_b), fetch(inv_in, inv),
    ]
    second = [
        fetch(mixed_two_in, mixed_two), fetch(wa_in.at[:, in_cols], wa.at[:, in_cols]),
        fetch(words_in.reshape(SEQ, D), operand),
    ]
    third = [
        fetch(after_in, after_one), fetch(branch_in, branch_one), fetch(grad_in, grad_after),
        fetch(mixed_in, mixed), fetch(tab_in, tab), fetch(tok_in.at[own_block], tok_own),
    ]
    greet(column(x, y, z, core) + rows + lines)
    model[...] = sums[...]
    head_sums[...] = jnp.zeros_like(head_sums)
    for i in range(6):
        head_sums[10 + i : 11 + i] = bias_sum[0:1, i * HW : (i + 1) * HW]
    refs_a, refs_b, early_refs, rest = rest[:14], rest[14:28], rest[28:32], rest[32:]
    vector_refs, (late, time_late, model_late), swap_refs = rest[:6], rest[6:9], rest[9:]
    hidden_rows = [
        swap_rows(src, dst, *swap_refs[3 * i : 3 * i + 3])
        for i, (src, dst) in enumerate(((owned_a, mlp_a), (owned_b, mlp_b), (owned_c, mlp_c)))
    ]
    for job in hidden_rows:
        advance(job)
    late[...] = jnp.zeros_like(late)
    grads_a, grads_b = refs_a[0], refs_b[0]
    job_a = reduce_batch(grads_a, sums_a, *refs_a[1:])
    job_b = reduce_batch(grads_b, sums_b, *refs_b[1:])
    stats = Stats(stat, stat_s, stat_r)
    drains = []

    for copy in first:
        copy.wait()
    held[...] = product(low_wide[...], wa[:, W_CROSS]).astype(BF)
    for copy in cross:
        copy.wait()
    attend_clip_back(qa, ka, va, held, gq, gk, gv)
    inverse_query, inverse_key, inverse_key_two, inverse_query_two = [inv[:, i : i + 1] for i in range(4)]
    dots = stats.start(
        0,
        [
            jnp.sum(lin_a[...] * (gq[...] * (1.0 + heads[8:9])), -1, keepdims=True),
            jnp.sum(lin_b[...] * (gk[...] * (1.0 + heads[9:10])), -1, keepdims=True),
        ],
    )
    head_sums[8:9] = column_sum(gq[...] * lin_a[...] * inverse_query_two)
    head_sums[9:10] = column_sum(gk[...] * lin_b[...] * inverse_key_two)
    low = gv[...].astype(BF)
    grad_kv[:, HW:] = low
    head_sums[7:8] = column_sum(low)
    for copy in second:
        copy.wait()
    weight_grad(low_wide, mixed_two[...], grads_a, 1, HW)
    dot_query, dot_key = dots()
    low = root_back(lin_a[...], inverse_query_two, gq[...] * (1.0 + heads[8:9]), dot_query)
    grad_query[...] = low
    head_sums[5:6] = column_sum(low)
    cross_copies = scatter_product(
        grad_query, wa[:, W_QUERY], part_cross, blocks.at[0], zs.at[0], zr.at[0]
    )
    low = root_back(lin_b[...], inverse_key_two, gk[...] * (1.0 + heads[9:10]), dot_key)
    grad_kv[:, :HW] = low
    head_sums[6:7] = column_sum(low)
    selfs = [
        fetch(query_rot_in, qa), fetch(key_rot_in, ka), fetch(value_low_in, va),
        fetch(query_lin_in, lin_a), fetch(key_lin_in, lin_b),
    ]
    weight_grad(operand, grad_kv[...], grads_a, 0, 0)
    next_operand = fetch(three_in, operand)
    next_operand.wait()
    weight_grad(operand, grad_query[...], grads_a, 1, 0)
    next_operand = fetch(one_in, operand)
    advance(job_a)
    part_words[...] = contract_last(grad_kv[...], wa[:, W_TEXT]).astype(BF)
    for copy in third:
        copy.wait()

    total = collect(part_cross, blocks.at[0], cross_copies)
    normed, inverse = plain_norm(after_one[...])
    model[4:5] = column_sum(total)
    model[3:4] = column_sum(total * normed)
    value = grad_after[...] + norm_back(total * (1.0 + vec[V_GAIN : V_GAIN + 1]), normed, inverse)
    grad_after[...] = value
    model[7:8] = column_sum(value * branch_one[...])
    low = (value * vec[2:3]).astype(BF)
    model[0:1] = column_sum(low)
    copies = spread_block(low_wide, low, gs, gr)
    drains += copies
    advance(job_a)
    for copy in copies:
        copy.wait_recv()
    early = vector_job(model, None, time_out, model_out, None, *early_refs)
    advance(early)
    word_copies = scatter_held(part_words, blocks.at[1], zs.at[1], zr.at[1], 0, TOK // 2)

    held[...] = product(low_wide[...], wa[:, W_SELF]).astype(BF)
    for copy in selfs:
        copy.wait()
    attend_clip_back(qa, ka, va, held, gq, gk, gv)
    cosine, sine = rope_pair(tab[...].reshape(SEQ, HEAD))
    for ref in (gq, gk):
        for h in range(HEADS):
            cols = head_slice(h)
            value = ref[:, cols]
            ref[:, cols] = value * cosine - swap_halves(value) * sine
    dots = stats.start(
        1,
        [
            jnp.sum(lin_a[...] * (gq[...] * (1.0 + heads[3:4])), -1, keepdims=True),
            jnp.sum(lin_b[...] * (gk[...] * (1.0 + heads[4:5])), -1, keepdims=True),
        ],
    )
    head_sums[3:4] = column_sum(gq[...] * lin_a[...] * inverse_query)
    head_sums[4:5] = column_sum(gk[...] * lin_b[...] * inverse_key)
    low = gv[...].astype(BF)
    grad_qkv[:, 2 * HW :] = low
    head_sums[2:3] = column_sum(low)
    next_operand.wait()
    weight_grad(low_wide, mixed[...], grads_b, 1, HW)
    for copy in cross_copies:
        copy.wait_send()
    advance(early, 2)
    dot_query, dot_key = dots()
    word_copies += scatter_held(part_words, blocks.at[1], zs.at[3], zr.at[3], TOK // 2, TOK // 2)
    drains += word_copies
    for i, (lin, inverse, ref, dot) in enumerate(
        ((lin_a, inverse_query, gq, dot_query), (lin_b, inverse_key, gk, dot_key))
    ):
        low = root_back(lin[...], inverse, ref[...] * (1.0 + heads[3 + i : 4 + i]), dot)
        grad_qkv[:, i * HW : (i + 1) * HW] = low
        head_sums[i : i + 1] = column_sum(low)
    copies = scatter_product(grad_qkv, wa[:, W_QKV], part_cross, blocks.at[0], zs.at[2], zr.at[2])
    drains += copies
    advance(job_a)
    weight_grad(operand, grad_qkv[:, : 2 * HW], grads_b, 0, 0)
    weight_grad(operand, grad_qkv[:, 2 * HW :], grads_b, 1, 0)
    advance(job_b)
    advance(early)
    advance(job_a)
    advance(job_b)
    finish(early)
    for job in hidden_rows:
        finish(job)
    low_words[...] = collect(part_words, blocks.at[1], word_copies).astype(BF)
    send_words, wait_words = deliver(low_words, out_words, ds.at[0], dr.at[0], loc.at[30])
    finish(job_a)

    total = collect(part_cross, blocks.at[0], copies)
    normed, inverse = plain_norm(tok_own[...].astype(F32))
    late[0:1] = column_sum(total)
    late[1:2] = column_sum(total * normed)
    vectors = vector_job(late, head_sums, time_late, model_late, head_out, *vector_refs)
    advance(vectors)
    value = grad_after[...] + norm_back(total * (1.0 + vec[1:2]), normed, inverse)
    low_tokens[...] = value.astype(BF)
    send_tokens, wait_tokens = deliver(low_tokens, out_tokens, ds.at[1], dr.at[1], loc.at[31])
    advance(vectors)
    send_tokens()
    send_words()
    advance(vectors)
    advance(job_b)
    advance(vectors)
    advance(job_b)
    advance(vectors)
    wait_tokens()
    advance(vectors)
    finish(job_b)
    finish(vectors)
    wait_words()
    time_out[0, 5:7] = time_late[0, 0:2]
    time_out[1, 5:7] = time_late[1, 0:2]
    model_out[5:7] = model_late[0:2]
    for copy in drains:
        copy.wait_send()


def backward(hbm, vmem):
    dma = pltpu.SemaphoreType.DMA
    sds = jax.ShapeDtypeStruct
    lin = pltpu.VMEM((SEQ, HW), F32)
    low = pltpu.VMEM((SEQ, HW), BF)
    wide = pltpu.VMEM((SEQ, D), BF)
    block = pltpu.VMEM((TOK, D), F32)
    low_block = pltpu.VMEM((TOK, D), BF)
    summed = sds((2, PAIR, BATCH), F32)
    outs = [
        (sds((2, TOK, D), BF), HB), (sds((2, TOK, D), BF), HB), (sds((2, 16, D), F32), VM),
        (sds((16, D), F32), VM), (sds((2, 16, HW), F32), VM), (summed, VM), (summed, VM),
        *[(sds((2, PAIR, BATCH), BF), VM)] * 3,
    ]
    batch = [pltpu.VMEM(GRADS, BF), *reduce_scratch()]
    return pl.pallas_call(
        backward_kernel,
        out_shape=[shape for shape, _ in outs],
        in_specs=[HB] * len(hbm) + [VM] * len(vmem),
        out_specs=[spec for _, spec in outs],
        scratch_shapes=[
            pltpu.VMEM((D, ATTN), BF), wide, block, block, lin, lin, low, low, low, low, low, wide,
            low_block, block, pltpu.VMEM((SIDE, TOK, HEAD), F32), pltpu.VMEM((SEQ, 128), F32),
            low, pltpu.VMEM((SEQ, 2 * HW), BF), pltpu.VMEM((SEQ, 3 * HW), BF), wide, wide,
            pltpu.VMEM((2, 3, TOK, D), BF), low, lin, lin, lin, pltpu.VMEM((16, D), F32),
            pltpu.VMEM((16, HW), F32), low_block, low_block,
            pltpu.VMEM((2, 4, 8, SEQ), F32),
            dma((2, 3)), dma((2, 3)), dma((4, 3)), dma((4, 3)), dma((3,)), dma((3,)), dma((2, 2)),
            dma((2, 2)), dma((32,)), *batch, *batch, *vector_scratch(16, False),
            *vector_scratch(8, True), pltpu.VMEM((8, D), F32), pltpu.VMEM((2, 8, D), F32), pltpu.VMEM((8, D), F32),
            *swap_sems(), *swap_sems(), *swap_sems(),
        ],
        compiler_params=params(2),
        name="backward",
    )(*hbm, *vmem)


def block_mask(size):
    row = lax.broadcasted_iota(jnp.int32, (size, size), 0)
    col = lax.broadcasted_iota(jnp.int32, (size, size), 1)
    return lax.div(row, ROWS) == lax.div(col, ROWS), row == col


def times(a, b):
    return jnp.dot(a, b, precision=HIGHEST, preferred_element_type=F32)


def gram_of(blocks):
    return lax.dot_general(
        blocks, blocks, (((1,), (1,)), ((), ())), precision=HIGHEST, preferred_element_type=F32
    )


def newton_factor(gram, size):
    same, eye = block_mask(size)
    gram = jnp.where(same, gram, 0.0)
    diagonal = jnp.where(eye, gram, 0.0)
    by_row = jnp.sum(diagonal, 1, keepdims=True)
    by_col = jnp.sum(diagonal, 0, keepdims=True)
    total_row = jnp.sum(jnp.where(same, by_col, 0.0), 1, keepdims=True)
    total_col = jnp.sum(jnp.where(same, by_row, 0.0), 0, keepdims=True)
    scale_row = 1.0 / (jnp.sqrt(total_row) + ORTHO_EPSILON)
    scale_col = 1.0 / (jnp.sqrt(total_col) + ORTHO_EPSILON)
    current = gram * scale_row * scale_col
    whole = None
    for turn in range(NS_STEPS):
        square = times(current, current)
        step = NEWTON_SECOND * current + NEWTON_THIRD * square + jnp.where(eye, NEWTON_FIRST, 0.0)
        whole = step if whole is None else times(step, whole)
        if turn + 1 < NS_STEPS:
            current = times(times(step, current), step)
    return whole * scale_col


WIDE = 2 * FF_REAL


def join_hidden(first, second):
    fill = jnp.zeros((first.shape[0], FF), F32)
    first = jnp.concatenate([first, fill], 1)
    second = pltpu.roll(jnp.concatenate([second, fill], 1), FF_REAL, 1)
    return (first + second)[:, :WIDE]


def gram_kernel(
    sum_a, sum_b, sum_c, attn_a, attn_b, in_m, out_m, mlp_m, narrow, wide, gram, mine, theirs, send, recv
):
    x, y, z, core = here()
    partner = chip(x, y, z + 2, core)
    greet([partner])

    def pair(ref, part, col):
        rows = slice(part * ROWS, (part + 1) * ROWS)
        return jnp.concatenate([ref[0, rows, col : col + HW], ref[1, rows, col : col + HW]], 1)

    n, w = 8 * ROWS, 2 * ROWS
    for j, (ref, part, col) in enumerate(
        ((attn_b, 0, 0), (attn_b, 0, HW), (attn_b, 1, 0), (attn_a, 1, 0), (attn_a, 0, 0), (attn_a, 0, HW))
    ):
        narrow[j * ROWS : (j + 1) * ROWS] = MOMENTUM * in_m[j] + pair(ref, part, col)
    for j, ref in enumerate((attn_b, attn_a)):
        narrow[(6 + j) * ROWS : (7 + j) * ROWS] = MOMENTUM * out_m[:, j, :] + pair(ref, 1, HW)
    mine[:n, :n] = gram_of(narrow[...])
    top, bottom = slice(0, ROWS), slice(ROWS, 2 * ROWS)
    for j, thirds in enumerate(
        (((sum_b, bottom), (sum_c, top), (sum_c, bottom)), ((sum_a, top), (sum_a, bottom), (sum_b, top)))
    ):
        chips = [jnp.concatenate([ref[i].astype(F32)[rows] for ref, rows in thirds], 1) for i in (0, 1)]
        wide[j * ROWS : (j + 1) * ROWS] = MOMENTUM * mlp_m[:, j, :] + join_hidden(*chips)
    mine[n:, n:] = gram_of(wide[...])
    mine[:n, n:] = jnp.zeros((n, w), F32)
    mine[n:, :n] = jnp.zeros((w, n), F32)
    copy = remote(mine, theirs, send.at[0], recv.at[0], partner)
    copy.start()
    copy.wait()
    gram[...] = mine[...] + theirs[...]


def gram_step(args, cid):
    sds = jax.ShapeDtypeStruct
    dma = pltpu.SemaphoreType.DMA
    size = 10 * ROWS
    return pl.pallas_call(
        gram_kernel,
        out_shape=[
            sds((8 * ROWS, 2 * HW), F32), sds((2 * ROWS, WIDE), F32), sds((size, size), F32),
        ],
        in_specs=[VM] * len(args),
        out_specs=[VM] * 3,
        scratch_shapes=[
            pltpu.VMEM((size, size), F32), pltpu.VMEM((size, size), F32), dma((1,)), dma((1,)),
        ],
        compiler_params=params(cid),
        name="gram",
    )(*args)


def finish_kernel(
    narrow, wide, gram, in_w, out_w, mlp_w, head_w, head_m, model_w, model_m, up_w, up_m, head_sum,
    model_sum, result, tokens, words, time_sum,
    new_in, new_out, new_mlp, new_in_m, new_out_m, new_mlp_m, new_head, new_model, new_up,
    new_head_m, new_model_m, new_up_m, out_result, out_tokens, out_words, out_time,
    block, stores,
):
    out_result[...] = result[...]
    copies = []
    for i, (src, dst) in enumerate(((tokens, out_tokens), (words, out_words))):
        for clip in (0, 1):
            block[2 * i + clip] = src[clip].astype(F32)
            copies.append(
                pltpu.make_async_copy(block.at[2 * i + clip], dst.at[clip], stores.at[2 * i + clip])
            )
            copies[-1].start()
    out_time[...] = time_sum[:, 5:11]
    value = MOMENTUM * head_m[...] + jnp.concatenate([head_sum[0, :10], head_sum[1, :10]], 1)
    new_head_m[...] = value
    new_head[...] = head_w[...] - RATE_VECTOR * value
    value = MOMENTUM * model_m[...] + model_sum[:11]
    new_model_m[...] = value
    new_model[...] = model_w[...] - RATE_VECTOR * value
    chips = [jnp.concatenate([head_sum[i, 10 + k : 11 + k] for k in range(6)], 1) for i in (0, 1)]
    value = MOMENTUM * up_m[...] + join_hidden(*chips)
    new_up_m[...] = value
    new_up[...] = up_w[...] - RATE_VECTOR * value
    n, w = narrow.shape[0], wide.shape[0]
    factor = newton_factor(gram[...], n + w)
    turned = times(factor[:n, :n], narrow[...])
    for j in range(6):
        rows = slice(j * ROWS, (j + 1) * ROWS)
        new_in_m[j] = narrow[rows]
        new_in[j] = in_w[j] * (1.0 - RATE_IN * DECAY) - RATE_IN * turned[rows]
    for j in range(2):
        rows = slice((6 + j) * ROWS, (7 + j) * ROWS)
        new_out_m[:, j, :] = narrow[rows]
        new_out[:, j, :] = out_w[:, j, :] * (1.0 - RATE_OUT * DECAY) - RATE_OUT * turned[rows]
    turned = times(factor[n:, n:], wide[...])
    for j in range(2):
        rows = slice(j * ROWS, (j + 1) * ROWS)
        new_mlp_m[:, j, :] = wide[rows]
        new_mlp[:, j, :] = mlp_w[:, j, :] * (1.0 - RATE_MLP * DECAY) - RATE_MLP * turned[rows]
    for copy in copies:
        copy.wait()


def finish_step(args):
    sds = jax.ShapeDtypeStruct
    matrices = [sds((6, ROWS, 2 * HW), F32), sds((ROWS, 2, 2 * HW), F32), sds((ROWS, 2, WIDE), F32)]
    vectors = [sds((10, 2 * HW), F32), sds((11, D), F32), sds((1, WIDE), F32)]
    blocks = [sds((2, TOK, D), BF), sds((2, TOK, D), F32), sds((2, TOK, D), F32)]
    return pl.pallas_call(
        finish_kernel,
        out_shape=matrices + matrices + vectors + vectors + blocks + [sds((2, 6, D), F32)],
        in_specs=[VM] * len(args),
        out_specs=[VM] * 13 + [HB] * 2 + [VM],
        scratch_shapes=[pltpu.VMEM((4, TOK, D), F32), pltpu.SemaphoreType.DMA((4,))],
        compiler_params=pltpu.CompilerParams(vmem_limit_bytes=VMEM_LIMIT),
        name="finish",
    )(*args)


def rope_tables(places):
    pair_index = jnp.arange(HEAD // 2, dtype=jnp.int32)
    side_pairs = HEAD // 6
    frame_pairs = (HEAD - 4 * side_pairs) // 2
    part_of = (pair_index >= frame_pairs).astype(jnp.int32) + (
        pair_index >= frame_pairs + side_pairs
    ).astype(jnp.int32)
    offset = jnp.where(
        part_of == 0, 0, jnp.where(part_of == 1, frame_pairs, frame_pairs + side_pairs)
    ).astype(jnp.int32)
    extent = jnp.where(part_of == 0, 2 * frame_pairs, 2 * side_pairs).astype(jnp.float32)
    frequency = jnp.exp(
        (pair_index - offset).astype(jnp.float32) * (-2.0 * math.log(10000.0)) / extent
    )
    chosen = (
        places[0][:, None] * (part_of == 0)
        + places[1][:, None] * (part_of == 1)
        + places[2][:, None] * (part_of == 2)
    )
    angles = chosen.astype(jnp.float32) * frequency
    return (jnp.cos(angles), jnp.sin(angles))


def plain_norm(values):
    centred = values - jnp.mean(values, -1, keepdims=True)
    inverse = lax.rsqrt(jnp.mean(centred * centred, -1, keepdims=True) + NORM_EPSILON)
    return (centred * inverse, inverse)


def norm_back(grads, normed, inverse):
    return inverse * (
        grads
        - jnp.mean(grads, -1, keepdims=True)
        - normed * jnp.mean(grads * normed, -1, keepdims=True)
    )


def product(left, right):
    return jnp.dot(left, right, preferred_element_type=F32)


def contract_last(left, right):
    return lax.dot_general(left, right, (((1,), (1,)), ((), ())), preferred_element_type=F32)


def contract_rows(left, right):
    return lax.dot_general(left, right, (((0,), (0,)), ((), ())), preferred_element_type=F32)


def body(
    tokens, text, time_embedding, positions, cotangent, attn_in, attn_out, mlp, head_vectors,
    model_vectors, up_bias, attn_in_moment, attn_out_moment, mlp_moment, head_moment, model_moment,
    up_moment,
):
    x, y, z, core = here()
    zl = lax.rem(z, 2)

    low_in = attn_in.astype(BF).reshape(ROWS, 6, 2, HW).transpose(2, 0, 1, 3).reshape(2, ROWS, -1)
    low_out = attn_out.astype(BF).reshape(ROWS, 2, 2, HW).transpose(2, 0, 1, 3).reshape(2, ROWS, -1)
    send_attn = jnp.concatenate([low_in, low_out], -1).reshape(2, ROWS, 2, ATTN // 2)
    send_attn = send_attn.transpose(0, 2, 1, 3).reshape(2, PAIR, ATTN // 2)
    send_mlp = jnp.pad(
        mlp.astype(BF).reshape(ROWS, 2, 2, FF_REAL).transpose(2, 1, 0, 3),
        ((0, 0), (0, 0), (0, 0), (0, FF - FF_REAL)),
    ).reshape(2, PAIR, FF)
    cosine, sine = rope_tables(positions.reshape(3, 2 * TOK))
    table = jnp.concatenate([cosine, sine], -1).reshape(2, TOK, HEAD)

    heads = jnp.pad(lax.dynamic_slice(head_vectors, (0, zl * HW), (10, HW)), ((0, 6), (0, 0)))
    bias_up = jnp.pad(lax.dynamic_slice(up_bias, (zl * FF_REAL,), (FF_REAL,)), (0, FF - FF_REAL))
    modulation = model_vectors[5:] + lax.dynamic_index_in_dim(time_embedding, core, 0, False)
    shift_one, scale_one, gate_one, shift_two, scale_two, gate_two = [modulation[i] for i in range(6)]
    vectors = jnp.pad(jnp.concatenate([modulation, model_vectors[:5]], 0), ((0, 5), (0, 0)))

    (
        w_attn, w_up, w_down, cot_all, tab_all, input_one, input_three, input_mlp, query_lin, key_lin,
        query_two_lin, key_two_lin, inv, query_rot, key_rot, value_low, query_two, key_two, value_two,
        mixed_low, mixed_two_low, branch_one, after_one, after_two, tok_all, txt_all,
    ) = forward(
        send_attn, send_mlp, tokens, text, cotangent, table, heads, vectors,
    )
    low_two, grad_after, sums, up_sum, out_result, *owned = mlp_pass(
        input_mlp, cot_all, w_up, w_down, after_two, vectors, bias_up[None]
    )
    out_tokens, out_words, time_sums, model_sums, head_totals, sums_a, sums_b, *mlp_sums = backward(
        [
            w_attn, low_two, after_one, branch_one, query_lin, key_lin, query_two_lin, key_two_lin,
            query_rot, key_rot, value_low, query_two, key_two, value_two, mixed_low, mixed_two_low,
            txt_all, input_three, input_one, tok_all, grad_after, tab_all, inv,
        ],
        [vectors, heads, sums, up_sum, *owned],
    )
    swap = lambda v: v.transpose(1, 0, 2)
    narrow, wide, gram = gram_step(
        [*mlp_sums, sums_a, sums_b, swap(attn_in_moment), attn_out_moment, mlp_moment], 3
    )
    (
        new_in, new_out, new_mlp, new_in_m, new_out_m, new_mlp_m, new_head, new_model, new_up,
        new_head_m, new_model_m, new_up_m, out_result, out_tokens, out_words, out_time,
    ) = finish_step(
        [
            narrow, wide, gram, swap(attn_in), attn_out, mlp, head_vectors, head_moment, model_vectors,
            model_moment, up_bias[None], up_moment[None], head_totals, model_sums, out_result,
            out_tokens, out_words, time_sums,
        ]
    )
    return (
        out_result, out_tokens, out_words, out_time, swap(new_in), new_out, new_mlp,
        swap(new_in_m), new_out_m, new_mlp_m, new_head, new_model, new_up.reshape(-1), new_head_m,
        new_model_m, new_up_m.reshape(-1),
    )


def solution(mesh):
    clip = P("fsdp", "ctx", None)
    whole = P("fsdp", None, None)
    matrix = P(("fsdp", "ctx"), None, "tp")
    in_specs = (
        clip, clip, whole, P(None, "fsdp", "ctx"), clip, matrix, matrix, matrix, P(None, "tp"), P(),
        P("tp"), matrix, matrix, matrix, P(None, "tp"), P(), P("tp"),
    )
    out_specs = (
        clip, clip, clip, whole, matrix, matrix, matrix, matrix, matrix, matrix, P(None, "tp"), P(),
        P("tp"), P(None, "tp"), P(), P("tp"),
    )
    return jax.shard_map(body, mesh=mesh, in_specs=in_specs, out_specs=out_specs, check_vma=False)
```

```python
from functools import partial
import math

import jax
import jax.numpy as jnp
from jax import lax
from jax.experimental import pallas as pl
from jax.experimental.pallas import tpu as pltpu
from jax.sharding import PartitionSpec as P

D = 1536
HEAD = 128
ROWS = 24
HEADS = 3
NORM_EPSILON = 1e-06
ORTHO_EPSILON = 1e-07
NEWTON_FIRST = 3.4445
NEWTON_SECOND = -4.775
NEWTON_THIRD = 2.0315
NS_STEPS = 5
MOMENTUM = 0.9
DECAY = 0.01
RATE_IN = 0.5
RATE_OUT = 4.0
RATE_MLP = 1.0
RATE_VECTOR = 0.005
HIGHEST = lax.Precision.HIGHEST

MESH = pl.DeviceIdType.MESH
BF = jnp.bfloat16
F32 = jnp.float32

SIDE = 4
TOK = 128
SEQ = SIDE * TOK
HW = HEADS * HEAD
FF_REAL = 2240
FF = 2304
PAIR = 2 * ROWS
VMEM_LIMIT = 57 * 1024 * 1024


def here():
    f = lax.axis_index("fsdp")
    c = lax.axis_index("ctx")
    t = lax.axis_index("tp")
    x, y = lax.div(f, SIDE), lax.rem(f, SIDE)
    zl, core = lax.div(c, 2), lax.rem(c, 2)
    return x, y, 2 * t + zl, core


def chip(x, y, z, core):
    x, y, z = lax.rem(x + SIDE, SIDE), lax.rem(y + SIDE, SIDE), lax.rem(z + SIDE, SIDE)
    return {"fsdp": x * SIDE + y, "ctx": lax.rem(z, 2) * 2 + core, "tp": lax.div(z, 2)}


def block_of(z):
    z = lax.rem(z + SIDE, SIDE)
    return 2 * lax.rem(z, 2) + lax.div(z, 2)


def greet(devices):
    barrier = pltpu.get_barrier_semaphore()
    for device in devices:
        pl.semaphore_signal(barrier, inc=1, device_id=device, device_id_type=MESH)
    pl.semaphore_wait(barrier, len(devices))


def column(x, y, z, core):
    return [chip(x, y, z + k, core) for k in (1, 2, 3)] + [
        chip(x, y, z + k, 1 - core) for k in range(4)
    ]


def remote(src, dst, send, recv, device):
    return pltpu.make_async_remote_copy(
        src_ref=src, dst_ref=dst, send_sem=send, recv_sem=recv, device_id=device, device_id_type=MESH
    )


def params(cid):
    return pltpu.CompilerParams(
        collective_id=cid, has_side_effects=True, vmem_limit_bytes=VMEM_LIMIT
    )


VM = pl.BlockSpec(memory_space=pltpu.VMEM)
HB = pl.BlockSpec(memory_space=pltpu.HBM)


def flat(a, b):
    return lax.rem(a + SIDE, SIDE) * SIDE + lax.rem(b + SIDE, SIDE)


def steps_of(x, y, z, core):
    return (
        (chip(x + 1, y, z, core), chip(x - 1, y, z, core)),
        (chip(x, y + 1, z, core), chip(x, y - 1, z, core)),
    )


def gather_xy(own, place, xs, xr, ks, kr):
    x, y, z, core = here()
    mine = x * SIDE + y
    steps = steps_of(x, y, z, core)
    sibling = chip(x, y, z, 1 - core)
    sends, sibs = [], []

    def push(part, slot, src, index, device, half=None):
        copy = remote(src, place(part, index, half), xs.at[part, slot], xr.at[part, slot], device)
        copy.start()
        sends.append(copy)
        return copy

    def to_sibling(part, slot, src, index):
        copy = remote(src, place(part, index), ks.at[part, slot], kr.at[part, slot], sibling)
        copy.start()
        sibs.append(copy)

    def index_of(part, first_off, second_off):
        if part == 0:
            return flat(x + first_off, y + second_off)
        return flat(x + second_off, y + first_off)

    one, two = {}, {}
    for part in (0, 1):
        a_next, a_prev = steps[part]
        one[part, "next"] = push(part, 0, own.at[part], mine, a_next)
        one[part, "prev"] = push(part, 1, own.at[part], mine, a_prev)
    for part in (0, 1):
        b_next, b_prev = steps[1 - part]
        two[part, 0, "next"] = push(part, 4, own.at[part], mine, b_next)
        two[part, 0, "prev"] = push(part, 5, own.at[part], mine, b_prev)
        to_sibling(part, 0, own.at[part], mine)

    def second_start(part, k, offset):
        b_next, b_prev = steps[1 - part]
        index = index_of(part, offset, 0)
        src = place(part, index)
        two[part, k, "next"] = push(part, 4 + 4 * k, src, index, b_next)
        two[part, k, "prev"] = push(part, 5 + 4 * k, src, index, b_prev)
        to_sibling(part, 4 * k, src, index)

    offsets = (0, -1, 1, 2)
    for part in (0, 1):
        a_next, a_prev = steps[part]
        yield
        one[part, "next"].wait_recv()
        index = index_of(part, -1, 0)
        one[part, "far0"] = push(part, 2, place(part, index, 0), index, a_next, 0)
        second_start(part, 1, -1)
        one[part, "prev"].wait_recv()
        index = index_of(part, 1, 0)
        one[part, "far1"] = push(part, 3, place(part, index, 1), index, a_prev, 1)
        second_start(part, 2, 1)

    def second_forward(part, k):
        b_next, b_prev = steps[1 - part]
        two[part, k, "next"].wait_recv()
        index = index_of(part, offsets[k], -1)
        two[part, k, "far0"] = push(part, 6 + 4 * k, place(part, index, 0), index, b_next, 0)
        to_sibling(part, 4 * k + 1, place(part, index), index)
        two[part, k, "prev"].wait_recv()
        index = index_of(part, offsets[k], 1)
        two[part, k, "far1"] = push(part, 7 + 4 * k, place(part, index, 1), index, b_prev, 1)
        to_sibling(part, 4 * k + 2, place(part, index), index)

    def second_finish(part, k):
        two[part, k, "far0"].wait_recv()
        two[part, k, "far1"].wait_recv()
        index = index_of(part, offsets[k], 2)
        to_sibling(part, 4 * k + 3, place(part, index), index)

    for part in (0, 1):
        yield
        second_forward(part, 0)
    for part in (0, 1):
        yield
        one[part, "far0"].wait_recv()
        one[part, "far1"].wait_recv()
        second_start(part, 3, 2)
    for k in (1, 2, 3):
        for part in (0, 1):
            yield
            second_forward(part, k)
        for part in (0, 1):
            second_finish(part, k - 1)
    for part in (0, 1):
        yield
        second_finish(part, 3)
    yield
    for copy in sends:
        copy.wait_send()
    for copy in sibs:
        copy.wait_send()
        copy.wait_recv()


GATHER_SEMS = ((2, 20), (2, 20), (2, 16), (2, 16))


def advance(job, count=1):
    for _ in range(count):
        next(job, None)


def finish(job):
    for _ in job:
        pass


def share_rows(send, recv, s, r, l):
    x, y, z, core = here()
    zl = lax.rem(z, 2)
    away = remote(send.at[1 - zl], recv.at[core], s.at[0], r.at[core], chip(x, y, z + 1 - 2 * zl, zl))
    near = remote(send.at[zl], recv.at[core], s.at[1], r.at[core], chip(x, y, z, zl))
    self_copy = pltpu.make_async_copy(send.at[zl], recv.at[core], l.at[0])

    def got(slot):
        remote(send.at[0], recv.at[slot], s.at[0], r.at[slot], chip(x, y, z, core)).wait_recv()

    def start():
        away.start()

        @pl.when(core == zl)
        def _():
            self_copy.start()

        @pl.when(core != zl)
        def _():
            near.start()

    def wait(own):
        @pl.when(core == zl)
        def _():
            self_copy.wait()
            got(1 - core)

        @pl.when(core != zl)
        def _():
            near.wait_send()
            got(0)
            got(1)

        first = recv[0].astype(F32)
        second = recv[1].astype(F32)
        own[0] = jnp.concatenate([first[:ROWS], second[:ROWS]], 0).astype(BF)
        own[1] = jnp.concatenate([first[ROWS:], second[ROWS:]], 0).astype(BF)

    return start, wait, away.wait_send


def share_clip(src, dst, s, r, l):
    x, y, z, core = here()
    put = dst.at[2 * lax.rem(z, 2) + core]
    copies = [
        remote(src.at[1 - core], put, s.at[0], r.at[0], chip(x, y, z, 1 - core)),
        remote(src.at[0], put, s.at[1], r.at[1 + core], chip(x, y, z + 1, 0)),
        remote(src.at[1], put, s.at[2], r.at[1 + core], chip(x, y, z - 1, 1)),
    ]
    local = pltpu.make_async_copy(src.at[core], put, l)

    def start():
        for copy in copies:
            copy.start()
        local.start()

    def wait():
        local.wait()
        for slot in range(3):
            remote(src.at[0], dst.at[0], s.at[0], r.at[slot], chip(x, y, z, core)).wait_recv()

    def drain():
        for copy in copies:
            copy.wait_send()

    return start, wait, drain


def split3(values):
    return [values[:, i * HW : (i + 1) * HW] for i in range(values.shape[1] // HW)]


def swap_halves(values):
    return pltpu.roll(values, HEAD // 2, 1)


def rope_pair(table):
    lane = lax.broadcasted_iota(jnp.int32, table.shape, 1)
    other = swap_halves(table)
    front = lane < HEAD // 2
    return jnp.where(front, table, other), jnp.where(front, -other, table)


def head_slice(h):
    return slice(h * HEAD, (h + 1) * HEAD)


SCALE = HEAD ** (-0.5)


def softmax_rows(query, keys):
    scores = contract_last(query, keys) * SCALE
    peak = jnp.max(scores, -1, keepdims=True)
    raised = jnp.exp(scores - peak)
    return raised * (1.0 / jnp.sum(raised, -1, keepdims=True))


def attend_clip(query, keys, values, out):
    for h in range(HEADS):
        cols = head_slice(h)
        for start in range(0, SEQ, 256):
            rows = slice(start, start + 256)
            weights = softmax_rows(query[rows, cols], keys[:, cols]).astype(BF)
            out[rows, cols] = product(weights, values[:, cols]).astype(BF)


class Stats:
    def __init__(self, buffer, send, recv):
        self.buffer, self.send, self.recv = buffer, send, recv

    def start(self, turn, columns):
        x, y, z, core = here()
        lane = lax.broadcasted_iota(jnp.int32, (SEQ, 128), 1)
        packed = jnp.zeros((SEQ, 128), F32)
        for i, column_values in enumerate(columns):
            packed = jnp.where(lane == i, column_values, packed)
        self.buffer[turn, 0] = packed.T[:8]
        copies = []
        for k in (2, 1, 3):
            copies.append(
                remote(self.buffer.at[turn, 0], self.buffer.at[turn, k], self.send.at[turn, k - 1],
                       self.recv.at[turn, k - 1], chip(x, y, z + k, core))
            )
            copies[-1].start()

        def wait():
            for copy in copies:
                copy.wait()
            total = (self.buffer[turn, 0] + self.buffer[turn, 1]) + (
                self.buffer[turn, 2] + self.buffer[turn, 3]
            )
            spread = jnp.concatenate([total, jnp.zeros((120, SEQ), F32)], 0).T
            return [spread[:, i : i + 1] for i in range(len(columns))]

        return wait


def block_slice(index):
    return pl.ds(pl.multiple_of(index * TOK, TOK), TOK)


HALF = TOK // 2


def half_rows(block, half):
    return pl.ds(pl.multiple_of(block * TOK + half * HALF, HALF), HALF)


class Scatter:
    def __init__(self, part, got, send, recv):
        self.part, self.got, self.send, self.recv = part, got, send, recv
        self.x, self.y, self.z, self.core = here()
        self.copies, self.relayed = [], False

    def push(self, slot, rows, dst, step):
        device = chip(self.x, self.y, self.z + step, self.core)
        copy = remote(self.part.at[rows], dst, self.send.at[slot], self.recv.at[slot], device)
        copy.start()
        self.copies.append(copy)

    def stage(self, k):
        front, rear = pl.ds(0, HALF), pl.ds(HALF, HALF)
        block = block_of(self.z + k)
        if k == 2:
            self.push(0, half_rows(block, 0), self.got.at[2, front], 1)
            self.push(1, half_rows(block, 1), self.got.at[2, rear], -1)
        elif k == 1:
            self.push(2, half_rows(block, 1), self.got.at[0, rear], 1)
        elif k == 3:
            self.push(3, half_rows(block, 0), self.got.at[1, front], -1)

    def held(self):
        for k in (2, 1, 3):
            self.stage(k)
        return self

    def product(self, left, right):
        for k in (2, 1, 3, 0):
            rows = block_slice(block_of(self.z + k))
            self.part[rows] = contract_last(left[rows], right).astype(BF)
            self.stage(k)
        return self

    def relay(self):
        if self.relayed:
            return
        self.relayed = True
        for slot, step in ((0, 1), (1, -1)):
            span = pl.ds(slot * HALF, HALF)
            rows = half_rows(block_of(self.z + step), slot)
            self.copies[slot].wait_recv()
            total = self.part[rows].astype(F32) + self.got[2, span].astype(F32)
            self.part[rows] = total.astype(BF)
            self.push(4 + slot, rows, self.got.at[slot, span], step)

    def total(self):
        self.relay()
        for copy in self.copies[2:]:
            copy.wait_recv()
        own = self.part[block_slice(block_of(self.z))].astype(F32)
        return own + (self.got[0].astype(F32) + self.got[1].astype(F32))

    def drain(self):
        for copy in self.copies:
            copy.wait_send()


class Spread:
    def __init__(self, out, value, send, recv):
        self.out, self.send, self.recv = out, send, recv
        self.x, self.y, self.z, self.core = here()
        self.copies, self.relayed = [], False
        block = block_of(self.z)
        out[block_slice(block)] = value
        self.push(0, half_rows(block, 0), 1)
        self.push(1, half_rows(block, 1), -1)
        self.push(2, half_rows(block, 1), 1)
        self.push(3, half_rows(block, 0), -1)

    def push(self, slot, rows, step):
        device = chip(self.x, self.y, self.z + step, self.core)
        rows = self.out.at[rows]
        copy = remote(rows, rows, self.send.at[slot], self.recv.at[slot], device)
        copy.start()
        self.copies.append(copy)

    def relay(self):
        if self.relayed:
            return
        self.relayed = True
        for slot, step in ((0, 1), (1, -1)):
            self.copies[slot].wait_recv()
            self.push(4 + slot, half_rows(block_of(self.z - step), slot), step)

    def wait(self):
        self.relay()
        for copy in self.copies[2:]:
            copy.wait_recv()

    def drain(self):
        for copy in self.copies:
            copy.wait_send()


def inverse_root(total):
    return lax.rsqrt(total * (1.0 / D) + NORM_EPSILON)


V_SELF, V_CROSS, V_DOWN, V_GAIN, V_BIAS = 6, 7, 8, 9, 10
W_QKV, W_QUERY, W_TEXT, W_SELF, W_CROSS = (
    slice(0, 3 * HW), slice(3 * HW, 4 * HW), slice(4 * HW, 6 * HW), slice(6 * HW, 7 * HW), slice(7 * HW, 8 * HW),
)
ATTN = 8 * HW


SAVED = 22


def forward_kernel(
    send_attn, send_mlp, tok, txt, cot, tab, heads, vec,
    w_attn, w_up, w_down, cot_all, *rest,
):
    saved, held, rest = rest[:SAVED], rest[SAVED : 2 * SAVED], rest[2 * SAVED :]
    (
        tab_all, input_one, input_three, input_mlp, query_lin, key_lin, query_two_lin, key_two_lin, inv,
        query_rot, key_rot, value_low, query_two, key_two, value_two, mixed, mixed_two, branch_one,
        after_one, after_two, tok_all, txt_all,
    ) = held
    (
        wa, got_attn, got_mlp, own_attn, own_mlp, part_one, part_two, blocks, stat,
        xs, xr, ks, kr, ms, mr, js, jr, rs, rr, cs, cr, loc, stat_s, stat_r, zs, zr, gs, gr, keep,
    ) = rest
    x, y, z, core = here()
    mine = x * SIDE + y
    stores = []

    def save(*refs):
        for ref in refs:
            i = [ref is other for other in held].index(True)
            stores.append(pltpu.make_async_copy(ref, saved[i], keep.at[i]))
            stores[-1].start()

    greet(
        [device for pair in steps_of(x, y, z, core) for device in pair] + column(x, y, z, core)
    )
    attn_start, attn_wait, attn_drain = share_rows(send_attn, got_attn, rs.at[0], rr.at[0], loc.at[0])
    mlp_start, mlp_wait, mlp_drain = share_rows(send_mlp, got_mlp, rs.at[1], rr.at[1], loc.at[1])
    acts = [
        share_clip(src, dst, cs.at[i], cr.at[i], loc.at[2 + i, 0])
        for i, (src, dst) in enumerate(
            ((tok, tok_all), (tab, tab_all), (txt, txt_all), (cot, cot_all))
        )
    ]
    attn_start()
    acts[0][0]()
    acts[1][0]()
    attn_wait(own_attn)

    def attn_place(part, index, half=None):
        start, size = part * (ATTN // 2), ATTN // 2
        if half is not None:
            start, size = start + half * (ATTN // 4), ATTN // 4
        rows = pl.ds(pl.multiple_of(index * (2 * PAIR) + core * PAIR, PAIR), PAIR)
        return wa.at[rows, pl.ds(start, size)]

    def mlp_place(part, index, half=None):
        start, size = (0, FF) if half is None else (half * (FF // 2), FF // 2)
        rows = pl.ds(pl.multiple_of(index * (2 * PAIR) + core * PAIR, PAIR), PAIR)
        return (w_up, w_down)[part].at[rows, pl.ds(start, size)]

    gather_attn = gather_xy(own_attn, attn_place, xs, xr, ks, kr)
    advance(gather_attn)
    for part in (0, 1):
        attn_place(part, mine)[...] = own_attn[part]
    acts[2][0]()
    mlp_start()

    def norm_block(i, carry):
        normed, _ = plain_norm(tok_all[i].astype(F32))
        input_one[block_slice(i)] = (normed * (1.0 + vec[1:2]) + vec[0:1]).astype(BF)
        return carry

    advance(gather_attn, 4)
    acts[3][0]()
    advance(gather_attn, 2)
    acts[0][1]()
    lax.fori_loop(0, 2, norm_block, 0)
    advance(gather_attn, 2)
    lax.fori_loop(2, 4, norm_block, 0)
    save(input_one, tok_all)
    advance(gather_attn, 2)
    mlp_wait(own_mlp)
    locals_ = []
    for part in (0, 1):
        locals_.append(pltpu.make_async_copy(own_mlp.at[part], mlp_place(part, mine), loc.at[6, part]))
        locals_[-1].start()
    advance(gather_attn, 2)
    gather_mlp = gather_xy(own_mlp, mlp_place, ms, mr, js, jr)
    advance(gather_mlp)
    finish(gather_attn)
    locals_.append(pltpu.make_async_copy(wa, w_attn, loc.at[7, 0]))
    locals_[-1].start()
    acts[1][1]()
    acts[2][1]()
    save(tab_all, txt_all)

    stats = Stats(stat, stat_s, stat_r)
    query_lin[...] = product(input_one[...], wa[:, 0:HW]) + heads[0:1]
    key_lin[...] = product(input_one[...], wa[:, HW : 2 * HW]) + heads[1:2]
    words = txt_all[...].reshape(SEQ, D)
    key_two_lin[...] = product(words, wa[:, 4 * HW : 5 * HW]) + heads[6:7]
    norm_wait = stats.start(
        0,
        [
            jnp.sum(ref[...] * ref[...], -1, keepdims=True)
            for ref in (query_lin, key_lin, key_two_lin)
        ],
    )
    value_low[...] = (product(input_one[...], wa[:, 2 * HW : 3 * HW]) + heads[2:3]).astype(BF)
    value_two[...] = (product(words, wa[:, 5 * HW : 6 * HW]) + heads[7:8]).astype(BF)
    save(query_lin, key_lin, key_two_lin, value_low, value_two)
    lane = lax.broadcasted_iota(jnp.int32, (SEQ, 128), 1)
    inverse_query, inverse_key, inverse_key_two = [inverse_root(v) for v in norm_wait()]
    inv[...] = jnp.where(
        lane == 0, inverse_query, jnp.where(lane == 1, inverse_key, jnp.where(lane == 2, inverse_key_two, 0.0))
    )
    cosine, sine = rope_pair(tab_all[...].reshape(SEQ, HEAD))
    for h in range(HEADS):
        cols = head_slice(h)
        for lin, inverse, gain, out in (
            (query_lin, inverse_query, 3, query_rot),
            (key_lin, inverse_key, 4, key_rot),
        ):
            value = lin[:, cols] * inverse * (1.0 + heads[gain : gain + 1, cols])
            out[:, cols] = (value * cosine + swap_halves(value) * sine).astype(BF)
    advance(gather_mlp, 2)
    attend_clip(query_rot, key_rot, value_low, mixed)
    scatter = Scatter(part_one, blocks.at[0], zs.at[0], zr.at[0]).product(mixed, wa[:, W_SELF])
    drains = [scatter]
    key_two[...] = (key_two_lin[...] * inverse_key_two * (1.0 + heads[9:10])).astype(BF)
    save(query_rot, key_rot, key_two, mixed)
    advance(gather_mlp, 2)
    scatter.relay()
    advance(gather_mlp, 5)
    branch = scatter.total() + vec[V_SELF : V_SELF + 1]
    branch_one[...] = branch
    after = tok_all[block_of(z)].astype(F32) + vec[2:3] * branch
    after_one[...] = after
    normed, _ = plain_norm(after)
    spread = Spread(
        input_three,
        (normed * (1.0 + vec[V_GAIN : V_GAIN + 1]) + vec[V_BIAS : V_BIAS + 1]).astype(BF),
        gs.at[0],
        gr.at[0],
    )
    drains.append(spread)
    save(branch_one, after_one)
    advance(gather_mlp, 2)
    spread.relay()
    finish(gather_mlp)
    spread.wait()
    query_two_lin[...] = product(input_three[...], wa[:, W_QUERY]) + heads[5:6]
    norm_wait = stats.start(1, [jnp.sum(query_two_lin[...] * query_two_lin[...], -1, keepdims=True)])
    save(input_three, query_two_lin)
    inverse_query_two = inverse_root(norm_wait()[0])
    inv[...] = jnp.where(lane == 3, inverse_query_two, inv[...])
    query_two[...] = (query_two_lin[...] * inverse_query_two * (1.0 + heads[8:9])).astype(BF)
    attend_clip(query_two, key_two, value_two, mixed_two)
    scatter = Scatter(part_two, blocks.at[1], zs.at[1], zr.at[1]).product(mixed_two, wa[:, W_CROSS])
    drains.append(scatter)
    save(inv, query_two, mixed_two)
    after = after_one[...] + scatter.total() + vec[V_CROSS : V_CROSS + 1]
    after_two[...] = after
    normed, _ = plain_norm(after)
    spread = Spread(
        input_mlp, (normed * (1.0 + vec[4:5]) + vec[3:4]).astype(BF), gs.at[1], gr.at[1]
    )
    drains.append(spread)
    save(after_two)
    spread.relay()
    for copy in locals_:
        copy.wait()
    acts[3][1]()
    for act in acts:
        act[2]()
    attn_drain()
    mlp_drain()
    spread.wait()
    save(input_mlp)
    for transfer in drains:
        transfer.drain()
    for copy in stores:
        copy.wait()


def forward(send_attn, send_mlp, tok, txt, cot, tab, heads, vec):
    dma = pltpu.SemaphoreType.DMA
    sds = jax.ShapeDtypeStruct
    wide, lin, low = sds((SEQ, D), BF), sds((SEQ, HW), F32), sds((SEQ, HW), BF)
    block = sds((TOK, D), F32)
    outs = [
        sds((SIDE, TOK, HEAD), F32), wide, wide, wide, lin, lin, lin, lin, sds((SEQ, 128), F32),
        low, low, low, low, low, low, low, low, block, block, block,
        sds((SIDE, TOK, D), BF), sds((SIDE, TOK, D), BF),
    ]
    weights = [sds((D, ATTN), BF), sds((D, FF), BF), sds((D, FF), BF), sds((SIDE, TOK, D), BF)]
    return pl.pallas_call(
        forward_kernel,
        out_shape=weights + outs,
        in_specs=[VM, VM, HB, HB, HB, VM, VM, VM],
        out_specs=[HB] * (len(weights) + len(outs)),
        scratch_shapes=[
            *[pltpu.VMEM(shape.shape, shape.dtype) for shape in outs],
            pltpu.VMEM((D, ATTN), BF),
            pltpu.VMEM((2, PAIR, ATTN // 2), BF),
            pltpu.VMEM((2, PAIR, FF), BF),
            pltpu.VMEM((2, PAIR, ATTN // 2), BF),
            pltpu.VMEM((2, PAIR, FF), BF),
            pltpu.VMEM((SEQ, D), BF),
            pltpu.VMEM((SEQ, D), BF),
            pltpu.VMEM((2, 3, TOK, D), BF),
            pltpu.VMEM((2, 4, 8, SEQ), F32),
            *[dma(s) for s in GATHER_SEMS],
            *[dma(s) for s in GATHER_SEMS],
            dma((2, 2)), dma((2, 2)), dma((4, 3)), dma((4, 3)), dma((8, 2)),
            dma((2, 3)), dma((2, 3)), dma((2, 6)), dma((2, 6)), dma((2, 6)), dma((2, 6)),
            dma((SAVED,)),
        ],
        compiler_params=params(0),
        name="forward",
    )(send_attn, send_mlp, tok, txt, cot, tab, heads, vec)


BATCH = 768


def peers_xy(x, y, z, core):
    rows = [chip(x + k, y, z, core) for k in (1, 2, 3)]
    lines = [chip(x, y + k, z, core) for k in (1, 2, 3)]
    return rows, lines


def reduce_batch(grads, out, sib, r1, r2, tosend, ss, sr, s1, q1, s2, q2, *swap_sems, gates=None):
    x, y, z, core = here()
    zl = lax.rem(z, 2)
    rows, lines = peers_xy(x, y, z, core)
    sibling = chip(x, y, z, 1 - core)
    wrap = lambda v: lax.rem(v, SIDE)
    swaps, one, two = [], {0: [], 1: []}, {0: [], 1: []}
    opens, waits = gates if gates is not None else (None, None)

    def signal(gate, devices):
        for device in devices:
            pl.semaphore_signal(gate, inc=1, device_id=device, device_id_type=MESH)

    if waits is not None:
        pl.semaphore_wait(waits[0], 1)
    for part in (0, 1):
        swaps.append(
            remote(grads.at[part, :, :, 1 - core], sib.at[part], ss.at[part], sr.at[part], sibling)
        )
        swaps[part].start()
    yield
    for part in (0, 1):
        swaps[part].wait_recv()

        def add_pair(k, carry):
            a, b = lax.div(k, SIDE), lax.rem(k, SIDE)
            grads[part, a, b, core] = grads[part, a, b, core] + sib[part, a, b]
            return carry

        lax.fori_loop(0, SIDE * SIDE, add_pair, 0)
        if part == 0 and waits is not None:
            pl.semaphore_wait(waits[1], 6)
        for k in (2, 1, 3):
            src = grads.at[0, :, wrap(y + k), core] if part == 0 else grads.at[1, wrap(x + k), :, core]
            device = (lines, rows)[part][k - 1]
            copy = remote(src, r1.at[part, k - 1], s1.at[part, k - 1], q1.at[part, k - 1], device)
            copy.start()
            one[part].append(copy)
    if opens is not None:
        signal(opens[0], [sibling])
    yield
    for part in (0, 1):
        for copy in one[part]:
            copy.wait_recv()

        def add_line(k, carry):
            a, b = (k, y) if part == 0 else (x, k)
            total = grads[part, a, b, core].astype(F32)
            for i in range(3):
                total = total + r1[part, i, k].astype(F32)
            grads[part, a, b, core] = total.astype(BF)
            return carry

        lax.fori_loop(0, SIDE, add_line, 0)
        for k in (2, 1, 3):
            src = grads.at[0, wrap(x + k), y, core] if part == 0 else grads.at[1, x, wrap(y + k), core]
            device = (rows, lines)[part][k - 1]
            copy = remote(src, r2.at[part, k - 1], s2.at[part, k - 1], q2.at[part, k - 1], device)
            copy.start()
            two[part].append(copy)
    yield
    final = []
    for part in (0, 1):
        for copy in two[part]:
            copy.wait_recv()
        total = grads[part, x, y, core].astype(F32)
        for i in range(3):
            total = total + r2[part, i].astype(F32)
        final.append(total)
    if opens is not None:
        signal(opens[1], [*rows, *lines])
    for target in (0, 1):
        span = slice(target * ROWS, target * ROWS + ROWS)
        tosend[target] = jnp.concatenate([final[0][span], final[1][span]], 0).astype(tosend.dtype)
    if out is not None:
        exchange = swap_rows(tosend, out, *swap_sems)
        next(exchange)
        yield
        finish(exchange)
    for copy in swaps + one[0] + one[1] + two[0] + two[1]:
        copy.wait_send()


def swap_rows(owned, out, s3, q3, l3):
    x, y, z, core = here()
    zl = lax.rem(z, 2)
    other = z + 1 - 2 * zl
    far = [
        remote(owned.at[t], out.at[zl], s3.at[t], q3.at[zl], chip(x, y, other, t)) for t in (0, 1)
    ]
    self_copy = pltpu.make_async_copy(owned.at[core], out.at[zl], l3.at[0])
    near = remote(owned.at[1 - core], out.at[zl], s3.at[0], q3.at[zl], chip(x, y, z, 1 - core))

    def got(slot):
        remote(owned.at[0], out.at[slot], s3.at[0], q3.at[slot], chip(x, y, z, core)).wait_recv()

    @pl.when(core == zl)
    def _():
        self_copy.start()
        near.start()

    @pl.when(core != zl)
    def _():
        for copy in far:
            copy.start()

    yield

    @pl.when(core == zl)
    def _():
        self_copy.wait()
        near.wait_send()
        got(1 - zl)

    @pl.when(core != zl)
    def _():
        for copy in far:
            copy.wait_send()
        got(zl)
        got(1 - zl)


def reduce_buffers():
    return [
        pltpu.VMEM((2, SIDE, SIDE, PAIR, BATCH), BF),
        pltpu.VMEM((2, 3, SIDE, PAIR, BATCH), BF),
        pltpu.VMEM((2, 3, PAIR, BATCH), BF),
    ]


def reduce_sems():
    dma = pltpu.SemaphoreType.DMA
    return [dma((2,)), dma((2,)), dma((2, 3)), dma((2, 3)), dma((2, 3)), dma((2, 3))]


def swap_sems():
    dma = pltpu.SemaphoreType.DMA
    return [dma((2,)), dma((2,)), dma((1,))]


def reduce_scratch():
    return [*reduce_buffers(), pltpu.VMEM((2, PAIR, BATCH), F32), *reduce_sems(), *swap_sems()]


GRADS = (2, SIDE, SIDE, 2, PAIR, BATCH)
SLAB = D // SIDE


def weight_grad(left, right, grads, part, start):
    width = right.shape[1]

    def slab(i, carry):
        turned = left[:, pl.ds(pl.multiple_of(i * SLAB, SLAB), SLAB)].T
        value = product(turned, right).astype(BF).reshape(SIDE, 2, PAIR, width)
        grads[part, i, :, :, :, start : start + width] = value
        return carry

    lax.fori_loop(0, SIDE, slab, 0)


def column_sum(values):
    return jnp.sum(values.astype(F32), 0, keepdims=True)


def deliver(src, dst, s, r, l):
    x, y, z, core = here()
    zh = lax.div(z, 2)
    far = remote(src, dst.at[core], s.at[0], r.at[core], chip(x, y, z + 2, zh))
    near = remote(src, dst.at[core], s.at[1], r.at[core], chip(x, y, z, zh))
    self_copy = pltpu.make_async_copy(src, dst.at[core], l)

    def got(slot):
        remote(src, dst.at[slot], s.at[0], r.at[slot], chip(x, y, z, core)).wait_recv()

    def start():
        far.start()

        @pl.when(core == zh)
        def _():
            self_copy.start()

        @pl.when(core != zh)
        def _():
            near.start()

    def wait():
        @pl.when(core == zh)
        def _():
            self_copy.wait()
            got(1 - core)

        @pl.when(core != zh)
        def _():
            near.wait_send()
            got(0)
            got(1)

        far.wait_send()

    return start, wait


CUBE = 0.044715
ROOT = math.sqrt(2.0 / math.pi)


def gelu_pair(u):
    square = u * u
    t = jnp.tanh(ROOT * u * (1.0 + CUBE * square))
    half = 0.5 * (1.0 + t)
    return u * half, half + 0.5 * u * (1.0 - t * t) * (ROOT * (1.0 + 3.0 * CUBE * square))


def mlp_kernel(
    a_in, cot_all, w_up, w_down, after_in, vec, bias,
    low_out, grad_after, sums, bias_sum, out_result, owned_a, owned_b, owned_c,
    a, low, ahead, behind, hidden, act, back, acc, part, after_two, low_two, result,
    blocks, zs, zr, gs, gr, ds, dr, loc, ring, gate_core, gate_chips, *rest,
):
    x, y, z, core = here()
    rows, lines = peers_xy(x, y, z, core)
    own_rows = block_slice(block_of(z))

    def load(src, dst, sem):
        copy = pltpu.make_async_copy(src, dst, sem)
        copy.start()
        return copy

    def third(n):
        return pl.ds(n % 3 * BATCH, BATCH)

    def weights(n):
        return ahead.at[n % 2].reshape(D, BATCH)

    def load_ahead(n):
        return load((w_up, w_down)[n // 3].at[:, third(n)], weights(n), ring.at[0, n % 2])

    def load_behind(n):
        return load((w_down, w_up)[n // 3].at[:, third(n)], behind.at[n % 2], ring.at[1, n % 2])

    aheads, behinds = {0: load_ahead(0)}, {}
    fetch_a = load(a_in, a, loc.at[0])
    behinds[0] = load_behind(0)
    fetch_low = load(cot_all.reshape(SEQ, D), low, loc.at[1])
    aheads[1], behinds[1] = load_ahead(1), load_behind(1)
    fetch_after = load(after_in, after_two, loc.at[2])
    greet(column(x, y, z, core) + rows + lines)
    sums[...] = jnp.zeros_like(sums)
    fetch_a.wait()
    aheads[0].wait()
    hidden[0] = product(a[...], weights(0)[...])
    aheads[2] = load_ahead(2)
    fetch_low.wait()
    dy = low[own_rows].astype(F32)
    for start in range(0, SEQ, TOK):
        block = slice(start, start + TOK)
        low[block] = (low[block].astype(F32) * vec[5:6]).astype(BF)
    sums[2:3] = column_sum(low[own_rows])
    fetch_after.wait()

    grads = [rest[0], rest[1], ahead]
    gates = (gate_core, gate_chips)
    first, second, sems = rest[2:5], rest[5:8], rest[8:]
    owned = (owned_a, owned_b, owned_c)
    jobs = [
        reduce_batch(
            grads[b], None, *(first, second, first)[b], owned[b], *sems[6 * b : 6 * b + 6],
            gates=((gates, None), None, (None, gates))[b],
        )
        for b in range(3)
    ]

    def step(n):
        if n < 5:
            aheads[n + 1].wait()
            left = a if n < 2 else low
            behinds[n].wait()
            hidden[(n + 1) % 2] = product(left[...], weights(n + 1)[...])
        else:
            behinds[n].wait()
        cols = slice(n % 3 * BATCH, (n % 3 + 1) * BATCH)
        if n < 3:
            value, slope = gelu_pair(hidden[n % 2] + bias[0:1, cols])
            value = value.astype(BF)
            act[:, cols] = value
            back[:, cols] = slope.astype(BF)
        else:
            value = (hidden[n % 2] * back[:, cols].astype(F32)).astype(BF)
            back[:, cols] = value
            bias_sum[0:1, cols] = column_sum(value)
        moved = contract_last(value, behind[n % 2])
        if n % 3 == 0:
            acc[...] = moved
        elif n % 3 == 1:
            acc[...] += moved
        else:
            part[...] = (acc[...] + moved).astype(BF)
        if n < 3:
            aheads[n + 3] = load_ahead(n + 3)
        if n < 4:
            behinds[n + 2] = load_behind(n + 2)

    def third_grads(n, b, half):
        cols = slice(n % 3 * BATCH, (n % 3 + 1) * BATCH)
        left, right = ((low, act), (a, back))[n // 3]
        weight_grad(left, right[:, cols], grads[b], half, 0)

    step(0)
    third_grads(0, 0, 0)
    step(1)
    third_grads(1, 0, 1)
    advance(jobs[0])
    step(2)
    down_sum = Scatter(part, blocks.at[0], zs.at[0], zr.at[0]).held()
    advance(jobs[0])
    third_grads(2, 1, 0)
    step(3)
    down_sum.relay()
    third_grads(3, 1, 1)
    advance(jobs[1])
    step(4)
    advance(jobs[1])
    advance(jobs[0])
    branch = down_sum.total() + vec[V_DOWN : V_DOWN + 1]
    down_sum.drain()
    result[...] = (after_two[...] + vec[5:6] * branch).astype(BF)
    sums[10:11] = column_sum(dy * branch)
    send_result, wait_result = deliver(result, out_result, ds, dr, loc.at[4])
    step(5)
    back_sum = Scatter(part, blocks.at[1], zs.at[1], zr.at[1]).held()
    third_grads(4, 2, 0)
    third_grads(5, 2, 1)
    back_sum.relay()
    advance(jobs[2])
    finish(jobs[0])
    advance(jobs[1])
    advance(jobs[2])
    total = back_sum.total()
    normed, inverse = plain_norm(after_two[...])
    sums[8:9] = column_sum(total)
    sums[9:10] = column_sum(total * normed)
    value = dy + norm_back(total * (1.0 + vec[4:5]), normed, inverse)
    grad_after[...] = value
    value = value.astype(BF)
    sums[1:2] = column_sum(value)
    spread = Spread(low_two, value, gs, gr)
    finish(jobs[1])
    spread.relay()
    send_result()
    advance(jobs[2])
    spread.wait()
    store = pltpu.make_async_copy(low_two, low_out, loc.at[3])
    store.start()
    finish(jobs[2])
    store.wait()
    wait_result()
    back_sum.drain()
    spread.drain()


def mlp_pass(a, cot, up, down, after, vec, bias):
    dma = pltpu.SemaphoreType.DMA
    sds = jax.ShapeDtypeStruct
    wide = pltpu.VMEM((SEQ, D), BF)
    tiles = pltpu.VMEM((2, D, BATCH), BF)
    units = pltpu.VMEM((SEQ, FF), BF)
    owned = sds((2, PAIR, BATCH), BF)
    outs = [
        (sds((SEQ, D), BF), HB), (sds((TOK, D), F32), VM), (sds((16, D), F32), VM),
        (sds((8, FF), F32), VM), (sds((2, TOK, D), BF), HB), (owned, VM), (owned, VM), (owned, VM),
    ]
    return pl.pallas_call(
        mlp_kernel,
        out_shape=[shape for shape, _ in outs],
        in_specs=[HB] * 5 + [VM] * 2,
        out_specs=[spec for _, spec in outs],
        scratch_shapes=[
            wide, wide, pltpu.VMEM(GRADS, BF), tiles, pltpu.VMEM((2, SEQ, BATCH), F32), units, units,
            pltpu.VMEM((SEQ, D), F32), wide, pltpu.VMEM((TOK, D), F32), wide, pltpu.VMEM((TOK, D), BF),
            pltpu.VMEM((2, 3, TOK, D), BF), dma((2, 6)), dma((2, 6)), dma((6,)), dma((6,)), dma((2,)),
            dma((2,)), dma((5,)), dma((2, 2)), pltpu.SemaphoreType.REGULAR, pltpu.SemaphoreType.REGULAR,
            pltpu.VMEM(GRADS, BF), pltpu.VMEM(GRADS, BF),
            *reduce_buffers(), *reduce_buffers(), *reduce_sems(), *reduce_sems(), *reduce_sems(),
        ],
        compiler_params=params(1),
        name="mlp",
    )(a, cot, up, down, after, vec, bias)


def sum_over_xy(held, sends, recvs):
    x, y, z, core = here()
    for stage, peers in enumerate(peers_xy(x, y, z, core)):
        base = 4 * stage
        copies = [
            remote(held.at[base], held.at[base + k], sends.at[stage, k], recvs.at[stage, k], peers[k - 1])
            for k in (2, 1, 3)
        ]
        for copy in copies:
            copy.start()
        yield
        for copy in copies:
            copy.wait()
        held[base + 4] = (held[base] + held[base + 1]) + (held[base + 2] + held[base + 3])


def model_job(model, time_out, col, held, sends, recvs):
    x, y, z, core = here()
    copies = [
        remote(model, col.at[k], sends.at[2, k], recvs.at[2, k], chip(x, y, z + k, core)) for k in (2, 1, 3)
    ]
    for copy in copies:
        copy.start()
    yield
    for copy in copies:
        copy.wait()
    time_out[core] = (model[...] + col[1]) + (col[2] + col[3])
    swap = remote(
        time_out.at[core], time_out.at[core], sends.at[2, 0], recvs.at[2, 0], chip(x, y, z, 1 - core)
    )
    swap.start()
    yield
    swap.wait()
    held[0] = time_out[0] + time_out[1]
    yield from sum_over_xy(held, sends, recvs)


def head_job(heads, head_out, other, held, sends, recvs):
    x, y, z, core = here()
    zl = lax.rem(z, 2)
    swap = remote(heads, other, sends.at[2, 0], recvs.at[2, 0], chip(x, y, z, 1 - core))
    swap.start()
    yield
    swap.wait()
    held[0] = heads[...] + other[...]
    yield from sum_over_xy(held, sends, recvs)
    head_out[zl] = held[8]
    last = remote(
        held.at[8], head_out.at[zl], sends.at[2, 1], recvs.at[2, 1], chip(x, y, z + 1 - 2 * zl, core)
    )
    last.start()
    yield
    last.wait()


def model_scratch(rows, width):
    dma = pltpu.SemaphoreType.DMA
    return [pltpu.VMEM((4, rows, width), F32), pltpu.VMEM((9, rows, width), F32), dma((3, 4)), dma((3, 4))]


def head_scratch():
    dma = pltpu.SemaphoreType.DMA
    return [pltpu.VMEM((16, HW), F32), pltpu.VMEM((9, 16, HW), F32), dma((3, 4)), dma((3, 4))]


def attend_clip_back(query, keys, values, grad, grad_query, grad_keys, grad_values):
    for h in range(HEADS):
        cols = head_slice(h)
        k, v = keys[:, cols], values[:, cols]
        for start in range(0, SEQ, 256):
            rows = slice(start, start + 256)
            q, do = query[rows, cols], grad[rows, cols]
            weights = softmax_rows(q, k)
            grad_weights = contract_last(do, v)
            delta = jnp.sum(weights * grad_weights, -1, keepdims=True)
            grad_scores = (weights * (grad_weights - delta)).astype(BF)
            grad_query[rows, cols] = product(grad_scores, k) * SCALE
            to_keys = contract_rows(grad_scores, q) * SCALE
            to_values = contract_rows(weights.astype(BF), do)
            if start:
                grad_keys[:, cols] += to_keys
                grad_values[:, cols] += to_values
            else:
                grad_keys[:, cols] = to_keys
                grad_values[:, cols] = to_values


def root_back(linear, inverse, scaled, dot):
    return (inverse * scaled - linear * (inverse * inverse * inverse * dot * (1.0 / D))).astype(BF)


def backward_kernel(
    wa_in, low_in, after_in, branch_in, query_lin_in, key_lin_in, query_two_lin_in, key_two_lin_in,
    query_rot_in, key_rot_in, value_low_in, query_two_in, key_two_in, value_two_in, mixed_in,
    mixed_two_in, words_in, three_in, one_in, tok_in, grad_in, tab_in, inv_in,
    vec, heads, sums, bias_sum, owned_a, owned_b, owned_c,
    out_tokens, low_words, time_out, model_out, head_out, sums_a, sums_b, mlp_a, mlp_b, mlp_c,
    wa, low_wide, after_one, branch_one, lin_a, lin_b, qa, ka, va, mixed, mixed_two, operand, tok_own,
    grad_after, tab, inv, grad_query, grad_kv, grad_qkv, part_cross, part_words, blocks,
    held, gq, gk, gv, model, head_sums, low_tokens,
    stat, stat_s, stat_r, zs, zr, gs, gr, ds, dr, loc, *rest,
):
    x, y, z, core = here()
    rows, lines = peers_xy(x, y, z, core)
    slots = iter(range(32))
    own_block = block_of(z)

    def fetch(src, dst):
        copy = pltpu.make_async_copy(src, dst, loc.at[next(slots)])
        copy.start()
        return copy

    out_cols, in_cols = pl.ds(6 * HW, 2 * HW), pl.ds(0, 6 * HW)
    first = [fetch(low_in, low_wide), fetch(wa_in.at[:, out_cols], wa.at[:, out_cols])]
    inputs = [
        fetch(query_two_in, qa), fetch(key_two_in, ka), fetch(value_two_in, va),
        fetch(query_two_lin_in, lin_a), fetch(key_two_lin_in, lin_b), fetch(inv_in, inv),
    ]
    second = [
        fetch(mixed_two_in, mixed_two), fetch(wa_in.at[:, in_cols], wa.at[:, in_cols]),
        fetch(words_in.reshape(SEQ, D), operand),
    ]
    third = [
        fetch(after_in, after_one), fetch(branch_in, branch_one), fetch(grad_in, grad_after),
        fetch(mixed_in, mixed), fetch(tab_in, tab), fetch(tok_in.at[own_block], tok_own),
    ]
    greet(column(x, y, z, core) + rows + lines)
    model[...] = sums[...]
    head_sums[...] = jnp.zeros_like(head_sums)
    for i in range(6):
        head_sums[10 + i : 11 + i] = bias_sum[0:1, i * HW : (i + 1) * HW]
    refs_a, refs_b, early_refs, late_refs, head_refs, rest = (
        rest[:14], rest[14:28], rest[28:32], rest[32:36], rest[36:40], rest[40:],
    )
    (late, time_late), swap_refs = rest[:2], rest[2:]
    hidden_rows = [
        swap_rows(src, dst, *swap_refs[3 * i : 3 * i + 3])
        for i, (src, dst) in enumerate(((owned_a, mlp_a), (owned_b, mlp_b), (owned_c, mlp_c)))
    ]
    for job in hidden_rows:
        advance(job)
    grads_a, grads_b = refs_a[0], refs_b[0]
    job_a = reduce_batch(grads_a, sums_a, *refs_a[1:])
    job_b = reduce_batch(grads_b, sums_b, *refs_b[1:])
    stats = Stats(stat, stat_s, stat_r)
    drains = []

    for copy in first:
        copy.wait()
    held[...] = product(low_wide[...], wa[:, W_CROSS]).astype(BF)
    for copy in inputs:
        copy.wait()
    attend_clip_back(qa, ka, va, held, gq, gk, gv)
    inverse_query, inverse_key, inverse_key_two, inverse_query_two = [inv[:, i : i + 1] for i in range(4)]
    dots = stats.start(
        0,
        [
            jnp.sum(lin_a[...] * (gq[...] * (1.0 + heads[8:9])), -1, keepdims=True),
            jnp.sum(lin_b[...] * (gk[...] * (1.0 + heads[9:10])), -1, keepdims=True),
        ],
    )
    head_sums[8:9] = column_sum(gq[...] * lin_a[...] * inverse_query_two)
    head_sums[9:10] = column_sum(gk[...] * lin_b[...] * inverse_key_two)
    low = gv[...].astype(BF)
    grad_kv[:, HW:] = low
    head_sums[7:8] = column_sum(low)
    for copy in second:
        copy.wait()
    weight_grad(low_wide, mixed_two[...], grads_a, 1, HW)
    dot_query, dot_key = dots()
    low = root_back(lin_a[...], inverse_query_two, gq[...] * (1.0 + heads[8:9]), dot_query)
    grad_query[...] = low
    head_sums[5:6] = column_sum(low)
    cross = Scatter(part_cross, blocks.at[0], zs.at[0], zr.at[0]).product(grad_query, wa[:, W_QUERY])
    low = root_back(lin_b[...], inverse_key_two, gk[...] * (1.0 + heads[9:10]), dot_key)
    grad_kv[:, :HW] = low
    head_sums[6:7] = column_sum(low)
    selfs = [
        fetch(query_rot_in, qa), fetch(key_rot_in, ka), fetch(value_low_in, va),
        fetch(query_lin_in, lin_a), fetch(key_lin_in, lin_b),
    ]
    weight_grad(operand, grad_kv[...], grads_a, 0, 0)
    next_operand = fetch(three_in, operand)
    next_operand.wait()
    cross.relay()
    weight_grad(operand, grad_query[...], grads_a, 1, 0)
    next_operand = fetch(one_in, operand)
    advance(job_a)
    part_words[...] = contract_last(grad_kv[...], wa[:, W_TEXT]).astype(BF)
    for copy in third:
        copy.wait()

    total = cross.total()
    normed, inverse = plain_norm(after_one[...])
    model[4:5] = column_sum(total)
    model[3:4] = column_sum(total * normed)
    value = grad_after[...] + norm_back(total * (1.0 + vec[V_GAIN : V_GAIN + 1]), normed, inverse)
    grad_after[...] = value
    model[7:8] = column_sum(value * branch_one[...])
    low = (value * vec[2:3]).astype(BF)
    model[0:1] = column_sum(low)
    spread = Spread(low_wide, low, gs, gr)
    drains.append(spread)
    advance(job_a)
    spread.relay()
    early = model_job(model, time_out, *early_refs)
    advance(early)
    spread.wait()
    word_sum = Scatter(part_words, blocks.at[1], zs.at[1], zr.at[1]).held()
    drains.append(word_sum)

    held[...] = product(low_wide[...], wa[:, W_SELF]).astype(BF)
    for copy in selfs:
        copy.wait()
    attend_clip_back(qa, ka, va, held, gq, gk, gv)
    cosine, sine = rope_pair(tab[...].reshape(SEQ, HEAD))
    for ref in (gq, gk):
        for h in range(HEADS):
            cols = head_slice(h)
            value = ref[:, cols]
            ref[:, cols] = value * cosine - swap_halves(value) * sine
    dots = stats.start(
        1,
        [
            jnp.sum(lin_a[...] * (gq[...] * (1.0 + heads[3:4])), -1, keepdims=True),
            jnp.sum(lin_b[...] * (gk[...] * (1.0 + heads[4:5])), -1, keepdims=True),
        ],
    )
    head_sums[3:4] = column_sum(gq[...] * lin_a[...] * inverse_query)
    head_sums[4:5] = column_sum(gk[...] * lin_b[...] * inverse_key)
    low = gv[...].astype(BF)
    grad_qkv[:, 2 * HW :] = low
    head_sums[2:3] = column_sum(low)
    next_operand.wait()
    weight_grad(low_wide, mixed[...], grads_b, 1, HW)
    cross.drain()
    advance(early)
    dot_query, dot_key = dots()
    word_sum.relay()
    for i, (lin, inverse, ref, dot) in enumerate(
        ((lin_a, inverse_query, gq, dot_query), (lin_b, inverse_key, gk, dot_key))
    ):
        low = root_back(lin[...], inverse, ref[...] * (1.0 + heads[3 + i : 4 + i]), dot)
        grad_qkv[:, i * HW : (i + 1) * HW] = low
        head_sums[i : i + 1] = column_sum(low)
    token_sum = Scatter(part_cross, blocks.at[0], zs.at[2], zr.at[2]).product(grad_qkv, wa[:, W_QKV])
    drains.append(token_sum)
    head_total = head_job(head_sums, head_out, *head_refs)
    advance(head_total)
    advance(job_a)
    advance(early)
    weight_grad(operand, grad_qkv[:, : 2 * HW], grads_b, 0, 0)
    weight_grad(operand, grad_qkv[:, 2 * HW :], grads_b, 1, 0)
    advance(job_b)
    token_sum.relay()
    advance(head_total)
    advance(job_a)
    advance(early)
    advance(job_b)
    advance(head_total)
    for job in hidden_rows:
        finish(job)

    total = token_sum.total()
    normed, inverse = plain_norm(tok_own[...].astype(F32))
    for i, row in enumerate((column_sum(total), column_sum(total * normed))):
        for k in range(SIDE):
            late[SIDE * i + k : SIDE * i + k + 1] = row[:, k * HW : (k + 1) * HW]
    late_total = model_job(late, time_late, *late_refs)
    advance(late_total)
    value = grad_after[...] + norm_back(total * (1.0 + vec[1:2]), normed, inverse)
    low_tokens[...] = value.astype(BF)
    send_tokens, wait_tokens = deliver(low_tokens, out_tokens, ds.at[1], dr.at[1], loc.at[31])
    advance(late_total)
    send_tokens()
    low_words[...] = word_sum.total().astype(BF)
    advance(late_total)
    finish(early)
    advance(job_b)
    advance(late_total)
    finish(job_a)
    advance(head_total)
    advance(job_b)
    finish(late_total)
    finish(head_total)
    wait_tokens()
    finish(job_b)
    model_out[...] = early_refs[1][8]
    for i in range(2):
        for k in range(SIDE):
            cols = slice(k * HW, (k + 1) * HW)
            row = slice(SIDE * i + k, SIDE * i + k + 1)
            model_out[5 + i : 6 + i, cols] = late_refs[1][8, row]
            for clip in (0, 1):
                time_out[clip, 5 + i : 6 + i, cols] = time_late[clip, row]
    for transfer in drains:
        transfer.drain()


def backward(hbm, vmem):
    dma = pltpu.SemaphoreType.DMA
    sds = jax.ShapeDtypeStruct
    lin = pltpu.VMEM((SEQ, HW), F32)
    low = pltpu.VMEM((SEQ, HW), BF)
    wide = pltpu.VMEM((SEQ, D), BF)
    block = pltpu.VMEM((TOK, D), F32)
    low_block = pltpu.VMEM((TOK, D), BF)
    summed = sds((2, PAIR, BATCH), F32)
    outs = [
        (sds((2, TOK, D), BF), HB), (sds((TOK, D), BF), VM), (sds((2, 16, D), F32), VM),
        (sds((16, D), F32), VM), (sds((2, 16, HW), F32), VM), (summed, VM), (summed, VM),
        *[(sds((2, PAIR, BATCH), BF), VM)] * 3,
    ]
    batch = [pltpu.VMEM(GRADS, BF), *reduce_scratch()]
    return pl.pallas_call(
        backward_kernel,
        out_shape=[shape for shape, _ in outs],
        in_specs=[HB] * len(hbm) + [VM] * len(vmem),
        out_specs=[spec for _, spec in outs],
        scratch_shapes=[
            pltpu.VMEM((D, ATTN), BF), wide, block, block, lin, lin, low, low, low, low, low, wide,
            low_block, block, pltpu.VMEM((SIDE, TOK, HEAD), F32), pltpu.VMEM((SEQ, 128), F32),
            low, pltpu.VMEM((SEQ, 2 * HW), BF), pltpu.VMEM((SEQ, 3 * HW), BF), wide, wide,
            pltpu.VMEM((2, 3, TOK, D), BF), low, lin, lin, lin, pltpu.VMEM((16, D), F32),
            pltpu.VMEM((16, HW), F32), low_block,
            pltpu.VMEM((2, 4, 8, SEQ), F32),
            dma((2, 3)), dma((2, 3)), dma((3, 6)), dma((3, 6)), dma((6,)), dma((6,)), dma((3, 2)),
            dma((3, 2)), dma((32,)), *batch, *batch, *model_scratch(16, D),
            *model_scratch(8, HW), *head_scratch(), pltpu.VMEM((8, HW), F32), pltpu.VMEM((2, 8, HW), F32),
            *swap_sems(), *swap_sems(), *swap_sems(),
        ],
        compiler_params=params(2),
        name="backward",
    )(*hbm, *vmem)


def block_mask(size):
    row = lax.broadcasted_iota(jnp.int32, (size, size), 0)
    col = lax.broadcasted_iota(jnp.int32, (size, size), 1)
    return lax.div(row, ROWS) == lax.div(col, ROWS), row == col


def times(a, b):
    return jnp.dot(a, b, precision=HIGHEST, preferred_element_type=F32)


def gram_of(blocks):
    return lax.dot_general(
        blocks, blocks, (((1,), (1,)), ((), ())), precision=HIGHEST, preferred_element_type=F32
    )


def newton_factor(gram, size):
    same, eye = block_mask(size)
    gram = jnp.where(same, gram, 0.0)
    diagonal = jnp.where(eye, gram, 0.0)
    by_row = jnp.sum(diagonal, 1, keepdims=True)
    by_col = jnp.sum(diagonal, 0, keepdims=True)
    total_row = jnp.sum(jnp.where(same, by_col, 0.0), 1, keepdims=True)
    total_col = jnp.sum(jnp.where(same, by_row, 0.0), 0, keepdims=True)
    scale_row = 1.0 / (jnp.sqrt(total_row) + ORTHO_EPSILON)
    scale_col = 1.0 / (jnp.sqrt(total_col) + ORTHO_EPSILON)
    current = gram * scale_row * scale_col
    whole = None
    for turn in range(NS_STEPS):
        square = times(current, current)
        step = NEWTON_SECOND * current + NEWTON_THIRD * square + jnp.where(eye, NEWTON_FIRST, 0.0)
        whole = step if whole is None else times(step, whole)
        if turn + 1 < NS_STEPS:
            current = times(times(step, current), step)
    return whole * scale_col


WIDE = 2 * FF_REAL


def join_hidden(first, second):
    fill = jnp.zeros((first.shape[0], FF), F32)
    first = jnp.concatenate([first, fill], 1)
    second = pltpu.roll(jnp.concatenate([second, fill], 1), FF_REAL, 1)
    return (first + second)[:, :WIDE]


def gram_kernel(
    sum_a, sum_b, sum_c, attn_a, attn_b, in_m, out_m, mlp_m, words, narrow, wide, gram, out_words,
    mine, theirs, send, recv, ds, dr, loc,
):
    x, y, z, core = here()
    partner = chip(x, y, z + 2, core)
    greet(column(x, y, z, core))
    send_words, wait_words = deliver(words, out_words, ds, dr, loc.at[0])

    def pair(ref, part, col):
        rows = slice(part * ROWS, (part + 1) * ROWS)
        return jnp.concatenate([ref[0, rows, col : col + HW], ref[1, rows, col : col + HW]], 1)

    n, w = 8 * ROWS, 2 * ROWS
    for j, (ref, part, col) in enumerate(
        ((attn_b, 0, 0), (attn_b, 0, HW), (attn_b, 1, 0), (attn_a, 1, 0), (attn_a, 0, 0), (attn_a, 0, HW))
    ):
        narrow[j * ROWS : (j + 1) * ROWS] = MOMENTUM * in_m[j] + pair(ref, part, col)
    for j, ref in enumerate((attn_b, attn_a)):
        narrow[(6 + j) * ROWS : (7 + j) * ROWS] = MOMENTUM * out_m[:, j, :] + pair(ref, 1, HW)
    mine[:n, :n] = gram_of(narrow[...])
    top, bottom = slice(0, ROWS), slice(ROWS, 2 * ROWS)
    for j, thirds in enumerate(
        (((sum_b, bottom), (sum_c, top), (sum_c, bottom)), ((sum_a, top), (sum_a, bottom), (sum_b, top)))
    ):
        chips = [jnp.concatenate([ref[i].astype(F32)[rows] for ref, rows in thirds], 1) for i in (0, 1)]
        wide[j * ROWS : (j + 1) * ROWS] = MOMENTUM * mlp_m[:, j, :] + join_hidden(*chips)
    mine[n:, n:] = gram_of(wide[...])
    mine[:n, n:] = jnp.zeros((n, w), F32)
    mine[n:, :n] = jnp.zeros((w, n), F32)
    copy = remote(mine, theirs, send.at[0], recv.at[0], partner)
    copy.start()
    send_words()
    copy.wait()
    gram[...] = mine[...] + theirs[...]
    wait_words()


def gram_step(args, cid):
    sds = jax.ShapeDtypeStruct
    dma = pltpu.SemaphoreType.DMA
    size = 10 * ROWS
    return pl.pallas_call(
        gram_kernel,
        out_shape=[
            sds((8 * ROWS, 2 * HW), F32), sds((2 * ROWS, WIDE), F32), sds((size, size), F32),
            sds((2, TOK, D), BF),
        ],
        in_specs=[VM] * len(args),
        out_specs=[VM] * 3 + [HB],
        scratch_shapes=[
            pltpu.VMEM((size, size), F32), pltpu.VMEM((size, size), F32), dma((1,)), dma((1,)),
            dma((2,)), dma((2,)), dma((1,)),
        ],
        compiler_params=params(cid),
        name="gram",
    )(*args)


def finish_kernel(
    narrow, wide, gram, in_w, out_w, mlp_w, head_w, head_m, model_w, model_m, up_w, up_m, head_sum,
    model_sum, result, tokens, words, time_sum,
    new_in, new_out, new_mlp, new_in_m, new_out_m, new_mlp_m, new_head, new_model, new_up,
    new_head_m, new_model_m, new_up_m, out_result, out_tokens, out_words, out_time,
    block, stores,
):
    out_result[...] = result[...]
    copies = []
    for i, (src, dst) in enumerate(((tokens, out_tokens), (words, out_words))):
        for clip in (0, 1):
            block[2 * i + clip] = src[clip].astype(F32)
            copies.append(
                pltpu.make_async_copy(block.at[2 * i + clip], dst.at[clip], stores.at[2 * i + clip])
            )
            copies[-1].start()
    for i in range(6):
        for clip in (0, 1):
            out_time[i, clip : clip + 1] = time_sum[clip, 5 + i : 6 + i]
    value = MOMENTUM * head_m[...] + jnp.concatenate([head_sum[0, :10], head_sum[1, :10]], 1)
    new_head_m[...] = value
    new_head[...] = head_w[...] - RATE_VECTOR * value
    value = MOMENTUM * model_m[...] + model_sum[:11]
    new_model_m[...] = value
    new_model[...] = model_w[...] - RATE_VECTOR * value
    chips = [jnp.concatenate([head_sum[i, 10 + k : 11 + k] for k in range(6)], 1) for i in (0, 1)]
    value = join_hidden(*chips)
    for i in range(WIDE // 128):
        row = slice(i, i + 1)
        new_up_m[row] = MOMENTUM * up_m[row] + value[:, i * 128 : (i + 1) * 128]
    new_up[...] = up_w[...] - RATE_VECTOR * new_up_m[...]
    n, w = narrow.shape[0], wide.shape[0]
    factor = newton_factor(gram[...], n + w)
    turned = times(factor[:n, :n], narrow[...])
    for j in range(6):
        rows = slice(j * ROWS, (j + 1) * ROWS)
        new_in_m[j] = narrow[rows]
        new_in[j] = in_w[j] * (1.0 - RATE_IN * DECAY) - RATE_IN * turned[rows]
    for j in range(2):
        rows = slice((6 + j) * ROWS, (7 + j) * ROWS)
        new_out_m[:, j, :] = narrow[rows]
        new_out[:, j, :] = out_w[:, j, :] * (1.0 - RATE_OUT * DECAY) - RATE_OUT * turned[rows]
    turned = times(factor[n:, n:], wide[...])
    for j in range(2):
        rows = slice(j * ROWS, (j + 1) * ROWS)
        new_mlp_m[:, j, :] = wide[rows]
        new_mlp[:, j, :] = mlp_w[:, j, :] * (1.0 - RATE_MLP * DECAY) - RATE_MLP * turned[rows]
    for copy in copies:
        copy.wait()


def finish_step(args):
    sds = jax.ShapeDtypeStruct
    matrices = [sds((6, ROWS, 2 * HW), F32), sds((ROWS, 2, 2 * HW), F32), sds((ROWS, 2, WIDE), F32)]
    vectors = [sds((10, 2 * HW), F32), sds((11, D), F32), sds((WIDE // 128, 128), F32)]
    blocks = [sds((2, TOK, D), BF), sds((2, TOK, D), F32), sds((2, TOK, D), F32)]
    return pl.pallas_call(
        finish_kernel,
        out_shape=matrices + matrices + vectors + vectors + blocks + [sds((6, 2, D), F32)],
        in_specs=[VM] * len(args),
        out_specs=[VM] * 13 + [HB] * 2 + [VM],
        scratch_shapes=[pltpu.VMEM((4, TOK, D), F32), pltpu.SemaphoreType.DMA((4,))],
        compiler_params=pltpu.CompilerParams(vmem_limit_bytes=VMEM_LIMIT),
        name="finish",
    )(*args)


def rope_tables(places):
    pair_index = jnp.arange(HEAD // 2, dtype=jnp.int32)
    side_pairs = HEAD // 6
    frame_pairs = (HEAD - 4 * side_pairs) // 2
    part_of = (pair_index >= frame_pairs).astype(jnp.int32) + (
        pair_index >= frame_pairs + side_pairs
    ).astype(jnp.int32)
    offset = jnp.where(
        part_of == 0, 0, jnp.where(part_of == 1, frame_pairs, frame_pairs + side_pairs)
    ).astype(jnp.int32)
    extent = jnp.where(part_of == 0, 2 * frame_pairs, 2 * side_pairs).astype(jnp.float32)
    frequency = jnp.exp(
        (pair_index - offset).astype(jnp.float32) * (-2.0 * math.log(10000.0)) / extent
    )
    chosen = (
        places[0][:, None] * (part_of == 0)
        + places[1][:, None] * (part_of == 1)
        + places[2][:, None] * (part_of == 2)
    )
    angles = chosen.astype(jnp.float32) * frequency
    return (jnp.cos(angles), jnp.sin(angles))


def plain_norm(values):
    centred = values - jnp.mean(values, -1, keepdims=True)
    inverse = lax.rsqrt(jnp.mean(centred * centred, -1, keepdims=True) + NORM_EPSILON)
    return (centred * inverse, inverse)


def norm_back(grads, normed, inverse):
    return inverse * (
        grads
        - jnp.mean(grads, -1, keepdims=True)
        - normed * jnp.mean(grads * normed, -1, keepdims=True)
    )


def product(left, right):
    return jnp.dot(left, right, preferred_element_type=F32)


def contract_last(left, right):
    return lax.dot_general(left, right, (((1,), (1,)), ((), ())), preferred_element_type=F32)


def contract_rows(left, right):
    return lax.dot_general(left, right, (((0,), (0,)), ((), ())), preferred_element_type=F32)


def body(
    tokens, text, time_embedding, positions, cotangent, attn_in, attn_out, mlp, head_vectors,
    model_vectors, up_bias, attn_in_moment, attn_out_moment, mlp_moment, head_moment, model_moment,
    up_moment,
):
    x, y, z, core = here()
    zl = lax.rem(z, 2)

    low_in = attn_in.astype(BF).reshape(ROWS, 6, 2, HW).transpose(2, 0, 1, 3).reshape(2, ROWS, -1)
    low_out = attn_out.astype(BF).reshape(ROWS, 2, 2, HW).transpose(2, 0, 1, 3).reshape(2, ROWS, -1)
    send_attn = jnp.concatenate([low_in, low_out], -1).reshape(2, ROWS, 2, ATTN // 2)
    send_attn = send_attn.transpose(0, 2, 1, 3).reshape(2, PAIR, ATTN // 2)
    send_mlp = jnp.pad(
        mlp.astype(BF).reshape(ROWS, 2, 2, FF_REAL).transpose(2, 1, 0, 3),
        ((0, 0), (0, 0), (0, 0), (0, FF - FF_REAL)),
    ).reshape(2, PAIR, FF)
    cosine, sine = rope_tables(positions.reshape(3, 2 * TOK))
    table = jnp.concatenate([cosine, sine], -1).reshape(2, TOK, HEAD)

    heads = jnp.pad(lax.dynamic_slice(head_vectors, (0, zl * HW), (10, HW)), ((0, 6), (0, 0)))
    bias_up = jnp.pad(lax.dynamic_slice(up_bias, (zl * FF_REAL,), (FF_REAL,)), (0, FF - FF_REAL))
    modulation = model_vectors[5:] + lax.dynamic_index_in_dim(time_embedding, core, 0, False)
    shift_one, scale_one, gate_one, shift_two, scale_two, gate_two = [modulation[i] for i in range(6)]
    vectors = jnp.pad(jnp.concatenate([modulation, model_vectors[:5]], 0), ((0, 5), (0, 0)))

    (
        w_attn, w_up, w_down, cot_all, tab_all, input_one, input_three, input_mlp, query_lin, key_lin,
        query_two_lin, key_two_lin, inv, query_rot, key_rot, value_low, query_two, key_two, value_two,
        mixed_low, mixed_two_low, branch_one, after_one, after_two, tok_all, txt_all,
    ) = forward(
        send_attn, send_mlp, tokens, text, cotangent, table, heads, vectors,
    )
    low_two, grad_after, sums, up_sum, out_result, *owned = mlp_pass(
        input_mlp, cot_all, w_up, w_down, after_two, vectors, bias_up[None]
    )
    out_tokens, low_words, time_sums, model_sums, head_totals, sums_a, sums_b, *mlp_sums = backward(
        [
            w_attn, low_two, after_one, branch_one, query_lin, key_lin, query_two_lin, key_two_lin,
            query_rot, key_rot, value_low, query_two, key_two, value_two, mixed_low, mixed_two_low,
            txt_all, input_three, input_one, tok_all, grad_after, tab_all, inv,
        ],
        [vectors, heads, sums, up_sum, *owned],
    )
    swap = lambda v: v.transpose(1, 0, 2)
    narrow, wide, gram, out_words = gram_step(
        [*mlp_sums, sums_a, sums_b, swap(attn_in_moment), attn_out_moment, mlp_moment, low_words], 3
    )
    (
        new_in, new_out, new_mlp, new_in_m, new_out_m, new_mlp_m, new_head, new_model, new_up,
        new_head_m, new_model_m, new_up_m, out_result, out_tokens, out_words, out_time,
    ) = finish_step(
        [
            narrow, wide, gram, swap(attn_in), attn_out, mlp, head_vectors, head_moment, model_vectors,
            model_moment, up_bias.reshape(-1, 128), up_moment.reshape(-1, 128), head_totals, model_sums, out_result,
            out_tokens, out_words, time_sums,
        ]
    )
    return (
        out_result, out_tokens, out_words, swap(out_time), swap(new_in), new_out, new_mlp,
        swap(new_in_m), new_out_m, new_mlp_m, new_head, new_model, new_up.reshape(-1), new_head_m,
        new_model_m, new_up_m.reshape(-1),
    )


def solution(mesh):
    clip = P("fsdp", "ctx", None)
    whole = P("fsdp", None, None)
    matrix = P(("fsdp", "ctx"), None, "tp")
    in_specs = (
        clip, clip, whole, P(None, "fsdp", "ctx"), clip, matrix, matrix, matrix, P(None, "tp"), P(),
        P("tp"), matrix, matrix, matrix, P(None, "tp"), P(), P("tp"),
    )
    out_specs = (
        clip, clip, clip, whole, matrix, matrix, matrix, matrix, matrix, matrix, P(None, "tp"), P(),
        P("tp"), P(None, "tp"), P(), P("tp"),
    )
    return jax.shard_map(body, mesh=mesh, in_specs=in_specs, out_specs=out_specs, check_vma=False)
```

```python
from functools import partial
import math

import jax
import jax.numpy as jnp
import numpy as np
from jax import lax
from jax.experimental import pallas as pl
from jax.experimental.pallas import tpu as pltpu
from jax.sharding import PartitionSpec as P

D = 1536
HEAD = 128
ROWS = 24
HEADS = 3
NORM_EPSILON = 1e-06
ORTHO_EPSILON = 1e-07
NEWTON_FIRST = 3.4445
NEWTON_SECOND = -4.775
NEWTON_THIRD = 2.0315
NS_STEPS = 5
MOMENTUM = 0.9
DECAY = 0.01
RATE_IN = 0.5
RATE_OUT = 4.0
RATE_MLP = 1.0
RATE_VECTOR = 0.005
HIGHEST = lax.Precision.HIGHEST

MESH = pl.DeviceIdType.MESH
BF = jnp.bfloat16
F32 = jnp.float32

SIDE = 4
TOK = 128
SEQ = SIDE * TOK
HW = HEADS * HEAD
FF_REAL = 2240
FF = 2304
WIDE = 2 * FF_REAL
PAIR = 2 * ROWS
VMEM_LIMIT = 60 * 1024 * 1024


def here():
    f = lax.axis_index("fsdp")
    c = lax.axis_index("ctx")
    t = lax.axis_index("tp")
    x, y = lax.div(f, SIDE), lax.rem(f, SIDE)
    zl, core = lax.div(c, 2), lax.rem(c, 2)
    return x, y, 2 * t + zl, core


def chip(x, y, z, core):
    x, y, z = lax.rem(x + SIDE, SIDE), lax.rem(y + SIDE, SIDE), lax.rem(z + SIDE, SIDE)
    return {"fsdp": x * SIDE + y, "ctx": lax.rem(z, 2) * 2 + core, "tp": lax.div(z, 2)}


def block_of(z):
    z = lax.rem(z + SIDE, SIDE)
    return 2 * lax.rem(z, 2) + lax.div(z, 2)


def knock(devices):
    barrier = pltpu.get_barrier_semaphore()
    for device in devices:
        pl.semaphore_signal(barrier, inc=1, device_id=device, device_id_type=MESH)
    return lambda: pl.semaphore_wait(barrier, len(devices))


def greet(devices):
    knock(devices)()


def column(x, y, z, core):
    return [chip(x, y, z + k, core) for k in (1, 2, 3)] + [
        chip(x, y, z + k, 1 - core) for k in range(4)
    ]


def remote(src, dst, send, recv, device):
    return pltpu.make_async_remote_copy(
        src_ref=src, dst_ref=dst, send_sem=send, recv_sem=recv, device_id=device, device_id_type=MESH
    )


def params(cid):
    return pltpu.CompilerParams(
        collective_id=cid, has_side_effects=True, vmem_limit_bytes=VMEM_LIMIT
    )


VM = pl.BlockSpec(memory_space=pltpu.VMEM)
HB = pl.BlockSpec(memory_space=pltpu.HBM)


def flat(a, b):
    return lax.rem(a + SIDE, SIDE) * SIDE + lax.rem(b + SIDE, SIDE)


def steps_of(x, y, z, core):
    return (
        (chip(x + 1, y, z, core), chip(x - 1, y, z, core)),
        (chip(x, y + 1, z, core), chip(x, y - 1, z, core)),
    )


def gather_xy(own, place, xs, xr, ks, kr):
    x, y, z, core = here()
    mine = x * SIDE + y
    steps = steps_of(x, y, z, core)
    far_x, far_y = chip(x + 2, y, z, core), chip(x, y + 2, z, core)
    sibling = chip(x, y, z, 1 - core)
    sends, sibs = [], []

    def push(part, slot, src, index, device, half=None):
        copy = remote(src, place(part, index, half), xs.at[part, slot], xr.at[part, slot], device)
        copy.start()
        sends.append(copy)
        return copy

    def to_sibling(part, slot, src, index):
        copy = remote(src, place(part, index), ks.at[part, slot], kr.at[part, slot], sibling)
        copy.start()
        sibs.append(copy)

    def index_of(part, first_off, second_off):
        if part == 0:
            return flat(x + first_off, y + second_off)
        return flat(x + second_off, y + first_off)

    one, two = {}, {}
    for part in (0, 1):
        a_next, a_prev = steps[part]
        one[part, "next"] = push(part, 0, own.at[part], mine, a_next)
        one[part, "prev"] = push(part, 1, own.at[part], mine, a_prev)
        one[part, "far"] = push(part, 2, own.at[part], mine, (far_x, far_y)[part])
    for part in (0, 1):
        b_next, b_prev = steps[1 - part]
        two[part, 0, "next"] = push(part, 4, own.at[part], mine, b_next)
        two[part, 0, "prev"] = push(part, 5, own.at[part], mine, b_prev)
        to_sibling(part, 0, own.at[part], mine)

    def second_start(part, k, offset):
        b_next, b_prev = steps[1 - part]
        index = index_of(part, offset, 0)
        src = place(part, index)
        two[part, k, "next"] = push(part, 4 + 4 * k, src, index, b_next)
        two[part, k, "prev"] = push(part, 5 + 4 * k, src, index, b_prev)
        to_sibling(part, 4 * k, src, index)

    offsets = (0, -1, 1, 2)
    for part in (0, 1):
        yield
        one[part, "next"].wait_recv()
        second_start(part, 1, -1)
        one[part, "prev"].wait_recv()
        second_start(part, 2, 1)

    def second_forward(part, k):
        b_next, b_prev = steps[1 - part]
        two[part, k, "next"].wait_recv()
        index = index_of(part, offsets[k], -1)
        two[part, k, "far0"] = push(part, 6 + 4 * k, place(part, index, 0), index, b_next, 0)
        to_sibling(part, 4 * k + 1, place(part, index), index)
        two[part, k, "prev"].wait_recv()
        index = index_of(part, offsets[k], 1)
        two[part, k, "far1"] = push(part, 7 + 4 * k, place(part, index, 1), index, b_prev, 1)
        to_sibling(part, 4 * k + 2, place(part, index), index)

    def second_finish(part, k):
        two[part, k, "far0"].wait_recv()
        two[part, k, "far1"].wait_recv()
        index = index_of(part, offsets[k], 2)
        to_sibling(part, 4 * k + 3, place(part, index), index)

    for part in (0, 1):
        yield
        second_forward(part, 0)
    for part in (0, 1):
        yield
        one[part, "far"].wait_recv()
        second_start(part, 3, 2)
    for k in (1, 2, 3):
        for part in (0, 1):
            yield
            second_forward(part, k)
        for part in (0, 1):
            second_finish(part, k - 1)
    for part in (0, 1):
        yield
        second_finish(part, 3)
    yield
    for copy in sends:
        copy.wait_send()
    for copy in sibs:
        copy.wait_send()
        copy.wait_recv()


GATHER_SEMS = ((2, 20), (2, 20), (2, 16), (2, 16))


def advance(job, count=1):
    for _ in range(count):
        next(job, None)


def finish(job):
    for _ in job:
        pass


def share_rows(send, recv, s, r, l):
    x, y, z, core = here()
    zl = lax.rem(z, 2)
    away = remote(send.at[1 - zl], recv.at[core], s.at[0], r.at[core], chip(x, y, z + 1 - 2 * zl, zl))
    near = remote(send.at[zl], recv.at[core], s.at[1], r.at[core], chip(x, y, z, zl))
    self_copy = pltpu.make_async_copy(send.at[zl], recv.at[core], l.at[0])

    def got(slot):
        remote(send.at[0], recv.at[slot], s.at[0], r.at[slot], chip(x, y, z, core)).wait_recv()

    def start():
        away.start()

        @pl.when(core == zl)
        def _():
            self_copy.start()

        @pl.when(core != zl)
        def _():
            near.start()

    def wait(own):
        @pl.when(core == zl)
        def _():
            self_copy.wait()
            got(1 - core)

        @pl.when(core != zl)
        def _():
            near.wait_send()
            got(0)
            got(1)

        first = recv[0].astype(F32)
        second = recv[1].astype(F32)
        own[0] = jnp.concatenate([first[:ROWS], second[:ROWS]], 0).astype(BF)
        own[1] = jnp.concatenate([first[ROWS:], second[ROWS:]], 0).astype(BF)

    return start, wait, away.wait_send


def share_clip(src, dst, s, r, l):
    x, y, z, core = here()
    put = dst.at[2 * lax.rem(z, 2) + core]
    copies = [
        remote(src.at[1 - core], put, s.at[0], r.at[0], chip(x, y, z, 1 - core)),
        remote(src.at[0], put, s.at[1], r.at[1 + core], chip(x, y, z + 1, 0)),
        remote(src.at[1], put, s.at[2], r.at[1 + core], chip(x, y, z - 1, 1)),
    ]
    local = pltpu.make_async_copy(src.at[core], put, l)

    def start():
        for copy in copies:
            copy.start()
        local.start()

    def wait():
        local.wait()
        for slot in range(3):
            remote(src.at[0], dst.at[0], s.at[0], r.at[slot], chip(x, y, z, core)).wait_recv()

    def drain():
        for copy in copies:
            copy.wait_send()

    return start, wait, drain


def split3(values):
    return [values[:, i * HW : (i + 1) * HW] for i in range(values.shape[1] // HW)]


def swap_halves(values):
    return pltpu.roll(values, HEAD // 2, 1)


def rope_pair(table):
    lane = lax.broadcasted_iota(jnp.int32, table.shape, 1)
    other = swap_halves(table)
    front = lane < HEAD // 2
    return jnp.where(front, table, other), jnp.where(front, -other, table)


def head_slice(h):
    return slice(h * HEAD, (h + 1) * HEAD)


SCALE = HEAD ** (-0.5)


def softmax_rows(query, keys):
    scores = contract_last(query, keys) * SCALE
    peak = jnp.max(scores, -1, keepdims=True)
    raised = jnp.exp(scores - peak)
    return raised * (1.0 / jnp.sum(raised, -1, keepdims=True))


def attend_clip(query, keys, values, out):
    for h in range(HEADS):
        cols = head_slice(h)
        for start in range(0, SEQ, 256):
            rows = slice(start, start + 256)
            weights = softmax_rows(query[rows, cols], keys[:, cols]).astype(BF)
            out[rows, cols] = product(weights, values[:, cols]).astype(BF)


class Stats:
    def __init__(self, buffer, send, recv):
        self.buffer, self.send, self.recv = buffer, send, recv

    def start(self, turn, columns):
        x, y, z, core = here()
        lane = lax.broadcasted_iota(jnp.int32, (SEQ, 128), 1)
        packed = jnp.zeros((SEQ, 128), F32)
        for i, column_values in enumerate(columns):
            packed = jnp.where(lane == i, column_values, packed)
        self.buffer[turn, 0] = packed.T[:8]
        copies = []
        for k in (2, 1, 3):
            copies.append(
                remote(self.buffer.at[turn, 0], self.buffer.at[turn, k], self.send.at[turn, k - 1],
                       self.recv.at[turn, k - 1], chip(x, y, z + k, core))
            )
            copies[-1].start()

        def wait():
            for copy in copies:
                copy.wait()
            total = (self.buffer[turn, 0] + self.buffer[turn, 1]) + (
                self.buffer[turn, 2] + self.buffer[turn, 3]
            )
            spread = jnp.concatenate([total, jnp.zeros((120, SEQ), F32)], 0).T
            return [spread[:, i : i + 1] for i in range(len(columns))]

        return wait


def block_slice(index):
    return pl.ds(pl.multiple_of(index * TOK, TOK), TOK)


HALF = TOK // 2


def half_rows(block, half):
    return pl.ds(pl.multiple_of(block * TOK + half * HALF, HALF), HALF)


class Scatter:
    def __init__(self, part, got, send, recv):
        self.part, self.got, self.send, self.recv = part, got, send, recv
        self.x, self.y, self.z, self.core = here()
        self.copies, self.relayed = [], False

    def push(self, slot, rows, dst, step):
        device = chip(self.x, self.y, self.z + step, self.core)
        copy = remote(self.part.at[rows], dst, self.send.at[slot], self.recv.at[slot], device)
        copy.start()
        self.copies.append(copy)

    def stage(self, k):
        front, rear = pl.ds(0, HALF), pl.ds(HALF, HALF)
        block = block_of(self.z + k)
        if k == 2:
            self.push(0, half_rows(block, 0), self.got.at[2, front], 1)
            self.push(1, half_rows(block, 1), self.got.at[2, rear], -1)
        elif k == 1:
            self.push(2, half_rows(block, 1), self.got.at[0, rear], 1)
        elif k == 3:
            self.push(3, half_rows(block, 0), self.got.at[1, front], -1)

    def held(self):
        for k in (2, 1, 3):
            self.stage(k)
        return self

    def product(self, left, right):
        for k in (2, 1, 3, 0):
            rows = block_slice(block_of(self.z + k))
            self.part[rows] = contract_last(left[rows], right).astype(BF)
            self.stage(k)
        return self

    def relay(self):
        if self.relayed:
            return
        self.relayed = True
        for slot, step in ((0, 1), (1, -1)):
            span = pl.ds(slot * HALF, HALF)
            rows = half_rows(block_of(self.z + step), slot)
            self.copies[slot].wait_recv()
            total = self.part[rows].astype(F32) + self.got[2, span].astype(F32)
            self.part[rows] = total.astype(BF)
            self.push(4 + slot, rows, self.got.at[slot, span], step)

    def total(self):
        self.relay()
        for copy in self.copies[2:]:
            copy.wait_recv()
        own = self.part[block_slice(block_of(self.z))].astype(F32)
        return own + (self.got[0].astype(F32) + self.got[1].astype(F32))

    def drain(self):
        for copy in self.copies:
            copy.wait_send()


class Spread:
    def __init__(self, out, value, send, recv):
        self.out, self.send, self.recv = out, send, recv
        self.x, self.y, self.z, self.core = here()
        self.copies, self.relayed = [], False
        block = block_of(self.z)
        out[block_slice(block)] = value
        self.push(0, half_rows(block, 0), 1)
        self.push(1, half_rows(block, 1), -1)
        self.push(2, half_rows(block, 1), 1)
        self.push(3, half_rows(block, 0), -1)

    def push(self, slot, rows, step):
        device = chip(self.x, self.y, self.z + step, self.core)
        rows = self.out.at[rows]
        copy = remote(rows, rows, self.send.at[slot], self.recv.at[slot], device)
        copy.start()
        self.copies.append(copy)

    def relay(self):
        if self.relayed:
            return
        self.relayed = True
        for slot, step in ((0, 1), (1, -1)):
            self.copies[slot].wait_recv()
            self.push(4 + slot, half_rows(block_of(self.z - step), slot), step)

    def wait(self):
        self.relay()
        for copy in self.copies[2:]:
            copy.wait_recv()

    def drain(self):
        for copy in self.copies:
            copy.wait_send()


def inverse_root(total):
    return lax.rsqrt(total * (1.0 / D) + NORM_EPSILON)


V_SELF, V_CROSS, V_DOWN, V_GAIN, V_BIAS = 6, 7, 8, 9, 10
W_QKV, W_QUERY, W_TEXT, W_SELF, W_CROSS = (
    slice(0, 3 * HW), slice(3 * HW, 4 * HW), slice(4 * HW, 6 * HW), slice(6 * HW, 7 * HW), slice(7 * HW, 8 * HW),
)
ATTN = 8 * HW


SAVED = 22


def forward_kernel(
    in_w, out_w, mlp_w, tok, txt, cot, places, rates, time_in, model_in, head_in,
    w_attn, w_up, w_down, cot_all, heads_out, vec_out, *rest,
):
    saved, held, rest = rest[:SAVED], rest[SAVED : 2 * SAVED], rest[2 * SAVED :]
    (
        tab_all, input_one, input_three, input_mlp, query_lin, key_lin, query_two_lin, key_two_lin, inv,
        query_rot, key_rot, value_low, query_two, key_two, value_two, mixed, mixed_two, branch_one,
        after_one, after_two, tok_all, txt_all,
    ) = held
    (
        send_attn, send_mlp, tab, heads, vec, wa, got_attn, got_mlp, own_attn, own_mlp, part_one, part_two, blocks, stat,
        xs, xr, ks, kr, ms, mr, js, jr, rs, rr, cs, cr, loc, stat_s, stat_r, zs, zr, gs, gr, keep,
    ) = rest
    x, y, z, core = here()
    mine = x * SIDE + y
    stores = []

    def keep_small(ref, out, i):
        stores.append(pltpu.make_async_copy(ref, out, keep.at[SAVED + i]))
        stores[-1].start()

    def save(*refs):
        for ref in refs:
            i = [ref is other for other in held].index(True)
            stores.append(pltpu.make_async_copy(ref, saved[i], keep.at[i]))
            stores[-1].start()

    def packed(values, cores_chip):
        return values[:, cores_chip * HW : (cores_chip + 1) * HW]

    for i in (0, 1):
        rows = [
            jnp.concatenate([packed(in_w[j], i) for j in range(4)], 1),
            jnp.concatenate([packed(in_w[j], i) for j in (4, 5)] + [packed(out_w[:, j, :], i) for j in (0, 1)], 1),
        ]
        send_attn[i] = jnp.concatenate(rows, 0).astype(BF)
    greet(
        [device for pair in steps_of(x, y, z, core) for device in pair]
        + [chip(x + 2, y, z, core), chip(x, y + 2, z, core)]
        + column(x, y, z, core)
    )
    attn_start, attn_wait, attn_drain = share_rows(send_attn, got_attn, rs.at[0], rr.at[0], loc.at[0])
    mlp_start, mlp_wait, mlp_drain = share_rows(send_mlp, got_mlp, rs.at[1], rr.at[1], loc.at[1])
    acts = [
        share_clip(src, dst, cs.at[i], cr.at[i], loc.at[2 + i, 0])
        for i, (src, dst) in enumerate(
            ((tok, tok_all), (tab, tab_all), (txt, txt_all), (cot, cot_all))
        )
    ]
    attn_start()
    acts[0][0]()
    zl = lax.rem(z, 2)
    for i in range(6):
        vec[i : i + 1] = model_in[5 + i : 6 + i] + time_in[i, pl.ds(core, 1)]
    vec[6:11] = model_in[0:5]
    vec[11:16] = jnp.zeros((5, D), F32)
    heads[0:10] = head_in[:, pl.ds(pl.multiple_of(zl * HW, HW), HW)]
    heads[10:16] = jnp.zeros((6, HW), F32)
    keep_small(heads, heads_out, 0)
    keep_small(vec, vec_out, 1)
    attn_wait(own_attn)

    def attn_place(part, index, half=None):
        start, size = part * (ATTN // 2), ATTN // 2
        if half is not None:
            start, size = start + half * (ATTN // 4), ATTN // 4
        rows = pl.ds(pl.multiple_of(index * (2 * PAIR) + core * PAIR, PAIR), PAIR)
        return wa.at[rows, pl.ds(start, size)]

    def mlp_place(part, index, half=None):
        start, size = (0, FF) if half is None else (half * (FF // 2), FF // 2)
        rows = pl.ds(pl.multiple_of(index * (2 * PAIR) + core * PAIR, PAIR), PAIR)
        return (w_up, w_down)[part].at[rows, pl.ds(start, size)]

    gather_attn = gather_xy(own_attn, attn_place, xs, xr, ks, kr)
    advance(gather_attn)
    for part in (0, 1):
        attn_place(part, mine)[...] = own_attn[part]
    acts[2][0]()
    fill = jnp.zeros((ROWS, 2 * FF - WIDE), F32)
    lane = lax.broadcasted_iota(jnp.int32, (ROWS, FF), 1)
    sides = ([], [])
    for j in (0, 1):
        whole = jnp.concatenate([mlp_w[:, j, :], fill], 1)
        sides[0].append(jnp.where(lane < FF_REAL, whole[:, :FF], 0.0))
        sides[1].append(pltpu.roll(whole, 2 * FF - FF_REAL, 1)[:, :FF])
    for i in (0, 1):
        send_mlp[i] = jnp.concatenate(sides[i], 0).astype(BF)
    mlp_start()
    lane = lax.broadcasted_iota(jnp.int32, (TOK, HEAD), 1)
    for i in (0, 1):
        spots = [places[c, i : i + 1, :].astype(F32) for c in range(3)]
        spots = jnp.concatenate(spots + [jnp.zeros((TOK - 3, TOK), F32)], 0).T
        angle = spots[:, 0:1] * rates[0:1] + spots[:, 1:2] * rates[1:2] + spots[:, 2:3] * rates[2:3]
        tab[i] = jnp.where(lane < HEAD // 2, jnp.cos(angle), jnp.sin(angle))
    acts[1][0]()

    def norm_block(i, carry):
        normed, _ = plain_norm(tok_all[i].astype(F32))
        input_one[block_slice(i)] = (normed * (1.0 + vec[1:2]) + vec[0:1]).astype(BF)
        return carry

    advance(gather_attn, 4)
    acts[3][0]()
    advance(gather_attn, 2)
    acts[0][1]()
    lax.fori_loop(0, 2, norm_block, 0)
    advance(gather_attn, 2)
    lax.fori_loop(2, 4, norm_block, 0)
    save(input_one, tok_all)
    advance(gather_attn, 2)
    mlp_wait(own_mlp)
    locals_ = []
    for part in (0, 1):
        locals_.append(pltpu.make_async_copy(own_mlp.at[part], mlp_place(part, mine), loc.at[6, part]))
        locals_[-1].start()
    advance(gather_attn, 2)
    gather_mlp = gather_xy(own_mlp, mlp_place, ms, mr, js, jr)
    advance(gather_mlp)
    finish(gather_attn)
    locals_.append(pltpu.make_async_copy(wa, w_attn, loc.at[7, 0]))
    locals_[-1].start()
    acts[1][1]()
    acts[2][1]()
    save(tab_all, txt_all)

    stats = Stats(stat, stat_s, stat_r)
    query_lin[...] = product(input_one[...], wa[:, 0:HW]) + heads[0:1]
    key_lin[...] = product(input_one[...], wa[:, HW : 2 * HW]) + heads[1:2]
    words = txt_all[...].reshape(SEQ, D)
    key_two_lin[...] = product(words, wa[:, 4 * HW : 5 * HW]) + heads[6:7]
    norm_wait = stats.start(
        0,
        [
            jnp.sum(ref[...] * ref[...], -1, keepdims=True)
            for ref in (query_lin, key_lin, key_two_lin)
        ],
    )
    value_low[...] = (product(input_one[...], wa[:, 2 * HW : 3 * HW]) + heads[2:3]).astype(BF)
    value_two[...] = (product(words, wa[:, 5 * HW : 6 * HW]) + heads[7:8]).astype(BF)
    save(query_lin, key_lin, key_two_lin, value_low, value_two)
    lane = lax.broadcasted_iota(jnp.int32, (SEQ, 128), 1)
    inverse_query, inverse_key, inverse_key_two = [inverse_root(v) for v in norm_wait()]
    inv[...] = jnp.where(
        lane == 0, inverse_query, jnp.where(lane == 1, inverse_key, jnp.where(lane == 2, inverse_key_two, 0.0))
    )
    cosine, sine = rope_pair(tab_all[...].reshape(SEQ, HEAD))
    for h in range(HEADS):
        cols = head_slice(h)
        for lin, inverse, gain, out in (
            (query_lin, inverse_query, 3, query_rot),
            (key_lin, inverse_key, 4, key_rot),
        ):
            value = lin[:, cols] * inverse * (1.0 + heads[gain : gain + 1, cols])
            out[:, cols] = (value * cosine + swap_halves(value) * sine).astype(BF)
    advance(gather_mlp, 2)
    attend_clip(query_rot, key_rot, value_low, mixed)
    scatter = Scatter(part_one, blocks.at[0], zs.at[0], zr.at[0]).product(mixed, wa[:, W_SELF])
    drains = [scatter]
    key_two[...] = (key_two_lin[...] * inverse_key_two * (1.0 + heads[9:10])).astype(BF)
    save(query_rot, key_rot, key_two, mixed)
    advance(gather_mlp, 2)
    scatter.relay()
    advance(gather_mlp, 5)
    branch = scatter.total() + vec[V_SELF : V_SELF + 1]
    branch_one[...] = branch
    after = tok_all[block_of(z)].astype(F32) + vec[2:3] * branch
    after_one[...] = after
    normed, _ = plain_norm(after)
    spread = Spread(
        input_three,
        (normed * (1.0 + vec[V_GAIN : V_GAIN + 1]) + vec[V_BIAS : V_BIAS + 1]).astype(BF),
        gs.at[0],
        gr.at[0],
    )
    drains.append(spread)
    save(branch_one, after_one)
    advance(gather_mlp, 2)
    spread.relay()
    finish(gather_mlp)
    spread.wait()
    query_two_lin[...] = product(input_three[...], wa[:, W_QUERY]) + heads[5:6]
    norm_wait = stats.start(1, [jnp.sum(query_two_lin[...] * query_two_lin[...], -1, keepdims=True)])
    save(input_three, query_two_lin)
    inverse_query_two = inverse_root(norm_wait()[0])
    inv[...] = jnp.where(lane == 3, inverse_query_two, inv[...])
    query_two[...] = (query_two_lin[...] * inverse_query_two * (1.0 + heads[8:9])).astype(BF)
    attend_clip(query_two, key_two, value_two, mixed_two)
    scatter = Scatter(part_two, blocks.at[1], zs.at[1], zr.at[1]).product(mixed_two, wa[:, W_CROSS])
    drains.append(scatter)
    save(inv, query_two, mixed_two)
    after = after_one[...] + scatter.total() + vec[V_CROSS : V_CROSS + 1]
    after_two[...] = after
    normed, _ = plain_norm(after)
    spread = Spread(
        input_mlp, (normed * (1.0 + vec[4:5]) + vec[3:4]).astype(BF), gs.at[1], gr.at[1]
    )
    drains.append(spread)
    save(after_two)
    spread.relay()
    for copy in locals_:
        copy.wait()
    acts[3][1]()
    for act in acts:
        act[2]()
    attn_drain()
    mlp_drain()
    spread.wait()
    save(input_mlp)
    for transfer in drains:
        transfer.drain()
    for copy in stores:
        copy.wait()


def forward(*args):
    dma = pltpu.SemaphoreType.DMA
    sds = jax.ShapeDtypeStruct
    wide, lin, low = sds((SEQ, D), BF), sds((SEQ, HW), F32), sds((SEQ, HW), BF)
    block = sds((TOK, D), F32)
    outs = [
        sds((SIDE, TOK, HEAD), F32), wide, wide, wide, lin, lin, lin, lin, sds((SEQ, 128), F32),
        low, low, low, low, low, low, low, low, block, block, block,
        sds((SIDE, TOK, D), BF), sds((SIDE, TOK, D), BF),
    ]
    weights = [
        sds((D, ATTN), BF), sds((D, FF), BF), sds((D, FF), BF), sds((SIDE, TOK, D), BF),
        sds((16, HW), F32), sds((16, D), F32),
    ]
    return pl.pallas_call(
        forward_kernel,
        out_shape=weights + outs,
        in_specs=[VM, VM, VM, HB, HB, HB, VM, VM, VM, VM, VM],
        out_specs=[HB] * (len(weights) + len(outs)),
        scratch_shapes=[
            *[pltpu.VMEM(shape.shape, shape.dtype) for shape in outs],
            pltpu.VMEM((2, PAIR, ATTN // 2), BF), pltpu.VMEM((2, PAIR, FF), BF),
            pltpu.VMEM((2, TOK, HEAD), F32), pltpu.VMEM((16, HW), F32), pltpu.VMEM((16, D), F32),
            pltpu.VMEM((D, ATTN), BF),
            pltpu.VMEM((2, PAIR, ATTN // 2), BF),
            pltpu.VMEM((2, PAIR, FF), BF),
            pltpu.VMEM((2, PAIR, ATTN // 2), BF),
            pltpu.VMEM((2, PAIR, FF), BF),
            pltpu.VMEM((SEQ, D), BF),
            pltpu.VMEM((SEQ, D), BF),
            pltpu.VMEM((2, 3, TOK, D), BF),
            pltpu.VMEM((2, 4, 8, SEQ), F32),
            *[dma(s) for s in GATHER_SEMS],
            *[dma(s) for s in GATHER_SEMS],
            dma((2, 2)), dma((2, 2)), dma((4, 3)), dma((4, 3)), dma((8, 2)),
            dma((2, 3)), dma((2, 3)), dma((2, 6)), dma((2, 6)), dma((2, 6)), dma((2, 6)),
            dma((SAVED + 2,)),
        ],
        compiler_params=params(0),
        name="forward",
    )(*args)


BATCH = 768


def peers_xy(x, y, z, core):
    rows = [chip(x + k, y, z, core) for k in (1, 2, 3)]
    lines = [chip(x, y + k, z, core) for k in (1, 2, 3)]
    return rows, lines


def reduce_batch(grads, out, sib, r1, r2, tosend, ss, sr, s1, q1, s2, q2, *swap_sems, gates=None):
    x, y, z, core = here()
    zl = lax.rem(z, 2)
    rows, lines = peers_xy(x, y, z, core)
    sibling = chip(x, y, z, 1 - core)
    wrap = lambda v: lax.rem(v, SIDE)
    swaps, one, two = [], {0: [], 1: []}, {0: [], 1: []}
    opens, waits = gates if gates is not None else (None, None)

    def signal(gate, devices):
        for device in devices:
            pl.semaphore_signal(gate, inc=1, device_id=device, device_id_type=MESH)

    def push(part, slot, target, half, place, step):
        span = pl.ds(2 * half, 2)
        src = (
            grads.at[0, span, wrap(y + target), core]
            if part == 0
            else grads.at[1, wrap(x + target), span, core]
        )
        device = (lines, rows)[part][step - 1]
        copy = remote(src, r1.at[part, place, span], s1.at[part, slot], q1.at[part, slot], device)
        copy.start()
        one[part].append(copy)

    if waits is not None:
        pl.semaphore_wait(waits[0], 1)
    for part in (0, 1):
        swaps.append(
            remote(grads.at[part, :, :, 1 - core], sib.at[part], ss.at[part], sr.at[part], sibling)
        )
        swaps[part].start()
    yield
    for part in (0, 1):
        swaps[part].wait_recv()

        def add_pair(k, carry):
            a, b = lax.div(k, SIDE), lax.rem(k, SIDE)
            grads[part, a, b, core] = grads[part, a, b, core] + sib[part, a, b]
            return carry

        lax.fori_loop(0, SIDE * SIDE, add_pair, 0)
        if part == 0 and waits is not None:
            pl.semaphore_wait(waits[1], 6)
        push(part, 0, 2, 0, 2, 1)
        push(part, 1, 2, 1, 2, 3)
        push(part, 2, 1, 1, 0, 1)
        push(part, 3, 3, 0, 1, 3)
    if opens is not None:
        signal(opens[0], [sibling])
    yield
    for part in (0, 1):
        for slot, step in ((0, 1), (1, 3)):
            one[part][slot].wait_recv()
            for i in (2 * slot, 2 * slot + 1):
                if part == 0:
                    grads[0, i, wrap(y + step), core] = grads[0, i, wrap(y + step), core] + r1[0, 2, i]
                else:
                    grads[1, wrap(x + step), i, core] = grads[1, wrap(x + step), i, core] + r1[1, 2, i]
            push(part, 4 + slot, step, slot, slot, step)
    yield
    for part in (0, 1):
        for copy in one[part][2:]:
            copy.wait_recv()

        def add_line(k, carry):
            a, b = (k, y) if part == 0 else (x, k)
            total = grads[part, a, b, core].astype(F32)
            total = total + (r1[part, 0, k].astype(F32) + r1[part, 1, k].astype(F32))
            grads[part, a, b, core] = total.astype(BF)
            return carry

        lax.fori_loop(0, SIDE, add_line, 0)
        for k in (2, 1, 3):
            src = grads.at[0, wrap(x + k), y, core] if part == 0 else grads.at[1, x, wrap(y + k), core]
            device = (rows, lines)[part][k - 1]
            copy = remote(src, r2.at[part, k - 1], s2.at[part, k - 1], q2.at[part, k - 1], device)
            copy.start()
            two[part].append(copy)
    yield
    final = []
    for part in (0, 1):
        for copy in two[part]:
            copy.wait_recv()
        total = grads[part, x, y, core].astype(F32)
        for i in range(3):
            total = total + r2[part, i].astype(F32)
        final.append(total)
    if opens is not None:
        signal(opens[1], [*rows, *lines])
    for target in (0, 1):
        span = slice(target * ROWS, target * ROWS + ROWS)
        tosend[target] = jnp.concatenate([final[0][span], final[1][span]], 0).astype(tosend.dtype)
    if out is not None:
        exchange = swap_rows(tosend, out, *swap_sems)
        next(exchange)
        yield
        finish(exchange)
    for copy in swaps + one[0] + one[1] + two[0] + two[1]:
        copy.wait_send()


def swap_rows(owned, out, s3, q3, l3):
    x, y, z, core = here()
    zl = lax.rem(z, 2)
    other = z + 1 - 2 * zl
    far = [
        remote(owned.at[t], out.at[zl], s3.at[t], q3.at[zl], chip(x, y, other, t)) for t in (0, 1)
    ]
    self_copy = pltpu.make_async_copy(owned.at[core], out.at[zl], l3.at[0])
    near = remote(owned.at[1 - core], out.at[zl], s3.at[0], q3.at[zl], chip(x, y, z, 1 - core))

    def got(slot):
        remote(owned.at[0], out.at[slot], s3.at[0], q3.at[slot], chip(x, y, z, core)).wait_recv()

    @pl.when(core == zl)
    def _():
        self_copy.start()
        near.start()

    @pl.when(core != zl)
    def _():
        for copy in far:
            copy.start()

    yield

    @pl.when(core == zl)
    def _():
        self_copy.wait()
        near.wait_send()
        got(1 - zl)

    @pl.when(core != zl)
    def _():
        for copy in far:
            copy.wait_send()
        got(zl)
        got(1 - zl)


def reduce_buffers():
    return [
        pltpu.VMEM((2, SIDE, SIDE, PAIR, BATCH), BF),
        pltpu.VMEM((2, 3, SIDE, PAIR, BATCH), BF),
        pltpu.VMEM((2, 3, PAIR, BATCH), BF),
    ]


def reduce_sems():
    dma = pltpu.SemaphoreType.DMA
    return [dma((2,)), dma((2,)), dma((2, 6)), dma((2, 6)), dma((2, 3)), dma((2, 3))]


def swap_sems():
    dma = pltpu.SemaphoreType.DMA
    return [dma((2,)), dma((2,)), dma((1,))]


def reduce_scratch():
    return [*reduce_buffers(), pltpu.VMEM((2, PAIR, BATCH), BF), *reduce_sems(), *swap_sems()]


GRADS = (2, SIDE, SIDE, 2, PAIR, BATCH)
SLAB = D // SIDE


def weight_grad(left, right, grads, part, start):
    width = right.shape[1]

    def slab(i, carry):
        turned = left[:, pl.ds(pl.multiple_of(i * SLAB, SLAB), SLAB)].T
        value = product(turned, right).astype(BF).reshape(SIDE, 2, PAIR, width)
        grads[part, i, :, :, :, start : start + width] = value
        return carry

    lax.fori_loop(0, SIDE, slab, 0)


def column_sum(values):
    return jnp.sum(values.astype(F32), 0, keepdims=True)


def deliver(src, dst, s, r, l):
    x, y, z, core = here()
    zh = lax.div(z, 2)
    far = remote(src, dst.at[core], s.at[0], r.at[core], chip(x, y, z + 2, zh))
    near = remote(src, dst.at[core], s.at[1], r.at[core], chip(x, y, z, zh))
    self_copy = pltpu.make_async_copy(src, dst.at[core], l)

    def got(slot):
        remote(src, dst.at[slot], s.at[0], r.at[slot], chip(x, y, z, core)).wait_recv()

    def start():
        far.start()

        @pl.when(core == zh)
        def _():
            self_copy.start()

        @pl.when(core != zh)
        def _():
            near.start()

    def wait():
        @pl.when(core == zh)
        def _():
            self_copy.wait()
            got(1 - core)

        @pl.when(core != zh)
        def _():
            near.wait_send()
            got(0)
            got(1)

        far.wait_send()

    return start, wait


CUBE = 0.044715
ROOT = math.sqrt(2.0 / math.pi)


def gelu_pair(u):
    square = u * u
    t = jnp.tanh(ROOT * u * (1.0 + CUBE * square))
    half = 0.5 * (1.0 + t)
    return u * half, half + 0.5 * u * (1.0 - t * t) * (ROOT * (1.0 + 3.0 * CUBE * square))


def mlp_kernel(
    a_in, cot_all, w_up, w_down, after_in, vec, up_bias,
    low_out, grad_out, sums_out, bias_out, result_out, owned_a_out, owned_b_out, owned_c_out,
    grad_after, sums, bias_sum, owned_a, owned_b, owned_c, keep, a, low, ahead, behind, hidden, act, back, acc, part, after_two, low_two, result, dy_own,
    blocks, bias, zs, zr, gs, gr, loc, ring, gate_core, gate_chips, *rest,
):
    x, y, z, core = here()
    rows, lines = peers_xy(x, y, z, core)
    own_rows = block_slice(block_of(z))

    def load(src, dst, sem):
        copy = pltpu.make_async_copy(src, dst, sem)
        copy.start()
        return copy

    def third(n):
        return pl.ds(n % 3 * BATCH, BATCH)

    def weights(n):
        return ahead.at[n % 2].reshape(D, BATCH)

    def load_ahead(n):
        return load((w_up, w_down)[n // 3].at[:, third(n)], weights(n), ring.at[0, n % 2])

    def load_behind(n):
        return load((w_down, w_up)[n // 3].at[:, third(n)], behind.at[n % 2], ring.at[1, n % 2])

    stores = []

    def save(ref, out):
        stores.append(load(ref, out, keep.at[len(stores)]))

    aheads, behinds = {0: load_ahead(0)}, {}
    fetch_a = load(a_in, a, loc.at[0])
    arrive = knock(column(x, y, z, core) + rows + lines)
    line = jnp.concatenate(
        [up_bias[i : i + 1] for i in range(WIDE // 128)] + [jnp.zeros((1, 2 * FF - WIDE), F32)], 1
    )
    moved_line = pltpu.roll(line, 2 * FF - FF_REAL, 1)
    lane = lax.broadcasted_iota(jnp.int32, (1, FF), 1)
    line = jnp.where(lax.rem(z, 2) == 0, line[:, :FF], moved_line[:, :FF])
    bias[0:1] = jnp.where(lane < FF_REAL, line, 0.0)
    sums[...] = jnp.zeros_like(sums)
    fetch_a.wait()
    aheads[0].wait()
    aheads[1], behinds[0] = load_ahead(1), load_behind(0)
    fetch_low = load(cot_all.reshape(SEQ, D), low, loc.at[1])
    behinds[1] = load_behind(1)
    fetch_after = load(after_in, after_two, loc.at[2])
    hidden[0] = product(a[...], weights(0)[...])
    aheads[2] = load_ahead(2)
    dy = dy_own

    grads = [rest[0], rest[1], ahead]
    gates = (gate_core, gate_chips)
    first, second, sems = rest[2:5], rest[5:8], rest[8:]
    owned = (owned_a, owned_b, owned_c)
    jobs = [
        reduce_batch(
            grads[b], None, *(first, second, first)[b], owned[b], *sems[6 * b : 6 * b + 6],
            gates=((gates, None), None, (None, gates))[b],
        )
        for b in range(3)
    ]

    def step(n):
        if n < 5:
            aheads[n + 1].wait()
            left = a if n < 2 else low
            behinds[n].wait()
            hidden[(n + 1) % 2] = product(left[...], weights(n + 1)[...])
        else:
            behinds[n].wait()
        cols = slice(n % 3 * BATCH, (n % 3 + 1) * BATCH)
        if n < 3:
            value, slope = gelu_pair(hidden[n % 2] + bias[0:1, cols])
            value = value.astype(BF)
            act[:, cols] = value
            back[:, cols] = slope.astype(BF)
        else:
            value = (hidden[n % 2] * back[:, cols].astype(F32)).astype(BF)
            back[:, cols] = value
            bias_sum[0:1, cols] = column_sum(value)
        moved = contract_last(value, behind[n % 2])
        if n % 3 == 0:
            acc[...] = moved
        elif n % 3 == 1:
            acc[...] += moved
        else:
            part[...] = (acc[...] + moved).astype(BF)
        if n < 3:
            aheads[n + 3] = load_ahead(n + 3)
        if n < 4:
            behinds[n + 2] = load_behind(n + 2)

    def third_grads(n, b, half):
        cols = slice(n % 3 * BATCH, (n % 3 + 1) * BATCH)
        left, right = ((low, act), (a, back))[n // 3]
        weight_grad(left, right[:, cols], grads[b], half, 0)

    step(0)
    fetch_low.wait()
    dy_own[...] = low[own_rows].astype(F32)
    for start in range(0, SEQ, TOK):
        block = slice(start, start + TOK)
        low[block] = (low[block].astype(F32) * vec[5:6]).astype(BF)
    sums[2:3] = column_sum(low[own_rows])
    step(1)
    third_grads(0, 0, 0)
    step(2)
    arrive()
    down_sum = Scatter(part, blocks.at[0], zs.at[0], zr.at[0]).held()
    third_grads(1, 0, 1)
    advance(jobs[0])
    third_grads(2, 1, 0)
    step(3)
    advance(jobs[0])
    down_sum.relay()
    third_grads(3, 1, 1)
    advance(jobs[1])
    step(4)
    advance(jobs[0])
    advance(jobs[1])
    fetch_after.wait()
    branch = down_sum.total() + vec[V_DOWN : V_DOWN + 1]
    result[...] = (after_two[...] + vec[5:6] * branch).astype(BF)
    save(result, result_out)
    sums[10:11] = column_sum(dy[...] * branch)
    down_sum.drain()
    step(5)
    save(bias_sum, bias_out)
    back_sum = Scatter(part, blocks.at[1], zs.at[1], zr.at[1]).held()
    third_grads(4, 2, 0)
    advance(jobs[0])
    third_grads(5, 2, 1)
    advance(jobs[2])
    advance(jobs[1])
    back_sum.relay()
    finish(jobs[0])
    save(owned_a, owned_a_out)
    advance(jobs[2])
    advance(jobs[1])
    total = back_sum.total()
    normed, inverse = plain_norm(after_two[...])
    sums[8:9] = column_sum(total)
    sums[9:10] = column_sum(total * normed)
    value = dy[...] + norm_back(total * (1.0 + vec[4:5]), normed, inverse)
    grad_after[...] = value
    value = value.astype(BF)
    spread = Spread(low_two, value, gs, gr)
    sums[1:2] = column_sum(value)
    save(grad_after, grad_out)
    save(sums, sums_out)
    advance(jobs[2])
    finish(jobs[1])
    save(owned_b, owned_b_out)
    spread.relay()
    advance(jobs[2])
    spread.wait()
    store = pltpu.make_async_copy(low_two, low_out, loc.at[3])
    store.start()
    finish(jobs[2])
    save(owned_c, owned_c_out)
    store.wait()
    for copy in stores:
        copy.wait()
    back_sum.drain()
    spread.drain()


def mlp_pass(a, cot, up, down, after, vec, bias):
    dma = pltpu.SemaphoreType.DMA
    sds = jax.ShapeDtypeStruct
    wide = pltpu.VMEM((SEQ, D), BF)
    tiles = pltpu.VMEM((2, D, BATCH), BF)
    units = pltpu.VMEM((SEQ, FF), BF)
    owned = sds((2, PAIR, BATCH), BF)
    outs = [
        (sds((SEQ, D), BF), HB), (sds((TOK, D), F32), VM), (sds((16, D), F32), VM),
        (sds((8, FF), F32), VM), (sds((TOK, D), BF), HB), (owned, VM), (owned, VM), (owned, VM),
    ]
    return pl.pallas_call(
        mlp_kernel,
        out_shape=[shape for shape, _ in outs],
        in_specs=[HB] * 5 + [VM] * 2,
        out_specs=[HB] * len(outs),
        scratch_shapes=[
            *[pltpu.VMEM(outs[i][0].shape, outs[i][0].dtype) for i in (1, 2, 3, 5, 6, 7)], dma((7,)),
            wide, wide, pltpu.VMEM(GRADS, BF), tiles, pltpu.VMEM((2, SEQ, BATCH), F32), units, units,
            pltpu.VMEM((SEQ, D), F32), wide, pltpu.VMEM((TOK, D), F32), wide, pltpu.VMEM((TOK, D), BF),
            pltpu.VMEM((TOK, D), F32),
            pltpu.VMEM((2, 3, TOK, D), BF), pltpu.VMEM((8, FF), F32), dma((2, 6)), dma((2, 6)), dma((6,)), dma((6,)),
            dma((5,)), dma((2, 2)), pltpu.SemaphoreType.REGULAR, pltpu.SemaphoreType.REGULAR,
            pltpu.VMEM(GRADS, BF), pltpu.VMEM(GRADS, BF),
            *reduce_buffers(), *reduce_buffers(), *reduce_sems(), *reduce_sems(), *reduce_sems(),
        ],
        compiler_params=params(1),
        name="mlp",
    )(a, cot, up, down, after, vec, bias)


def sum_over_xy(held, sends, recvs):
    x, y, z, core = here()
    for stage, peers in enumerate(peers_xy(x, y, z, core)):
        base = 4 * stage
        copies = [
            remote(held.at[base], held.at[base + k], sends.at[stage, k], recvs.at[stage, k], peers[k - 1])
            for k in (2, 1, 3)
        ]
        for copy in copies:
            copy.start()
        yield
        for copy in copies:
            copy.wait()
        held[base + 4] = (held[base] + held[base + 1]) + (held[base + 2] + held[base + 3])


def model_job(model, time_out, col, held, sends, recvs):
    x, y, z, core = here()
    copies = [
        remote(model, col.at[k], sends.at[2, k], recvs.at[2, k], chip(x, y, z + k, core)) for k in (2, 1, 3)
    ]
    for copy in copies:
        copy.start()
    yield
    for copy in copies:
        copy.wait()
    time_out[core] = (model[...] + col[1]) + (col[2] + col[3])
    swap = remote(
        time_out.at[core], time_out.at[core], sends.at[2, 0], recvs.at[2, 0], chip(x, y, z, 1 - core)
    )
    swap.start()
    yield
    swap.wait()
    held[0] = time_out[0] + time_out[1]
    yield from sum_over_xy(held, sends, recvs)


def head_job(heads, head_out, other, held, sends, recvs):
    x, y, z, core = here()
    zl = lax.rem(z, 2)
    swap = remote(heads, other, sends.at[2, 0], recvs.at[2, 0], chip(x, y, z, 1 - core))
    swap.start()
    yield
    swap.wait()
    held[0] = heads[...] + other[...]
    yield from sum_over_xy(held, sends, recvs)
    head_out[zl] = held[8]
    last = remote(
        held.at[8], head_out.at[zl], sends.at[2, 1], recvs.at[2, 1], chip(x, y, z + 1 - 2 * zl, core)
    )
    last.start()
    yield
    last.wait()


def model_scratch(rows, width):
    dma = pltpu.SemaphoreType.DMA
    return [pltpu.VMEM((4, rows, width), F32), pltpu.VMEM((9, rows, width), F32), dma((3, 4)), dma((3, 4))]


def head_scratch():
    dma = pltpu.SemaphoreType.DMA
    return [pltpu.VMEM((16, HW), F32), pltpu.VMEM((9, 16, HW), F32), dma((3, 4)), dma((3, 4))]


def attend_clip_back(query, keys, values, grad, grad_query, grad_keys, grad_values):
    for h in range(HEADS):
        cols = head_slice(h)
        k, v = keys[:, cols], values[:, cols]
        for start in range(0, SEQ, 256):
            rows = slice(start, start + 256)
            q, do = query[rows, cols], grad[rows, cols]
            weights = softmax_rows(q, k)
            grad_weights = contract_last(do, v)
            delta = jnp.sum(weights * grad_weights, -1, keepdims=True)
            grad_scores = (weights * (grad_weights - delta)).astype(BF)
            grad_query[rows, cols] = product(grad_scores, k) * SCALE
            to_keys = contract_rows(grad_scores, q) * SCALE
            to_values = contract_rows(weights.astype(BF), do)
            if start:
                grad_keys[:, cols] += to_keys
                grad_values[:, cols] += to_values
            else:
                grad_keys[:, cols] = to_keys
                grad_values[:, cols] = to_values


def root_back(linear, inverse, scaled, dot):
    return (inverse * scaled - linear * (inverse * inverse * inverse * dot * (1.0 / D))).astype(BF)


EARLY, LATE = (0, 1, 3, 4, 7, 8, 9, 10), (5, 6, 2)


def backward_kernel(
    wa_in, low_in, after_in, branch_in, query_lin_in, key_lin_in, query_two_lin_in, key_two_lin_in,
    query_rot_in, key_rot_in, value_low_in, query_two_in, key_two_in, value_two_in, mixed_in,
    mixed_two_in, words_in, three_in, one_in, tok_in, grad_in, tab_in, inv_in, result,
    vec, heads, sums, bias_sum, owned_a, owned_b, owned_c, in_m, out_m, mlp_m,
    out_result, out_tokens, out_words, time_sum_out, model_sum_out, head_sum_out, narrow_out, wide_out, gram_out,
    time_out, model_out, head_out, narrow, wide, gram, keep,
    wa, low_wide, after_one, branch_one, lin_a, lin_b, qa, ka, va, mixed, operand, tok_own,
    grad_after, tab, inv, grad_query, grad_kv, grad_qkv, part_cross, part_words, blocks,
    held, gq, gk, gv, model, head_sums, low_tokens, low_words, mine, theirs,
    sums_a, sums_b, mlp_a, mlp_b, mlp_c,
    stat, stat_s, stat_r, zs, zr, gs, gr, ds, dr, loc, *rest,
):
    x, y, z, core = here()
    rows, lines = peers_xy(x, y, z, core)
    slots = iter(range(32))
    own_block = block_of(z)

    def fetch(src, dst):
        copy = pltpu.make_async_copy(src, dst, loc.at[next(slots)])
        copy.start()
        return copy

    out_cols, in_cols = pl.ds(6 * HW, 2 * HW), pl.ds(0, 6 * HW)
    first = [fetch(low_in, low_wide), fetch(wa_in.at[:, out_cols], wa.at[:, out_cols])]
    inputs = [
        fetch(query_two_in, qa), fetch(key_two_in, ka), fetch(value_two_in, va),
        fetch(query_two_lin_in, lin_a), fetch(key_two_lin_in, lin_b), fetch(inv_in, inv),
    ]
    second = [
        fetch(mixed_two_in, mixed), fetch(wa_in.at[:, in_cols], wa.at[:, in_cols]),
        fetch(words_in.reshape(SEQ, D), operand),
    ]
    third = [
        fetch(after_in, after_one), fetch(branch_in, branch_one), fetch(grad_in, grad_after),
        fetch(tab_in, tab), fetch(tok_in.at[own_block], tok_own),
    ]
    arrive = knock(column(x, y, z, core) + rows + lines)
    for row in (1, 8, 9, 10):
        i = EARLY.index(row)
        model[i : i + 1] = sums[row : row + 1]
    head_sums[...] = jnp.zeros_like(head_sums)
    for i in range(6):
        head_sums[10 + i : 11 + i] = bias_sum[0:1, i * HW : (i + 1) * HW]
    refs_a, refs_b, early_refs, late_refs, head_refs, rest = (
        rest[:14], rest[14:28], rest[28:32], rest[32:36], rest[36:40], rest[40:],
    )
    (late, time_late, time_early, gram_sems), swap_refs = rest[:4], rest[4:]
    late[...] = jnp.zeros_like(late)
    n, w = 8 * ROWS, 2 * ROWS
    halves = (slice(0, ROWS), slice(ROWS, 2 * ROWS))

    stores = []

    def save(ref, out):
        copy = pltpu.make_async_copy(ref, out, keep.at[len(stores)])
        copy.start()
        stores.append(copy)

    def new_narrow(j, ref, part, col):
        rows = halves[part]
        grad = jnp.concatenate([ref[i].astype(F32)[rows, col : col + HW] for i in (0, 1)], 1)
        old = in_m[j] if j < 6 else out_m[:, j - 6, :]
        narrow[j * ROWS : (j + 1) * ROWS] = MOMENTUM * old + grad

    def new_wide(j, thirds):
        chips = [jnp.concatenate([ref[i].astype(F32)[rows] for ref, rows in thirds], 1) for i in (0, 1)]
        wide[j * ROWS : (j + 1) * ROWS] = MOMENTUM * mlp_m[:, j, :] + join_hidden(*chips)

    hidden_rows = [
        swap_rows(src, dst, *swap_refs[3 * i : 3 * i + 3])
        for i, (src, dst) in enumerate(((owned_a, mlp_a), (owned_b, mlp_b), (owned_c, mlp_c)))
    ]
    grads_a, grads_b = refs_a[0], refs_b[0]
    job_a = reduce_batch(grads_a, sums_a, *refs_a[1:])
    job_b = reduce_batch(grads_b, sums_b, *refs_b[1:])
    stats = Stats(stat, stat_s, stat_r)
    drains = []

    arrive()
    send_result, wait_result = deliver(result, out_result, ds.at[2], dr.at[2], loc.at[29])
    send_result()
    for copy in first:
        copy.wait()
    held[...] = product(low_wide[...], wa[:, W_CROSS]).astype(BF)
    for copy in inputs:
        copy.wait()
    attend_clip_back(qa, ka, va, held, gq, gk, gv)
    inverse_query, inverse_key, inverse_key_two, inverse_query_two = [inv[:, i : i + 1] for i in range(4)]
    dots = stats.start(
        0,
        [
            jnp.sum(lin_a[...] * (gq[...] * (1.0 + heads[8:9])), -1, keepdims=True),
            jnp.sum(lin_b[...] * (gk[...] * (1.0 + heads[9:10])), -1, keepdims=True),
        ],
    )
    for job in hidden_rows:
        advance(job)
    head_sums[8:9] = column_sum(gq[...] * lin_a[...] * inverse_query_two)
    head_sums[9:10] = column_sum(gk[...] * lin_b[...] * inverse_key_two)
    low = gv[...].astype(BF)
    grad_kv[:, HW:] = low
    head_sums[7:8] = column_sum(low)
    for copy in second:
        copy.wait()
    weight_grad(low_wide, mixed[...], grads_a, 1, HW)
    dot_query, dot_key = dots()
    low = root_back(lin_a[...], inverse_query_two, gq[...] * (1.0 + heads[8:9]), dot_query)
    grad_query[...] = low
    head_sums[5:6] = column_sum(low)
    cross = Scatter(part_cross, blocks.at[0], zs.at[0], zr.at[0]).product(grad_query, wa[:, W_QUERY])
    low = root_back(lin_b[...], inverse_key_two, gk[...] * (1.0 + heads[9:10]), dot_key)
    grad_kv[:, :HW] = low
    head_sums[6:7] = column_sum(low)
    selfs = [
        fetch(query_rot_in, qa), fetch(key_rot_in, ka), fetch(value_low_in, va),
        fetch(query_lin_in, lin_a), fetch(key_lin_in, lin_b), fetch(mixed_in, mixed),
    ]
    weight_grad(operand, grad_kv[...], grads_a, 0, 0)
    next_operand = fetch(three_in, operand)
    next_operand.wait()
    cross.relay()
    weight_grad(operand, grad_query[...], grads_a, 1, 0)
    next_operand = fetch(one_in, operand)
    advance(job_a)
    part_words[...] = contract_last(grad_kv[...], wa[:, W_TEXT]).astype(BF)
    for copy in third:
        copy.wait()

    total = cross.total()
    normed, inverse = plain_norm(after_one[...])
    model[3 : 4] = column_sum(total)
    model[2 : 3] = column_sum(total * normed)
    value = grad_after[...] + norm_back(total * (1.0 + vec[V_GAIN : V_GAIN + 1]), normed, inverse)
    grad_after[...] = value
    model[4 : 5] = column_sum(value * branch_one[...])
    low = (value * vec[2:3]).astype(BF)
    model[0 : 1] = column_sum(low)
    spread = Spread(low_wide, low, gs, gr)
    drains.append(spread)
    advance(job_a)
    spread.relay()
    early = model_job(model, time_early, *early_refs)
    advance(early)
    spread.wait()
    advance(job_a)
    word_sum = Scatter(part_words, blocks.at[1], zs.at[1], zr.at[1]).held()
    drains.append(word_sum)

    held[...] = product(low_wide[...], wa[:, W_SELF]).astype(BF)
    for copy in selfs:
        copy.wait()
    attend_clip_back(qa, ka, va, held, gq, gk, gv)
    cosine, sine = rope_pair(tab[...].reshape(SEQ, HEAD))
    for ref in (gq, gk):
        for h in range(HEADS):
            cols = head_slice(h)
            value = ref[:, cols]
            ref[:, cols] = value * cosine - swap_halves(value) * sine
    dots = stats.start(
        1,
        [
            jnp.sum(lin_a[...] * (gq[...] * (1.0 + heads[3:4])), -1, keepdims=True),
            jnp.sum(lin_b[...] * (gk[...] * (1.0 + heads[4:5])), -1, keepdims=True),
        ],
    )
    head_sums[3:4] = column_sum(gq[...] * lin_a[...] * inverse_query)
    head_sums[4:5] = column_sum(gk[...] * lin_b[...] * inverse_key)
    low = gv[...].astype(BF)
    grad_qkv[:, 2 * HW :] = low
    head_sums[2:3] = column_sum(low)
    next_operand.wait()
    weight_grad(low_wide, mixed[...], grads_b, 1, HW)
    cross.drain()
    advance(early)
    dot_query, dot_key = dots()
    word_sum.relay()
    advance(job_a)
    for i, (lin, inverse, ref, dot) in enumerate(
        ((lin_a, inverse_query, gq, dot_query), (lin_b, inverse_key, gk, dot_key))
    ):
        low = root_back(lin[...], inverse, ref[...] * (1.0 + heads[3 + i : 4 + i]), dot)
        grad_qkv[:, i * HW : (i + 1) * HW] = low
        head_sums[i : i + 1] = column_sum(low)
    token_sum = Scatter(part_cross, blocks.at[0], zs.at[2], zr.at[2]).product(grad_qkv, wa[:, W_QKV])
    drains.append(token_sum)
    advance(job_a)
    head_total = head_job(head_sums, head_out, *head_refs)
    advance(head_total)
    weight_grad(operand, grad_qkv[:, : 2 * HW], grads_b, 0, 0)
    weight_grad(operand, grad_qkv[:, 2 * HW :], grads_b, 1, 0)
    advance(job_b)
    token_sum.relay()
    low_words[...] = word_sum.total().astype(BF)
    send_words, wait_words = deliver(low_words, out_words, ds.at[0], dr.at[0], loc.at[30])
    send_words()
    advance(head_total)
    for job in hidden_rows:
        finish(job)
    top, bottom = halves
    new_wide(0, ((mlp_b, bottom), (mlp_c, top), (mlp_c, bottom)))
    new_wide(1, ((mlp_a, top), (mlp_a, bottom), (mlp_b, top)))
    save(wide, wide_out)
    advance(job_b)
    mine[:n, n:] = jnp.zeros((n, w), F32)
    mine[n:, :n] = jnp.zeros((w, n), F32)
    mine[n:, n:] = gram_of(wide[...])
    advance(early)

    total = token_sum.total()
    normed, inverse = plain_norm(tok_own[...].astype(F32))
    for i, row in enumerate((column_sum(total), column_sum(total * normed), sums[2:3])):
        for k in range(SIDE):
            late[SIDE * i + k : SIDE * i + k + 1] = row[:, k * HW : (k + 1) * HW]
    late_total = model_job(late, time_late, *late_refs)
    advance(late_total)
    advance(job_b)
    value = grad_after[...] + norm_back(total * (1.0 + vec[1:2]), normed, inverse)
    low_tokens[...] = value.astype(BF)
    send_tokens, wait_tokens = deliver(low_tokens, out_tokens, ds.at[1], dr.at[1], loc.at[31])
    send_tokens()
    advance(head_total)
    advance(late_total)
    advance(early)
    advance(job_b)
    advance(late_total)
    finish(job_a)
    for j, ref, part, col in ((3, sums_a, 1, 0), (4, sums_a, 0, 0), (5, sums_a, 0, HW), (7, sums_a, 1, HW)):
        new_narrow(j, ref, part, col)
    advance(head_total)
    advance(job_b)
    advance(late_total)
    finish(early)
    finish(job_b)
    for j, ref, part, col in ((0, sums_b, 0, 0), (1, sums_b, 0, HW), (2, sums_b, 1, 0), (6, sums_b, 1, HW)):
        new_narrow(j, ref, part, col)
    save(narrow, narrow_out)
    mine[:n, :n] = gram_of(narrow[...])
    same, _ = block_mask(10 * ROWS)
    blocks_only = jnp.where(same, mine[...], 0.0)
    compact = blocks_only[:ROWS]
    for j in range(1, 10):
        compact = compact + blocks_only[j * ROWS : (j + 1) * ROWS]
    theirs[0] = compact
    swap = remote(theirs.at[0], theirs.at[1], gram_sems.at[0], gram_sems.at[1], chip(x, y, z + 2, core))
    swap.start()
    finish(late_total)
    finish(head_total)
    save(head_out, head_sum_out)
    for i, row in enumerate(EARLY):
        model_out[row : row + 1] = early_refs[1][8, i : i + 1]
        if row > 4:
            for clip in (0, 1):
                time_out[row - 5, clip : clip + 1] = time_early[clip, i : i + 1]
    for i, row in enumerate(LATE):
        for k in range(SIDE):
            cols = slice(k * HW, (k + 1) * HW)
            part = slice(SIDE * i + k, SIDE * i + k + 1)
            model_out[row : row + 1, cols] = late_refs[1][8, part]
            if row > 4:
                for clip in (0, 1):
                    time_out[row - 5, clip : clip + 1, cols] = time_late[clip, part]
    save(time_out, time_sum_out)
    save(model_out, model_sum_out)
    wait_result()
    wait_tokens()
    wait_words()
    swap.wait()
    gram[...] = theirs[0] + theirs[1]
    save(gram, gram_out)
    for copy in stores:
        copy.wait()
    for transfer in drains:
        transfer.drain()


def backward(hbm, vmem):
    dma = pltpu.SemaphoreType.DMA
    sds = jax.ShapeDtypeStruct
    lin = pltpu.VMEM((SEQ, HW), F32)
    low = pltpu.VMEM((SEQ, HW), BF)
    wide = pltpu.VMEM((SEQ, D), BF)
    block = pltpu.VMEM((TOK, D), F32)
    low_block = pltpu.VMEM((TOK, D), BF)
    summed = pltpu.VMEM((2, PAIR, BATCH), BF)
    size = 10 * ROWS
    square = pltpu.VMEM((size, size), F32)
    outs = [
        *[(sds((2, TOK, D), BF), HB)] * 3, (sds((6, 2, D), F32), VM),
        (sds((16, D), F32), VM), (sds((2, 16, HW), F32), VM), (sds((8 * ROWS, 2 * HW), F32), VM),
        (sds((2 * ROWS, WIDE), F32), VM), (sds((ROWS, size), F32), VM),
    ]
    batch = [pltpu.VMEM(GRADS, BF), *reduce_scratch()]
    return pl.pallas_call(
        backward_kernel,
        out_shape=[shape for shape, _ in outs],
        in_specs=[HB] * len(hbm) + [VM] * len(vmem),
        out_specs=[HB] * len(outs),
        scratch_shapes=[
            *[pltpu.VMEM(shape.shape, shape.dtype) for shape, _ in outs[3:]], dma((6,)),
            pltpu.VMEM((D, ATTN), BF), wide, block, block, lin, lin, low, low, low, low, wide,
            low_block, block, pltpu.VMEM((SIDE, TOK, HEAD), F32), pltpu.VMEM((SEQ, 128), F32),
            low, pltpu.VMEM((SEQ, 2 * HW), BF), pltpu.VMEM((SEQ, 3 * HW), BF), wide, wide,
            pltpu.VMEM((2, 3, TOK, D), BF), low, lin, lin, lin, pltpu.VMEM((8, D), F32),
            pltpu.VMEM((16, HW), F32), low_block, low_block, square, pltpu.VMEM((2, ROWS, size), F32),
            summed, summed, summed, summed, summed,
            pltpu.VMEM((2, 4, 8, SEQ), F32),
            dma((2, 3)), dma((2, 3)), dma((3, 6)), dma((3, 6)), dma((6,)), dma((6,)), dma((3, 2)),
            dma((3, 2)), dma((32,)), *batch, *batch, *model_scratch(8, D),
            *model_scratch(16, HW), *head_scratch(), pltpu.VMEM((16, HW), F32), pltpu.VMEM((2, 16, HW), F32),
            pltpu.VMEM((2, 8, D), F32), dma((2,)), *swap_sems(), *swap_sems(), *swap_sems(),
        ],
        compiler_params=params(2),
        name="backward",
    )(*hbm, *vmem)


def block_mask(size):
    row = lax.broadcasted_iota(jnp.int32, (size, size), 0)
    col = lax.broadcasted_iota(jnp.int32, (size, size), 1)
    return lax.div(row, ROWS) == lax.div(col, ROWS), row == col


def times(a, b):
    return jnp.dot(a, b, precision=HIGHEST, preferred_element_type=F32)


def gram_of(blocks):
    return lax.dot_general(
        blocks, blocks, (((1,), (1,)), ((), ())), precision=HIGHEST, preferred_element_type=F32
    )


def newton_factor(gram, size):
    same, eye = block_mask(size)
    gram = jnp.where(same, jnp.concatenate([gram] * (size // ROWS), 0), 0.0)
    diagonal = jnp.where(eye, gram, 0.0)
    by_row = jnp.sum(diagonal, 1, keepdims=True)
    by_col = jnp.sum(diagonal, 0, keepdims=True)
    total_row = jnp.sum(jnp.where(same, by_col, 0.0), 1, keepdims=True)
    total_col = jnp.sum(jnp.where(same, by_row, 0.0), 0, keepdims=True)
    scale_row = 1.0 / (jnp.sqrt(total_row) + ORTHO_EPSILON)
    scale_col = 1.0 / (jnp.sqrt(total_col) + ORTHO_EPSILON)
    current = gram * scale_row * scale_col
    whole = None
    for turn in range(NS_STEPS):
        square = times(current, current)
        step = NEWTON_SECOND * current + NEWTON_THIRD * square + jnp.where(eye, NEWTON_FIRST, 0.0)
        whole = step if whole is None else times(step, whole)
        if turn + 1 < NS_STEPS:
            current = times(times(step, current), step)
    return whole * scale_col


def join_hidden(first, second):
    fill = jnp.zeros((first.shape[0], FF), F32)
    first = jnp.concatenate([first, fill], 1)
    second = pltpu.roll(jnp.concatenate([second, fill], 1), FF_REAL, 1)
    return (first + second)[:, :WIDE]


def finish_kernel(
    narrow, wide, gram, in_w, out_w, mlp_w, head_w, head_m, model_w, model_m, up_w, up_m, head_sum,
    model_sum, result, tokens, words, time_sum,
    new_in, new_out, new_mlp, new_in_m, new_out_m, new_mlp_m, new_head, new_model, new_up,
    new_head_m, new_model_m, new_up_m, out_result, out_tokens, out_words, out_time,
    block, stores,
):
    out_result[...] = result[...]
    copies = []
    for i, (src, dst) in enumerate(((tokens, out_tokens), (words, out_words))):
        for clip in (0, 1):
            block[2 * i + clip] = src[clip].astype(F32)
            copies.append(
                pltpu.make_async_copy(block.at[2 * i + clip], dst.at[clip], stores.at[2 * i + clip])
            )
            copies[-1].start()
    out_time[...] = time_sum[...]
    value = MOMENTUM * head_m[...] + jnp.concatenate([head_sum[0, :10], head_sum[1, :10]], 1)
    new_head_m[...] = value
    new_head[...] = head_w[...] - RATE_VECTOR * value
    value = MOMENTUM * model_m[...] + model_sum[:11]
    new_model_m[...] = value
    new_model[...] = model_w[...] - RATE_VECTOR * value
    chips = [jnp.concatenate([head_sum[i, 10 + k : 11 + k] for k in range(6)], 1) for i in (0, 1)]
    value = join_hidden(*chips)
    for i in range(WIDE // 128):
        row = slice(i, i + 1)
        new_up_m[row] = MOMENTUM * up_m[row] + value[:, i * 128 : (i + 1) * 128]
    new_up[...] = up_w[...] - RATE_VECTOR * new_up_m[...]
    n, w = narrow.shape[0], wide.shape[0]
    factor = newton_factor(gram[...], n + w)
    turned = times(factor[:n, :n], narrow[...])
    for j in range(6):
        rows = slice(j * ROWS, (j + 1) * ROWS)
        new_in_m[j] = narrow[rows]
        new_in[j] = in_w[j] * (1.0 - RATE_IN * DECAY) - RATE_IN * turned[rows]
    for j in range(2):
        rows = slice((6 + j) * ROWS, (7 + j) * ROWS)
        new_out_m[:, j, :] = narrow[rows]
        new_out[:, j, :] = out_w[:, j, :] * (1.0 - RATE_OUT * DECAY) - RATE_OUT * turned[rows]
    turned = times(factor[n:, n:], wide[...])
    for j in range(2):
        rows = slice(j * ROWS, (j + 1) * ROWS)
        new_mlp_m[:, j, :] = wide[rows]
        new_mlp[:, j, :] = mlp_w[:, j, :] * (1.0 - RATE_MLP * DECAY) - RATE_MLP * turned[rows]
    for copy in copies:
        copy.wait()


def finish_step(args):
    sds = jax.ShapeDtypeStruct
    matrices = [sds((6, ROWS, 2 * HW), F32), sds((ROWS, 2, 2 * HW), F32), sds((ROWS, 2, WIDE), F32)]
    vectors = [sds((10, 2 * HW), F32), sds((11, D), F32), sds((WIDE // 128, 128), F32)]
    blocks = [sds((2, TOK, D), BF), sds((2, TOK, D), F32), sds((2, TOK, D), F32)]
    return pl.pallas_call(
        finish_kernel,
        out_shape=matrices + matrices + vectors + vectors + blocks + [sds((6, 2, D), F32)],
        in_specs=[VM] * len(args),
        out_specs=[VM] * 13 + [HB] * 2 + [VM],
        scratch_shapes=[pltpu.VMEM((4, TOK, D), F32), pltpu.SemaphoreType.DMA((4,))],
        compiler_params=pltpu.CompilerParams(vmem_limit_bytes=VMEM_LIMIT),
        name="finish",
    )(*args)


def rope_rates():
    pair = np.arange(HEAD // 2)
    side = HEAD // 6
    frame = (HEAD - 4 * side) // 2
    part = (pair >= frame).astype(np.int32) + (pair >= frame + side)
    offset = np.array([0, frame, frame + side])[part]
    extent = np.array([2 * frame, 2 * side, 2 * side])[part]
    rate = np.exp((pair - offset) * (-2.0 * math.log(10000.0)) / extent).astype(np.float32)
    rates = np.zeros((8, HEAD), np.float32)
    for component in range(3):
        rates[component] = np.tile(np.where(part == component, rate, 0.0), 2)
    return jnp.asarray(rates)


def plain_norm(values):
    centred = values - jnp.mean(values, -1, keepdims=True)
    inverse = lax.rsqrt(jnp.mean(centred * centred, -1, keepdims=True) + NORM_EPSILON)
    return (centred * inverse, inverse)


def norm_back(grads, normed, inverse):
    return inverse * (
        grads
        - jnp.mean(grads, -1, keepdims=True)
        - normed * jnp.mean(grads * normed, -1, keepdims=True)
    )


def product(left, right):
    return jnp.dot(left, right, preferred_element_type=F32)


def contract_last(left, right):
    return lax.dot_general(left, right, (((1,), (1,)), ((), ())), preferred_element_type=F32)


def contract_rows(left, right):
    return lax.dot_general(left, right, (((0,), (0,)), ((), ())), preferred_element_type=F32)


def body(
    tokens, text, time_embedding, positions, cotangent, attn_in, attn_out, mlp, head_vectors,
    model_vectors, up_bias, attn_in_moment, attn_out_moment, mlp_moment, head_moment, model_moment,
    up_moment,
):
    swap = lambda v: v.transpose(1, 0, 2)
    (
        w_attn, w_up, w_down, cot_all, heads, vectors, tab_all, input_one, input_three, input_mlp, query_lin, key_lin,
        query_two_lin, key_two_lin, inv, query_rot, key_rot, value_low, query_two, key_two, value_two,
        mixed_low, mixed_two_low, branch_one, after_one, after_two, tok_all, txt_all,
    ) = forward(
        swap(attn_in), attn_out, mlp, tokens, text, cotangent, positions, rope_rates(),
        swap(time_embedding), model_vectors, head_vectors,
    )
    low_two, grad_after, sums, up_sum, result, *owned = mlp_pass(
        input_mlp, cot_all, w_up, w_down, after_two, vectors, up_bias.reshape(-1, 128)
    )
    out_result, out_tokens, out_words, time_sums, model_sums, head_totals, narrow, wide, gram = backward(
        [
            w_attn, low_two, after_one, branch_one, query_lin, key_lin, query_two_lin, key_two_lin,
            query_rot, key_rot, value_low, query_two, key_two, value_two, mixed_low, mixed_two_low,
            txt_all, input_three, input_one, tok_all, grad_after, tab_all, inv, result,
        ],
        [
            vectors, heads, sums, up_sum, *owned, swap(attn_in_moment), attn_out_moment, mlp_moment,
        ],
    )
    (
        new_in, new_out, new_mlp, new_in_m, new_out_m, new_mlp_m, new_head, new_model, new_up,
        new_head_m, new_model_m, new_up_m, out_result, out_tokens, out_words, out_time,
    ) = finish_step(
        [
            narrow, wide, gram, swap(attn_in), attn_out, mlp, head_vectors, head_moment, model_vectors,
            model_moment, up_bias.reshape(-1, 128), up_moment.reshape(-1, 128), head_totals, model_sums, out_result,
            out_tokens, out_words, time_sums,
        ]
    )
    return (
        out_result, out_tokens, out_words, swap(out_time), swap(new_in), new_out, new_mlp,
        swap(new_in_m), new_out_m, new_mlp_m, new_head, new_model, new_up.reshape(-1), new_head_m,
        new_model_m, new_up_m.reshape(-1),
    )


def solution(mesh):
    clip = P("fsdp", "ctx", None)
    whole = P("fsdp", None, None)
    matrix = P(("fsdp", "ctx"), None, "tp")
    in_specs = (
        clip, clip, whole, P(None, "fsdp", "ctx"), clip, matrix, matrix, matrix, P(None, "tp"), P(),
        P("tp"), matrix, matrix, matrix, P(None, "tp"), P(), P("tp"),
    )
    out_specs = (
        clip, clip, clip, whole, matrix, matrix, matrix, matrix, matrix, matrix, P(None, "tp"), P(),
        P("tp"), P(None, "tp"), P(), P("tp"),
    )
    return jax.shard_map(body, mesh=mesh, in_specs=in_specs, out_specs=out_specs, check_vma=False)
```

```python
from functools import partial
import math

import jax
import jax.numpy as jnp
import numpy as np
from jax import lax
from jax.experimental import pallas as pl
from jax.experimental.pallas import tpu as pltpu
from jax.sharding import PartitionSpec as P

D = 1536
HEAD = 128
ROWS = 24
HEADS = 3
NORM_EPSILON = 1e-06
ORTHO_EPSILON = 1e-07
NEWTON_FIRST = 3.4445
NEWTON_SECOND = -4.775
NEWTON_THIRD = 2.0315
NS_STEPS = 5
MOMENTUM = 0.9
DECAY = 0.01
RATE_IN = 0.5
RATE_OUT = 4.0
RATE_MLP = 1.0
RATE_VECTOR = 0.005
HIGHEST = lax.Precision.HIGHEST

MESH = pl.DeviceIdType.MESH
BF = jnp.bfloat16
F32 = jnp.float32

SIDE = 4
TOK = 128
SEQ = SIDE * TOK
HW = HEADS * HEAD
FF_REAL = 2240
FF = 2304
WIDE = 2 * FF_REAL
PAIR = 2 * ROWS
VMEM_LIMIT = 60 * 1024 * 1024


def here():
    f = lax.axis_index("fsdp")
    c = lax.axis_index("ctx")
    t = lax.axis_index("tp")
    x, y = lax.div(f, SIDE), lax.rem(f, SIDE)
    zl, core = lax.div(c, 2), lax.rem(c, 2)
    return x, y, 2 * t + zl, core


def chip(x, y, z, core):
    x, y, z = lax.rem(x + SIDE, SIDE), lax.rem(y + SIDE, SIDE), lax.rem(z + SIDE, SIDE)
    return {"fsdp": x * SIDE + y, "ctx": lax.rem(z, 2) * 2 + core, "tp": lax.div(z, 2)}


def block_of(z):
    z = lax.rem(z + SIDE, SIDE)
    return 2 * lax.rem(z, 2) + lax.div(z, 2)


def knock(devices):
    barrier = pltpu.get_barrier_semaphore()
    for device in devices:
        pl.semaphore_signal(barrier, inc=1, device_id=device, device_id_type=MESH)
    return lambda: pl.semaphore_wait(barrier, len(devices))


def greet(devices):
    knock(devices)()


def column(x, y, z, core):
    return [chip(x, y, z + k, core) for k in (1, 2, 3)] + [
        chip(x, y, z + k, 1 - core) for k in range(4)
    ]


def remote(src, dst, send, recv, device):
    return pltpu.make_async_remote_copy(
        src_ref=src, dst_ref=dst, send_sem=send, recv_sem=recv, device_id=device, device_id_type=MESH
    )


def params(cid):
    return pltpu.CompilerParams(
        collective_id=cid, has_side_effects=True, vmem_limit_bytes=VMEM_LIMIT
    )


VM = pl.BlockSpec(memory_space=pltpu.VMEM)
HB = pl.BlockSpec(memory_space=pltpu.HBM)


def flat(a, b):
    return lax.rem(a + SIDE, SIDE) * SIDE + lax.rem(b + SIDE, SIDE)


def steps_of(x, y, z, core):
    return (
        (chip(x + 1, y, z, core), chip(x - 1, y, z, core)),
        (chip(x, y + 1, z, core), chip(x, y - 1, z, core)),
    )


def gather_xy(own, place, xs, xr, ks, kr):
    x, y, z, core = here()
    mine = x * SIDE + y
    steps = steps_of(x, y, z, core)
    far_x, far_y = chip(x + 2, y, z, core), chip(x, y + 2, z, core)
    sibling = chip(x, y, z, 1 - core)
    sends, sibs = [], []

    def push(part, slot, src, index, device, half=None):
        copy = remote(src, place(part, index, half), xs.at[part, slot], xr.at[part, slot], device)
        copy.start()
        sends.append(copy)
        return copy

    def to_sibling(part, slot, src, index):
        copy = remote(src, place(part, index), ks.at[part, slot], kr.at[part, slot], sibling)
        copy.start()
        sibs.append(copy)

    def index_of(part, first_off, second_off):
        if part == 0:
            return flat(x + first_off, y + second_off)
        return flat(x + second_off, y + first_off)

    one, two = {}, {}
    for part in (0, 1):
        one[part, "far"] = push(part, 2, own.at[part], mine, (far_x, far_y)[part])
    for part in (0, 1):
        a_next, a_prev = steps[part]
        one[part, "next"] = push(part, 0, own.at[part], mine, a_next)
        one[part, "prev"] = push(part, 1, own.at[part], mine, a_prev)
    for part in (0, 1):
        to_sibling(part, 0, own.at[part], mine)
    offsets = (0, -1, 1, 2)

    def second_start(part, k):
        b_next, b_prev = steps[1 - part]
        index = index_of(part, offsets[k], 0)
        src = place(part, index) if k else own.at[part]
        two[part, k, "next"] = push(part, 4 + 4 * k, src, index, b_next)
        two[part, k, "prev"] = push(part, 5 + 4 * k, src, index, b_prev)

    def second_forward(part, k):
        b_next, b_prev = steps[1 - part]
        two[part, k, "next"].wait_recv()
        index = index_of(part, offsets[k], -1)
        two[part, k, "far0"] = push(part, 6 + 4 * k, place(part, index, 0), index, b_next, 0)
        to_sibling(part, 4 * k + 1, place(part, index), index)
        two[part, k, "prev"].wait_recv()
        index = index_of(part, offsets[k], 1)
        two[part, k, "far1"] = push(part, 7 + 4 * k, place(part, index, 1), index, b_prev, 1)
        to_sibling(part, 4 * k + 2, place(part, index), index)

    def second_finish(part, k):
        two[part, k, "far0"].wait_recv()
        two[part, k, "far1"].wait_recv()
        index = index_of(part, offsets[k], 2)
        to_sibling(part, 4 * k + 3, place(part, index), index)

    for part in (0, 1):
        second_start(part, 0)
    yield
    for part in (0, 1):
        one[part, "next"].wait_recv()
        one[part, "prev"].wait_recv()
        second_start(part, 1)
        for k in (1, 2):
            index = index_of(part, offsets[k], 0)
            to_sibling(part, 4 * k, place(part, index), index)
    yield
    for part in (0, 1):
        second_forward(part, 0)
        second_start(part, 2)
    yield
    for part in (0, 1):
        one[part, "far"].wait_recv()
        index = index_of(part, 2, 0)
        to_sibling(part, 12, place(part, index), index)
        second_forward(part, 1)
        second_start(part, 3)
    yield
    for part in (0, 1):
        second_forward(part, 2)
        second_finish(part, 0)
    yield
    for part in (0, 1):
        second_forward(part, 3)
        second_finish(part, 1)
    yield
    for part in (0, 1):
        second_finish(part, 2)
    yield
    for part in (0, 1):
        second_finish(part, 3)
    yield
    for copy in sends:
        copy.wait_send()
    for copy in sibs:
        copy.wait_send()
        copy.wait_recv()


GATHER_SEMS = ((2, 20), (2, 20), (2, 16), (2, 16))


def advance(job, count=1):
    for _ in range(count):
        next(job, None)


def finish(job):
    for _ in job:
        pass


def share_rows(send, recv, s, r, l):
    x, y, z, core = here()
    zl = lax.rem(z, 2)
    away = remote(send.at[1 - zl], recv.at[core], s.at[0], r.at[core], chip(x, y, z + 1 - 2 * zl, zl))
    near = remote(send.at[zl], recv.at[core], s.at[1], r.at[core], chip(x, y, z, zl))
    self_copy = pltpu.make_async_copy(send.at[zl], recv.at[core], l.at[0])

    def got(slot):
        remote(send.at[0], recv.at[slot], s.at[0], r.at[slot], chip(x, y, z, core)).wait_recv()

    def start():
        away.start()

        @pl.when(core == zl)
        def _():
            self_copy.start()

        @pl.when(core != zl)
        def _():
            near.start()

    def wait(own):
        @pl.when(core == zl)
        def _():
            self_copy.wait()
            got(1 - core)

        @pl.when(core != zl)
        def _():
            near.wait_send()
            got(0)
            got(1)

        first = recv[0].astype(F32)
        second = recv[1].astype(F32)
        own[0] = jnp.concatenate([first[:ROWS], second[:ROWS]], 0).astype(BF)
        own[1] = jnp.concatenate([first[ROWS:], second[ROWS:]], 0).astype(BF)

    return start, wait, away.wait_send


def share_clip(src, dst, s, r, l):
    x, y, z, core = here()
    put = dst.at[2 * lax.rem(z, 2) + core]
    copies = [
        remote(src.at[1 - core], put, s.at[0], r.at[0], chip(x, y, z, 1 - core)),
        remote(src.at[0], put, s.at[1], r.at[1 + core], chip(x, y, z + 1, 0)),
        remote(src.at[1], put, s.at[2], r.at[1 + core], chip(x, y, z - 1, 1)),
    ]
    local = pltpu.make_async_copy(src.at[core], put, l)

    def start():
        for copy in copies:
            copy.start()
        local.start()

    def wait():
        local.wait()
        for slot in range(3):
            remote(src.at[0], dst.at[0], s.at[0], r.at[slot], chip(x, y, z, core)).wait_recv()

    def drain():
        for copy in copies:
            copy.wait_send()

    return start, wait, drain


def split3(values):
    return [values[:, i * HW : (i + 1) * HW] for i in range(values.shape[1] // HW)]


def swap_halves(values):
    return pltpu.roll(values, HEAD // 2, 1)


def rope_pair(table):
    lane = lax.broadcasted_iota(jnp.int32, table.shape, 1)
    other = swap_halves(table)
    front = lane < HEAD // 2
    return jnp.where(front, table, other), jnp.where(front, -other, table)


def head_slice(h):
    return slice(h * HEAD, (h + 1) * HEAD)


SCALE = HEAD ** (-0.5)


def softmax_rows(query, keys):
    scores = contract_last(query, keys) * SCALE
    peak = jnp.max(scores, -1, keepdims=True)
    raised = jnp.exp(scores - peak)
    return raised * (1.0 / jnp.sum(raised, -1, keepdims=True))


def attend_clip(query, keys, values, out):
    for h in range(HEADS):
        cols = head_slice(h)
        for start in range(0, SEQ, 256):
            rows = slice(start, start + 256)
            weights = softmax_rows(query[rows, cols], keys[:, cols]).astype(BF)
            out[rows, cols] = product(weights, values[:, cols]).astype(BF)


class Stats:
    def __init__(self, buffer, send, recv):
        self.buffer, self.send, self.recv = buffer, send, recv

    def start(self, turn, columns):
        x, y, z, core = here()
        lane = lax.broadcasted_iota(jnp.int32, (SEQ, 128), 1)
        packed = jnp.zeros((SEQ, 128), F32)
        for i, column_values in enumerate(columns):
            packed = jnp.where(lane == i, column_values, packed)
        self.buffer[turn, 0] = packed.T[:8]
        copies = []
        for k in (2, 1, 3):
            copies.append(
                remote(self.buffer.at[turn, 0], self.buffer.at[turn, k], self.send.at[turn, k - 1],
                       self.recv.at[turn, k - 1], chip(x, y, z + k, core))
            )
            copies[-1].start()

        def wait():
            for copy in copies:
                copy.wait()
            total = (self.buffer[turn, 0] + self.buffer[turn, 1]) + (
                self.buffer[turn, 2] + self.buffer[turn, 3]
            )
            spread = jnp.concatenate([total, jnp.zeros((120, SEQ), F32)], 0).T
            return [spread[:, i : i + 1] for i in range(len(columns))]

        return wait


def block_slice(index):
    return pl.ds(pl.multiple_of(index * TOK, TOK), TOK)


HALF = TOK // 2


def half_rows(block, half):
    return pl.ds(pl.multiple_of(block * TOK + half * HALF, HALF), HALF)


class Scatter:
    def __init__(self, part, got, send, recv):
        self.part, self.got, self.send, self.recv = part, got, send, recv
        self.x, self.y, self.z, self.core = here()
        self.copies, self.relayed = [], False

    def push(self, slot, rows, dst, step):
        device = chip(self.x, self.y, self.z + step, self.core)
        copy = remote(self.part.at[rows], dst, self.send.at[slot], self.recv.at[slot], device)
        copy.start()
        self.copies.append(copy)

    def stage(self, k):
        front, rear = pl.ds(0, HALF), pl.ds(HALF, HALF)
        block = block_of(self.z + k)
        if k == 2:
            self.push(0, half_rows(block, 0), self.got.at[2, front], 1)
            self.push(1, half_rows(block, 1), self.got.at[2, rear], -1)
        elif k == 1:
            self.push(2, half_rows(block, 1), self.got.at[0, rear], 1)
        elif k == 3:
            self.push(3, half_rows(block, 0), self.got.at[1, front], -1)

    def held(self):
        for k in (2, 1, 3):
            self.stage(k)
        return self

    def product(self, left, right):
        for k in (2, 1, 3, 0):
            rows = block_slice(block_of(self.z + k))
            self.part[rows] = contract_last(left[rows], right).astype(BF)
            self.stage(k)
        return self

    def relay(self):
        if self.relayed:
            return
        self.relayed = True
        for slot, step in ((0, 1), (1, -1)):
            span = pl.ds(slot * HALF, HALF)
            rows = half_rows(block_of(self.z + step), slot)
            self.copies[slot].wait_recv()
            total = self.part[rows].astype(F32) + self.got[2, span].astype(F32)
            self.part[rows] = total.astype(BF)
            self.push(4 + slot, rows, self.got.at[slot, span], step)

    def total(self):
        self.relay()
        for copy in self.copies[2:]:
            copy.wait_recv()
        own = self.part[block_slice(block_of(self.z))].astype(F32)
        return own + (self.got[0].astype(F32) + self.got[1].astype(F32))

    def drain(self):
        for copy in self.copies:
            copy.wait_send()


class Spread:
    def __init__(self, out, value, send, recv):
        self.out, self.send, self.recv = out, send, recv
        self.x, self.y, self.z, self.core = here()
        self.copies, self.relayed = [], False
        block = block_of(self.z)
        out[block_slice(block)] = value
        self.push(0, half_rows(block, 0), 1)
        self.push(1, half_rows(block, 1), -1)
        self.push(2, half_rows(block, 1), 1)
        self.push(3, half_rows(block, 0), -1)

    def push(self, slot, rows, step):
        device = chip(self.x, self.y, self.z + step, self.core)
        rows = self.out.at[rows]
        copy = remote(rows, rows, self.send.at[slot], self.recv.at[slot], device)
        copy.start()
        self.copies.append(copy)

    def relay(self):
        if self.relayed:
            return
        self.relayed = True
        for slot, step in ((0, 1), (1, -1)):
            self.copies[slot].wait_recv()
            self.push(4 + slot, half_rows(block_of(self.z - step), slot), step)

    def wait(self):
        self.relay()
        for copy in self.copies[2:]:
            copy.wait_recv()

    def drain(self):
        for copy in self.copies:
            copy.wait_send()


def inverse_root(total):
    return lax.rsqrt(total * (1.0 / D) + NORM_EPSILON)


V_SELF, V_CROSS, V_DOWN, V_GAIN, V_BIAS = 6, 7, 8, 9, 10
W_QKV, W_QUERY, W_TEXT, W_SELF, W_CROSS = (
    slice(0, 3 * HW), slice(3 * HW, 4 * HW), slice(4 * HW, 6 * HW), slice(6 * HW, 7 * HW), slice(7 * HW, 8 * HW),
)
ATTN = 8 * HW


SAVED = 22


def forward_kernel(
    in_w, out_w, mlp_w, tok, txt, cot, places, rates, time_in, model_in, head_in,
    w_attn, w_up, w_down, cot_all, heads_out, vec_out, *rest,
):
    saved, held, rest = rest[:SAVED], rest[SAVED : 2 * SAVED], rest[2 * SAVED :]
    (
        tab_all, input_one, input_three, input_mlp, query_lin, key_lin, query_two_lin, key_two_lin, inv,
        query_rot, key_rot, value_low, query_two, key_two, value_two, mixed, mixed_two, branch_one,
        after_one, after_two, tok_all, txt_all,
    ) = held
    (
        send_attn, send_mlp, tab, heads, vec, wa, got_attn, got_mlp, own_attn, own_mlp, part_one, part_two, blocks, stat,
        xs, xr, ks, kr, ms, mr, js, jr, rs, rr, cs, cr, loc, stat_s, stat_r, zs, zr, gs, gr, keep,
    ) = rest
    x, y, z, core = here()
    mine = x * SIDE + y
    stores = []

    def keep_small(ref, out, i):
        stores.append(pltpu.make_async_copy(ref, out, keep.at[SAVED + i]))
        stores[-1].start()

    def save(*refs):
        for ref in refs:
            i = [ref is other for other in held].index(True)
            stores.append(pltpu.make_async_copy(ref, saved[i], keep.at[i]))
            stores[-1].start()

    def packed(values, cores_chip):
        return values[:, cores_chip * HW : (cores_chip + 1) * HW]

    for i in (0, 1):
        rows = [
            jnp.concatenate([packed(in_w[j], i) for j in range(4)], 1),
            jnp.concatenate([packed(in_w[j], i) for j in (4, 5)] + [packed(out_w[:, j, :], i) for j in (0, 1)], 1),
        ]
        send_attn[i] = jnp.concatenate(rows, 0).astype(BF)
    greet(
        [device for pair in steps_of(x, y, z, core) for device in pair]
        + [chip(x + 2, y, z, core), chip(x, y + 2, z, core)]
        + column(x, y, z, core)
    )
    attn_start, attn_wait, attn_drain = share_rows(send_attn, got_attn, rs.at[0], rr.at[0], loc.at[0])
    mlp_start, mlp_wait, mlp_drain = share_rows(send_mlp, got_mlp, rs.at[1], rr.at[1], loc.at[1])
    acts = [
        share_clip(src, dst, cs.at[i], cr.at[i], loc.at[2 + i, 0])
        for i, (src, dst) in enumerate(
            ((tok, tok_all), (tab, tab_all), (txt, txt_all), (cot, cot_all))
        )
    ]
    attn_start()
    acts[0][0]()
    zl = lax.rem(z, 2)
    for i in range(6):
        vec[i : i + 1] = model_in[5 + i : 6 + i] + time_in[i, pl.ds(core, 1)]
    vec[6:11] = model_in[0:5]
    vec[11:16] = jnp.zeros((5, D), F32)
    heads[0:10] = head_in[:, pl.ds(pl.multiple_of(zl * HW, HW), HW)]
    heads[10:16] = jnp.zeros((6, HW), F32)
    keep_small(heads, heads_out, 0)
    keep_small(vec, vec_out, 1)
    attn_wait(own_attn)

    def attn_place(part, index, half=None):
        start, size = part * (ATTN // 2), ATTN // 2
        if half is not None:
            start, size = start + half * (ATTN // 4), ATTN // 4
        rows = pl.ds(pl.multiple_of(index * (2 * PAIR) + core * PAIR, PAIR), PAIR)
        return wa.at[rows, pl.ds(start, size)]

    def mlp_place(part, index, half=None):
        start, size = (0, FF) if half is None else (half * (FF // 2), FF // 2)
        rows = pl.ds(pl.multiple_of(index * (2 * PAIR) + core * PAIR, PAIR), PAIR)
        return (w_up, w_down)[part].at[rows, pl.ds(start, size)]

    gather_attn = gather_xy(own_attn, attn_place, xs, xr, ks, kr)
    advance(gather_attn)
    for part in (0, 1):
        attn_place(part, mine)[...] = own_attn[part]
    acts[2][0]()
    fill = jnp.zeros((ROWS, 2 * FF - WIDE), F32)
    lane = lax.broadcasted_iota(jnp.int32, (ROWS, FF), 1)
    sides = ([], [])
    for j in (0, 1):
        whole = jnp.concatenate([mlp_w[:, j, :], fill], 1)
        sides[0].append(jnp.where(lane < FF_REAL, whole[:, :FF], 0.0))
        sides[1].append(pltpu.roll(whole, 2 * FF - FF_REAL, 1)[:, :FF])
    for i in (0, 1):
        send_mlp[i] = jnp.concatenate(sides[i], 0).astype(BF)
    mlp_start()
    lane = lax.broadcasted_iota(jnp.int32, (TOK, HEAD), 1)
    for i in (0, 1):
        spots = [places[c, i : i + 1, :].astype(F32) for c in range(3)]
        spots = jnp.concatenate(spots + [jnp.zeros((TOK - 3, TOK), F32)], 0).T
        angle = spots[:, 0:1] * rates[0:1] + spots[:, 1:2] * rates[1:2] + spots[:, 2:3] * rates[2:3]
        tab[i] = jnp.where(lane < HEAD // 2, jnp.cos(angle), jnp.sin(angle))
    acts[1][0]()

    def norm_block(i, carry):
        normed, _ = plain_norm(tok_all[i].astype(F32))
        input_one[block_slice(i)] = (normed * (1.0 + vec[1:2]) + vec[0:1]).astype(BF)
        return carry

    advance(gather_attn, 2)
    acts[3][0]()
    advance(gather_attn, 1)
    acts[0][1]()
    lax.fori_loop(0, 2, norm_block, 0)
    advance(gather_attn, 1)
    lax.fori_loop(2, 4, norm_block, 0)
    save(input_one, tok_all)
    advance(gather_attn, 1)
    mlp_wait(own_mlp)
    locals_ = []
    for part in (0, 1):
        locals_.append(pltpu.make_async_copy(own_mlp.at[part], mlp_place(part, mine), loc.at[6, part]))
        locals_[-1].start()
    advance(gather_attn, 1)
    gather_mlp = gather_xy(own_mlp, mlp_place, ms, mr, js, jr)
    advance(gather_mlp)
    finish(gather_attn)
    locals_.append(pltpu.make_async_copy(wa, w_attn, loc.at[7, 0]))
    locals_[-1].start()
    acts[1][1]()
    acts[2][1]()
    save(tab_all, txt_all)

    stats = Stats(stat, stat_s, stat_r)
    query_lin[...] = product(input_one[...], wa[:, 0:HW]) + heads[0:1]
    key_lin[...] = product(input_one[...], wa[:, HW : 2 * HW]) + heads[1:2]
    words = txt_all[...].reshape(SEQ, D)
    key_two_lin[...] = product(words, wa[:, 4 * HW : 5 * HW]) + heads[6:7]
    norm_wait = stats.start(
        0,
        [
            jnp.sum(ref[...] * ref[...], -1, keepdims=True)
            for ref in (query_lin, key_lin, key_two_lin)
        ],
    )
    value_low[...] = (product(input_one[...], wa[:, 2 * HW : 3 * HW]) + heads[2:3]).astype(BF)
    value_two[...] = (product(words, wa[:, 5 * HW : 6 * HW]) + heads[7:8]).astype(BF)
    save(query_lin, key_lin, key_two_lin, value_low, value_two)
    lane = lax.broadcasted_iota(jnp.int32, (SEQ, 128), 1)
    inverse_query, inverse_key, inverse_key_two = [inverse_root(v) for v in norm_wait()]
    inv[...] = jnp.where(
        lane == 0, inverse_query, jnp.where(lane == 1, inverse_key, jnp.where(lane == 2, inverse_key_two, 0.0))
    )
    cosine, sine = rope_pair(tab_all[...].reshape(SEQ, HEAD))
    for h in range(HEADS):
        cols = head_slice(h)
        for lin, inverse, gain, out in (
            (query_lin, inverse_query, 3, query_rot),
            (key_lin, inverse_key, 4, key_rot),
        ):
            value = lin[:, cols] * inverse * (1.0 + heads[gain : gain + 1, cols])
            out[:, cols] = (value * cosine + swap_halves(value) * sine).astype(BF)
    advance(gather_mlp, 1)
    attend_clip(query_rot, key_rot, value_low, mixed)
    scatter = Scatter(part_one, blocks.at[0], zs.at[0], zr.at[0]).product(mixed, wa[:, W_SELF])
    drains = [scatter]
    key_two[...] = (key_two_lin[...] * inverse_key_two * (1.0 + heads[9:10])).astype(BF)
    save(query_rot, key_rot, key_two, mixed)
    advance(gather_mlp, 1)
    scatter.relay()
    advance(gather_mlp, 2)
    branch = scatter.total() + vec[V_SELF : V_SELF + 1]
    branch_one[...] = branch
    after = tok_all[block_of(z)].astype(F32) + vec[2:3] * branch
    after_one[...] = after
    normed, _ = plain_norm(after)
    spread = Spread(
        input_three,
        (normed * (1.0 + vec[V_GAIN : V_GAIN + 1]) + vec[V_BIAS : V_BIAS + 1]).astype(BF),
        gs.at[0],
        gr.at[0],
    )
    drains.append(spread)
    save(branch_one, after_one)
    advance(gather_mlp, 1)
    spread.relay()
    finish(gather_mlp)
    spread.wait()
    query_two_lin[...] = product(input_three[...], wa[:, W_QUERY]) + heads[5:6]
    norm_wait = stats.start(1, [jnp.sum(query_two_lin[...] * query_two_lin[...], -1, keepdims=True)])
    save(input_three, query_two_lin)
    inverse_query_two = inverse_root(norm_wait()[0])
    inv[...] = jnp.where(lane == 3, inverse_query_two, inv[...])
    query_two[...] = (query_two_lin[...] * inverse_query_two * (1.0 + heads[8:9])).astype(BF)
    attend_clip(query_two, key_two, value_two, mixed_two)
    scatter = Scatter(part_two, blocks.at[1], zs.at[1], zr.at[1]).product(mixed_two, wa[:, W_CROSS])
    drains.append(scatter)
    save(inv, query_two, mixed_two)
    after = after_one[...] + scatter.total() + vec[V_CROSS : V_CROSS + 1]
    after_two[...] = after
    normed, _ = plain_norm(after)
    spread = Spread(
        input_mlp, (normed * (1.0 + vec[4:5]) + vec[3:4]).astype(BF), gs.at[1], gr.at[1]
    )
    drains.append(spread)
    save(after_two)
    spread.relay()
    for copy in locals_:
        copy.wait()
    acts[3][1]()
    for act in acts:
        act[2]()
    attn_drain()
    mlp_drain()
    spread.wait()
    save(input_mlp)
    for transfer in drains:
        transfer.drain()
    for copy in stores:
        copy.wait()


def forward(*args):
    dma = pltpu.SemaphoreType.DMA
    sds = jax.ShapeDtypeStruct
    wide, lin, low = sds((SEQ, D), BF), sds((SEQ, HW), F32), sds((SEQ, HW), BF)
    block = sds((TOK, D), F32)
    outs = [
        sds((SIDE, TOK, HEAD), F32), wide, wide, wide, lin, lin, lin, lin, sds((SEQ, 128), F32),
        low, low, low, low, low, low, low, low, block, block, block,
        sds((SIDE, TOK, D), BF), sds((SIDE, TOK, D), BF),
    ]
    weights = [
        sds((D, ATTN), BF), sds((D, FF), BF), sds((D, FF), BF), sds((SIDE, TOK, D), BF),
        sds((16, HW), F32), sds((16, D), F32),
    ]
    return pl.pallas_call(
        forward_kernel,
        out_shape=weights + outs,
        in_specs=[VM, VM, VM, HB, HB, HB, VM, VM, VM, VM, VM],
        out_specs=[HB] * (len(weights) + len(outs)),
        scratch_shapes=[
            *[pltpu.VMEM(shape.shape, shape.dtype) for shape in outs],
            pltpu.VMEM((2, PAIR, ATTN // 2), BF), pltpu.VMEM((2, PAIR, FF), BF),
            pltpu.VMEM((2, TOK, HEAD), F32), pltpu.VMEM((16, HW), F32), pltpu.VMEM((16, D), F32),
            pltpu.VMEM((D, ATTN), BF),
            pltpu.VMEM((2, PAIR, ATTN // 2), BF),
            pltpu.VMEM((2, PAIR, FF), BF),
            pltpu.VMEM((2, PAIR, ATTN // 2), BF),
            pltpu.VMEM((2, PAIR, FF), BF),
            pltpu.VMEM((SEQ, D), BF),
            pltpu.VMEM((SEQ, D), BF),
            pltpu.VMEM((2, 3, TOK, D), BF),
            pltpu.VMEM((2, 4, 8, SEQ), F32),
            *[dma(s) for s in GATHER_SEMS],
            *[dma(s) for s in GATHER_SEMS],
            dma((2, 2)), dma((2, 2)), dma((4, 3)), dma((4, 3)), dma((8, 2)),
            dma((2, 3)), dma((2, 3)), dma((2, 6)), dma((2, 6)), dma((2, 6)), dma((2, 6)),
            dma((SAVED + 2,)),
        ],
        compiler_params=params(0),
        name="forward",
    )(*args)


BATCH = 768


def peers_xy(x, y, z, core):
    rows = [chip(x + k, y, z, core) for k in (1, 2, 3)]
    lines = [chip(x, y + k, z, core) for k in (1, 2, 3)]
    return rows, lines


def reduce_batch(grads, out, sib, r1, r2, tosend, ss, sr, s1, q1, s2, q2, *swap_sems, gates=None):
    x, y, z, core = here()
    zl = lax.rem(z, 2)
    rows, lines = peers_xy(x, y, z, core)
    sibling = chip(x, y, z, 1 - core)
    wrap = lambda v: lax.rem(v, SIDE)
    swaps, one, two = [], {0: [], 1: []}, {0: [], 1: []}
    opens, waits = gates if gates is not None else (None, None)

    def signal(gate, devices):
        for device in devices:
            pl.semaphore_signal(gate, inc=1, device_id=device, device_id_type=MESH)

    def push(part, slot, target, half, place, step):
        span = pl.ds(2 * half, 2)
        src = (
            grads.at[0, span, wrap(y + target), core]
            if part == 0
            else grads.at[1, wrap(x + target), span, core]
        )
        device = (lines, rows)[part][step - 1]
        copy = remote(src, r1.at[part, place, span], s1.at[part, slot], q1.at[part, slot], device)
        copy.start()
        one[part].append(copy)

    if waits is not None:
        pl.semaphore_wait(waits[0], 1)
    for part in (0, 1):
        swaps.append(
            remote(grads.at[part, :, :, 1 - core], sib.at[part], ss.at[part], sr.at[part], sibling)
        )
        swaps[part].start()
    yield
    for part in (0, 1):
        swaps[part].wait_recv()

        def add_pair(k, carry):
            a, b = lax.div(k, SIDE), lax.rem(k, SIDE)
            grads[part, a, b, core] = grads[part, a, b, core] + sib[part, a, b]
            return carry

        lax.fori_loop(0, SIDE * SIDE, add_pair, 0)
        if part == 0 and waits is not None:
            pl.semaphore_wait(waits[1], 6)
        push(part, 0, 2, 0, 2, 1)
        push(part, 1, 2, 1, 2, 3)
        push(part, 2, 1, 1, 0, 1)
        push(part, 3, 3, 0, 1, 3)
    if opens is not None:
        signal(opens[0], [sibling])
    yield
    for part in (0, 1):
        for slot, step in ((0, 1), (1, 3)):
            one[part][slot].wait_recv()
            for i in (2 * slot, 2 * slot + 1):
                if part == 0:
                    grads[0, i, wrap(y + step), core] = grads[0, i, wrap(y + step), core] + r1[0, 2, i]
                else:
                    grads[1, wrap(x + step), i, core] = grads[1, wrap(x + step), i, core] + r1[1, 2, i]
            push(part, 4 + slot, step, slot, slot, step)
    yield
    for part in (0, 1):
        for copy in one[part][2:]:
            copy.wait_recv()

        def add_line(k, carry):
            a, b = (k, y) if part == 0 else (x, k)
            total = grads[part, a, b, core].astype(F32)
            total = total + (r1[part, 0, k].astype(F32) + r1[part, 1, k].astype(F32))
            grads[part, a, b, core] = total.astype(BF)
            return carry

        lax.fori_loop(0, SIDE, add_line, 0)
        for k in (2, 1, 3):
            src = grads.at[0, wrap(x + k), y, core] if part == 0 else grads.at[1, x, wrap(y + k), core]
            device = (rows, lines)[part][k - 1]
            copy = remote(src, r2.at[part, k - 1], s2.at[part, k - 1], q2.at[part, k - 1], device)
            copy.start()
            two[part].append(copy)
    yield
    final = []
    for part in (0, 1):
        for copy in two[part]:
            copy.wait_recv()
        total = grads[part, x, y, core].astype(F32)
        for i in range(3):
            total = total + r2[part, i].astype(F32)
        final.append(total)
    if opens is not None:
        signal(opens[1], [*rows, *lines])
    for target in (0, 1):
        span = slice(target * ROWS, target * ROWS + ROWS)
        tosend[target] = jnp.concatenate([final[0][span], final[1][span]], 0).astype(tosend.dtype)
    if out is not None:
        exchange = swap_rows(tosend, out, *swap_sems)
        next(exchange)
        yield
        finish(exchange)
    for copy in swaps + one[0] + one[1] + two[0] + two[1]:
        copy.wait_send()


def swap_rows(owned, out, s3, q3, l3):
    x, y, z, core = here()
    zl = lax.rem(z, 2)
    other = z + 1 - 2 * zl
    far = [
        remote(owned.at[t], out.at[zl], s3.at[t], q3.at[zl], chip(x, y, other, t)) for t in (0, 1)
    ]
    self_copy = pltpu.make_async_copy(owned.at[core], out.at[zl], l3.at[0])
    near = remote(owned.at[1 - core], out.at[zl], s3.at[0], q3.at[zl], chip(x, y, z, 1 - core))

    def got(slot):
        remote(owned.at[0], out.at[slot], s3.at[0], q3.at[slot], chip(x, y, z, core)).wait_recv()

    @pl.when(core == zl)
    def _():
        self_copy.start()
        near.start()

    @pl.when(core != zl)
    def _():
        for copy in far:
            copy.start()

    yield

    @pl.when(core == zl)
    def _():
        self_copy.wait()
        near.wait_send()
        got(1 - zl)

    @pl.when(core != zl)
    def _():
        for copy in far:
            copy.wait_send()
        got(zl)
        got(1 - zl)


def reduce_buffers():
    return [
        pltpu.VMEM((2, SIDE, SIDE, PAIR, BATCH), BF),
        pltpu.VMEM((2, 3, SIDE, PAIR, BATCH), BF),
        pltpu.VMEM((2, 3, PAIR, BATCH), BF),
    ]


def reduce_sems():
    dma = pltpu.SemaphoreType.DMA
    return [dma((2,)), dma((2,)), dma((2, 6)), dma((2, 6)), dma((2, 3)), dma((2, 3))]


def swap_sems():
    dma = pltpu.SemaphoreType.DMA
    return [dma((2,)), dma((2,)), dma((1,))]


def reduce_scratch():
    return [*reduce_buffers(), pltpu.VMEM((2, PAIR, BATCH), BF), *reduce_sems(), *swap_sems()]


GRADS = (2, SIDE, SIDE, 2, PAIR, BATCH)
SLAB = D // SIDE


def weight_grad(left, right, grads, part, start):
    width = right.shape[1]

    def slab(i, carry):
        turned = left[:, pl.ds(pl.multiple_of(i * SLAB, SLAB), SLAB)].T
        value = product(turned, right).astype(BF).reshape(SIDE, 2, PAIR, width)
        grads[part, i, :, :, :, start : start + width] = value
        return carry

    lax.fori_loop(0, SIDE, slab, 0)


def column_sum(values):
    return jnp.sum(values.astype(F32), 0, keepdims=True)


def deliver(src, dst, s, r, l):
    x, y, z, core = here()
    zh = lax.div(z, 2)
    far = remote(src, dst.at[core], s.at[0], r.at[core], chip(x, y, z + 2, zh))
    near = remote(src, dst.at[core], s.at[1], r.at[core], chip(x, y, z, zh))
    self_copy = pltpu.make_async_copy(src, dst.at[core], l)

    def got(slot):
        remote(src, dst.at[slot], s.at[0], r.at[slot], chip(x, y, z, core)).wait_recv()

    def start():
        far.start()

        @pl.when(core == zh)
        def _():
            self_copy.start()

        @pl.when(core != zh)
        def _():
            near.start()

    def wait():
        @pl.when(core == zh)
        def _():
            self_copy.wait()
            got(1 - core)

        @pl.when(core != zh)
        def _():
            near.wait_send()
            got(0)
            got(1)

        far.wait_send()

    return start, wait


CUBE = 0.044715
ROOT = math.sqrt(2.0 / math.pi)


def gelu_pair(u):
    square = u * u
    t = jnp.tanh(ROOT * u * (1.0 + CUBE * square))
    half = 0.5 * (1.0 + t)
    return u * half, half + 0.5 * u * (1.0 - t * t) * (ROOT * (1.0 + 3.0 * CUBE * square))


def mlp_kernel(
    a_in, cot_all, w_up, w_down, after_in, vec, up_bias,
    low_out, grad_out, sums_out, bias_out, result_out, owned_a_out, owned_b_out, owned_c_out,
    grad_after, sums, bias_sum, owned_a, owned_b, owned_c, keep, a, low, ahead, behind, hidden, act, back, acc, part, part_back, after_two, low_two, result, dy_own,
    blocks, bias, zs, zr, gs, gr, loc, ring, gate_core, gate_chips, *rest,
):
    x, y, z, core = here()
    rows, lines = peers_xy(x, y, z, core)
    own_rows = block_slice(block_of(z))

    def load(src, dst, sem):
        copy = pltpu.make_async_copy(src, dst, sem)
        copy.start()
        return copy

    def third(n):
        return pl.ds(n % 3 * BATCH, BATCH)

    def weights(n):
        return ahead.at[n % 2].reshape(D, BATCH)

    def load_ahead(n):
        return load((w_up, w_down)[n // 3].at[:, third(n)], weights(n), ring.at[0, n % 2])

    def load_behind(n):
        return load((w_down, w_up)[n // 3].at[:, third(n)], behind.at[n % 2], ring.at[1, n % 2])

    stores = []

    def save(ref, out):
        stores.append(load(ref, out, keep.at[len(stores)]))

    aheads, behinds = {0: load_ahead(0)}, {}
    fetch_a = load(a_in, a, loc.at[0])
    arrive = knock(column(x, y, z, core) + rows + lines)
    line = jnp.concatenate(
        [up_bias[i : i + 1] for i in range(WIDE // 128)] + [jnp.zeros((1, 2 * FF - WIDE), F32)], 1
    )
    moved_line = pltpu.roll(line, 2 * FF - FF_REAL, 1)
    lane = lax.broadcasted_iota(jnp.int32, (1, FF), 1)
    line = jnp.where(lax.rem(z, 2) == 0, line[:, :FF], moved_line[:, :FF])
    bias[0:1] = jnp.where(lane < FF_REAL, line, 0.0)
    sums[...] = jnp.zeros_like(sums)
    fetch_a.wait()
    aheads[0].wait()
    aheads[1], behinds[0] = load_ahead(1), load_behind(0)
    fetch_low = load(cot_all.reshape(SEQ, D), low, loc.at[1])
    behinds[1] = load_behind(1)
    fetch_after = load(after_in, after_two, loc.at[2])
    hidden[0] = product(a[...], weights(0)[...])
    aheads[2] = load_ahead(2)
    dy = dy_own

    grads = [rest[0], rest[1], ahead]
    gates = (gate_core, gate_chips)
    first, second, sems = rest[2:5], rest[5:8], rest[8:]
    owned = (owned_a, owned_b, owned_c)
    jobs = [
        reduce_batch(
            grads[b], None, *(first, second, first)[b], owned[b], *sems[6 * b : 6 * b + 6],
            gates=((gates, None), None, (None, gates))[b],
        )
        for b in range(3)
    ]

    def step(n):
        if n < 5:
            aheads[n + 1].wait()
            left = a if n < 2 else low
            behinds[n].wait()
            hidden[(n + 1) % 2] = product(left[...], weights(n + 1)[...])
        else:
            behinds[n].wait()
        cols = slice(n % 3 * BATCH, (n % 3 + 1) * BATCH)
        if n < 3:
            value, slope = gelu_pair(hidden[n % 2] + bias[0:1, cols])
            value = value.astype(BF)
            act[:, cols] = value
            back[:, cols] = slope.astype(BF)
        else:
            value = (hidden[n % 2] * back[:, cols].astype(F32)).astype(BF)
            back[:, cols] = value
            bias_sum[0:1, cols] = column_sum(value)
        moved = contract_last(value, behind[n % 2])
        if n % 3 == 0:
            acc[...] = moved
        elif n % 3 == 1:
            acc[...] += moved
        else:
            (part, part_back)[n // 3][...] = (acc[...] + moved).astype(BF)
        if n < 3:
            aheads[n + 3] = load_ahead(n + 3)
        if n < 4:
            behinds[n + 2] = load_behind(n + 2)

    def third_grads(n, b, half):
        cols = slice(n % 3 * BATCH, (n % 3 + 1) * BATCH)
        left, right = ((low, act), (a, back))[n // 3]
        weight_grad(left, right[:, cols], grads[b], half, 0)

    step(0)
    fetch_low.wait()
    dy_own[...] = low[own_rows].astype(F32)
    for start in range(0, SEQ, TOK):
        block = slice(start, start + TOK)
        low[block] = (low[block].astype(F32) * vec[5:6]).astype(BF)
    sums[2:3] = column_sum(low[own_rows])
    step(1)
    third_grads(0, 0, 0)
    third_grads(1, 0, 1)
    arrive()
    advance(jobs[0])
    step(2)
    down_sum = Scatter(part, blocks.at[0], zs.at[0], zr.at[0]).held()
    advance(jobs[0])
    third_grads(2, 1, 0)
    step(3)
    advance(jobs[0])
    third_grads(3, 1, 1)
    advance(jobs[1])
    down_sum.relay()
    step(4)
    advance(jobs[0])
    advance(jobs[1])
    step(5)
    back_sum = Scatter(part_back, blocks.at[1], zs.at[1], zr.at[1]).held()
    save(bias_sum, bias_out)
    third_grads(4, 2, 0)
    third_grads(5, 2, 1)
    advance(jobs[2])
    finish(jobs[0])
    save(owned_a, owned_a_out)
    back_sum.relay()
    advance(jobs[1])
    fetch_after.wait()
    branch = down_sum.total() + vec[V_DOWN : V_DOWN + 1]
    result[...] = (after_two[...] + vec[5:6] * branch).astype(BF)
    save(result, result_out)
    sums[10:11] = column_sum(dy[...] * branch)
    advance(jobs[2])
    advance(jobs[1])
    total = back_sum.total()
    normed, inverse = plain_norm(after_two[...])
    sums[8:9] = column_sum(total)
    sums[9:10] = column_sum(total * normed)
    value = dy[...] + norm_back(total * (1.0 + vec[4:5]), normed, inverse)
    grad_after[...] = value
    value = value.astype(BF)
    spread = Spread(low_two, value, gs, gr)
    sums[1:2] = column_sum(value)
    save(grad_after, grad_out)
    save(sums, sums_out)
    advance(jobs[2])
    finish(jobs[1])
    save(owned_b, owned_b_out)
    spread.relay()
    advance(jobs[2])
    spread.wait()
    store = pltpu.make_async_copy(low_two, low_out, loc.at[3])
    store.start()
    finish(jobs[2])
    save(owned_c, owned_c_out)
    store.wait()
    for copy in stores:
        copy.wait()
    down_sum.drain()
    back_sum.drain()
    spread.drain()


def mlp_pass(a, cot, up, down, after, vec, bias):
    dma = pltpu.SemaphoreType.DMA
    sds = jax.ShapeDtypeStruct
    wide = pltpu.VMEM((SEQ, D), BF)
    tiles = pltpu.VMEM((2, D, BATCH), BF)
    units = pltpu.VMEM((SEQ, FF), BF)
    owned = sds((2, PAIR, BATCH), BF)
    outs = [
        (sds((SEQ, D), BF), HB), (sds((TOK, D), F32), VM), (sds((16, D), F32), VM),
        (sds((8, FF), F32), VM), (sds((TOK, D), BF), HB), (owned, VM), (owned, VM), (owned, VM),
    ]
    return pl.pallas_call(
        mlp_kernel,
        out_shape=[shape for shape, _ in outs],
        in_specs=[HB] * 5 + [VM] * 2,
        out_specs=[HB] * len(outs),
        scratch_shapes=[
            *[pltpu.VMEM(outs[i][0].shape, outs[i][0].dtype) for i in (1, 2, 3, 5, 6, 7)], dma((7,)),
            wide, wide, pltpu.VMEM(GRADS, BF), tiles, pltpu.VMEM((2, SEQ, BATCH), F32), units, units,
            pltpu.VMEM((SEQ, D), F32), wide, wide, pltpu.VMEM((TOK, D), F32), wide, pltpu.VMEM((TOK, D), BF),
            pltpu.VMEM((TOK, D), F32),
            pltpu.VMEM((2, 3, TOK, D), BF), pltpu.VMEM((8, FF), F32), dma((2, 6)), dma((2, 6)), dma((6,)), dma((6,)),
            dma((5,)), dma((2, 2)), pltpu.SemaphoreType.REGULAR, pltpu.SemaphoreType.REGULAR,
            pltpu.VMEM(GRADS, BF), pltpu.VMEM(GRADS, BF),
            *reduce_buffers(), *reduce_buffers(), *reduce_sems(), *reduce_sems(), *reduce_sems(),
        ],
        compiler_params=params(1),
        name="mlp",
    )(a, cot, up, down, after, vec, bias)


def sum_over_xy(held, sends, recvs):
    x, y, z, core = here()
    for stage, peers in enumerate(peers_xy(x, y, z, core)):
        base = 4 * stage
        copies = [
            remote(held.at[base], held.at[base + k], sends.at[stage, k], recvs.at[stage, k], peers[k - 1])
            for k in (2, 1, 3)
        ]
        for copy in copies:
            copy.start()
        yield
        for copy in copies:
            copy.wait()
        held[base + 4] = (held[base] + held[base + 1]) + (held[base + 2] + held[base + 3])


def model_job(model, time_out, col, held, sends, recvs):
    x, y, z, core = here()
    copies = [
        remote(model, col.at[k], sends.at[2, k], recvs.at[2, k], chip(x, y, z + k, core)) for k in (2, 1, 3)
    ]
    for copy in copies:
        copy.start()
    yield
    for copy in copies:
        copy.wait()
    time_out[core] = (model[...] + col[1]) + (col[2] + col[3])
    swap = remote(
        time_out.at[core], time_out.at[core], sends.at[2, 0], recvs.at[2, 0], chip(x, y, z, 1 - core)
    )
    swap.start()
    yield
    swap.wait()
    held[0] = time_out[0] + time_out[1]
    yield from sum_over_xy(held, sends, recvs)


def head_job(heads, head_out, other, held, sends, recvs):
    x, y, z, core = here()
    zl = lax.rem(z, 2)
    swap = remote(heads, other, sends.at[2, 0], recvs.at[2, 0], chip(x, y, z, 1 - core))
    swap.start()
    yield
    swap.wait()
    held[0] = heads[...] + other[...]
    yield from sum_over_xy(held, sends, recvs)
    head_out[zl] = held[8]
    last = remote(
        held.at[8], head_out.at[zl], sends.at[2, 1], recvs.at[2, 1], chip(x, y, z + 1 - 2 * zl, core)
    )
    last.start()
    yield
    last.wait()


def model_scratch(rows, width):
    dma = pltpu.SemaphoreType.DMA
    return [pltpu.VMEM((4, rows, width), F32), pltpu.VMEM((9, rows, width), F32), dma((3, 4)), dma((3, 4))]


def head_scratch():
    dma = pltpu.SemaphoreType.DMA
    return [pltpu.VMEM((16, HW), F32), pltpu.VMEM((9, 16, HW), F32), dma((3, 4)), dma((3, 4))]


def attend_clip_back(query, keys, values, grad, grad_query, grad_keys, grad_values):
    for h in range(HEADS):
        cols = head_slice(h)
        k, v = keys[:, cols], values[:, cols]
        for start in range(0, SEQ, 256):
            rows = slice(start, start + 256)
            q, do = query[rows, cols], grad[rows, cols]
            weights = softmax_rows(q, k)
            grad_weights = contract_last(do, v)
            delta = jnp.sum(weights * grad_weights, -1, keepdims=True)
            grad_scores = (weights * (grad_weights - delta)).astype(BF)
            grad_query[rows, cols] = product(grad_scores, k) * SCALE
            to_keys = contract_rows(grad_scores, q) * SCALE
            to_values = contract_rows(weights.astype(BF), do)
            if start:
                grad_keys[:, cols] += to_keys
                grad_values[:, cols] += to_values
            else:
                grad_keys[:, cols] = to_keys
                grad_values[:, cols] = to_values


def root_back(linear, inverse, scaled, dot):
    return (inverse * scaled - linear * (inverse * inverse * inverse * dot * (1.0 / D))).astype(BF)


EARLY, LATE = (0, 1, 3, 4, 7, 8, 9, 10), (5, 6, 2)


def backward_kernel(
    wa_in, low_in, after_in, branch_in, query_lin_in, key_lin_in, query_two_lin_in, key_two_lin_in,
    query_rot_in, key_rot_in, value_low_in, query_two_in, key_two_in, value_two_in, mixed_in,
    mixed_two_in, words_in, three_in, one_in, tok_in, grad_in, tab_in, inv_in, result,
    vec, heads, sums, bias_sum, owned_a, owned_b, owned_c, in_m, out_m, mlp_m,
    out_result, out_tokens, out_words, time_sum_out, model_sum_out, head_sum_out, narrow_out, wide_out, gram_out,
    time_out, model_out, head_out, narrow, wide, gram, keep,
    wa, low_wide, after_one, branch_one, lin_a, lin_b, qa, ka, va, mixed, operand, tok_own,
    grad_after, tab, inv, grad_query, grad_kv, grad_qkv, part_cross, part_words, blocks,
    held, gq, gk, gv, model, head_sums, low_tokens, low_words, mine, theirs,
    sums_a, sums_b, mlp_a, mlp_b, mlp_c,
    stat, stat_s, stat_r, zs, zr, gs, gr, ds, dr, loc, *rest,
):
    x, y, z, core = here()
    rows, lines = peers_xy(x, y, z, core)
    slots = iter(range(32))
    own_block = block_of(z)

    def fetch(src, dst):
        copy = pltpu.make_async_copy(src, dst, loc.at[next(slots)])
        copy.start()
        return copy

    out_cols, in_cols = pl.ds(6 * HW, 2 * HW), pl.ds(0, 6 * HW)
    first = [fetch(low_in, low_wide), fetch(wa_in.at[:, out_cols], wa.at[:, out_cols])]
    inputs = [
        fetch(query_two_in, qa), fetch(key_two_in, ka), fetch(value_two_in, va),
        fetch(query_two_lin_in, lin_a), fetch(key_two_lin_in, lin_b), fetch(inv_in, inv),
    ]
    second = [
        fetch(mixed_two_in, mixed), fetch(wa_in.at[:, in_cols], wa.at[:, in_cols]),
        fetch(words_in.reshape(SEQ, D), operand),
    ]
    third = [
        fetch(after_in, after_one), fetch(branch_in, branch_one), fetch(grad_in, grad_after),
        fetch(tab_in, tab), fetch(tok_in.at[own_block], tok_own),
    ]
    arrive = knock(column(x, y, z, core) + rows + lines)
    for row in (1, 8, 9, 10):
        i = EARLY.index(row)
        model[i : i + 1] = sums[row : row + 1]
    head_sums[...] = jnp.zeros_like(head_sums)
    for i in range(6):
        head_sums[10 + i : 11 + i] = bias_sum[0:1, i * HW : (i + 1) * HW]
    refs_a, refs_b, early_refs, late_refs, head_refs, rest = (
        rest[:14], rest[14:28], rest[28:32], rest[32:36], rest[36:40], rest[40:],
    )
    (late, time_late, time_early, gram_sems), swap_refs = rest[:4], rest[4:]
    late[...] = jnp.zeros_like(late)
    n, w = 8 * ROWS, 2 * ROWS
    halves = (slice(0, ROWS), slice(ROWS, 2 * ROWS))

    stores = []

    def save(ref, out):
        copy = pltpu.make_async_copy(ref, out, keep.at[len(stores)])
        copy.start()
        stores.append(copy)

    def new_narrow(j, ref, part, col):
        rows = halves[part]
        grad = jnp.concatenate([ref[i].astype(F32)[rows, col : col + HW] for i in (0, 1)], 1)
        old = in_m[j] if j < 6 else out_m[:, j - 6, :]
        narrow[j * ROWS : (j + 1) * ROWS] = MOMENTUM * old + grad

    def new_wide(j, thirds):
        chips = [jnp.concatenate([ref[i].astype(F32)[rows] for ref, rows in thirds], 1) for i in (0, 1)]
        wide[j * ROWS : (j + 1) * ROWS] = MOMENTUM * mlp_m[:, j, :] + join_hidden(*chips)

    hidden_rows = [
        swap_rows(src, dst, *swap_refs[3 * i : 3 * i + 3])
        for i, (src, dst) in enumerate(((owned_a, mlp_a), (owned_b, mlp_b), (owned_c, mlp_c)))
    ]
    grads_a, grads_b = refs_a[0], refs_b[0]
    job_a = reduce_batch(grads_a, sums_a, *refs_a[1:])
    job_b = reduce_batch(grads_b, sums_b, *refs_b[1:])
    stats = Stats(stat, stat_s, stat_r)
    drains = []

    arrive()
    send_result, wait_result = deliver(result, out_result, ds.at[2], dr.at[2], loc.at[29])
    send_result()
    for copy in first:
        copy.wait()
    held[...] = product(low_wide[...], wa[:, W_CROSS]).astype(BF)
    for copy in inputs:
        copy.wait()
    attend_clip_back(qa, ka, va, held, gq, gk, gv)
    inverse_query, inverse_key, inverse_key_two, inverse_query_two = [inv[:, i : i + 1] for i in range(4)]
    dots = stats.start(
        0,
        [
            jnp.sum(lin_a[...] * (gq[...] * (1.0 + heads[8:9])), -1, keepdims=True),
            jnp.sum(lin_b[...] * (gk[...] * (1.0 + heads[9:10])), -1, keepdims=True),
        ],
    )
    for job in hidden_rows:
        advance(job)
    head_sums[8:9] = column_sum(gq[...] * lin_a[...] * inverse_query_two)
    head_sums[9:10] = column_sum(gk[...] * lin_b[...] * inverse_key_two)
    low = gv[...].astype(BF)
    grad_kv[:, HW:] = low
    head_sums[7:8] = column_sum(low)
    for copy in second:
        copy.wait()
    weight_grad(low_wide, mixed[...], grads_a, 1, HW)
    dot_query, dot_key = dots()
    low = root_back(lin_a[...], inverse_query_two, gq[...] * (1.0 + heads[8:9]), dot_query)
    grad_query[...] = low
    head_sums[5:6] = column_sum(low)
    cross = Scatter(part_cross, blocks.at[0], zs.at[0], zr.at[0]).product(grad_query, wa[:, W_QUERY])
    low = root_back(lin_b[...], inverse_key_two, gk[...] * (1.0 + heads[9:10]), dot_key)
    grad_kv[:, :HW] = low
    head_sums[6:7] = column_sum(low)
    selfs = [
        fetch(query_rot_in, qa), fetch(key_rot_in, ka), fetch(value_low_in, va),
        fetch(query_lin_in, lin_a), fetch(key_lin_in, lin_b), fetch(mixed_in, mixed),
    ]
    weight_grad(operand, grad_kv[...], grads_a, 0, 0)
    next_operand = fetch(three_in, operand)
    next_operand.wait()
    cross.relay()
    weight_grad(operand, grad_query[...], grads_a, 1, 0)
    next_operand = fetch(one_in, operand)
    advance(job_a)
    part_words[...] = contract_last(grad_kv[...], wa[:, W_TEXT]).astype(BF)
    for copy in third:
        copy.wait()

    total = cross.total()
    normed, inverse = plain_norm(after_one[...])
    model[3 : 4] = column_sum(total)
    model[2 : 3] = column_sum(total * normed)
    value = grad_after[...] + norm_back(total * (1.0 + vec[V_GAIN : V_GAIN + 1]), normed, inverse)
    grad_after[...] = value
    model[4 : 5] = column_sum(value * branch_one[...])
    low = (value * vec[2:3]).astype(BF)
    model[0 : 1] = column_sum(low)
    spread = Spread(low_wide, low, gs, gr)
    drains.append(spread)
    advance(job_a)
    spread.relay()
    early = model_job(model, time_early, *early_refs)
    advance(early)
    spread.wait()
    advance(job_a)
    word_sum = Scatter(part_words, blocks.at[1], zs.at[1], zr.at[1]).held()
    drains.append(word_sum)

    held[...] = product(low_wide[...], wa[:, W_SELF]).astype(BF)
    for copy in selfs:
        copy.wait()
    attend_clip_back(qa, ka, va, held, gq, gk, gv)
    cosine, sine = rope_pair(tab[...].reshape(SEQ, HEAD))
    for ref in (gq, gk):
        for h in range(HEADS):
            cols = head_slice(h)
            value = ref[:, cols]
            ref[:, cols] = value * cosine - swap_halves(value) * sine
    dots = stats.start(
        1,
        [
            jnp.sum(lin_a[...] * (gq[...] * (1.0 + heads[3:4])), -1, keepdims=True),
            jnp.sum(lin_b[...] * (gk[...] * (1.0 + heads[4:5])), -1, keepdims=True),
        ],
    )
    head_sums[3:4] = column_sum(gq[...] * lin_a[...] * inverse_query)
    head_sums[4:5] = column_sum(gk[...] * lin_b[...] * inverse_key)
    low = gv[...].astype(BF)
    grad_qkv[:, 2 * HW :] = low
    head_sums[2:3] = column_sum(low)
    next_operand.wait()
    weight_grad(low_wide, mixed[...], grads_b, 1, HW)
    cross.drain()
    advance(early)
    dot_query, dot_key = dots()
    word_sum.relay()
    advance(job_a)
    for i, (lin, inverse, ref, dot) in enumerate(
        ((lin_a, inverse_query, gq, dot_query), (lin_b, inverse_key, gk, dot_key))
    ):
        low = root_back(lin[...], inverse, ref[...] * (1.0 + heads[3 + i : 4 + i]), dot)
        grad_qkv[:, i * HW : (i + 1) * HW] = low
        head_sums[i : i + 1] = column_sum(low)
    token_sum = Scatter(part_cross, blocks.at[0], zs.at[2], zr.at[2]).product(grad_qkv, wa[:, W_QKV])
    drains.append(token_sum)
    advance(job_a)
    head_total = head_job(head_sums, head_out, *head_refs)
    advance(head_total)
    weight_grad(operand, grad_qkv[:, : 2 * HW], grads_b, 0, 0)
    weight_grad(operand, grad_qkv[:, 2 * HW :], grads_b, 1, 0)
    advance(job_b)
    token_sum.relay()
    advance(head_total)
    for job in hidden_rows:
        finish(job)
    top, bottom = halves
    new_wide(0, ((mlp_b, bottom), (mlp_c, top), (mlp_c, bottom)))
    new_wide(1, ((mlp_a, top), (mlp_a, bottom), (mlp_b, top)))
    save(wide, wide_out)
    advance(job_b)
    mine[:n, n:] = jnp.zeros((n, w), F32)
    mine[n:, :n] = jnp.zeros((w, n), F32)
    mine[n:, n:] = gram_of(wide[...])
    advance(early)

    total = token_sum.total()
    normed, inverse = plain_norm(tok_own[...].astype(F32))
    for i, row in enumerate((column_sum(total), column_sum(total * normed), sums[2:3])):
        for k in range(SIDE):
            late[SIDE * i + k : SIDE * i + k + 1] = row[:, k * HW : (k + 1) * HW]
    late_total = model_job(late, time_late, *late_refs)
    advance(late_total)
    advance(job_b)
    value = grad_after[...] + norm_back(total * (1.0 + vec[1:2]), normed, inverse)
    low_tokens[...] = value.astype(BF)
    send_tokens, wait_tokens = deliver(low_tokens, out_tokens, ds.at[1], dr.at[1], loc.at[31])
    low_words[...] = word_sum.total().astype(BF)
    send_words, wait_words = deliver(low_words, out_words, ds.at[0], dr.at[0], loc.at[30])
    advance(late_total)
    send_tokens()
    advance(job_b)
    advance(late_total)
    send_words()
    finish(job_a)
    for j, ref, part, col in ((3, sums_a, 1, 0), (4, sums_a, 0, 0), (5, sums_a, 0, HW), (7, sums_a, 1, HW)):
        new_narrow(j, ref, part, col)
    advance(head_total)
    advance(early)
    advance(job_b)
    advance(late_total)
    advance(head_total)
    finish(early)
    finish(job_b)
    for j, ref, part, col in ((0, sums_b, 0, 0), (1, sums_b, 0, HW), (2, sums_b, 1, 0), (6, sums_b, 1, HW)):
        new_narrow(j, ref, part, col)
    save(narrow, narrow_out)
    mine[:n, :n] = gram_of(narrow[...])
    same, _ = block_mask(10 * ROWS)
    blocks_only = jnp.where(same, mine[...], 0.0)
    compact = blocks_only[:ROWS]
    for j in range(1, 10):
        compact = compact + blocks_only[j * ROWS : (j + 1) * ROWS]
    theirs[0] = compact
    swap = remote(theirs.at[0], theirs.at[1], gram_sems.at[0], gram_sems.at[1], chip(x, y, z + 2, core))
    swap.start()
    finish(late_total)
    finish(head_total)
    save(head_out, head_sum_out)
    for i, row in enumerate(EARLY):
        model_out[row : row + 1] = early_refs[1][8, i : i + 1]
        if row > 4:
            for clip in (0, 1):
                time_out[row - 5, clip : clip + 1] = time_early[clip, i : i + 1]
    for i, row in enumerate(LATE):
        for k in range(SIDE):
            cols = slice(k * HW, (k + 1) * HW)
            part = slice(SIDE * i + k, SIDE * i + k + 1)
            model_out[row : row + 1, cols] = late_refs[1][8, part]
            if row > 4:
                for clip in (0, 1):
                    time_out[row - 5, clip : clip + 1, cols] = time_late[clip, part]
    save(time_out, time_sum_out)
    save(model_out, model_sum_out)
    wait_result()
    wait_tokens()
    wait_words()
    swap.wait()
    gram[...] = theirs[0] + theirs[1]
    save(gram, gram_out)
    for copy in stores:
        copy.wait()
    for transfer in drains:
        transfer.drain()


def backward(hbm, vmem):
    dma = pltpu.SemaphoreType.DMA
    sds = jax.ShapeDtypeStruct
    lin = pltpu.VMEM((SEQ, HW), F32)
    low = pltpu.VMEM((SEQ, HW), BF)
    wide = pltpu.VMEM((SEQ, D), BF)
    block = pltpu.VMEM((TOK, D), F32)
    low_block = pltpu.VMEM((TOK, D), BF)
    summed = pltpu.VMEM((2, PAIR, BATCH), BF)
    size = 10 * ROWS
    square = pltpu.VMEM((size, size), F32)
    outs = [
        *[(sds((2, TOK, D), BF), HB)] * 3, (sds((6, 2, D), F32), VM),
        (sds((16, D), F32), VM), (sds((2, 16, HW), F32), VM), (sds((8 * ROWS, 2 * HW), F32), VM),
        (sds((2 * ROWS, WIDE), F32), VM), (sds((ROWS, size), F32), VM),
    ]
    batch = [pltpu.VMEM(GRADS, BF), *reduce_scratch()]
    return pl.pallas_call(
        backward_kernel,
        out_shape=[shape for shape, _ in outs],
        in_specs=[HB] * len(hbm) + [VM] * len(vmem),
        out_specs=[HB] * len(outs),
        scratch_shapes=[
            *[pltpu.VMEM(shape.shape, shape.dtype) for shape, _ in outs[3:]], dma((6,)),
            pltpu.VMEM((D, ATTN), BF), wide, block, block, lin, lin, low, low, low, low, wide,
            low_block, block, pltpu.VMEM((SIDE, TOK, HEAD), F32), pltpu.VMEM((SEQ, 128), F32),
            low, pltpu.VMEM((SEQ, 2 * HW), BF), pltpu.VMEM((SEQ, 3 * HW), BF), wide, wide,
            pltpu.VMEM((2, 3, TOK, D), BF), low, lin, lin, lin, pltpu.VMEM((8, D), F32),
            pltpu.VMEM((16, HW), F32), low_block, low_block, square, pltpu.VMEM((2, ROWS, size), F32),
            summed, summed, summed, summed, summed,
            pltpu.VMEM((2, 4, 8, SEQ), F32),
            dma((2, 3)), dma((2, 3)), dma((3, 6)), dma((3, 6)), dma((6,)), dma((6,)), dma((3, 2)),
            dma((3, 2)), dma((32,)), *batch, *batch, *model_scratch(8, D),
            *model_scratch(16, HW), *head_scratch(), pltpu.VMEM((16, HW), F32), pltpu.VMEM((2, 16, HW), F32),
            pltpu.VMEM((2, 8, D), F32), dma((2,)), *swap_sems(), *swap_sems(), *swap_sems(),
        ],
        compiler_params=params(2),
        name="backward",
    )(*hbm, *vmem)


def block_mask(size):
    row = lax.broadcasted_iota(jnp.int32, (size, size), 0)
    col = lax.broadcasted_iota(jnp.int32, (size, size), 1)
    return lax.div(row, ROWS) == lax.div(col, ROWS), row == col


def times(a, b):
    return jnp.dot(a, b, precision=HIGHEST, preferred_element_type=F32)


def gram_of(blocks):
    return lax.dot_general(
        blocks, blocks, (((1,), (1,)), ((), ())), precision=HIGHEST, preferred_element_type=F32
    )


def newton_factor(gram, size):
    same, eye = block_mask(size)
    gram = jnp.where(same, jnp.concatenate([gram] * (size // ROWS), 0), 0.0)
    diagonal = jnp.where(eye, gram, 0.0)
    by_row = jnp.sum(diagonal, 1, keepdims=True)
    by_col = jnp.sum(diagonal, 0, keepdims=True)
    total_row = jnp.sum(jnp.where(same, by_col, 0.0), 1, keepdims=True)
    total_col = jnp.sum(jnp.where(same, by_row, 0.0), 0, keepdims=True)
    scale_row = 1.0 / (jnp.sqrt(total_row) + ORTHO_EPSILON)
    scale_col = 1.0 / (jnp.sqrt(total_col) + ORTHO_EPSILON)
    current = gram * scale_row * scale_col
    whole = None
    for turn in range(NS_STEPS):
        square = times(current, current)
        step = NEWTON_SECOND * current + NEWTON_THIRD * square + jnp.where(eye, NEWTON_FIRST, 0.0)
        whole = step if whole is None else times(step, whole)
        if turn + 1 < NS_STEPS:
            current = times(times(step, current), step)
    return whole * scale_col


def join_hidden(first, second):
    fill = jnp.zeros((first.shape[0], FF), F32)
    first = jnp.concatenate([first, fill], 1)
    second = pltpu.roll(jnp.concatenate([second, fill], 1), FF_REAL, 1)
    return (first + second)[:, :WIDE]


def finish_kernel(
    gram, head_w, head_m, model_w, model_m, up_w, up_m, head_sum, model_sum, time_sum,
    narrow_in, wide_in, in_w_in, out_w_in, mlp_w_in, result, tokens_in, words_in,
    new_head, new_model, new_up, new_head_m, new_model_m, new_up_m, out_time,
    new_in_out, new_out_out, new_mlp_out, new_in_m_out, new_out_m_out, new_mlp_m_out, out_result,
    out_tokens, out_words,
    narrow, wide, in_w, out_w, mlp_w, low_result, tokens, words, block, new_in, new_out, new_mlp,
    new_out_m, new_mlp_m, loads, stores,
):
    fetched = []
    for i, (src, dst) in enumerate(
        (
            (narrow_in, narrow), (wide_in, wide), (in_w_in, in_w), (out_w_in, out_w), (mlp_w_in, mlp_w),
            (result, low_result), (tokens_in, tokens), (words_in, words),
        )
    ):
        fetched.append(pltpu.make_async_copy(src, dst, loads.at[i]))
        fetched[-1].start()
    copies = []

    def save(ref, out):
        copies.append(pltpu.make_async_copy(ref, out, stores.at[len(copies)]))
        copies[-1].start()

    out_time[...] = time_sum[...]
    value = MOMENTUM * head_m[...] + jnp.concatenate([head_sum[0, :10], head_sum[1, :10]], 1)
    new_head_m[...] = value
    new_head[...] = head_w[...] - RATE_VECTOR * value
    value = MOMENTUM * model_m[...] + model_sum[:11]
    new_model_m[...] = value
    new_model[...] = model_w[...] - RATE_VECTOR * value
    chips = [jnp.concatenate([head_sum[i, 10 + k : 11 + k] for k in range(6)], 1) for i in (0, 1)]
    value = join_hidden(*chips)
    for i in range(WIDE // 128):
        row = slice(i, i + 1)
        new_up_m[row] = MOMENTUM * up_m[row] + value[:, i * 128 : (i + 1) * 128]
    new_up[...] = up_w[...] - RATE_VECTOR * new_up_m[...]
    n, w = narrow.shape[0], wide.shape[0]
    factor = newton_factor(gram[...], n + w)
    for copy in fetched:
        copy.wait()
    save(low_result, out_result)
    for i, (src, dst) in enumerate(((tokens, out_tokens), (words, out_words))):
        for clip in (0, 1):
            block[2 * i + clip] = src[clip].astype(F32)
            save(block.at[2 * i + clip], dst.at[clip])
    turned = times(factor[:n, :n], narrow[...])
    for j in range(6):
        rows = slice(j * ROWS, (j + 1) * ROWS)
        save(narrow.at[rows], new_in_m_out.at[j])
        new_in[j] = in_w[j] * (1.0 - RATE_IN * DECAY) - RATE_IN * turned[rows]
    save(new_in, new_in_out)
    for j in range(2):
        rows = slice((6 + j) * ROWS, (7 + j) * ROWS)
        new_out_m[:, j, :] = narrow[rows]
        new_out[:, j, :] = out_w[:, j, :] * (1.0 - RATE_OUT * DECAY) - RATE_OUT * turned[rows]
    save(new_out_m, new_out_m_out)
    save(new_out, new_out_out)
    for j in range(2):
        new_mlp_m[:, j, :] = wide[j * ROWS : (j + 1) * ROWS]
    save(new_mlp_m, new_mlp_m_out)
    turned = times(factor[n:, n:], wide[...])
    for j in range(2):
        rows = slice(j * ROWS, (j + 1) * ROWS)
        new_mlp[:, j, :] = mlp_w[:, j, :] * (1.0 - RATE_MLP * DECAY) - RATE_MLP * turned[rows]
    save(new_mlp, new_mlp_out)
    for copy in copies:
        copy.wait()


def finish_step(small, large):
    sds = jax.ShapeDtypeStruct
    matrices = [sds((6, ROWS, 2 * HW), F32), sds((ROWS, 2, 2 * HW), F32), sds((ROWS, 2, WIDE), F32)]
    vectors = [sds((10, 2 * HW), F32), sds((11, D), F32), sds((WIDE // 128, 128), F32)]
    blocks = [sds((2, TOK, D), BF), sds((2, TOK, D), F32), sds((2, TOK, D), F32)]
    held = [pltpu.VMEM(v.shape, v.dtype) for v in large]
    news = [pltpu.VMEM(v.shape, F32) for v in matrices + matrices[1:]]
    return pl.pallas_call(
        finish_kernel,
        out_shape=vectors + vectors + [sds((6, 2, D), F32)] + matrices + matrices + blocks,
        in_specs=[VM] * len(small) + [HB] * len(large),
        out_specs=[VM] * 7 + [HB] * 9,
        scratch_shapes=[
            *held, pltpu.VMEM((4, TOK, D), F32), *news, pltpu.SemaphoreType.DMA((8,)),
            pltpu.SemaphoreType.DMA((16,)),
        ],
        compiler_params=pltpu.CompilerParams(vmem_limit_bytes=VMEM_LIMIT),
        name="finish",
    )(*small, *large)


def rope_rates():
    pair = np.arange(HEAD // 2)
    side = HEAD // 6
    frame = (HEAD - 4 * side) // 2
    part = (pair >= frame).astype(np.int32) + (pair >= frame + side)
    offset = np.array([0, frame, frame + side])[part]
    extent = np.array([2 * frame, 2 * side, 2 * side])[part]
    rate = np.exp((pair - offset) * (-2.0 * math.log(10000.0)) / extent).astype(np.float32)
    rates = np.zeros((8, HEAD), np.float32)
    for component in range(3):
        rates[component] = np.tile(np.where(part == component, rate, 0.0), 2)
    return jnp.asarray(rates)


def plain_norm(values):
    centred = values - jnp.mean(values, -1, keepdims=True)
    inverse = lax.rsqrt(jnp.mean(centred * centred, -1, keepdims=True) + NORM_EPSILON)
    return (centred * inverse, inverse)


def norm_back(grads, normed, inverse):
    return inverse * (
        grads
        - jnp.mean(grads, -1, keepdims=True)
        - normed * jnp.mean(grads * normed, -1, keepdims=True)
    )


def product(left, right):
    return jnp.dot(left, right, preferred_element_type=F32)


def contract_last(left, right):
    return lax.dot_general(left, right, (((1,), (1,)), ((), ())), preferred_element_type=F32)


def contract_rows(left, right):
    return lax.dot_general(left, right, (((0,), (0,)), ((), ())), preferred_element_type=F32)


def body(
    tokens, text, time_embedding, positions, cotangent, attn_in, attn_out, mlp, head_vectors,
    model_vectors, up_bias, attn_in_moment, attn_out_moment, mlp_moment, head_moment, model_moment,
    up_moment,
):
    swap = lambda v: v.transpose(1, 0, 2)
    (
        w_attn, w_up, w_down, cot_all, heads, vectors, tab_all, input_one, input_three, input_mlp, query_lin, key_lin,
        query_two_lin, key_two_lin, inv, query_rot, key_rot, value_low, query_two, key_two, value_two,
        mixed_low, mixed_two_low, branch_one, after_one, after_two, tok_all, txt_all,
    ) = forward(
        swap(attn_in), attn_out, mlp, tokens, text, cotangent, positions, rope_rates(),
        swap(time_embedding), model_vectors, head_vectors,
    )
    low_two, grad_after, sums, up_sum, result, *owned = mlp_pass(
        input_mlp, cot_all, w_up, w_down, after_two, vectors, up_bias.reshape(-1, 128)
    )
    out_result, out_tokens, out_words, time_sums, model_sums, head_totals, narrow, wide, gram = backward(
        [
            w_attn, low_two, after_one, branch_one, query_lin, key_lin, query_two_lin, key_two_lin,
            query_rot, key_rot, value_low, query_two, key_two, value_two, mixed_low, mixed_two_low,
            txt_all, input_three, input_one, tok_all, grad_after, tab_all, inv, result,
        ],
        [
            vectors, heads, sums, up_sum, *owned, swap(attn_in_moment), attn_out_moment, mlp_moment,
        ],
    )
    (
        new_head, new_model, new_up, new_head_m, new_model_m, new_up_m, out_time,
        new_in, new_out, new_mlp, new_in_m, new_out_m, new_mlp_m, out_result, out_tokens, out_words,
    ) = finish_step(
        [
            gram, head_vectors, head_moment, model_vectors, model_moment, up_bias.reshape(-1, 128),
            up_moment.reshape(-1, 128), head_totals, model_sums, time_sums,
        ],
        [narrow, wide, swap(attn_in), attn_out, mlp, out_result, out_tokens, out_words],
    )
    return (
        out_result, out_tokens, out_words, swap(out_time), swap(new_in), new_out, new_mlp,
        swap(new_in_m), new_out_m, new_mlp_m, new_head, new_model, new_up.reshape(-1), new_head_m,
        new_model_m, new_up_m.reshape(-1),
    )


def solution(mesh):
    clip = P("fsdp", "ctx", None)
    whole = P("fsdp", None, None)
    matrix = P(("fsdp", "ctx"), None, "tp")
    in_specs = (
        clip, clip, whole, P(None, "fsdp", "ctx"), clip, matrix, matrix, matrix, P(None, "tp"), P(),
        P("tp"), matrix, matrix, matrix, P(None, "tp"), P(), P("tp"),
    )
    out_specs = (
        clip, clip, clip, whole, matrix, matrix, matrix, matrix, matrix, matrix, P(None, "tp"), P(),
        P("tp"), P(None, "tp"), P(), P("tp"),
    )
    return jax.shard_map(body, mesh=mesh, in_specs=in_specs, out_specs=out_specs, check_vma=False)
```

```python
from functools import partial
import math

import jax
import jax.numpy as jnp
import numpy as np
from jax import lax
from jax.experimental import pallas as pl
from jax.experimental.pallas import tpu as pltpu
from jax.sharding import PartitionSpec as P

D = 1536
HEAD = 128
ROWS = 24
HEADS = 3
NORM_EPSILON = 1e-06
ORTHO_EPSILON = 1e-07
NEWTON_FIRST = 3.4445
NEWTON_SECOND = -4.775
NEWTON_THIRD = 2.0315
NS_STEPS = 5
MOMENTUM = 0.9
DECAY = 0.01
RATE_IN = 0.5
RATE_OUT = 4.0
RATE_MLP = 1.0
RATE_VECTOR = 0.005
HIGHEST = lax.Precision.HIGHEST

MESH = pl.DeviceIdType.MESH
BF = jnp.bfloat16
F32 = jnp.float32

SIDE = 4
TOK = 128
SEQ = SIDE * TOK
HW = HEADS * HEAD
FF_REAL = 2240
FF = 2304
WIDE = 2 * FF_REAL
PAIR = 2 * ROWS
VMEM_LIMIT = 60 * 1024 * 1024


def here():
    f = lax.axis_index("fsdp")
    c = lax.axis_index("ctx")
    t = lax.axis_index("tp")
    x, y = lax.div(f, SIDE), lax.rem(f, SIDE)
    zl, core = lax.div(c, 2), lax.rem(c, 2)
    return x, y, 2 * t + zl, core


def chip(x, y, z, core):
    x, y, z = lax.rem(x + SIDE, SIDE), lax.rem(y + SIDE, SIDE), lax.rem(z + SIDE, SIDE)
    return {"fsdp": x * SIDE + y, "ctx": lax.rem(z, 2) * 2 + core, "tp": lax.div(z, 2)}


def block_of(z):
    z = lax.rem(z + SIDE, SIDE)
    return 2 * lax.rem(z, 2) + lax.div(z, 2)


def knock(devices):
    barrier = pltpu.get_barrier_semaphore()
    for device in devices:
        pl.semaphore_signal(barrier, inc=1, device_id=device, device_id_type=MESH)
    return lambda: pl.semaphore_wait(barrier, len(devices))


def greet(devices):
    knock(devices)()


def column(x, y, z, core):
    return [chip(x, y, z + k, core) for k in (1, 2, 3)] + [
        chip(x, y, z + k, 1 - core) for k in range(4)
    ]


def remote(src, dst, send, recv, device):
    return pltpu.make_async_remote_copy(
        src_ref=src, dst_ref=dst, send_sem=send, recv_sem=recv, device_id=device, device_id_type=MESH
    )


def params(cid):
    return pltpu.CompilerParams(
        collective_id=cid, has_side_effects=True, vmem_limit_bytes=VMEM_LIMIT
    )


VM = pl.BlockSpec(memory_space=pltpu.VMEM)
HB = pl.BlockSpec(memory_space=pltpu.HBM)


def flat(a, b):
    return lax.rem(a + SIDE, SIDE) * SIDE + lax.rem(b + SIDE, SIDE)


def steps_of(x, y, z, core):
    return (
        (chip(x + 1, y, z, core), chip(x - 1, y, z, core)),
        (chip(x, y + 1, z, core), chip(x, y - 1, z, core)),
    )


def gather_xy(own, place, xs, xr, ks, kr):
    x, y, z, core = here()
    mine = x * SIDE + y
    steps = steps_of(x, y, z, core)
    far_x, far_y = chip(x + 2, y, z, core), chip(x, y + 2, z, core)
    sibling = chip(x, y, z, 1 - core)
    sends, sibs = [], []

    def push(part, slot, src, index, device, half=None):
        copy = remote(src, place(part, index, half), xs.at[part, slot], xr.at[part, slot], device)
        copy.start()
        sends.append(copy)
        return copy

    def to_sibling(part, slot, src, index):
        copy = remote(src, place(part, index), ks.at[part, slot], kr.at[part, slot], sibling)
        copy.start()
        sibs.append(copy)

    def index_of(part, first_off, second_off):
        if part == 0:
            return flat(x + first_off, y + second_off)
        return flat(x + second_off, y + first_off)

    one, two = {}, {}
    for part in (0, 1):
        one[part, "far"] = push(part, 2, own.at[part], mine, (far_x, far_y)[part])
    for part in (0, 1):
        a_next, a_prev = steps[part]
        one[part, "next"] = push(part, 0, own.at[part], mine, a_next)
        one[part, "prev"] = push(part, 1, own.at[part], mine, a_prev)
    for part in (0, 1):
        to_sibling(part, 0, own.at[part], mine)
    offsets = (0, -1, 1, 2)

    def second_start(part, k):
        b_next, b_prev = steps[1 - part]
        index = index_of(part, offsets[k], 0)
        src = place(part, index) if k else own.at[part]
        two[part, k, "next"] = push(part, 4 + 4 * k, src, index, b_next)
        two[part, k, "prev"] = push(part, 5 + 4 * k, src, index, b_prev)

    def second_forward(part, k):
        b_next, b_prev = steps[1 - part]
        two[part, k, "next"].wait_recv()
        index = index_of(part, offsets[k], -1)
        two[part, k, "far0"] = push(part, 6 + 4 * k, place(part, index, 0), index, b_next, 0)
        to_sibling(part, 4 * k + 1, place(part, index), index)
        two[part, k, "prev"].wait_recv()
        index = index_of(part, offsets[k], 1)
        two[part, k, "far1"] = push(part, 7 + 4 * k, place(part, index, 1), index, b_prev, 1)
        to_sibling(part, 4 * k + 2, place(part, index), index)

    def second_finish(part, k):
        two[part, k, "far0"].wait_recv()
        two[part, k, "far1"].wait_recv()
        index = index_of(part, offsets[k], 2)
        to_sibling(part, 4 * k + 3, place(part, index), index)

    for part in (0, 1):
        second_start(part, 0)
    yield
    for part in (0, 1):
        one[part, "next"].wait_recv()
        one[part, "prev"].wait_recv()
        second_start(part, 1)
        for k in (1, 2):
            index = index_of(part, offsets[k], 0)
            to_sibling(part, 4 * k, place(part, index), index)
    yield
    for part in (0, 1):
        second_forward(part, 0)
        second_start(part, 2)
    yield
    for part in (0, 1):
        one[part, "far"].wait_recv()
        index = index_of(part, 2, 0)
        to_sibling(part, 12, place(part, index), index)
        second_forward(part, 1)
        second_start(part, 3)
    yield
    for part in (0, 1):
        second_forward(part, 2)
        second_finish(part, 0)
    yield
    for part in (0, 1):
        second_forward(part, 3)
        second_finish(part, 1)
    yield
    for part in (0, 1):
        second_finish(part, 2)
    yield
    for part in (0, 1):
        second_finish(part, 3)
    yield
    for copy in sends:
        copy.wait_send()
    for copy in sibs:
        copy.wait_send()
        copy.wait_recv()


GATHER_SEMS = ((2, 20), (2, 20), (2, 16), (2, 16))


def advance(job, count=1):
    for _ in range(count):
        next(job, None)


def finish(job):
    for _ in job:
        pass


def share_rows(send, recv, s, r, l):
    x, y, z, core = here()
    zl = lax.rem(z, 2)
    away = remote(send.at[1 - zl], recv.at[core], s.at[0], r.at[core], chip(x, y, z + 1 - 2 * zl, zl))
    near = remote(send.at[zl], recv.at[core], s.at[1], r.at[core], chip(x, y, z, zl))
    self_copy = pltpu.make_async_copy(send.at[zl], recv.at[core], l.at[0])

    def got(slot):
        remote(send.at[0], recv.at[slot], s.at[0], r.at[slot], chip(x, y, z, core)).wait_recv()

    def start():
        away.start()

        @pl.when(core == zl)
        def _():
            self_copy.start()

        @pl.when(core != zl)
        def _():
            near.start()

    def wait(own):
        @pl.when(core == zl)
        def _():
            self_copy.wait()
            got(1 - core)

        @pl.when(core != zl)
        def _():
            near.wait_send()
            got(0)
            got(1)

        first = recv[0].astype(F32)
        second = recv[1].astype(F32)
        own[0] = jnp.concatenate([first[:ROWS], second[:ROWS]], 0).astype(BF)
        own[1] = jnp.concatenate([first[ROWS:], second[ROWS:]], 0).astype(BF)

    return start, wait, away.wait_send


def share_clip(src, dst, s, r, l):
    x, y, z, core = here()
    put = dst.at[2 * lax.rem(z, 2) + core]
    copies = [
        remote(src.at[1 - core], put, s.at[0], r.at[0], chip(x, y, z, 1 - core)),
        remote(src.at[0], put, s.at[1], r.at[1 + core], chip(x, y, z + 1, 0)),
        remote(src.at[1], put, s.at[2], r.at[1 + core], chip(x, y, z - 1, 1)),
    ]
    local = pltpu.make_async_copy(src.at[core], put, l)

    def start():
        for copy in copies:
            copy.start()
        local.start()

    def wait():
        local.wait()
        for slot in range(3):
            remote(src.at[0], dst.at[0], s.at[0], r.at[slot], chip(x, y, z, core)).wait_recv()

    def drain():
        for copy in copies:
            copy.wait_send()

    return start, wait, drain


def split3(values):
    return [values[:, i * HW : (i + 1) * HW] for i in range(values.shape[1] // HW)]


def swap_halves(values):
    return pltpu.roll(values, HEAD // 2, 1)


def rope_pair(table):
    lane = lax.broadcasted_iota(jnp.int32, table.shape, 1)
    other = swap_halves(table)
    front = lane < HEAD // 2
    return jnp.where(front, table, other), jnp.where(front, -other, table)


def head_slice(h):
    return slice(h * HEAD, (h + 1) * HEAD)


SCALE = HEAD ** (-0.5)


def softmax_rows(query, keys):
    scores = contract_last(query, keys) * SCALE
    peak = jnp.max(scores, -1, keepdims=True)
    raised = jnp.exp(scores - peak)
    return raised * (1.0 / jnp.sum(raised, -1, keepdims=True))


def attend_clip(query, keys, values, out):
    for h in range(HEADS):
        cols = head_slice(h)
        for start in range(0, SEQ, 256):
            rows = slice(start, start + 256)
            weights = softmax_rows(query[rows, cols], keys[:, cols]).astype(BF)
            out[rows, cols] = product(weights, values[:, cols]).astype(BF)


class Stats:
    def __init__(self, buffer, send, recv):
        self.buffer, self.send, self.recv = buffer, send, recv

    def start(self, turn, columns):
        x, y, z, core = here()
        lane = lax.broadcasted_iota(jnp.int32, (SEQ, 128), 1)
        packed = jnp.zeros((SEQ, 128), F32)
        for i, column_values in enumerate(columns):
            packed = jnp.where(lane == i, column_values, packed)
        self.buffer[turn, 0] = packed.T[:8]
        copies = []
        for k in (2, 1, 3):
            copies.append(
                remote(self.buffer.at[turn, 0], self.buffer.at[turn, k], self.send.at[turn, k - 1],
                       self.recv.at[turn, k - 1], chip(x, y, z + k, core))
            )
            copies[-1].start()

        def wait():
            for copy in copies:
                copy.wait()
            total = (self.buffer[turn, 0] + self.buffer[turn, 1]) + (
                self.buffer[turn, 2] + self.buffer[turn, 3]
            )
            spread = jnp.concatenate([total, jnp.zeros((120, SEQ), F32)], 0).T
            return [spread[:, i : i + 1] for i in range(len(columns))]

        return wait


def block_slice(index):
    return pl.ds(pl.multiple_of(index * TOK, TOK), TOK)


HALF = TOK // 2


def half_rows(block, half):
    return pl.ds(pl.multiple_of(block * TOK + half * HALF, HALF), HALF)


class Scatter:
    def __init__(self, part, got, send, recv):
        self.part, self.got, self.send, self.recv = part, got, send, recv
        self.x, self.y, self.z, self.core = here()
        self.copies, self.relayed = [], False

    def push(self, slot, rows, dst, step):
        device = chip(self.x, self.y, self.z + step, self.core)
        copy = remote(self.part.at[rows], dst, self.send.at[slot], self.recv.at[slot], device)
        copy.start()
        self.copies.append(copy)

    def stage(self, k):
        front, rear = pl.ds(0, HALF), pl.ds(HALF, HALF)
        block = block_of(self.z + k)
        if k == 2:
            self.push(0, half_rows(block, 0), self.got.at[2, front], 1)
            self.push(1, half_rows(block, 1), self.got.at[2, rear], -1)
        elif k == 1:
            self.push(2, half_rows(block, 1), self.got.at[0, rear], 1)
        elif k == 3:
            self.push(3, half_rows(block, 0), self.got.at[1, front], -1)

    def held(self):
        for k in (2, 1, 3):
            self.stage(k)
        return self

    def product(self, left, right, blocks=(2, 1, 3, 0)):
        for k in blocks:
            rows = block_slice(block_of(self.z + k))
            self.part[rows] = contract_last(left[rows], right).astype(BF)
            self.stage(k)
        return self

    def relay(self):
        if self.relayed:
            return
        self.relayed = True
        for slot, step in ((0, 1), (1, -1)):
            span = pl.ds(slot * HALF, HALF)
            rows = half_rows(block_of(self.z + step), slot)
            self.copies[slot].wait_recv()
            total = self.part[rows].astype(F32) + self.got[2, span].astype(F32)
            self.part[rows] = total.astype(BF)
            self.push(4 + slot, rows, self.got.at[slot, span], step)

    def total(self):
        self.relay()
        for copy in self.copies[2:]:
            copy.wait_recv()
        own = self.part[block_slice(block_of(self.z))].astype(F32)
        return own + (self.got[0].astype(F32) + self.got[1].astype(F32))

    def drain(self):
        for copy in self.copies:
            copy.wait_send()


class Spread:
    def __init__(self, out, value, send, recv):
        self.out, self.send, self.recv = out, send, recv
        self.x, self.y, self.z, self.core = here()
        self.copies, self.relayed = [], False
        block = block_of(self.z)
        out[block_slice(block)] = value
        self.push(0, half_rows(block, 0), 1)
        self.push(1, half_rows(block, 1), -1)
        self.push(2, half_rows(block, 1), 1)
        self.push(3, half_rows(block, 0), -1)

    def push(self, slot, rows, step):
        device = chip(self.x, self.y, self.z + step, self.core)
        rows = self.out.at[rows]
        copy = remote(rows, rows, self.send.at[slot], self.recv.at[slot], device)
        copy.start()
        self.copies.append(copy)

    def relay(self):
        if self.relayed:
            return
        self.relayed = True
        for slot, step in ((0, 1), (1, -1)):
            self.copies[slot].wait_recv()
            self.push(4 + slot, half_rows(block_of(self.z - step), slot), step)

    def wait(self):
        self.relay()
        for copy in self.copies[2:]:
            copy.wait_recv()

    def drain(self):
        for copy in self.copies:
            copy.wait_send()


def inverse_root(total):
    return lax.rsqrt(total * (1.0 / D) + NORM_EPSILON)


V_SELF, V_CROSS, V_DOWN, V_GAIN, V_BIAS = 6, 7, 8, 9, 10
W_QKV, W_QUERY, W_TEXT, W_SELF, W_CROSS = (
    slice(0, 3 * HW), slice(3 * HW, 4 * HW), slice(4 * HW, 6 * HW), slice(6 * HW, 7 * HW), slice(7 * HW, 8 * HW),
)
ATTN = 8 * HW


SAVED = 22


def forward_kernel(
    in_w, out_w, mlp_w, tok, txt, cot, places, rates, time_in, model_in, head_in,
    w_attn, w_up, w_down, cot_all, heads_out, vec_out, *rest,
):
    saved, held, rest = rest[:SAVED], rest[SAVED : 2 * SAVED], rest[2 * SAVED :]
    (
        tab_all, input_one, input_three, input_mlp, query_lin, key_lin, query_two_lin, key_two_lin, inv,
        query_rot, key_rot, value_low, query_two, key_two, value_two, mixed, mixed_two, branch_one,
        after_one, after_two, tok_all, txt_all,
    ) = held
    (
        send_attn, send_mlp, tab, heads, vec, wa, got_attn, got_mlp, own_attn, own_mlp, part_one, part_two, blocks, stat,
        xs, xr, ks, kr, ms, mr, js, jr, rs, rr, cs, cr, loc, stat_s, stat_r, zs, zr, gs, gr, keep,
    ) = rest
    x, y, z, core = here()
    mine = x * SIDE + y
    stores = []

    def keep_small(ref, out, i):
        stores.append(pltpu.make_async_copy(ref, out, keep.at[SAVED + i]))
        stores[-1].start()

    def save(*refs):
        for ref in refs:
            i = [ref is other for other in held].index(True)
            stores.append(pltpu.make_async_copy(ref, saved[i], keep.at[i]))
            stores[-1].start()

    def packed(values, cores_chip):
        return values[:, cores_chip * HW : (cores_chip + 1) * HW]

    for i in (0, 1):
        rows = [
            jnp.concatenate([packed(in_w[j], i) for j in range(4)], 1),
            jnp.concatenate([packed(in_w[j], i) for j in (4, 5)] + [packed(out_w[:, j, :], i) for j in (0, 1)], 1),
        ]
        send_attn[i] = jnp.concatenate(rows, 0).astype(BF)
    greet(
        [device for pair in steps_of(x, y, z, core) for device in pair]
        + [chip(x + 2, y, z, core), chip(x, y + 2, z, core)]
        + column(x, y, z, core)
    )
    attn_start, attn_wait, attn_drain = share_rows(send_attn, got_attn, rs.at[0], rr.at[0], loc.at[0])
    mlp_start, mlp_wait, mlp_drain = share_rows(send_mlp, got_mlp, rs.at[1], rr.at[1], loc.at[1])
    acts = [
        share_clip(src, dst, cs.at[i], cr.at[i], loc.at[2 + i, 0])
        for i, (src, dst) in enumerate(
            ((tok, tok_all), (tab, tab_all), (txt, txt_all), (cot, cot_all))
        )
    ]
    attn_start()
    acts[0][0]()
    zl = lax.rem(z, 2)
    for i in range(6):
        vec[i : i + 1] = model_in[5 + i : 6 + i] + time_in[i, pl.ds(core, 1)]
    vec[6:11] = model_in[0:5]
    vec[11:16] = jnp.zeros((5, D), F32)
    heads[0:10] = head_in[:, pl.ds(pl.multiple_of(zl * HW, HW), HW)]
    heads[10:16] = jnp.zeros((6, HW), F32)
    keep_small(heads, heads_out, 0)
    keep_small(vec, vec_out, 1)
    attn_wait(own_attn)

    def attn_place(part, index, half=None):
        start, size = part * (ATTN // 2), ATTN // 2
        if half is not None:
            start, size = start + half * (ATTN // 4), ATTN // 4
        rows = pl.ds(pl.multiple_of(index * (2 * PAIR) + core * PAIR, PAIR), PAIR)
        return wa.at[rows, pl.ds(start, size)]

    def mlp_place(part, index, half=None):
        start, size = (0, FF) if half is None else (half * (FF // 2), FF // 2)
        rows = pl.ds(pl.multiple_of(index * (2 * PAIR) + core * PAIR, PAIR), PAIR)
        return (w_up, w_down)[part].at[rows, pl.ds(start, size)]

    gather_attn = gather_xy(own_attn, attn_place, xs, xr, ks, kr)
    advance(gather_attn)
    for part in (0, 1):
        attn_place(part, mine)[...] = own_attn[part]
    acts[2][0]()
    fill = jnp.zeros((ROWS, 2 * FF - WIDE), F32)
    lane = lax.broadcasted_iota(jnp.int32, (ROWS, FF), 1)
    sides = ([], [])
    for j in (0, 1):
        whole = jnp.concatenate([mlp_w[:, j, :], fill], 1)
        sides[0].append(jnp.where(lane < FF_REAL, whole[:, :FF], 0.0))
        sides[1].append(pltpu.roll(whole, 2 * FF - FF_REAL, 1)[:, :FF])
    for i in (0, 1):
        send_mlp[i] = jnp.concatenate(sides[i], 0).astype(BF)
    mlp_start()
    lane = lax.broadcasted_iota(jnp.int32, (TOK, HEAD), 1)
    for i in (0, 1):
        spots = [places[c, i : i + 1, :].astype(F32) for c in range(3)]
        spots = jnp.concatenate(spots + [jnp.zeros((TOK - 3, TOK), F32)], 0).T
        angle = spots[:, 0:1] * rates[0:1] + spots[:, 1:2] * rates[1:2] + spots[:, 2:3] * rates[2:3]
        tab[i] = jnp.where(lane < HEAD // 2, jnp.cos(angle), jnp.sin(angle))
    acts[1][0]()

    def norm_block(i, carry):
        normed, _ = plain_norm(tok_all[i].astype(F32))
        input_one[block_slice(i)] = (normed * (1.0 + vec[1:2]) + vec[0:1]).astype(BF)
        return carry

    advance(gather_attn, 2)
    acts[3][0]()
    advance(gather_attn, 1)
    acts[0][1]()
    lax.fori_loop(0, 2, norm_block, 0)
    advance(gather_attn, 1)
    lax.fori_loop(2, 4, norm_block, 0)
    save(input_one, tok_all)
    advance(gather_attn, 1)
    mlp_wait(own_mlp)
    locals_ = []
    for part in (0, 1):
        locals_.append(pltpu.make_async_copy(own_mlp.at[part], mlp_place(part, mine), loc.at[6, part]))
        locals_[-1].start()
    advance(gather_attn, 1)
    gather_mlp = gather_xy(own_mlp, mlp_place, ms, mr, js, jr)
    advance(gather_mlp)
    finish(gather_attn)
    locals_.append(pltpu.make_async_copy(wa, w_attn, loc.at[7, 0]))
    locals_[-1].start()
    acts[1][1]()
    acts[2][1]()
    save(tab_all, txt_all)

    stats = Stats(stat, stat_s, stat_r)
    query_lin[...] = product(input_one[...], wa[:, 0:HW]) + heads[0:1]
    key_lin[...] = product(input_one[...], wa[:, HW : 2 * HW]) + heads[1:2]
    words = txt_all[...].reshape(SEQ, D)
    key_two_lin[...] = product(words, wa[:, 4 * HW : 5 * HW]) + heads[6:7]
    norm_wait = stats.start(
        0,
        [
            jnp.sum(ref[...] * ref[...], -1, keepdims=True)
            for ref in (query_lin, key_lin, key_two_lin)
        ],
    )
    value_low[...] = (product(input_one[...], wa[:, 2 * HW : 3 * HW]) + heads[2:3]).astype(BF)
    value_two[...] = (product(words, wa[:, 5 * HW : 6 * HW]) + heads[7:8]).astype(BF)
    save(query_lin, key_lin, key_two_lin, value_low, value_two)
    lane = lax.broadcasted_iota(jnp.int32, (SEQ, 128), 1)
    inverse_query, inverse_key, inverse_key_two = [inverse_root(v) for v in norm_wait()]
    inv[...] = jnp.where(
        lane == 0, inverse_query, jnp.where(lane == 1, inverse_key, jnp.where(lane == 2, inverse_key_two, 0.0))
    )
    cosine, sine = rope_pair(tab_all[...].reshape(SEQ, HEAD))
    for h in range(HEADS):
        cols = head_slice(h)
        for lin, inverse, gain, out in (
            (query_lin, inverse_query, 3, query_rot),
            (key_lin, inverse_key, 4, key_rot),
        ):
            value = lin[:, cols] * inverse * (1.0 + heads[gain : gain + 1, cols])
            out[:, cols] = (value * cosine + swap_halves(value) * sine).astype(BF)
    advance(gather_mlp, 1)
    attend_clip(query_rot, key_rot, value_low, mixed)
    scatter = Scatter(part_one, blocks.at[0], zs.at[0], zr.at[0]).product(mixed, wa[:, W_SELF])
    drains = [scatter]
    key_two[...] = (key_two_lin[...] * inverse_key_two * (1.0 + heads[9:10])).astype(BF)
    save(query_rot, key_rot, key_two, mixed)
    advance(gather_mlp, 1)
    scatter.relay()
    advance(gather_mlp, 2)
    branch = scatter.total() + vec[V_SELF : V_SELF + 1]
    branch_one[...] = branch
    after = tok_all[block_of(z)].astype(F32) + vec[2:3] * branch
    after_one[...] = after
    normed, _ = plain_norm(after)
    spread = Spread(
        input_three,
        (normed * (1.0 + vec[V_GAIN : V_GAIN + 1]) + vec[V_BIAS : V_BIAS + 1]).astype(BF),
        gs.at[0],
        gr.at[0],
    )
    drains.append(spread)
    save(branch_one, after_one)
    advance(gather_mlp, 1)
    spread.relay()
    finish(gather_mlp)
    spread.wait()
    query_two_lin[...] = product(input_three[...], wa[:, W_QUERY]) + heads[5:6]
    norm_wait = stats.start(1, [jnp.sum(query_two_lin[...] * query_two_lin[...], -1, keepdims=True)])
    save(input_three, query_two_lin)
    inverse_query_two = inverse_root(norm_wait()[0])
    inv[...] = jnp.where(lane == 3, inverse_query_two, inv[...])
    query_two[...] = (query_two_lin[...] * inverse_query_two * (1.0 + heads[8:9])).astype(BF)
    attend_clip(query_two, key_two, value_two, mixed_two)
    scatter = Scatter(part_two, blocks.at[1], zs.at[1], zr.at[1]).product(mixed_two, wa[:, W_CROSS])
    drains.append(scatter)
    save(inv, query_two, mixed_two)
    after = after_one[...] + scatter.total() + vec[V_CROSS : V_CROSS + 1]
    after_two[...] = after
    normed, _ = plain_norm(after)
    spread = Spread(
        input_mlp, (normed * (1.0 + vec[4:5]) + vec[3:4]).astype(BF), gs.at[1], gr.at[1]
    )
    drains.append(spread)
    save(after_two)
    spread.relay()
    for copy in locals_:
        copy.wait()
    acts[3][1]()
    for act in acts:
        act[2]()
    attn_drain()
    mlp_drain()
    spread.wait()
    save(input_mlp)
    for transfer in drains:
        transfer.drain()
    for copy in stores:
        copy.wait()


def forward(*args):
    dma = pltpu.SemaphoreType.DMA
    sds = jax.ShapeDtypeStruct
    wide, lin, low = sds((SEQ, D), BF), sds((SEQ, HW), F32), sds((SEQ, HW), BF)
    block = sds((TOK, D), F32)
    outs = [
        sds((SIDE, TOK, HEAD), F32), wide, wide, wide, lin, lin, lin, lin, sds((SEQ, 128), F32),
        low, low, low, low, low, low, low, low, block, block, block,
        sds((SIDE, TOK, D), BF), sds((SIDE, TOK, D), BF),
    ]
    weights = [
        sds((D, ATTN), BF), sds((D, FF), BF), sds((D, FF), BF), sds((SIDE, TOK, D), BF),
        sds((16, HW), F32), sds((16, D), F32),
    ]
    return pl.pallas_call(
        forward_kernel,
        out_shape=weights + outs,
        in_specs=[VM, VM, VM, HB, HB, HB, VM, VM, VM, VM, VM],
        out_specs=[HB] * (len(weights) + len(outs)),
        scratch_shapes=[
            *[pltpu.VMEM(shape.shape, shape.dtype) for shape in outs],
            pltpu.VMEM((2, PAIR, ATTN // 2), BF), pltpu.VMEM((2, PAIR, FF), BF),
            pltpu.VMEM((2, TOK, HEAD), F32), pltpu.VMEM((16, HW), F32), pltpu.VMEM((16, D), F32),
            pltpu.VMEM((D, ATTN), BF),
            pltpu.VMEM((2, PAIR, ATTN // 2), BF),
            pltpu.VMEM((2, PAIR, FF), BF),
            pltpu.VMEM((2, PAIR, ATTN // 2), BF),
            pltpu.VMEM((2, PAIR, FF), BF),
            pltpu.VMEM((SEQ, D), BF),
            pltpu.VMEM((SEQ, D), BF),
            pltpu.VMEM((2, 3, TOK, D), BF),
            pltpu.VMEM((2, 4, 8, SEQ), F32),
            *[dma(s) for s in GATHER_SEMS],
            *[dma(s) for s in GATHER_SEMS],
            dma((2, 2)), dma((2, 2)), dma((4, 3)), dma((4, 3)), dma((8, 2)),
            dma((2, 3)), dma((2, 3)), dma((2, 6)), dma((2, 6)), dma((2, 6)), dma((2, 6)),
            dma((SAVED + 2,)),
        ],
        compiler_params=params(0),
        name="forward",
    )(*args)


BATCH = 768


def peers_xy(x, y, z, core):
    rows = [chip(x + k, y, z, core) for k in (1, 2, 3)]
    lines = [chip(x, y + k, z, core) for k in (1, 2, 3)]
    return rows, lines


def reduce_batch(grads, out, sib, r1, r2, tosend, ss, sr, s1, q1, s2, q2, *swap_sems, gates=None):
    x, y, z, core = here()
    zl = lax.rem(z, 2)
    rows, lines = peers_xy(x, y, z, core)
    sibling = chip(x, y, z, 1 - core)
    wrap = lambda v: lax.rem(v, SIDE)
    swaps, one, two = [], {0: [], 1: []}, {0: [], 1: []}
    opens, waits = gates if gates is not None else (None, None)

    def signal(gate, devices):
        for device in devices:
            pl.semaphore_signal(gate, inc=1, device_id=device, device_id_type=MESH)

    def push(part, slot, target, half, place, step):
        span = pl.ds(2 * half, 2)
        src = (
            grads.at[0, span, wrap(y + target), core]
            if part == 0
            else grads.at[1, wrap(x + target), span, core]
        )
        device = (lines, rows)[part][step - 1]
        copy = remote(src, r1.at[part, place, span], s1.at[part, slot], q1.at[part, slot], device)
        copy.start()
        one[part].append(copy)

    if waits is not None:
        pl.semaphore_wait(waits[0], 1)
    for part in (0, 1):
        swaps.append(
            remote(grads.at[part, :, :, 1 - core], sib.at[part], ss.at[part], sr.at[part], sibling)
        )
        swaps[part].start()
    yield
    for part in (0, 1):
        swaps[part].wait_recv()

        def add_pair(k, carry):
            a, b = lax.div(k, SIDE), lax.rem(k, SIDE)
            grads[part, a, b, core] = grads[part, a, b, core] + sib[part, a, b]
            return carry

        lax.fori_loop(0, SIDE * SIDE, add_pair, 0)
        if part == 0 and waits is not None:
            pl.semaphore_wait(waits[1], 6)
        push(part, 0, 2, 0, 2, 1)
        push(part, 1, 2, 1, 2, 3)
        push(part, 2, 1, 1, 0, 1)
        push(part, 3, 3, 0, 1, 3)
    if opens is not None:
        signal(opens[0], [sibling])
    yield
    for part in (0, 1):
        for slot, step in ((0, 1), (1, 3)):
            one[part][slot].wait_recv()
            for i in (2 * slot, 2 * slot + 1):
                if part == 0:
                    grads[0, i, wrap(y + step), core] = grads[0, i, wrap(y + step), core] + r1[0, 2, i]
                else:
                    grads[1, wrap(x + step), i, core] = grads[1, wrap(x + step), i, core] + r1[1, 2, i]
            push(part, 4 + slot, step, slot, slot, step)
    yield
    for part in (0, 1):
        for copy in one[part][2:]:
            copy.wait_recv()

        def add_line(k, carry):
            a, b = (k, y) if part == 0 else (x, k)
            total = grads[part, a, b, core].astype(F32)
            total = total + (r1[part, 0, k].astype(F32) + r1[part, 1, k].astype(F32))
            grads[part, a, b, core] = total.astype(BF)
            return carry

        lax.fori_loop(0, SIDE, add_line, 0)
        for k in (2, 1, 3):
            src = grads.at[0, wrap(x + k), y, core] if part == 0 else grads.at[1, x, wrap(y + k), core]
            device = (rows, lines)[part][k - 1]
            copy = remote(src, r2.at[part, k - 1], s2.at[part, k - 1], q2.at[part, k - 1], device)
            copy.start()
            two[part].append(copy)
    yield
    final = []
    for part in (0, 1):
        for copy in two[part]:
            copy.wait_recv()
        total = grads[part, x, y, core].astype(F32)
        for i in range(3):
            total = total + r2[part, i].astype(F32)
        final.append(total)
    if opens is not None:
        signal(opens[1], [*rows, *lines])
    for target in (0, 1):
        span = slice(target * ROWS, target * ROWS + ROWS)
        tosend[target] = jnp.concatenate([final[0][span], final[1][span]], 0).astype(tosend.dtype)
    if out is not None:
        exchange = swap_rows(tosend, out, *swap_sems)
        next(exchange)
        yield
        finish(exchange)
    for copy in swaps + one[0] + one[1] + two[0] + two[1]:
        copy.wait_send()


def swap_rows(owned, out, s3, q3, l3):
    x, y, z, core = here()
    zl = lax.rem(z, 2)
    other = z + 1 - 2 * zl
    far = [
        remote(owned.at[t], out.at[zl], s3.at[t], q3.at[zl], chip(x, y, other, t)) for t in (0, 1)
    ]
    self_copy = pltpu.make_async_copy(owned.at[core], out.at[zl], l3.at[0])
    near = remote(owned.at[1 - core], out.at[zl], s3.at[0], q3.at[zl], chip(x, y, z, 1 - core))

    def got(slot):
        remote(owned.at[0], out.at[slot], s3.at[0], q3.at[slot], chip(x, y, z, core)).wait_recv()

    @pl.when(core == zl)
    def _():
        self_copy.start()
        near.start()

    @pl.when(core != zl)
    def _():
        for copy in far:
            copy.start()

    yield

    @pl.when(core == zl)
    def _():
        self_copy.wait()
        near.wait_send()
        got(1 - zl)

    @pl.when(core != zl)
    def _():
        for copy in far:
            copy.wait_send()
        got(zl)
        got(1 - zl)


def reduce_buffers():
    return [
        pltpu.VMEM((2, SIDE, SIDE, PAIR, BATCH), BF),
        pltpu.VMEM((2, 3, SIDE, PAIR, BATCH), BF),
        pltpu.VMEM((2, 3, PAIR, BATCH), BF),
    ]


def reduce_sems():
    dma = pltpu.SemaphoreType.DMA
    return [dma((2,)), dma((2,)), dma((2, 6)), dma((2, 6)), dma((2, 3)), dma((2, 3))]


def swap_sems():
    dma = pltpu.SemaphoreType.DMA
    return [dma((2,)), dma((2,)), dma((1,))]


def reduce_scratch():
    return [*reduce_buffers(), pltpu.VMEM((2, PAIR, BATCH), BF), *reduce_sems(), *swap_sems()]


GRADS = (2, SIDE, SIDE, 2, PAIR, BATCH)
SLAB = D // SIDE


def weight_grad(left, right, grads, part, start):
    width = right.shape[1]

    def slab(i, carry):
        turned = left[:, pl.ds(pl.multiple_of(i * SLAB, SLAB), SLAB)].T
        value = product(turned, right).astype(BF).reshape(SIDE, 2, PAIR, width)
        grads[part, i, :, :, :, start : start + width] = value
        return carry

    lax.fori_loop(0, SIDE, slab, 0)


def column_sum(values):
    return jnp.sum(values.astype(F32), 0, keepdims=True)


def deliver(src, dst, s, r, l):
    x, y, z, core = here()
    zh = lax.div(z, 2)
    far = remote(src, dst.at[core], s.at[0], r.at[core], chip(x, y, z + 2, zh))
    near = remote(src, dst.at[core], s.at[1], r.at[core], chip(x, y, z, zh))
    self_copy = pltpu.make_async_copy(src, dst.at[core], l)

    def got(slot):
        remote(src, dst.at[slot], s.at[0], r.at[slot], chip(x, y, z, core)).wait_recv()

    def start():
        far.start()

        @pl.when(core == zh)
        def _():
            self_copy.start()

        @pl.when(core != zh)
        def _():
            near.start()

    def wait():
        @pl.when(core == zh)
        def _():
            self_copy.wait()
            got(1 - core)

        @pl.when(core != zh)
        def _():
            near.wait_send()
            got(0)
            got(1)

        far.wait_send()

    return start, wait


CUBE = 0.044715
ROOT = math.sqrt(2.0 / math.pi)


def gelu_pair(u):
    square = u * u
    t = jnp.tanh(ROOT * u * (1.0 + CUBE * square))
    half = 0.5 * (1.0 + t)
    return u * half, half + 0.5 * u * (1.0 - t * t) * (ROOT * (1.0 + 3.0 * CUBE * square))


def mlp_kernel(
    a_in, cot_all, w_up, w_down, after_in, vec, up_bias,
    low_out, grad_out, sums_out, bias_out, result_out, owned_a_out, owned_b_out, owned_c_out,
    grad_after, sums, bias_sum, owned_a, owned_b, owned_c, keep, a, low, ahead, behind, hidden, act, back, acc, part, part_back, after_two, low_two, result, dy_own,
    blocks, bias, zs, zr, gs, gr, loc, ring, gate_core, gate_chips, *rest,
):
    x, y, z, core = here()
    rows, lines = peers_xy(x, y, z, core)
    own_rows = block_slice(block_of(z))

    def load(src, dst, sem):
        copy = pltpu.make_async_copy(src, dst, sem)
        copy.start()
        return copy

    def third(n):
        return pl.ds(n % 3 * BATCH, BATCH)

    def weights(n):
        return ahead.at[n % 2].reshape(D, BATCH)

    def load_ahead(n):
        return load((w_up, w_down)[n // 3].at[:, third(n)], weights(n), ring.at[0, n % 2])

    def load_behind(n):
        return load((w_down, w_up)[n // 3].at[:, third(n)], behind.at[n % 2], ring.at[1, n % 2])

    stores = []

    def save(ref, out):
        stores.append(load(ref, out, keep.at[len(stores)]))

    aheads, behinds = {0: load_ahead(0)}, {}
    fetch_a = load(a_in, a, loc.at[0])
    arrive = knock(column(x, y, z, core) + rows + lines)
    line = jnp.concatenate(
        [up_bias[i : i + 1] for i in range(WIDE // 128)] + [jnp.zeros((1, 2 * FF - WIDE), F32)], 1
    )
    moved_line = pltpu.roll(line, 2 * FF - FF_REAL, 1)
    lane = lax.broadcasted_iota(jnp.int32, (1, FF), 1)
    line = jnp.where(lax.rem(z, 2) == 0, line[:, :FF], moved_line[:, :FF])
    bias[0:1] = jnp.where(lane < FF_REAL, line, 0.0)
    sums[...] = jnp.zeros_like(sums)
    fetch_a.wait()
    aheads[0].wait()
    aheads[1], behinds[0] = load_ahead(1), load_behind(0)
    fetch_low = load(cot_all.reshape(SEQ, D), low, loc.at[1])
    behinds[1] = load_behind(1)
    fetch_after = load(after_in, after_two, loc.at[2])
    hidden[0] = product(a[...], weights(0)[...])
    aheads[2] = load_ahead(2)
    dy = dy_own

    grads = [rest[0], rest[1], ahead]
    gates = (gate_core, gate_chips)
    first, second, sems = rest[2:5], rest[5:8], rest[8:]
    owned = (owned_a, owned_b, owned_c)
    jobs = [
        reduce_batch(
            grads[b], None, *(first, second, first)[b], owned[b], *sems[6 * b : 6 * b + 6],
            gates=((gates, None), None, (None, gates))[b],
        )
        for b in range(3)
    ]

    def step(n):
        if n < 5:
            aheads[n + 1].wait()
            left = a if n < 2 else low
            behinds[n].wait()
            hidden[(n + 1) % 2] = product(left[...], weights(n + 1)[...])
        else:
            behinds[n].wait()
        cols = slice(n % 3 * BATCH, (n % 3 + 1) * BATCH)
        if n < 3:
            value, slope = gelu_pair(hidden[n % 2] + bias[0:1, cols])
            value = value.astype(BF)
            act[:, cols] = value
            back[:, cols] = slope.astype(BF)
        else:
            value = (hidden[n % 2] * back[:, cols].astype(F32)).astype(BF)
            back[:, cols] = value
            bias_sum[0:1, cols] = column_sum(value)
        moved = contract_last(value, behind[n % 2])
        if n % 3 == 0:
            acc[...] = moved
        elif n % 3 == 1:
            acc[...] += moved
        else:
            (part, part_back)[n // 3][...] = (acc[...] + moved).astype(BF)
        if n < 3:
            aheads[n + 3] = load_ahead(n + 3)
        if n < 4:
            behinds[n + 2] = load_behind(n + 2)

    def third_grads(n, b, half):
        cols = slice(n % 3 * BATCH, (n % 3 + 1) * BATCH)
        left, right = ((low, act), (a, back))[n // 3]
        weight_grad(left, right[:, cols], grads[b], half, 0)

    step(0)
    fetch_low.wait()
    dy_own[...] = low[own_rows].astype(F32)
    for start in range(0, SEQ, TOK):
        block = slice(start, start + TOK)
        low[block] = (low[block].astype(F32) * vec[5:6]).astype(BF)
    sums[2:3] = column_sum(low[own_rows])
    step(1)
    third_grads(0, 0, 0)
    third_grads(1, 0, 1)
    arrive()
    advance(jobs[0])
    step(2)
    down_sum = Scatter(part, blocks.at[0], zs.at[0], zr.at[0]).held()
    advance(jobs[0])
    third_grads(2, 1, 0)
    step(3)
    advance(jobs[0])
    third_grads(3, 1, 1)
    advance(jobs[1])
    down_sum.relay()
    step(4)
    advance(jobs[0])
    advance(jobs[1])
    step(5)
    back_sum = Scatter(part_back, blocks.at[1], zs.at[1], zr.at[1]).held()
    save(bias_sum, bias_out)
    third_grads(4, 2, 0)
    third_grads(5, 2, 1)
    advance(jobs[2])
    finish(jobs[0])
    save(owned_a, owned_a_out)
    back_sum.relay()
    advance(jobs[1])
    fetch_after.wait()
    branch = down_sum.total() + vec[V_DOWN : V_DOWN + 1]
    result[...] = (after_two[...] + vec[5:6] * branch).astype(BF)
    save(result, result_out)
    sums[10:11] = column_sum(dy[...] * branch)
    advance(jobs[2])
    advance(jobs[1])
    total = back_sum.total()
    normed, inverse = plain_norm(after_two[...])
    sums[8:9] = column_sum(total)
    sums[9:10] = column_sum(total * normed)
    value = dy[...] + norm_back(total * (1.0 + vec[4:5]), normed, inverse)
    grad_after[...] = value
    value = value.astype(BF)
    spread = Spread(low_two, value, gs, gr)
    sums[1:2] = column_sum(value)
    save(grad_after, grad_out)
    save(sums, sums_out)
    advance(jobs[2])
    finish(jobs[1])
    save(owned_b, owned_b_out)
    spread.relay()
    advance(jobs[2])
    spread.wait()
    store = pltpu.make_async_copy(low_two, low_out, loc.at[3])
    store.start()
    finish(jobs[2])
    save(owned_c, owned_c_out)
    store.wait()
    for copy in stores:
        copy.wait()
    down_sum.drain()
    back_sum.drain()
    spread.drain()


def mlp_pass(a, cot, up, down, after, vec, bias):
    dma = pltpu.SemaphoreType.DMA
    sds = jax.ShapeDtypeStruct
    wide = pltpu.VMEM((SEQ, D), BF)
    tiles = pltpu.VMEM((2, D, BATCH), BF)
    units = pltpu.VMEM((SEQ, FF), BF)
    owned = sds((2, PAIR, BATCH), BF)
    outs = [
        (sds((SEQ, D), BF), HB), (sds((TOK, D), F32), VM), (sds((16, D), F32), VM),
        (sds((8, FF), F32), VM), (sds((TOK, D), BF), HB), (owned, VM), (owned, VM), (owned, VM),
    ]
    return pl.pallas_call(
        mlp_kernel,
        out_shape=[shape for shape, _ in outs],
        in_specs=[HB] * 5 + [VM] * 2,
        out_specs=[HB] * len(outs),
        scratch_shapes=[
            *[pltpu.VMEM(outs[i][0].shape, outs[i][0].dtype) for i in (1, 2, 3, 5, 6, 7)], dma((7,)),
            wide, wide, pltpu.VMEM(GRADS, BF), tiles, pltpu.VMEM((2, SEQ, BATCH), F32), units, units,
            pltpu.VMEM((SEQ, D), F32), wide, wide, pltpu.VMEM((TOK, D), F32), wide, pltpu.VMEM((TOK, D), BF),
            pltpu.VMEM((TOK, D), F32),
            pltpu.VMEM((2, 3, TOK, D), BF), pltpu.VMEM((8, FF), F32), dma((2, 6)), dma((2, 6)), dma((6,)), dma((6,)),
            dma((5,)), dma((2, 2)), pltpu.SemaphoreType.REGULAR, pltpu.SemaphoreType.REGULAR,
            pltpu.VMEM(GRADS, BF), pltpu.VMEM(GRADS, BF),
            *reduce_buffers(), *reduce_buffers(), *reduce_sems(), *reduce_sems(), *reduce_sems(),
        ],
        compiler_params=params(1),
        name="mlp",
    )(a, cot, up, down, after, vec, bias)


def sum_over_xy(held, sends, recvs):
    x, y, z, core = here()
    for stage, peers in enumerate(peers_xy(x, y, z, core)):
        base = 4 * stage
        copies = [
            remote(held.at[base], held.at[base + k], sends.at[stage, k], recvs.at[stage, k], peers[k - 1])
            for k in (2, 1, 3)
        ]
        for copy in copies:
            copy.start()
        yield
        for copy in copies:
            copy.wait()
        held[base + 4] = (held[base] + held[base + 1]) + (held[base + 2] + held[base + 3])


def model_job(model, time_out, col, held, sends, recvs):
    x, y, z, core = here()
    copies = [
        remote(model, col.at[k], sends.at[2, k], recvs.at[2, k], chip(x, y, z + k, core)) for k in (2, 1, 3)
    ]
    for copy in copies:
        copy.start()
    yield
    for copy in copies:
        copy.wait()
    time_out[core] = (model[...] + col[1]) + (col[2] + col[3])
    swap = remote(
        time_out.at[core], time_out.at[core], sends.at[2, 0], recvs.at[2, 0], chip(x, y, z, 1 - core)
    )
    swap.start()
    yield
    swap.wait()
    held[0] = time_out[0] + time_out[1]
    yield from sum_over_xy(held, sends, recvs)


def head_job(heads, head_out, other, held, sends, recvs):
    x, y, z, core = here()
    zl = lax.rem(z, 2)
    swap = remote(heads, other, sends.at[2, 0], recvs.at[2, 0], chip(x, y, z, 1 - core))
    swap.start()
    yield
    swap.wait()
    held[0] = heads[...] + other[...]
    yield from sum_over_xy(held, sends, recvs)
    head_out[zl] = held[8]
    last = remote(
        held.at[8], head_out.at[zl], sends.at[2, 1], recvs.at[2, 1], chip(x, y, z + 1 - 2 * zl, core)
    )
    last.start()
    yield
    last.wait()


def model_scratch(rows, width):
    dma = pltpu.SemaphoreType.DMA
    return [pltpu.VMEM((4, rows, width), F32), pltpu.VMEM((9, rows, width), F32), dma((3, 4)), dma((3, 4))]


def head_scratch():
    dma = pltpu.SemaphoreType.DMA
    return [pltpu.VMEM((16, HW), F32), pltpu.VMEM((9, 16, HW), F32), dma((3, 4)), dma((3, 4))]


def attend_clip_back(query, keys, values, grad, grad_query, grad_keys, grad_values):
    for h in range(HEADS):
        cols = head_slice(h)
        k, v = keys[:, cols], values[:, cols]
        for start in range(0, SEQ, 256):
            rows = slice(start, start + 256)
            q, do = query[rows, cols], grad[rows, cols]
            weights = softmax_rows(q, k)
            grad_weights = contract_last(do, v)
            delta = jnp.sum(weights * grad_weights, -1, keepdims=True)
            grad_scores = (weights * (grad_weights - delta)).astype(BF)
            grad_query[rows, cols] = product(grad_scores, k) * SCALE
            to_keys = contract_rows(grad_scores, q) * SCALE
            to_values = contract_rows(weights.astype(BF), do)
            if start:
                grad_keys[:, cols] += to_keys
                grad_values[:, cols] += to_values
            else:
                grad_keys[:, cols] = to_keys
                grad_values[:, cols] = to_values


def root_back(linear, inverse, scaled, dot):
    return (inverse * scaled - linear * (inverse * inverse * inverse * dot * (1.0 / D))).astype(BF)


EARLY, LATE = (0, 1, 3, 4, 7, 8, 9, 10), (5, 6, 2)


def backward_kernel(
    wa_in, low_in, after_in, branch_in, query_lin_in, key_lin_in, query_two_lin_in, key_two_lin_in,
    query_rot_in, key_rot_in, value_low_in, query_two_in, key_two_in, value_two_in, mixed_in,
    mixed_two_in, words_in, three_in, one_in, tok_in, grad_in, tab_in, inv_in, result,
    vec, heads, sums, bias_sum, owned_a, owned_b, owned_c, in_m, out_m, mlp_m,
    out_result, out_tokens, out_words, time_sum_out, model_sum_out, head_sum_out, narrow_out, wide_out, gram_out,
    time_out, model_out, head_out, narrow, wide, gram, keep,
    wa, low_wide, after_one, branch_one, lin_a, lin_b, qa, ka, va, mixed, operand, tok_own,
    grad_after, tab, inv, grad_query, grad_kv, grad_qkv, part_cross, part_words, blocks,
    held, gq, gk, gv, model, head_sums, low_tokens, low_words, mine, theirs,
    sums_a, sums_b, mlp_a, mlp_b, mlp_c,
    stat, stat_s, stat_r, zs, zr, gs, gr, ds, dr, loc, *rest,
):
    x, y, z, core = here()
    rows, lines = peers_xy(x, y, z, core)
    slots = iter(range(32))
    own_block = block_of(z)

    def fetch(src, dst):
        copy = pltpu.make_async_copy(src, dst, loc.at[next(slots)])
        copy.start()
        return copy

    out_cols, in_cols = pl.ds(6 * HW, 2 * HW), pl.ds(0, 6 * HW)
    first = [fetch(low_in, low_wide), fetch(wa_in.at[:, out_cols], wa.at[:, out_cols])]
    inputs = [
        fetch(query_two_in, qa), fetch(key_two_in, ka), fetch(value_two_in, va),
        fetch(query_two_lin_in, lin_a), fetch(key_two_lin_in, lin_b), fetch(inv_in, inv),
    ]
    second = [
        fetch(mixed_two_in, mixed), fetch(wa_in.at[:, in_cols], wa.at[:, in_cols]),
        fetch(words_in.reshape(SEQ, D), operand),
    ]
    third = [
        fetch(after_in, after_one), fetch(branch_in, branch_one), fetch(grad_in, grad_after),
        fetch(tab_in, tab), fetch(tok_in.at[own_block], tok_own),
    ]
    arrive = knock(column(x, y, z, core) + rows + lines)
    for row in (1, 8, 9, 10):
        i = EARLY.index(row)
        model[i : i + 1] = sums[row : row + 1]
    head_sums[...] = jnp.zeros_like(head_sums)
    for i in range(6):
        head_sums[10 + i : 11 + i] = bias_sum[0:1, i * HW : (i + 1) * HW]
    refs_a, refs_b, early_refs, late_refs, head_refs, rest = (
        rest[:14], rest[14:28], rest[28:32], rest[32:36], rest[36:40], rest[40:],
    )
    (late, time_late, time_early, gram_sems), swap_refs = rest[:4], rest[4:]
    late[...] = jnp.zeros_like(late)
    n, w = 8 * ROWS, 2 * ROWS
    halves = (slice(0, ROWS), slice(ROWS, 2 * ROWS))

    stores = []

    def save(ref, out):
        copy = pltpu.make_async_copy(ref, out, keep.at[len(stores)])
        copy.start()
        stores.append(copy)

    def new_narrow(j, ref, part, col):
        rows = halves[part]
        grad = jnp.concatenate([ref[i].astype(F32)[rows, col : col + HW] for i in (0, 1)], 1)
        old = in_m[j] if j < 6 else out_m[:, j - 6, :]
        narrow[j * ROWS : (j + 1) * ROWS] = MOMENTUM * old + grad

    def new_wide(j, thirds):
        chips = [jnp.concatenate([ref[i].astype(F32)[rows] for ref, rows in thirds], 1) for i in (0, 1)]
        wide[j * ROWS : (j + 1) * ROWS] = MOMENTUM * mlp_m[:, j, :] + join_hidden(*chips)

    hidden_rows = [
        swap_rows(src, dst, *swap_refs[3 * i : 3 * i + 3])
        for i, (src, dst) in enumerate(((owned_a, mlp_a), (owned_b, mlp_b), (owned_c, mlp_c)))
    ]
    grads_a, grads_b = refs_a[0], refs_b[0]
    job_a = reduce_batch(grads_a, sums_a, *refs_a[1:])
    job_b = reduce_batch(grads_b, sums_b, *refs_b[1:])
    stats = Stats(stat, stat_s, stat_r)
    drains = []

    arrive()
    send_result, wait_result = deliver(result, out_result, ds.at[2], dr.at[2], loc.at[29])
    send_result()
    for copy in first:
        copy.wait()
    held[...] = product(low_wide[...], wa[:, W_CROSS]).astype(BF)
    for copy in inputs:
        copy.wait()
    attend_clip_back(qa, ka, va, held, gq, gk, gv)
    inverse_query, inverse_key, inverse_key_two, inverse_query_two = [inv[:, i : i + 1] for i in range(4)]
    dots = stats.start(
        0,
        [
            jnp.sum(lin_a[...] * (gq[...] * (1.0 + heads[8:9])), -1, keepdims=True),
            jnp.sum(lin_b[...] * (gk[...] * (1.0 + heads[9:10])), -1, keepdims=True),
        ],
    )
    for job in hidden_rows:
        advance(job)
    head_sums[8:9] = column_sum(gq[...] * lin_a[...] * inverse_query_two)
    head_sums[9:10] = column_sum(gk[...] * lin_b[...] * inverse_key_two)
    low = gv[...].astype(BF)
    grad_kv[:, HW:] = low
    head_sums[7:8] = column_sum(low)
    for copy in second:
        copy.wait()
    weight_grad(low_wide, mixed[...], grads_a, 1, HW)
    dot_query, dot_key = dots()
    low = root_back(lin_a[...], inverse_query_two, gq[...] * (1.0 + heads[8:9]), dot_query)
    grad_query[...] = low
    head_sums[5:6] = column_sum(low)
    cross = Scatter(part_cross, blocks.at[0], zs.at[0], zr.at[0]).product(grad_query, wa[:, W_QUERY])
    low = root_back(lin_b[...], inverse_key_two, gk[...] * (1.0 + heads[9:10]), dot_key)
    grad_kv[:, :HW] = low
    head_sums[6:7] = column_sum(low)
    selfs = [
        fetch(query_rot_in, qa), fetch(key_rot_in, ka), fetch(value_low_in, va),
        fetch(query_lin_in, lin_a), fetch(key_lin_in, lin_b), fetch(mixed_in, mixed),
    ]
    weight_grad(operand, grad_kv[...], grads_a, 0, 0)
    next_operand = fetch(three_in, operand)
    next_operand.wait()
    cross.relay()
    weight_grad(operand, grad_query[...], grads_a, 1, 0)
    next_operand = fetch(one_in, operand)
    advance(job_a)
    part_words[...] = contract_last(grad_kv[...], wa[:, W_TEXT]).astype(BF)
    for copy in third:
        copy.wait()

    total = cross.total()
    normed, inverse = plain_norm(after_one[...])
    model[3 : 4] = column_sum(total)
    model[2 : 3] = column_sum(total * normed)
    value = grad_after[...] + norm_back(total * (1.0 + vec[V_GAIN : V_GAIN + 1]), normed, inverse)
    grad_after[...] = value
    model[4 : 5] = column_sum(value * branch_one[...])
    low = (value * vec[2:3]).astype(BF)
    model[0 : 1] = column_sum(low)
    spread = Spread(low_wide, low, gs, gr)
    drains.append(spread)
    advance(job_a)
    spread.relay()
    early = model_job(model, time_early, *early_refs)
    advance(early)
    spread.wait()
    advance(job_a)
    word_sum = Scatter(part_words, blocks.at[1], zs.at[1], zr.at[1]).held()
    drains.append(word_sum)

    held[...] = product(low_wide[...], wa[:, W_SELF]).astype(BF)
    for copy in selfs:
        copy.wait()
    attend_clip_back(qa, ka, va, held, gq, gk, gv)
    cosine, sine = rope_pair(tab[...].reshape(SEQ, HEAD))
    for ref in (gq, gk):
        for h in range(HEADS):
            cols = head_slice(h)
            value = ref[:, cols]
            ref[:, cols] = value * cosine - swap_halves(value) * sine
    dots = stats.start(
        1,
        [
            jnp.sum(lin_a[...] * (gq[...] * (1.0 + heads[3:4])), -1, keepdims=True),
            jnp.sum(lin_b[...] * (gk[...] * (1.0 + heads[4:5])), -1, keepdims=True),
        ],
    )
    head_sums[3:4] = column_sum(gq[...] * lin_a[...] * inverse_query)
    head_sums[4:5] = column_sum(gk[...] * lin_b[...] * inverse_key)
    low = gv[...].astype(BF)
    grad_qkv[:, 2 * HW :] = low
    head_sums[2:3] = column_sum(low)
    next_operand.wait()
    weight_grad(low_wide, mixed[...], grads_b, 1, HW)
    cross.drain()
    advance(early)
    dot_query, dot_key = dots()
    word_sum.relay()
    advance(job_a)
    for i, (lin, inverse, ref, dot) in enumerate(
        ((lin_a, inverse_query, gq, dot_query), (lin_b, inverse_key, gk, dot_key))
    ):
        low = root_back(lin[...], inverse, ref[...] * (1.0 + heads[3 + i : 4 + i]), dot)
        grad_qkv[:, i * HW : (i + 1) * HW] = low
        head_sums[i : i + 1] = column_sum(low)
    token_sum = Scatter(part_cross, blocks.at[0], zs.at[2], zr.at[2])
    token_sum.product(grad_qkv, wa[:, W_QKV], (2, 1, 3))
    drains.append(token_sum)
    advance(job_a)
    head_total = head_job(head_sums, head_out, *head_refs)
    advance(head_total)
    weight_grad(operand, grad_qkv[:, : 2 * HW], grads_b, 0, 0)
    weight_grad(operand, grad_qkv[:, 2 * HW :], grads_b, 1, 0)
    advance(job_b)
    token_sum.relay()
    token_sum.product(grad_qkv, wa[:, W_QKV], (0,))
    advance(head_total)
    for job in hidden_rows:
        finish(job)
    top, bottom = halves
    new_wide(0, ((mlp_b, bottom), (mlp_c, top), (mlp_c, bottom)))
    new_wide(1, ((mlp_a, top), (mlp_a, bottom), (mlp_b, top)))
    save(wide, wide_out)
    advance(job_b)
    mine[:n, n:] = jnp.zeros((n, w), F32)
    mine[n:, :n] = jnp.zeros((w, n), F32)
    mine[n:, n:] = gram_of(wide[...])
    advance(early)

    total = token_sum.total()
    normed, inverse = plain_norm(tok_own[...].astype(F32))
    for i, row in enumerate((column_sum(total), column_sum(total * normed), sums[2:3])):
        for k in range(SIDE):
            late[SIDE * i + k : SIDE * i + k + 1] = row[:, k * HW : (k + 1) * HW]
    late_total = model_job(late, time_late, *late_refs)
    advance(late_total)
    advance(job_b)
    value = grad_after[...] + norm_back(total * (1.0 + vec[1:2]), normed, inverse)
    low_tokens[...] = value.astype(BF)
    send_tokens, wait_tokens = deliver(low_tokens, out_tokens, ds.at[1], dr.at[1], loc.at[31])
    low_words[...] = word_sum.total().astype(BF)
    send_words, wait_words = deliver(low_words, out_words, ds.at[0], dr.at[0], loc.at[30])
    advance(late_total)
    send_tokens()
    advance(job_b)
    advance(late_total)
    send_words()
    finish(job_a)
    for j, ref, part, col in ((3, sums_a, 1, 0), (4, sums_a, 0, 0), (5, sums_a, 0, HW), (7, sums_a, 1, HW)):
        new_narrow(j, ref, part, col)
    advance(head_total)
    advance(early)
    advance(job_b)
    advance(late_total)
    advance(head_total)
    finish(early)
    finish(job_b)
    for j, ref, part, col in ((0, sums_b, 0, 0), (1, sums_b, 0, HW), (2, sums_b, 1, 0), (6, sums_b, 1, HW)):
        new_narrow(j, ref, part, col)
    save(narrow, narrow_out)
    mine[:n, :n] = gram_of(narrow[...])
    same, _ = block_mask(10 * ROWS)
    blocks_only = jnp.where(same, mine[...], 0.0)
    compact = blocks_only[:ROWS]
    for j in range(1, 10):
        compact = compact + blocks_only[j * ROWS : (j + 1) * ROWS]
    theirs[0] = compact
    swap = remote(theirs.at[0], theirs.at[1], gram_sems.at[0], gram_sems.at[1], chip(x, y, z + 2, core))
    swap.start()
    finish(late_total)
    finish(head_total)
    save(head_out, head_sum_out)
    for i, row in enumerate(EARLY):
        model_out[row : row + 1] = early_refs[1][8, i : i + 1]
        if row > 4:
            for clip in (0, 1):
                time_out[row - 5, clip : clip + 1] = time_early[clip, i : i + 1]
    for i, row in enumerate(LATE):
        for k in range(SIDE):
            cols = slice(k * HW, (k + 1) * HW)
            part = slice(SIDE * i + k, SIDE * i + k + 1)
            model_out[row : row + 1, cols] = late_refs[1][8, part]
            if row > 4:
                for clip in (0, 1):
                    time_out[row - 5, clip : clip + 1, cols] = time_late[clip, part]
    save(time_out, time_sum_out)
    save(model_out, model_sum_out)
    wait_result()
    wait_tokens()
    wait_words()
    swap.wait()
    gram[...] = theirs[0] + theirs[1]
    save(gram, gram_out)
    for copy in stores:
        copy.wait()
    for transfer in drains:
        transfer.drain()


def backward(hbm, vmem):
    dma = pltpu.SemaphoreType.DMA
    sds = jax.ShapeDtypeStruct
    lin = pltpu.VMEM((SEQ, HW), F32)
    low = pltpu.VMEM((SEQ, HW), BF)
    wide = pltpu.VMEM((SEQ, D), BF)
    block = pltpu.VMEM((TOK, D), F32)
    low_block = pltpu.VMEM((TOK, D), BF)
    summed = pltpu.VMEM((2, PAIR, BATCH), BF)
    size = 10 * ROWS
    square = pltpu.VMEM((size, size), F32)
    outs = [
        *[(sds((2, TOK, D), BF), HB)] * 3, (sds((6, 2, D), F32), VM),
        (sds((16, D), F32), VM), (sds((2, 16, HW), F32), VM), (sds((8 * ROWS, 2 * HW), F32), VM),
        (sds((2 * ROWS, WIDE), F32), VM), (sds((ROWS, size), F32), VM),
    ]
    batch = [pltpu.VMEM(GRADS, BF), *reduce_scratch()]
    return pl.pallas_call(
        backward_kernel,
        out_shape=[shape for shape, _ in outs],
        in_specs=[HB] * len(hbm) + [VM] * len(vmem),
        out_specs=[HB] * len(outs),
        scratch_shapes=[
            *[pltpu.VMEM(shape.shape, shape.dtype) for shape, _ in outs[3:]], dma((6,)),
            pltpu.VMEM((D, ATTN), BF), wide, block, block, lin, lin, low, low, low, low, wide,
            low_block, block, pltpu.VMEM((SIDE, TOK, HEAD), F32), pltpu.VMEM((SEQ, 128), F32),
            low, pltpu.VMEM((SEQ, 2 * HW), BF), pltpu.VMEM((SEQ, 3 * HW), BF), wide, wide,
            pltpu.VMEM((2, 3, TOK, D), BF), low, lin, lin, lin, pltpu.VMEM((8, D), F32),
            pltpu.VMEM((16, HW), F32), low_block, low_block, square, pltpu.VMEM((2, ROWS, size), F32),
            summed, summed, summed, summed, summed,
            pltpu.VMEM((2, 4, 8, SEQ), F32),
            dma((2, 3)), dma((2, 3)), dma((3, 6)), dma((3, 6)), dma((6,)), dma((6,)), dma((3, 2)),
            dma((3, 2)), dma((32,)), *batch, *batch, *model_scratch(8, D),
            *model_scratch(16, HW), *head_scratch(), pltpu.VMEM((16, HW), F32), pltpu.VMEM((2, 16, HW), F32),
            pltpu.VMEM((2, 8, D), F32), dma((2,)), *swap_sems(), *swap_sems(), *swap_sems(),
        ],
        compiler_params=params(2),
        name="backward",
    )(*hbm, *vmem)


def block_mask(size):
    row = lax.broadcasted_iota(jnp.int32, (size, size), 0)
    col = lax.broadcasted_iota(jnp.int32, (size, size), 1)
    return lax.div(row, ROWS) == lax.div(col, ROWS), row == col


def times(a, b):
    return jnp.dot(a, b, precision=HIGHEST, preferred_element_type=F32)


def gram_of(blocks):
    return lax.dot_general(
        blocks, blocks, (((1,), (1,)), ((), ())), precision=HIGHEST, preferred_element_type=F32
    )


def newton_factor(gram, size):
    same, eye = block_mask(size)
    gram = jnp.where(same, jnp.concatenate([gram] * (size // ROWS), 0), 0.0)
    diagonal = jnp.where(eye, gram, 0.0)
    by_row = jnp.sum(diagonal, 1, keepdims=True)
    by_col = jnp.sum(diagonal, 0, keepdims=True)
    total_row = jnp.sum(jnp.where(same, by_col, 0.0), 1, keepdims=True)
    total_col = jnp.sum(jnp.where(same, by_row, 0.0), 0, keepdims=True)
    scale_row = 1.0 / (jnp.sqrt(total_row) + ORTHO_EPSILON)
    scale_col = 1.0 / (jnp.sqrt(total_col) + ORTHO_EPSILON)
    current = gram * scale_row * scale_col
    whole = None
    for turn in range(NS_STEPS):
        square = times(current, current)
        step = NEWTON_SECOND * current + NEWTON_THIRD * square + jnp.where(eye, NEWTON_FIRST, 0.0)
        whole = step if whole is None else times(step, whole)
        if turn + 1 < NS_STEPS:
            current = times(times(step, current), step)
    return whole * scale_col


def join_hidden(first, second):
    fill = jnp.zeros((first.shape[0], FF), F32)
    first = jnp.concatenate([first, fill], 1)
    second = pltpu.roll(jnp.concatenate([second, fill], 1), FF_REAL, 1)
    return (first + second)[:, :WIDE]


def finish_kernel(
    gram, head_w, head_m, model_w, model_m, up_w, up_m, head_sum, model_sum, time_sum,
    narrow_in, wide_in, in_w_in, out_w_in, mlp_w_in, result, tokens_in, words_in,
    new_head, new_model, new_up, new_head_m, new_model_m, new_up_m, out_time,
    new_in_out, new_out_out, new_mlp_out, new_in_m_out, new_out_m_out, new_mlp_m_out, out_result,
    out_tokens, out_words,
    narrow, wide, in_w, out_w, mlp_w, low_result, tokens, words, block, new_in, new_out, new_mlp,
    new_out_m, new_mlp_m, loads, stores,
):
    fetched = []
    for i, (src, dst) in enumerate(
        (
            (narrow_in, narrow), (wide_in, wide), (in_w_in, in_w), (out_w_in, out_w), (mlp_w_in, mlp_w),
            (result, low_result), (tokens_in, tokens), (words_in, words),
        )
    ):
        fetched.append(pltpu.make_async_copy(src, dst, loads.at[i]))
        fetched[-1].start()
    copies = []

    def save(ref, out):
        copies.append(pltpu.make_async_copy(ref, out, stores.at[len(copies)]))
        copies[-1].start()

    out_time[...] = time_sum[...]
    value = MOMENTUM * head_m[...] + jnp.concatenate([head_sum[0, :10], head_sum[1, :10]], 1)
    new_head_m[...] = value
    new_head[...] = head_w[...] - RATE_VECTOR * value
    value = MOMENTUM * model_m[...] + model_sum[:11]
    new_model_m[...] = value
    new_model[...] = model_w[...] - RATE_VECTOR * value
    chips = [jnp.concatenate([head_sum[i, 10 + k : 11 + k] for k in range(6)], 1) for i in (0, 1)]
    value = join_hidden(*chips)
    for i in range(WIDE // 128):
        row = slice(i, i + 1)
        new_up_m[row] = MOMENTUM * up_m[row] + value[:, i * 128 : (i + 1) * 128]
    new_up[...] = up_w[...] - RATE_VECTOR * new_up_m[...]
    n, w = narrow.shape[0], wide.shape[0]
    factor = newton_factor(gram[...], n + w)
    for copy in fetched:
        copy.wait()
    save(low_result, out_result)
    for i, (src, dst) in enumerate(((tokens, out_tokens), (words, out_words))):
        for clip in (0, 1):
            block[2 * i + clip] = src[clip].astype(F32)
            save(block.at[2 * i + clip], dst.at[clip])
    turned = times(factor[:n, :n], narrow[...])
    for j in range(6):
        rows = slice(j * ROWS, (j + 1) * ROWS)
        save(narrow.at[rows], new_in_m_out.at[j])
        new_in[j] = in_w[j] * (1.0 - RATE_IN * DECAY) - RATE_IN * turned[rows]
    save(new_in, new_in_out)
    for j in range(2):
        rows = slice((6 + j) * ROWS, (7 + j) * ROWS)
        new_out_m[:, j, :] = narrow[rows]
        new_out[:, j, :] = out_w[:, j, :] * (1.0 - RATE_OUT * DECAY) - RATE_OUT * turned[rows]
    save(new_out_m, new_out_m_out)
    save(new_out, new_out_out)
    for j in range(2):
        new_mlp_m[:, j, :] = wide[j * ROWS : (j + 1) * ROWS]
    save(new_mlp_m, new_mlp_m_out)
    turned = times(factor[n:, n:], wide[...])
    for j in range(2):
        rows = slice(j * ROWS, (j + 1) * ROWS)
        new_mlp[:, j, :] = mlp_w[:, j, :] * (1.0 - RATE_MLP * DECAY) - RATE_MLP * turned[rows]
    save(new_mlp, new_mlp_out)
    for copy in copies:
        copy.wait()


def finish_step(small, large):
    sds = jax.ShapeDtypeStruct
    matrices = [sds((6, ROWS, 2 * HW), F32), sds((ROWS, 2, 2 * HW), F32), sds((ROWS, 2, WIDE), F32)]
    vectors = [sds((10, 2 * HW), F32), sds((11, D), F32), sds((WIDE // 128, 128), F32)]
    blocks = [sds((2, TOK, D), BF), sds((2, TOK, D), F32), sds((2, TOK, D), F32)]
    held = [pltpu.VMEM(v.shape, v.dtype) for v in large]
    news = [pltpu.VMEM(v.shape, F32) for v in matrices + matrices[1:]]
    return pl.pallas_call(
        finish_kernel,
        out_shape=vectors + vectors + [sds((6, 2, D), F32)] + matrices + matrices + blocks,
        in_specs=[VM] * len(small) + [HB] * len(large),
        out_specs=[VM] * 7 + [HB] * 9,
        scratch_shapes=[
            *held, pltpu.VMEM((4, TOK, D), F32), *news, pltpu.SemaphoreType.DMA((8,)),
            pltpu.SemaphoreType.DMA((16,)),
        ],
        compiler_params=pltpu.CompilerParams(vmem_limit_bytes=VMEM_LIMIT),
        name="finish",
    )(*small, *large)


def rope_rates():
    pair = np.arange(HEAD // 2)
    side = HEAD // 6
    frame = (HEAD - 4 * side) // 2
    part = (pair >= frame).astype(np.int32) + (pair >= frame + side)
    offset = np.array([0, frame, frame + side])[part]
    extent = np.array([2 * frame, 2 * side, 2 * side])[part]
    rate = np.exp((pair - offset) * (-2.0 * math.log(10000.0)) / extent).astype(np.float32)
    rates = np.zeros((8, HEAD), np.float32)
    for component in range(3):
        rates[component] = np.tile(np.where(part == component, rate, 0.0), 2)
    return jnp.asarray(rates)


def plain_norm(values):
    centred = values - jnp.mean(values, -1, keepdims=True)
    inverse = lax.rsqrt(jnp.mean(centred * centred, -1, keepdims=True) + NORM_EPSILON)
    return (centred * inverse, inverse)


def norm_back(grads, normed, inverse):
    return inverse * (
        grads
        - jnp.mean(grads, -1, keepdims=True)
        - normed * jnp.mean(grads * normed, -1, keepdims=True)
    )


def product(left, right):
    return jnp.dot(left, right, preferred_element_type=F32)


def contract_last(left, right):
    return lax.dot_general(left, right, (((1,), (1,)), ((), ())), preferred_element_type=F32)


def contract_rows(left, right):
    return lax.dot_general(left, right, (((0,), (0,)), ((), ())), preferred_element_type=F32)


def body(
    tokens, text, time_embedding, positions, cotangent, attn_in, attn_out, mlp, head_vectors,
    model_vectors, up_bias, attn_in_moment, attn_out_moment, mlp_moment, head_moment, model_moment,
    up_moment,
):
    swap = lambda v: v.transpose(1, 0, 2)
    (
        w_attn, w_up, w_down, cot_all, heads, vectors, tab_all, input_one, input_three, input_mlp, query_lin, key_lin,
        query_two_lin, key_two_lin, inv, query_rot, key_rot, value_low, query_two, key_two, value_two,
        mixed_low, mixed_two_low, branch_one, after_one, after_two, tok_all, txt_all,
    ) = forward(
        swap(attn_in), attn_out, mlp, tokens, text, cotangent, positions, rope_rates(),
        swap(time_embedding), model_vectors, head_vectors,
    )
    low_two, grad_after, sums, up_sum, result, *owned = mlp_pass(
        input_mlp, cot_all, w_up, w_down, after_two, vectors, up_bias.reshape(-1, 128)
    )
    out_result, out_tokens, out_words, time_sums, model_sums, head_totals, narrow, wide, gram = backward(
        [
            w_attn, low_two, after_one, branch_one, query_lin, key_lin, query_two_lin, key_two_lin,
            query_rot, key_rot, value_low, query_two, key_two, value_two, mixed_low, mixed_two_low,
            txt_all, input_three, input_one, tok_all, grad_after, tab_all, inv, result,
        ],
        [
            vectors, heads, sums, up_sum, *owned, swap(attn_in_moment), attn_out_moment, mlp_moment,
        ],
    )
    (
        new_head, new_model, new_up, new_head_m, new_model_m, new_up_m, out_time,
        new_in, new_out, new_mlp, new_in_m, new_out_m, new_mlp_m, out_result, out_tokens, out_words,
    ) = finish_step(
        [
            gram, head_vectors, head_moment, model_vectors, model_moment, up_bias.reshape(-1, 128),
            up_moment.reshape(-1, 128), head_totals, model_sums, time_sums,
        ],
        [narrow, wide, swap(attn_in), attn_out, mlp, out_result, out_tokens, out_words],
    )
    return (
        out_result, out_tokens, out_words, swap(out_time), swap(new_in), new_out, new_mlp,
        swap(new_in_m), new_out_m, new_mlp_m, new_head, new_model, new_up.reshape(-1), new_head_m,
        new_model_m, new_up_m.reshape(-1),
    )


def solution(mesh):
    clip = P("fsdp", "ctx", None)
    whole = P("fsdp", None, None)
    matrix = P(("fsdp", "ctx"), None, "tp")
    in_specs = (
        clip, clip, whole, P(None, "fsdp", "ctx"), clip, matrix, matrix, matrix, P(None, "tp"), P(),
        P("tp"), matrix, matrix, matrix, P(None, "tp"), P(), P("tp"),
    )
    out_specs = (
        clip, clip, clip, whole, matrix, matrix, matrix, matrix, matrix, matrix, P(None, "tp"), P(),
        P("tp"), P(None, "tp"), P(), P("tp"),
    )
    return jax.shard_map(body, mesh=mesh, in_specs=in_specs, out_specs=out_specs, check_vma=False)
```
